32 devices in a mesh: groups: 2 (over y), loop: 4 (over z), heads: 2 (over x), pair: 2 (over core).
Axes of the slice: x: 2, y: 2, z: 4, core: 2. Of those that a mesh axis runs over, the one named last changes fastest.
Arguments:
- queries: bfloat16 [5120, 2048], P(('groups', 'loop'), ('heads', 'pair')), parts along dimension 0, may hold values from -96 to 96
- suffix_kv: bfloat16 [5120, 2, 256], P(('groups', 'loop'), 'heads'), parts along dimension 0, may hold values from -4 to 4
- prompt_kv: bfloat16 [2048, 2, 256], P(('groups', 'loop'), 'heads'), parts along dimension 0, may hold values from -4 to 4
- lengths: int32 [16], P('groups'), parts along dimension 0, may hold values from 128 to 320, as said below
Outputs:
- attended: bfloat16 [5120, 2048], P(('groups', 'loop'), ('heads', 'pair')), parts along dimension 0
The draws below stay inside these ranges and needn't reach their ends.
There are 2 independent parts, one for each index of `groups`. The reference program is written for one: setup_inputs(seed, part) draws one part's arguments, and reference() takes and returns one part's arrays. A program takes and returns all parts, laid end to end along the dimension named above; each array names one. Nothing has to cross between parts.
Inputs may be any that keep to these rules, and one draw needn't show every extreme that they name: Each agent's suffix has 128 to 320 tokens, and agents d * 2 to d * 2 + 1 belong to loop index d, so their lengths add up to at most 640 slots.
All inputs are finite; a program needn't handle non-finite values.
Results may differ from the reference program's by a relative error of at most 0.0065.
Values may be sent and summed in bfloat16 or wider, within the bound.
No kernel may reach another device: no remote copies, remote signals or barrier semaphores. Data moves between devices by JAX's collectives and lax.ppermute only.
A program may use at most 64 MiB of HBM per device.

```python
import math
import jax
import jax.numpy as jnp
from jax import lax

HD = 128
QPK = 8
AG_DEV = 2
MINLEN = 128
MAXLEN = 320
KVH = 2
QH = 16
ROWS = 640
NTOT = 2560
AGENTS = 8
PROMPT = 1024
N_LOOP = 4


def prompt_keys(key):
    keys_drawn = jax.random.truncated_normal(jax.random.fold_in(key, 11), -4.0, 4.0, (PROMPT, KVH, HD), jnp.float32)
    return keys_drawn


def draw_prompt_kv(key, part):
    keys_drawn = prompt_keys(key)
    values_drawn = jax.random.truncated_normal(jax.random.fold_in(key, 12), -4.0, 4.0, (PROMPT, KVH, HD), jnp.float32)
    return jnp.concatenate([keys_drawn, values_drawn], axis=2).astype(jnp.bfloat16)


def draw_queries(key, part):
    drawn_queries = 2.5 * jax.random.truncated_normal(jax.random.fold_in(key, 13), -4.0, 4.0, (NTOT, QH * HD), jnp.float32)
    return drawn_queries.astype(jnp.bfloat16)


def draw_lengths(key, part):
    loop_count = NTOT // ROWS
    heavy_flag = jax.random.randint(jax.random.fold_in(key, 31), (loop_count,), 0, 4) == 0
    heavy_flag = heavy_flag.at[0].set(True).at[1].set(False)
    heavy_len = jax.random.randint(jax.random.fold_in(key, 32), (loop_count, AG_DEV), MAXLEN * 4 // 5, MAXLEN + 1)
    light_len = jax.random.randint(jax.random.fold_in(key, 33), (loop_count, AG_DEV), MINLEN, MAXLEN // 2 + 1)
    agent_lengths = jnp.where(heavy_flag[:, None], heavy_len, light_len)
    agent_lengths = agent_lengths.at[0, :].set(MAXLEN).at[1, 0].set(MINLEN)
    return agent_lengths.reshape(AGENTS).astype(jnp.int32)


def levels(key, dims, shards, low, top_value):
    def one(dim, parts):
        heights = jax.random.uniform(jax.random.fold_in(jax.random.fold_in(key, 6), dim), (parts,), jnp.float32, low / len(shards), top_value / len(shards))
        return jnp.repeat(jnp.exp(heights), dims[dim] // parts).reshape((-1,) + (1,) * (len(dims) - dim - 1))

    level = one(*shards[0])
    for cut in shards[1:]:
        level = level * one(*cut)
    return level


def scatter_about(stream_key, dims, width, limit, cuts=(), kind=jnp.bfloat16):
    values = jax.random.normal(stream_key, dims, jnp.float32) * width
    if len(cuts) > 0:
        values = levels(stream_key, dims, cuts, -0.22, 0.18) * values
    return jnp.clip(values, min=-limit, max=limit).astype(kind)


def setup_inputs(seed: int = 0, part: int = 0) -> dict:
    splits = jax.random.split(jax.random.key(seed), 5)
    own_keys = jax.random.split(jax.random.fold_in(splits[4], part), 5)
    return {
        "queries": draw_queries(jax.random.fold_in(jax.random.fold_in(splits[4], part), 71), part),
        "suffix_kv": scatter_about(own_keys[1], (NTOT, KVH, 2 * HD), 1.0, 4.0, ((0, 4), (1, 2))),
        "prompt_kv": draw_prompt_kv(jax.random.fold_in(jax.random.fold_in(splits[4], part), 71), part),
        "lengths": draw_lengths(jax.random.fold_in(jax.random.fold_in(splits[4], part), 71), part),
    }


def reference(queries, suffix_kv, prompt_kv, lengths):
    score_scale = 1.0 / math.sqrt(HD)
    positions = jnp.arange(ROWS, dtype=jnp.int32)

    def one_device(device):
        row_start = (device * ROWS).astype(jnp.int32)
        query_rows = lax.dynamic_slice_in_dim(queries, row_start, ROWS, 0)
        suffix_rows = lax.dynamic_slice_in_dim(suffix_kv, row_start, ROWS, 0)
        agent_lengths = lax.dynamic_slice_in_dim(lengths, (device * AG_DEV).astype(jnp.int32), AG_DEV, 0)
        agent_ends = jnp.cumsum(agent_lengths)
        agent_of = lax.optimization_barrier(jnp.sum((positions[:, None] >= agent_ends[None, :]).astype(jnp.int32), axis=1))
        live_rows = positions < agent_ends[-1]
        allowed = (agent_of[:, None] == agent_of[None, :]) & (positions[None, :] <= positions[:, None]) & live_rows[:, None]
        allowed = jnp.repeat(allowed, QPK, axis=0)
        live_rep = jnp.repeat(live_rows, QPK)

        def one_head(key_head):
            query_head = lax.dynamic_slice_in_dim(query_rows, (key_head * QPK * HD).astype(jnp.int32), QPK * HD, 1).reshape(ROWS * QPK, HD)
            prompt_head = lax.dynamic_index_in_dim(prompt_kv, key_head, 1, keepdims=False)
            suffix_head = lax.dynamic_index_in_dim(suffix_rows, key_head, 1, keepdims=False)
            prompt_scores = jnp.dot(query_head, prompt_head[:, :HD].T, preferred_element_type=jnp.float32) * score_scale
            suffix_scores = jnp.dot(query_head, suffix_head[:, :HD].T, preferred_element_type=jnp.float32) * score_scale
            suffix_scores = jnp.where(allowed, suffix_scores, -jnp.inf)
            row_best = jnp.maximum(lax.optimization_barrier(jnp.max(prompt_scores, axis=1)), lax.optimization_barrier(jnp.max(suffix_scores, axis=1)))
            prompt_weights = jnp.exp(prompt_scores - row_best[:, None])
            suffix_weights = jnp.where(allowed, jnp.exp(suffix_scores - row_best[:, None]), 0.0)
            row_total = lax.optimization_barrier(jnp.sum(prompt_weights, axis=1)) + lax.optimization_barrier(jnp.sum(suffix_weights, axis=1))
            weighted_sum = jnp.dot(prompt_weights.astype(jnp.bfloat16), prompt_head[:, HD:], preferred_element_type=jnp.float32)
            weighted_sum = weighted_sum + jnp.dot(suffix_weights.astype(jnp.bfloat16), suffix_head[:, HD:], preferred_element_type=jnp.float32)
            safe_total = jnp.where(live_rep, row_total, 1.0)
            result = jnp.where(live_rep[:, None], weighted_sum / safe_total[:, None], 0.0)
            return result.reshape(ROWS, QPK * HD)
        per_head = lax.map(one_head, jnp.arange(KVH, dtype=jnp.int32))
        return jnp.transpose(per_head, (1, 0, 2)).reshape(ROWS, KVH * QPK * HD).astype(jnp.bfloat16)
    outputs = lax.map(one_device, jnp.arange(N_LOOP, dtype=jnp.int32))
    return outputs.reshape(N_LOOP * ROWS, KVH * QPK * HD)
```

```python
import functools
import math

import jax
import jax.numpy as jnp
from jax import lax
from jax.experimental import pallas as pl
from jax.experimental.pallas import tpu as pltpu
from jax.sharding import PartitionSpec as P

HD = 128
AG_DEV = 2
MAXLEN = 320
BLK = 128

masked_score = -1e30
total_limit = 2.0**100
score_scale = math.log2(math.e) / math.sqrt(HD)


def scores_of(query_rows, key_rows):
    return lax.dot_general(
        query_rows, key_rows, (((1,), (1,)), ((), ())), preferred_element_type=jnp.float32
    )


def with_ones(value_rows):
    return jnp.concatenate([value_rows, jnp.ones_like(value_rows)], axis=1)


def stacked(ref, rows, head_count):
    return jnp.concatenate([ref[rows, h * HD : (h + 1) * HD] for h in range(head_count)], axis=0)


def unstack(ref, rows, head_count, value):
    count = value.shape[0] // head_count
    for h in range(head_count):
        ref[rows, h * HD : (h + 1) * HD] = value[h * count : (h + 1) * count]


def widen(row_value, width):
    return jnp.concatenate([row_value] * (width // HD), axis=1)


def local_stage(lengths_ref, query_ref, suffix_ref, own_ref, best_ref, total_ref, sum_ref):
    rows_all = query_ref.shape[0]
    heads = query_ref.shape[1] // HD
    position = lax.axis_index("loop")
    own_keys = own_ref[:, :HD]
    own_values = with_ones(own_ref[:, HD:])
    window = BLK * ((MAXLEN + BLK - 2) // BLK) + BLK
    for block in range(rows_all // BLK):
        stop = (block + 1) * BLK
        start = max(0, stop - window)
        rows = slice(block * BLK, stop)
        row_at = block * BLK + lax.broadcasted_iota(jnp.int32, (BLK, stop - start), 0)
        key_at = start + lax.broadcasted_iota(jnp.int32, (BLK, stop - start), 1)
        first = jnp.zeros_like(row_at)
        agent_end = 0
        for agent in range(AG_DEV):
            agent_end = agent_end + lengths_ref[position * AG_DEV + agent]
            first = jnp.where(row_at >= agent_end, agent_end, first)
        allowed = (key_at <= row_at) & (key_at >= first)
        queries = stacked(query_ref, rows, heads)
        suffix_values = with_ones(suffix_ref[start:stop, HD:])
        own_scores = scores_of(queries, own_keys) * score_scale
        suffix_scores = scores_of(queries, suffix_ref[start:stop, :HD]) * score_scale
        suffix_scores = jnp.where(
            jnp.concatenate([allowed] * heads, axis=0), suffix_scores, masked_score
        )
        best = jnp.maximum(
            jnp.max(own_scores, axis=1, keepdims=True),
            jnp.max(suffix_scores, axis=1, keepdims=True),
        )
        own_weights = jnp.exp2(own_scores - best).astype(jnp.bfloat16)
        suffix_weights = jnp.exp2(suffix_scores - best).astype(jnp.bfloat16)
        result = jnp.dot(own_weights, own_values, preferred_element_type=jnp.float32)
        result = result + jnp.dot(
            suffix_weights, suffix_values, preferred_element_type=jnp.float32
        )
        unstack(best_ref, rows, heads, jnp.broadcast_to(best, (heads * BLK, HD)))
        unstack(sum_ref, rows, heads, result[:, :HD])
        unstack(total_ref, rows, heads, result[:, HD:])


def remote_stage(shard_count, *refs):
    lengths_ref, query_ref, best_ref, total_ref, sum_ref = refs[:5]
    shard_refs = refs[5 : 5 + shard_count]
    out_ref = refs[5 + shard_count]
    rows_all = query_ref.shape[0]
    heads = query_ref.shape[1] // HD
    position = lax.axis_index("loop")
    live = 0
    for agent in range(AG_DEV):
        live = live + lengths_ref[position * AG_DEV + agent]

    def finish(rows, first_row, total, weighted):
        row_at = first_row + lax.broadcasted_iota(jnp.int32, (BLK, HD), 0)
        is_live = jnp.concatenate([row_at < live] * heads, axis=0)
        unstack(
            out_ref, rows, heads, jnp.where(is_live, weighted / total, 0.0).astype(jnp.bfloat16)
        )

    trusted = jnp.full((8, HD), True)
    keys = [ref[:, :HD] for ref in shard_refs]
    values = [with_ones(ref[:, HD:]) for ref in shard_refs]
    for block in range(rows_all // BLK):
        rows = slice(block * BLK, (block + 1) * BLK)
        queries = stacked(query_ref, rows, heads)
        best = stacked(best_ref, rows, heads)
        weighted = stacked(sum_ref, rows, heads)
        total = stacked(total_ref, rows, heads)
        for key_rows, value_rows in zip(keys, values):
            scores = scores_of(queries, key_rows) * score_scale
            weights = jnp.exp2(scores - widen(best, scores.shape[1])).astype(jnp.bfloat16)
            result = jnp.dot(weights, value_rows, preferred_element_type=jnp.float32)
            weighted = weighted + result[:, :HD]
            total = total + result[:, HD:]
        good = (total < total_limit).reshape(heads * BLK // 8, 8, HD)
        trusted = trusted & jnp.all(good, axis=0)
        finish(rows, block * BLK, total, weighted)

    @pl.when(jnp.logical_not(jnp.all(trusted)))
    def exact_maximum():
        def visit(block, unused):
            first_row = pl.multiple_of(block * BLK, BLK)
            rows = pl.ds(first_row, BLK)
            queries = stacked(query_ref, rows, heads)
            best = stacked(best_ref, rows, heads)
            weighted = stacked(sum_ref, rows, heads)
            total = stacked(total_ref, rows, heads)
            for key_rows, value_rows in zip(keys, values):
                scores = scores_of(queries, key_rows) * score_scale
                new_best = jnp.maximum(best, jnp.max(scores, axis=1, keepdims=True))
                factor = jnp.exp2(best - new_best)
                weights = jnp.exp2(scores - widen(new_best, scores.shape[1]))
                result = jnp.dot(
                    weights.astype(jnp.bfloat16), value_rows, preferred_element_type=jnp.float32
                )
                weighted = weighted * factor + result[:, :HD]
                total = total * factor + result[:, HD:]
                best = new_best
            finish(rows, first_row, total, weighted)
            return unused

        lax.fori_loop(0, rows_all // BLK, visit, 0)


def shards(queries, suffix_kv, prompt_kv, lengths):
    slots, width = queries.shape
    loop_size = lax.axis_size("loop")
    own = prompt_kv[:, 0, :]
    suffix = suffix_kv[:, 0, :]
    shard_rows = own.shape[0]
    arrived = []
    for step in range(1, loop_size):
        pairs = [(i, (i + step) % loop_size) for i in range(loop_size)]
        arrived.append(lax.ppermute(own, "loop", pairs))
    in_smem = pl.BlockSpec(memory_space=pltpu.SMEM)
    in_vmem = pl.BlockSpec(memory_space=pltpu.VMEM)
    state = jax.ShapeDtypeStruct((slots, width), jnp.float32)
    heads = width // HD
    local_pairs = slots * heads * (shard_rows + MAXLEN)
    best, total, weighted = pl.pallas_call(
        local_stage,
        name="local_stage",
        out_shape=[state] * 3,
        in_specs=[in_smem] + [in_vmem] * 3,
        out_specs=[in_vmem] * 3,
        compiler_params=pltpu.CompilerParams(vmem_limit_bytes=24 * 2**20),
        cost_estimate=pl.CostEstimate(
            flops=local_pairs * HD * 4,
            bytes_accessed=slots * width * 14,
            transcendentals=local_pairs,
        ),
    )(lengths, queries, suffix, own)
    remote_pairs = slots * heads * shard_rows * (loop_size - 1)
    return pl.pallas_call(
        functools.partial(remote_stage, loop_size - 1),
        name="remote_stage",
        out_shape=jax.ShapeDtypeStruct((slots, width), jnp.bfloat16),
        in_specs=[in_smem] + [in_vmem] * (3 + loop_size),
        out_specs=in_vmem,
        compiler_params=pltpu.CompilerParams(vmem_limit_bytes=32 * 2**20),
        cost_estimate=pl.CostEstimate(
            flops=remote_pairs * HD * 4,
            bytes_accessed=slots * width * 16,
            transcendentals=remote_pairs,
        ),
    )(lengths, queries, best, total, weighted, *arrived)


def solution(mesh):
    placed = (
        P(("groups", "loop"), ("heads", "pair")),
        P(("groups", "loop"), "heads", None),
        P(("groups", "loop"), "heads", None),
        P("groups"),
    )
    return jax.shard_map(
        shards,
        mesh=mesh,
        in_specs=placed,
        out_specs=P(("groups", "loop"), ("heads", "pair")),
        check_vma=False,
    )
```

```python
import functools
import math

import jax
import jax.numpy as jnp
from jax import lax
from jax.experimental import pallas as pl
from jax.experimental.pallas import tpu as pltpu
from jax.sharding import PartitionSpec as P

HD = 128
AG_DEV = 2
MAXLEN = 320
BLK = 128

masked_score = -1e30
empty_best = 1e30
total_limit = 2.0**100
score_scale = math.log2(math.e) / math.sqrt(HD)


def scores_of(query_rows, key_rows):
    return (
        lax.dot_general(
            query_rows, key_rows, (((1,), (1,)), ((), ())), preferred_element_type=jnp.float32
        )
        * score_scale
    )


def with_ones(value_rows):
    return jnp.concatenate([value_rows, jnp.ones_like(value_rows)], axis=1)


def stacked(ref, rows, head_count):
    return jnp.concatenate([ref[rows, h * HD : (h + 1) * HD] for h in range(head_count)], axis=0)


def unstack(ref, rows, head_count, value):
    count = value.shape[0] // head_count
    for h in range(head_count):
        ref[rows, h * HD : (h + 1) * HD] = value[h * count : (h + 1) * count]


def widen(row_value, width):
    return jnp.concatenate([row_value] * (width // HD), axis=1)


def local_stage(
    lengths_hbm,
    query_hbm,
    suffix_hbm,
    own_hbm,
    best_ref,
    total_ref,
    sum_ref,
    query_ref,
    lengths_ref,
    suffix_ref,
    own_ref,
    whole_sems,
    block_sems,
):
    rows_all = query_ref.shape[0]
    heads = query_ref.shape[1] // HD
    blocks = rows_all // BLK
    whole = [
        pltpu.make_async_copy(source, target, whole_sems.at[i])
        for i, (source, target) in enumerate(
            [(lengths_hbm, lengths_ref), (own_hbm, own_ref), (suffix_hbm, suffix_ref)]
        )
    ]
    pieces = [
        pltpu.make_async_copy(
            query_hbm.at[pl.ds(block * BLK, BLK)],
            query_ref.at[pl.ds(block * BLK, BLK)],
            block_sems.at[block],
        )
        for block in range(blocks)
    ]
    for copy in whole + pieces:
        copy.start()
    for copy in whole:
        copy.wait()
    position = lax.axis_index("loop")
    own_keys = own_ref[:, :HD]
    own_values = with_ones(own_ref[:, HD:])
    window = BLK * ((MAXLEN + BLK - 2) // BLK) + BLK
    for block in range(blocks):
        stop = (block + 1) * BLK
        start = max(0, stop - window)
        rows = slice(block * BLK, stop)
        row_at = block * BLK + lax.broadcasted_iota(jnp.int32, (BLK, stop - start), 0)
        key_at = start + lax.broadcasted_iota(jnp.int32, (BLK, stop - start), 1)
        first = jnp.zeros_like(row_at)
        agent_end = 0
        for agent in range(AG_DEV):
            agent_end = agent_end + lengths_ref[position * AG_DEV + agent]
            first = jnp.where(row_at >= agent_end, agent_end, first)
        allowed = (key_at <= row_at) & (key_at >= first)
        pieces[block].wait()
        queries = stacked(query_ref, rows, heads)
        own_scores = scores_of(queries, own_keys)
        suffix_scores = jnp.where(
            jnp.concatenate([allowed] * heads, axis=0),
            scores_of(queries, suffix_ref[start:stop, :HD]),
            masked_score,
        )
        best = jnp.maximum(
            jnp.max(own_scores, axis=1, keepdims=True),
            jnp.max(suffix_scores, axis=1, keepdims=True),
        )
        own_weights = jnp.exp2(own_scores - best).astype(jnp.bfloat16)
        suffix_weights = jnp.exp2(suffix_scores - best).astype(jnp.bfloat16)
        result = jnp.dot(own_weights, own_values, preferred_element_type=jnp.float32)
        result = result + jnp.dot(
            suffix_weights,
            with_ones(suffix_ref[start:stop, HD:]),
            preferred_element_type=jnp.float32,
        )
        row_at = block * BLK + lax.broadcasted_iota(jnp.int32, (BLK, HD), 0)
        live = jnp.concatenate([row_at < agent_end] * heads, axis=0)
        unstack(best_ref, rows, heads, jnp.where(live, best, empty_best))
        unstack(sum_ref, rows, heads, jnp.where(live, result[:, :HD], 0.0))
        unstack(total_ref, rows, heads, jnp.where(live, result[:, HD:], 1.0))


def add_pieces(query_ref, best_ref, rows, heads, pieces, total, weighted):
    queries = stacked(query_ref, rows, heads)
    best = stacked(best_ref, rows, heads)
    for key_rows, value_rows in pieces:
        scores = scores_of(queries, key_rows)
        weights = jnp.exp2(scores - widen(best, scores.shape[1])).astype(jnp.bfloat16)
        result = jnp.dot(weights, value_rows, preferred_element_type=jnp.float32)
        weighted = weighted + result[:, :HD]
        total = total + result[:, HD:]
    return total, weighted


def loaded(piece_refs):
    return [(ref[:, :HD], with_ones(ref[:, HD:])) for ref in piece_refs]


def first_half_stage(*refs):
    query_ref, best_ref, total_ref, sum_ref = refs[:4]
    piece_refs = refs[4:-2]
    total_out, sum_out = refs[-2:]
    heads = query_ref.shape[1] // HD
    pieces = loaded(piece_refs)
    for block in range(query_ref.shape[0] // BLK):
        rows = slice(block * BLK, (block + 1) * BLK)
        total, weighted = add_pieces(
            query_ref,
            best_ref,
            rows,
            heads,
            pieces,
            stacked(total_ref, rows, heads),
            stacked(sum_ref, rows, heads),
        )
        unstack(total_out, rows, heads, total)
        unstack(sum_out, rows, heads, weighted)


def second_half_stage(count, *refs):
    query_ref, best_ref, old_total_ref, old_sum_ref, total_ref, sum_ref = refs[:6]
    early_refs = refs[6 : 6 + count]
    late_refs = refs[6 + count : 6 + 2 * count]
    out_hbm, out_ref, out_sems = refs[6 + 2 * count :]
    heads = query_ref.shape[1] // HD
    blocks = query_ref.shape[0] // BLK

    def out_copy(block):
        rows = pl.ds(block * BLK, BLK)
        return pltpu.make_async_copy(out_ref.at[rows], out_hbm.at[rows], out_sems.at[block])

    def finish(rows, total, weighted):
        unstack(out_ref, rows, heads, (weighted / total).astype(jnp.bfloat16))

    trusted = jnp.full((8, HD), True)
    late = loaded(late_refs)
    for block in range(blocks):
        rows = slice(block * BLK, (block + 1) * BLK)
        total, weighted = add_pieces(
            query_ref,
            best_ref,
            rows,
            heads,
            late,
            stacked(total_ref, rows, heads),
            stacked(sum_ref, rows, heads),
        )
        good = (total < total_limit).reshape(heads * BLK // 8, 8, HD)
        trusted = trusted & jnp.all(good, axis=0)
        finish(rows, total, weighted)
        out_copy(block).start()
    for block in range(blocks):
        out_copy(block).wait()

    @pl.when(jnp.logical_not(jnp.all(trusted)))
    def exact_maximum():
        def visit(block, unused):
            rows = pl.ds(pl.multiple_of(block * BLK, BLK), BLK)
            queries = stacked(query_ref, rows, heads)
            best = stacked(best_ref, rows, heads)
            weighted = stacked(old_sum_ref, rows, heads)
            total = stacked(old_total_ref, rows, heads)
            for key_rows, value_rows in loaded(early_refs + late_refs):
                scores = scores_of(queries, key_rows)
                new_best = jnp.maximum(best, jnp.max(scores, axis=1, keepdims=True))
                factor = jnp.exp2(best - new_best)
                weights = jnp.exp2(scores - widen(new_best, scores.shape[1]))
                result = jnp.dot(
                    weights.astype(jnp.bfloat16), value_rows, preferred_element_type=jnp.float32
                )
                weighted = weighted * factor + result[:, :HD]
                total = total * factor + result[:, HD:]
                best = new_best
            finish(rows, total, weighted)
            copy = out_copy(block)
            copy.start()
            copy.wait()
            return unused

        lax.fori_loop(0, blocks, visit, 0)


def shards(queries, suffix_kv, prompt_kv, lengths):
    slots, width = queries.shape
    heads = width // HD
    loop_size = lax.axis_size("loop")
    pair_size = lax.axis_size("pair")
    own = prompt_kv[:, 0, :]
    suffix = suffix_kv[:, 0, :]
    shard_rows = own.shape[0]
    half_rows = shard_rows // pair_size
    half = lax.dynamic_slice_in_dim(own, lax.axis_index("pair") * half_rows, half_rows, 0)
    early, late = [], []
    for step in range(1, loop_size):
        around = [(i, (i + step) % loop_size) for i in range(loop_size)]
        early.append(lax.ppermute(half, "loop", around))
    in_hbm = pl.BlockSpec(memory_space=pltpu.HBM)
    in_vmem = pl.BlockSpec(memory_space=pltpu.VMEM)
    state = jax.ShapeDtypeStruct((slots, width), jnp.float32)

    def cost(keys):
        return pl.CostEstimate(
            flops=slots * heads * keys * HD * 4,
            bytes_accessed=slots * width * 14,
            transcendentals=slots * heads * keys,
        )

    best, total, weighted, queries = pl.pallas_call(
        local_stage,
        name="local_stage",
        out_shape=[state] * 3 + [jax.ShapeDtypeStruct((slots, width), queries.dtype)],
        in_specs=[in_hbm] * 4,
        out_specs=[in_vmem] * 4,
        scratch_shapes=[
            pltpu.SMEM(lengths.shape, lengths.dtype),
            pltpu.VMEM(suffix.shape, suffix.dtype),
            pltpu.VMEM(own.shape, own.dtype),
            pltpu.SemaphoreType.DMA((3,)),
            pltpu.SemaphoreType.DMA((slots // BLK,)),
        ],
        compiler_params=pltpu.CompilerParams(vmem_limit_bytes=24 * 2**20),
        cost_estimate=cost(shard_rows + MAXLEN),
    )(*(pltpu.with_memory_space_constraint(x, pltpu.HBM) for x in (lengths, queries, suffix, own)))
    early, best = lax.optimization_barrier((early, best))
    for piece in early:
        for turn in range(1, pair_size):
            across = [(i, (i + turn) % pair_size) for i in range(pair_size)]
            late.append(lax.ppermute(piece, "pair", across))
    early_total, early_weighted = pl.pallas_call(
        first_half_stage,
        name="first_half_stage",
        out_shape=[state] * 2,
        in_specs=[in_vmem] * (4 + len(early)),
        out_specs=[in_vmem] * 2,
        compiler_params=pltpu.CompilerParams(vmem_limit_bytes=24 * 2**20),
        cost_estimate=cost(half_rows * len(early)),
    )(queries, best, total, weighted, *early)
    return pl.pallas_call(
        functools.partial(second_half_stage, len(early)),
        name="second_half_stage",
        out_shape=jax.ShapeDtypeStruct((slots, width), jnp.bfloat16),
        in_specs=[in_vmem] * (6 + len(early) + len(late)),
        out_specs=in_hbm,
        scratch_shapes=[
            pltpu.VMEM((slots, width), jnp.bfloat16),
            pltpu.SemaphoreType.DMA((slots // BLK,)),
        ],
        compiler_params=pltpu.CompilerParams(vmem_limit_bytes=24 * 2**20),
        cost_estimate=cost(half_rows * len(late)),
    )(queries, best, total, weighted, early_total, early_weighted, *early, *late)


def solution(mesh):
    placed = (
        P(("groups", "loop"), ("heads", "pair")),
        P(("groups", "loop"), "heads", None),
        P(("groups", "loop"), "heads", None),
        P("groups"),
    )
    return jax.shard_map(
        shards,
        mesh=mesh,
        in_specs=placed,
        out_specs=P(("groups", "loop"), ("heads", "pair")),
        check_vma=False,
    )
```

```python
import functools
import math

import jax
import jax.numpy as jnp
from jax import lax
from jax.experimental import pallas as pl
from jax.experimental.pallas import tpu as pltpu
from jax.sharding import PartitionSpec as P

HD = 128
AG_DEV = 2
MAXLEN = 320
BLK = 128

masked_score = -1e30
empty_best = 1e30
total_limit = 2.0**100
score_scale = math.log2(math.e) / math.sqrt(HD)


def scores_of(query_rows, key_rows):
    return (
        lax.dot_general(
            query_rows, key_rows, (((1,), (1,)), ((), ())), preferred_element_type=jnp.float32
        )
        * score_scale
    )


def with_ones(value_rows):
    return jnp.concatenate([value_rows, jnp.ones_like(value_rows)], axis=1)


def stacked(ref, rows, head_count):
    return jnp.concatenate([ref[rows, h * HD : (h + 1) * HD] for h in range(head_count)], axis=0)


def unstack(ref, rows, head_count, value):
    count = value.shape[0] // head_count
    for h in range(head_count):
        ref[rows, h * HD : (h + 1) * HD] = value[h * count : (h + 1) * count]


def widen(row_value, width):
    return jnp.concatenate([row_value] * (width // HD), axis=1)


def local_stage(
    lengths_hbm,
    query_hbm,
    suffix_hbm,
    own_hbm,
    best_ref,
    total_ref,
    sum_ref,
    query_ref,
    lengths_ref,
    suffix_ref,
    own_ref,
    whole_sems,
    block_sems,
):
    rows_all = query_ref.shape[0]
    heads = query_ref.shape[1] // HD
    blocks = rows_all // BLK
    whole = [
        pltpu.make_async_copy(source, target, whole_sems.at[i])
        for i, (source, target) in enumerate(
            [(lengths_hbm, lengths_ref), (own_hbm, own_ref), (suffix_hbm, suffix_ref)]
        )
    ]
    pieces = [
        pltpu.make_async_copy(
            query_hbm.at[pl.ds(block * BLK, BLK)],
            query_ref.at[pl.ds(block * BLK, BLK)],
            block_sems.at[block],
        )
        for block in range(blocks)
    ]
    for copy in whole + pieces:
        copy.start()
    for copy in whole + pieces:
        copy.wait()
    position = lax.axis_index("loop")
    own_keys = own_ref[:, :HD]
    own_values = with_ones(own_ref[:, HD:])
    window = BLK * ((MAXLEN + BLK - 2) // BLK) + BLK
    for block in range(blocks):
        stop = (block + 1) * BLK
        start = max(0, stop - window)
        rows = slice(block * BLK, stop)
        row_at = block * BLK + lax.broadcasted_iota(jnp.int32, (BLK, stop - start), 0)
        key_at = start + lax.broadcasted_iota(jnp.int32, (BLK, stop - start), 1)
        first = jnp.zeros_like(row_at)
        agent_end = 0
        for agent in range(AG_DEV):
            agent_end = agent_end + lengths_ref[position * AG_DEV + agent]
            first = jnp.where(row_at >= agent_end, agent_end, first)
        allowed = (key_at <= row_at) & (key_at >= first)
        queries = stacked(query_ref, rows, heads)
        own_scores = scores_of(queries, own_keys)
        suffix_scores = jnp.where(
            jnp.concatenate([allowed] * heads, axis=0),
            scores_of(queries, suffix_ref[start:stop, :HD]),
            masked_score,
        )
        best = jnp.maximum(
            jnp.max(own_scores, axis=1, keepdims=True),
            jnp.max(suffix_scores, axis=1, keepdims=True),
        )
        own_weights = jnp.exp2(own_scores - best).astype(jnp.bfloat16)
        suffix_weights = jnp.exp2(suffix_scores - best).astype(jnp.bfloat16)
        result = jnp.dot(own_weights, own_values, preferred_element_type=jnp.float32)
        result = result + jnp.dot(
            suffix_weights,
            with_ones(suffix_ref[start:stop, HD:]),
            preferred_element_type=jnp.float32,
        )
        row_at = block * BLK + lax.broadcasted_iota(jnp.int32, (BLK, HD), 0)
        live = jnp.concatenate([row_at < agent_end] * heads, axis=0)
        unstack(best_ref, rows, heads, jnp.where(live, best, empty_best))
        unstack(sum_ref, rows, heads, jnp.where(live, result[:, :HD], 0.0))
        unstack(total_ref, rows, heads, jnp.where(live, result[:, HD:], 1.0))


def add_shard(queries, best, key_rows, value_rows, total, weighted):
    scores = scores_of(queries, key_rows)
    weights = jnp.exp2(scores - widen(best, scores.shape[1])).astype(jnp.bfloat16)
    result = jnp.dot(weights, value_rows, preferred_element_type=jnp.float32)
    return total + result[:, HD:], weighted + result[:, :HD]


def row_blocks(count):
    step = next(size for size in (160, 128, count) if count % size == 0)
    return [slice(first, first + step) for first in range(0, count, step)]


def early_stage(*refs):
    query_ref, best_ref, total_ref, sum_ref = refs[:4]
    shard_refs = refs[4:-2]
    total_out, sum_out = refs[-2:]
    heads = query_ref.shape[1] // HD
    shards_here = [(ref[:, :HD], with_ones(ref[:, HD:])) for ref in shard_refs]
    for rows in row_blocks(query_ref.shape[0]):
        queries = stacked(query_ref, rows, heads)
        best = stacked(best_ref, rows, heads)
        total = stacked(total_ref, rows, heads)
        weighted = stacked(sum_ref, rows, heads)
        for key_rows, value_rows in shards_here:
            total, weighted = add_shard(queries, best, key_rows, value_rows, total, weighted)
        unstack(total_out, rows, heads, total)
        unstack(sum_out, rows, heads, weighted)


def late_stage(early_count, late_count, half_count, *refs):
    query_ref, best_ref, old_total_ref, old_sum_ref, total_ref, sum_ref = refs[:6]
    refs = refs[6:]
    early_refs, refs = refs[:early_count], refs[early_count:]
    late_refs, refs = refs[:late_count], refs[late_count:]
    direct_refs, refs = refs[:half_count], refs[half_count:]
    passed_refs, refs = refs[:half_count], refs[half_count:]
    out_hbm, out_ref, out_sems = refs
    heads = query_ref.shape[1] // HD
    blocks = row_blocks(query_ref.shape[0])
    is_direct = lax.axis_index("pair") == 0

    def load(early):
        loaded = [ref[...] for ref in early + late_refs]
        for direct_ref, passed_ref in zip(direct_refs, passed_refs):
            loaded.append(jnp.where(is_direct, direct_ref[...], passed_ref[...]))
        return [(shard[:, :HD], with_ones(shard[:, HD:])) for shard in loaded]

    def out_copy(index, rows):
        return pltpu.make_async_copy(out_ref.at[rows], out_hbm.at[rows], out_sems.at[index])

    def finish(rows, total, weighted):
        unstack(out_ref, rows, heads, (weighted / total).astype(jnp.bfloat16))

    trusted = jnp.full((8, HD), True)
    shards_here = load(())
    for index, rows in enumerate(blocks):
        queries = stacked(query_ref, rows, heads)
        best = stacked(best_ref, rows, heads)
        total = stacked(total_ref, rows, heads)
        weighted = stacked(sum_ref, rows, heads)
        for key_rows, value_rows in shards_here:
            total, weighted = add_shard(queries, best, key_rows, value_rows, total, weighted)
        good = (total < total_limit).reshape(total.shape[0] // 8, 8, HD)
        trusted = trusted & jnp.all(good, axis=0)
        finish(rows, total, weighted)
        out_copy(index, rows).start()
    for index, rows in enumerate(blocks):
        out_copy(index, rows).wait()

    @pl.when(jnp.logical_not(jnp.all(trusted)))
    def exact_maximum():
        size = query_ref.shape[0] // len(blocks)

        def visit(index, unused):
            rows = pl.ds(pl.multiple_of(index * size, size), size)
            queries = stacked(query_ref, rows, heads)
            best = stacked(best_ref, rows, heads)
            weighted = stacked(old_sum_ref, rows, heads)
            total = stacked(old_total_ref, rows, heads)
            for key_rows, value_rows in load(early_refs):
                scores = scores_of(queries, key_rows)
                new_best = jnp.maximum(best, jnp.max(scores, axis=1, keepdims=True))
                factor = jnp.exp2(best - new_best)
                weights = jnp.exp2(scores - widen(new_best, scores.shape[1]))
                result = jnp.dot(
                    weights.astype(jnp.bfloat16), value_rows, preferred_element_type=jnp.float32
                )
                weighted = weighted * factor + result[:, :HD]
                total = total * factor + result[:, HD:]
                best = new_best
            finish(rows, total, weighted)
            copy = out_copy(index, rows)
            copy.start()
            copy.wait()
            return unused

        lax.fori_loop(0, len(blocks), visit, 0)


def shards(queries, suffix_kv, prompt_kv, lengths):
    slots, width = queries.shape
    heads = width // HD
    loop_size = lax.axis_size("loop")
    own = prompt_kv[:, 0, :]
    suffix = suffix_kv[:, 0, :]
    shard_rows = own.shape[0]

    def place(loop_index, pair_index):
        return loop_index % loop_size * 2 + pair_index

    early, direct = [], []
    for step in range(1, (loop_size + 1) // 2):
        hops = [(place(i, 0), place(i + step, 0)) for i in range(loop_size)]
        hops += [(place(i, 1), place(i - step, 1)) for i in range(loop_size)]
        early.append(lax.ppermute(own, ("loop", "pair"), hops))
    if loop_size % 2 == 0:
        hops = [(place(i, 0), place(i + loop_size // 2, 0)) for i in range(loop_size)]
        direct.append(lax.ppermute(own, ("loop", "pair"), hops))
    in_hbm = pl.BlockSpec(memory_space=pltpu.HBM)
    in_vmem = pl.BlockSpec(memory_space=pltpu.VMEM)
    state = jax.ShapeDtypeStruct((slots, width), jnp.float32)

    def cost(keys):
        return pl.CostEstimate(
            flops=slots * heads * keys * HD * 4,
            bytes_accessed=slots * width * 14,
            transcendentals=slots * heads * keys,
        )

    best, total, weighted, queries = pl.pallas_call(
        local_stage,
        name="local_stage",
        out_shape=[state] * 3 + [jax.ShapeDtypeStruct((slots, width), queries.dtype)],
        in_specs=[in_hbm] * 4,
        out_specs=[in_vmem] * 4,
        scratch_shapes=[
            pltpu.SMEM(lengths.shape, lengths.dtype),
            pltpu.VMEM(suffix.shape, suffix.dtype),
            pltpu.VMEM(own.shape, own.dtype),
            pltpu.SemaphoreType.DMA((3,)),
            pltpu.SemaphoreType.DMA((slots // BLK,)),
        ],
        compiler_params=pltpu.CompilerParams(vmem_limit_bytes=24 * 2**20),
        cost_estimate=cost(shard_rows + MAXLEN),
    )(*(pltpu.with_memory_space_constraint(x, pltpu.HBM) for x in (lengths, queries, suffix, own)))
    early, direct, best = lax.optimization_barrier((early, direct, best))
    late = [
        lax.ppermute(shard, ("loop", "pair"), [(p, p ^ 1) for p in range(2 * loop_size)])
        for shard in early
    ]
    passed = [
        lax.ppermute(shard, ("loop", "pair"), [(2 * i, 2 * i + 1) for i in range(loop_size)])
        for shard in direct
    ]
    early_total, early_weighted = total, weighted
    if early:
        early_total, early_weighted = pl.pallas_call(
            early_stage,
            name="early_stage",
            out_shape=[state] * 2,
            in_specs=[in_vmem] * (4 + len(early)),
            out_specs=[in_vmem] * 2,
            compiler_params=pltpu.CompilerParams(vmem_limit_bytes=24 * 2**20),
            cost_estimate=cost(shard_rows * len(early)),
        )(queries, best, total, weighted, *early)
    last_inputs = (queries, best, total, weighted, early_total, early_weighted)
    last_inputs += (*early, *late, *direct, *passed)
    return pl.pallas_call(
        functools.partial(late_stage, len(early), len(late), len(direct)),
        name="late_stage",
        out_shape=jax.ShapeDtypeStruct((slots, width), jnp.bfloat16),
        in_specs=[in_vmem] * len(last_inputs),
        out_specs=in_hbm,
        scratch_shapes=[
            pltpu.VMEM((slots, width), jnp.bfloat16),
            pltpu.SemaphoreType.DMA((len(row_blocks(slots)),)),
        ],
        compiler_params=pltpu.CompilerParams(vmem_limit_bytes=32 * 2**20),
        cost_estimate=cost(shard_rows * (len(late) + len(direct))),
    )(*last_inputs)


def solution(mesh):
    placed = (
        P(("groups", "loop"), ("heads", "pair")),
        P(("groups", "loop"), "heads", None),
        P(("groups", "loop"), "heads", None),
        P("groups"),
    )
    return jax.shard_map(
        shards,
        mesh=mesh,
        in_specs=placed,
        out_specs=P(("groups", "loop"), ("heads", "pair")),
        check_vma=False,
    )
```

```python
import functools
import math

import jax
import jax.numpy as jnp
from jax import lax
from jax.experimental import pallas as pl
from jax.experimental.pallas import tpu as pltpu
from jax.sharding import PartitionSpec as P

HD = 128
AG_DEV = 2
MAXLEN = 320
BLK = 128

masked_score = -1e30
empty_best = 1e30
total_limit = 2.0**100
score_scale = math.log2(math.e) / math.sqrt(HD)


def scores_of(query_rows, key_rows):
    return (
        lax.dot_general(
            query_rows, key_rows, (((1,), (1,)), ((), ())), preferred_element_type=jnp.float32
        )
        * score_scale
    )


def with_ones(value_rows):
    return jnp.concatenate([value_rows, jnp.ones_like(value_rows)], axis=1)


def stacked(ref, rows, head_count):
    return jnp.concatenate([ref[rows, h * HD : (h + 1) * HD] for h in range(head_count)], axis=0)


def unstack(ref, rows, head_count, value):
    count = value.shape[0] // head_count
    for h in range(head_count):
        ref[rows, h * HD : (h + 1) * HD] = value[h * count : (h + 1) * count]


def widen(row_value, width):
    return jnp.concatenate([row_value] * (width // HD), axis=1)


def local_stage(
    lengths_hbm,
    query_hbm,
    suffix_hbm,
    own_hbm,
    best_ref,
    total_ref,
    sum_ref,
    query_ref,
    lengths_ref,
    suffix_ref,
    own_ref,
    whole_sems,
    block_sems,
):
    rows_all = query_ref.shape[0]
    heads = query_ref.shape[1] // HD
    blocks = rows_all // BLK
    whole = [
        pltpu.make_async_copy(source, target, whole_sems.at[i])
        for i, (source, target) in enumerate(
            [(lengths_hbm, lengths_ref), (own_hbm, own_ref), (suffix_hbm, suffix_ref)]
        )
    ]
    pieces = [
        pltpu.make_async_copy(
            query_hbm.at[pl.ds(block * BLK, BLK)],
            query_ref.at[pl.ds(block * BLK, BLK)],
            block_sems.at[block],
        )
        for block in range(blocks)
    ]
    for copy in whole + pieces:
        copy.start()
    for copy in whole + pieces:
        copy.wait()
    position = lax.axis_index("loop")
    own_keys = own_ref[:, :HD]
    own_values = with_ones(own_ref[:, HD:])
    window = BLK * ((MAXLEN + BLK - 2) // BLK) + BLK
    for block in range(blocks):
        stop = (block + 1) * BLK
        start = max(0, stop - window)
        rows = slice(block * BLK, stop)
        row_at = block * BLK + lax.broadcasted_iota(jnp.int32, (BLK, stop - start), 0)
        key_at = start + lax.broadcasted_iota(jnp.int32, (BLK, stop - start), 1)
        first = jnp.zeros_like(row_at)
        agent_end = 0
        for agent in range(AG_DEV):
            agent_end = agent_end + lengths_ref[position * AG_DEV + agent]
            first = jnp.where(row_at >= agent_end, agent_end, first)
        allowed = (key_at <= row_at) & (key_at >= first)
        queries = stacked(query_ref, rows, heads)
        own_scores = scores_of(queries, own_keys)
        suffix_scores = jnp.where(
            jnp.concatenate([allowed] * heads, axis=0),
            scores_of(queries, suffix_ref[start:stop, :HD]),
            masked_score,
        )
        best = jnp.maximum(
            jnp.max(own_scores, axis=1, keepdims=True),
            jnp.max(suffix_scores, axis=1, keepdims=True),
        )
        own_weights = jnp.exp2(own_scores - best).astype(jnp.bfloat16)
        suffix_weights = jnp.exp2(suffix_scores - best).astype(jnp.bfloat16)
        result = jnp.dot(own_weights, own_values, preferred_element_type=jnp.float32)
        result = result + jnp.dot(
            suffix_weights,
            with_ones(suffix_ref[start:stop, HD:]),
            preferred_element_type=jnp.float32,
        )
        row_at = block * BLK + lax.broadcasted_iota(jnp.int32, (BLK, HD), 0)
        live = jnp.concatenate([row_at < agent_end] * heads, axis=0)
        unstack(best_ref, rows, heads, jnp.where(live, best, empty_best))
        unstack(sum_ref, rows, heads, jnp.where(live, result[:, :HD], 0.0))
        unstack(total_ref, rows, heads, jnp.where(live, result[:, HD:], 1.0))


def add_shard(queries, best, key_rows, value_rows, total, weighted):
    scores = scores_of(queries, key_rows)
    weights = jnp.exp2(scores - widen(best, scores.shape[1])).astype(jnp.bfloat16)
    result = jnp.dot(weights, value_rows, preferred_element_type=jnp.float32)
    return total + result[:, HD:], weighted + result[:, :HD]


def row_blocks(count):
    step = next(size for size in (160, 128, count) if count % size == 0)
    return [slice(first, first + step) for first in range(0, count, step)]


def early_stage(*refs):
    query_ref, best_ref, total_ref, sum_ref = refs[:4]
    shard_refs = refs[4:-2]
    total_out, sum_out = refs[-2:]
    heads = query_ref.shape[1] // HD
    shards_here = [(ref[:, :HD], with_ones(ref[:, HD:])) for ref in shard_refs]
    for rows in row_blocks(query_ref.shape[0]):
        queries = stacked(query_ref, rows, heads)
        best = stacked(best_ref, rows, heads)
        total = stacked(total_ref, rows, heads)
        weighted = stacked(sum_ref, rows, heads)
        for key_rows, value_rows in shards_here:
            total, weighted = add_shard(queries, best, key_rows, value_rows, total, weighted)
        unstack(total_out, rows, heads, total)
        unstack(sum_out, rows, heads, weighted)


def late_stage(early_count, late_count, half_count, *refs):
    query_ref, best_ref, old_total_ref, old_sum_ref, total_ref, sum_ref = refs[:6]
    refs = refs[6:]
    early_refs, refs = refs[:early_count], refs[early_count:]
    late_refs, refs = refs[:late_count], refs[late_count:]
    direct_refs, refs = refs[:half_count], refs[half_count:]
    passed_refs, refs = refs[:half_count], refs[half_count:]
    out_hbm, out_ref, out_sems = refs
    heads = query_ref.shape[1] // HD
    blocks = row_blocks(query_ref.shape[0])
    is_direct = lax.axis_index("pair") == 0

    def load(early):
        loaded = [ref[...] for ref in early + late_refs]
        for direct_ref, passed_ref in zip(direct_refs, passed_refs):
            loaded.append(jnp.where(is_direct, direct_ref[...], passed_ref[...]))
        return [(shard[:, :HD], with_ones(shard[:, HD:])) for shard in loaded]

    def out_copy(index, rows):
        return pltpu.make_async_copy(out_ref.at[rows], out_hbm.at[rows], out_sems.at[index])

    def finish(rows, total, weighted):
        unstack(out_ref, rows, heads, (weighted / total).astype(jnp.bfloat16))

    trusted = jnp.full((8, HD), True)
    shards_here = load(())
    for index, rows in enumerate(blocks):
        queries = stacked(query_ref, rows, heads)
        best = stacked(best_ref, rows, heads)
        total = stacked(total_ref, rows, heads)
        weighted = stacked(sum_ref, rows, heads)
        for key_rows, value_rows in shards_here:
            total, weighted = add_shard(queries, best, key_rows, value_rows, total, weighted)
        good = (total < total_limit).reshape(total.shape[0] // 8, 8, HD)
        trusted = trusted & jnp.all(good, axis=0)
        finish(rows, total, weighted)
        out_copy(index, rows).start()
    for index, rows in enumerate(blocks):
        out_copy(index, rows).wait()

    @pl.when(jnp.logical_not(jnp.all(trusted)))
    def exact_maximum():
        size = query_ref.shape[0] // len(blocks)

        def visit(index, unused):
            rows = pl.ds(pl.multiple_of(index * size, size), size)
            queries = stacked(query_ref, rows, heads)
            best = stacked(best_ref, rows, heads)
            weighted = stacked(old_sum_ref, rows, heads)
            total = stacked(old_total_ref, rows, heads)
            for key_rows, value_rows in load(early_refs):
                scores = scores_of(queries, key_rows)
                new_best = jnp.maximum(best, jnp.max(scores, axis=1, keepdims=True))
                factor = jnp.exp2(best - new_best)
                weights = jnp.exp2(scores - widen(new_best, scores.shape[1]))
                result = jnp.dot(
                    weights.astype(jnp.bfloat16), value_rows, preferred_element_type=jnp.float32
                )
                weighted = weighted * factor + result[:, :HD]
                total = total * factor + result[:, HD:]
                best = new_best
            finish(rows, total, weighted)
            copy = out_copy(index, rows)
            copy.start()
            copy.wait()
            return unused

        lax.fori_loop(0, len(blocks), visit, 0)


def shards(queries, suffix_kv, prompt_kv, lengths):
    slots, width = queries.shape
    heads = width // HD
    loop_size = lax.axis_size("loop")
    own = prompt_kv[:, 0, :]
    suffix = suffix_kv[:, 0, :]
    shard_rows = own.shape[0]

    def place(loop_index, pair_index):
        return loop_index % loop_size * 2 + pair_index

    early, direct = [], []
    if loop_size % 2 == 0:
        hops = [(place(i, 0), place(i + loop_size // 2, 0)) for i in range(loop_size)]
        hops += [(place(i, 1), place(i, 1)) for i in range(loop_size)]
        direct.append(lax.ppermute(own, ("loop", "pair"), hops))
    for step in reversed(range(1, (loop_size + 1) // 2)):
        hops = [(place(i, 0), place(i + step, 0)) for i in range(loop_size)]
        hops += [(place(i, 1), place(i - step, 1)) for i in range(loop_size)]
        early.append(lax.ppermute(own, ("loop", "pair"), hops))
    in_hbm = pl.BlockSpec(memory_space=pltpu.HBM)
    in_vmem = pl.BlockSpec(memory_space=pltpu.VMEM)
    state = jax.ShapeDtypeStruct((slots, width), jnp.float32)

    def cost(keys):
        return pl.CostEstimate(
            flops=slots * heads * keys * HD * 4,
            bytes_accessed=slots * width * 14,
            transcendentals=slots * heads * keys,
        )

    best, total, weighted, queries = pl.pallas_call(
        local_stage,
        name="local_stage",
        out_shape=[state] * 3 + [jax.ShapeDtypeStruct((slots, width), queries.dtype)],
        in_specs=[in_hbm] * 4,
        out_specs=[in_vmem] * 4,
        scratch_shapes=[
            pltpu.SMEM(lengths.shape, lengths.dtype),
            pltpu.VMEM(suffix.shape, suffix.dtype),
            pltpu.VMEM(own.shape, own.dtype),
            pltpu.SemaphoreType.DMA((3,)),
            pltpu.SemaphoreType.DMA((slots // BLK,)),
        ],
        compiler_params=pltpu.CompilerParams(vmem_limit_bytes=24 * 2**20),
        cost_estimate=cost(shard_rows + MAXLEN),
    )(*(pltpu.with_memory_space_constraint(x, pltpu.HBM) for x in (lengths, queries, suffix, own)))
    early, direct, best = lax.optimization_barrier((early, direct, best))
    swap = [(p, p ^ 1) for p in range(2 * loop_size)]
    late = [lax.ppermute(shard, ("loop", "pair"), swap) for shard in early]
    passed = [lax.ppermute(shard, ("loop", "pair"), swap) for shard in direct]
    early_total, early_weighted = total, weighted
    if early:
        early_total, early_weighted = pl.pallas_call(
            early_stage,
            name="early_stage",
            out_shape=[state] * 2,
            in_specs=[in_vmem] * (4 + len(early)),
            out_specs=[in_vmem] * 2,
            compiler_params=pltpu.CompilerParams(vmem_limit_bytes=24 * 2**20),
            cost_estimate=cost(shard_rows * len(early)),
        )(queries, best, total, weighted, *early)
    last_inputs = (queries, best, total, weighted, early_total, early_weighted)
    last_inputs += (*early, *late, *direct, *passed)
    return pl.pallas_call(
        functools.partial(late_stage, len(early), len(late), len(direct)),
        name="late_stage",
        out_shape=jax.ShapeDtypeStruct((slots, width), jnp.bfloat16),
        in_specs=[in_vmem] * len(last_inputs),
        out_specs=in_hbm,
        scratch_shapes=[
            pltpu.VMEM((slots, width), jnp.bfloat16),
            pltpu.SemaphoreType.DMA((len(row_blocks(slots)),)),
        ],
        compiler_params=pltpu.CompilerParams(vmem_limit_bytes=32 * 2**20),
        cost_estimate=cost(shard_rows * (len(late) + len(direct))),
    )(*last_inputs)


def solution(mesh):
    placed = (
        P(("groups", "loop"), ("heads", "pair")),
        P(("groups", "loop"), "heads", None),
        P(("groups", "loop"), "heads", None),
        P("groups"),
    )
    return jax.shard_map(
        shards,
        mesh=mesh,
        in_specs=placed,
        out_specs=P(("groups", "loop"), ("heads", "pair")),
        check_vma=False,
    )
```

```python
import functools
import math

import jax
import jax.numpy as jnp
from jax import lax
from jax.experimental import pallas as pl
from jax.experimental.pallas import tpu as pltpu
from jax.sharding import PartitionSpec as P

HD = 128
AG_DEV = 2
MAXLEN = 320
BLK = 128

masked_score = -1e30
empty_best = 1e30
total_limit = 2.0**100
score_scale = math.log2(math.e) / math.sqrt(HD)


def scores_of(query_rows, key_rows):
    return (
        lax.dot_general(
            query_rows, key_rows, (((1,), (1,)), ((), ())), preferred_element_type=jnp.float32
        )
        * score_scale
    )


def with_ones(value_rows):
    return jnp.concatenate([value_rows, jnp.ones_like(value_rows)], axis=1)


def stacked(ref, rows, head_count):
    return jnp.concatenate([ref[rows, h * HD : (h + 1) * HD] for h in range(head_count)], axis=0)


def unstack(ref, rows, head_count, value):
    count = value.shape[0] // head_count
    for h in range(head_count):
        ref[rows, h * HD : (h + 1) * HD] = value[h * count : (h + 1) * count]


def widen(row_value, width):
    return jnp.concatenate([row_value] * (width // HD), axis=1)


def local_stage(
    lengths_hbm,
    query_hbm,
    suffix_hbm,
    own_hbm,
    best_ref,
    total_ref,
    sum_ref,
    query_ref,
    lengths_ref,
    suffix_ref,
    own_ref,
    whole_sems,
    block_sems,
):
    rows_all = query_ref.shape[0]
    heads = query_ref.shape[1] // HD
    blocks = rows_all // BLK
    whole = [
        pltpu.make_async_copy(source, target, whole_sems.at[i])
        for i, (source, target) in enumerate(
            [(lengths_hbm, lengths_ref), (own_hbm, own_ref), (suffix_hbm, suffix_ref)]
        )
    ]
    pieces = [
        pltpu.make_async_copy(
            query_hbm.at[pl.ds(block * BLK, BLK)],
            query_ref.at[pl.ds(block * BLK, BLK)],
            block_sems.at[block],
        )
        for block in range(blocks)
    ]
    for copy in whole + pieces:
        copy.start()
    for copy in whole + pieces:
        copy.wait()
    position = lax.axis_index("loop")
    own_keys = own_ref[:, :HD]
    own_values = with_ones(own_ref[:, HD:])
    window = BLK * ((MAXLEN + BLK - 2) // BLK) + BLK
    for block in range(blocks):
        stop = (block + 1) * BLK
        start = max(0, stop - window)
        rows = slice(block * BLK, stop)
        row_at = block * BLK + lax.broadcasted_iota(jnp.int32, (BLK, stop - start), 0)
        key_at = start + lax.broadcasted_iota(jnp.int32, (BLK, stop - start), 1)
        first = jnp.zeros_like(row_at)
        agent_end = 0
        for agent in range(AG_DEV):
            agent_end = agent_end + lengths_ref[position * AG_DEV + agent]
            first = jnp.where(row_at >= agent_end, agent_end, first)
        allowed = (key_at <= row_at) & (key_at >= first)
        queries = stacked(query_ref, rows, heads)
        own_scores = scores_of(queries, own_keys)
        suffix_scores = jnp.where(
            jnp.concatenate([allowed] * heads, axis=0),
            scores_of(queries, suffix_ref[start:stop, :HD]),
            masked_score,
        )
        best = jnp.maximum(
            jnp.max(own_scores, axis=1, keepdims=True),
            jnp.max(suffix_scores, axis=1, keepdims=True),
        )
        own_weights = jnp.exp2(own_scores - best).astype(jnp.bfloat16)
        suffix_weights = jnp.exp2(suffix_scores - best).astype(jnp.bfloat16)
        result = jnp.dot(own_weights, own_values, preferred_element_type=jnp.float32)
        result = result + jnp.dot(
            suffix_weights,
            with_ones(suffix_ref[start:stop, HD:]),
            preferred_element_type=jnp.float32,
        )
        row_at = block * BLK + lax.broadcasted_iota(jnp.int32, (BLK, HD), 0)
        live = jnp.concatenate([row_at < agent_end] * heads, axis=0)
        unstack(best_ref, rows, heads, jnp.where(live, best, empty_best))
        unstack(sum_ref, rows, heads, jnp.where(live, result[:, :HD], 0.0))
        unstack(total_ref, rows, heads, jnp.where(live, result[:, HD:], 1.0))


def add_shard(queries, best, key_rows, value_rows, total, weighted):
    scores = scores_of(queries, key_rows)
    weights = jnp.exp2(scores - widen(best, scores.shape[1])).astype(jnp.bfloat16)
    result = jnp.dot(weights, value_rows, preferred_element_type=jnp.float32)
    return total + result[:, HD:], weighted + result[:, :HD]


def row_blocks(count):
    step = next(size for size in (160, 128, count) if count % size == 0)
    return [slice(first, first + step) for first in range(0, count, step)]


def late_stage(
    query_ref, best_ref, total_ref, sum_ref, gathered_ref, out_hbm, out_ref, out_sems
):
    old_total_ref, old_sum_ref = total_ref, sum_ref
    heads = query_ref.shape[1] // HD
    blocks = row_blocks(query_ref.shape[0])
    loop_size = gathered_ref.shape[0]
    position = lax.axis_index("loop")

    def load(unused):
        loaded = [gathered_ref[lax.rem(position + i, loop_size)] for i in range(1, loop_size)]
        return [(shard[:, :HD], with_ones(shard[:, HD:])) for shard in loaded]

    def out_copy(index, rows):
        return pltpu.make_async_copy(out_ref.at[rows], out_hbm.at[rows], out_sems.at[index])

    def finish(rows, total, weighted):
        unstack(out_ref, rows, heads, (weighted / total).astype(jnp.bfloat16))

    trusted = jnp.full((8, HD), True)
    shards_here = load(())
    for index, rows in enumerate(blocks):
        queries = stacked(query_ref, rows, heads)
        best = stacked(best_ref, rows, heads)
        total = stacked(total_ref, rows, heads)
        weighted = stacked(sum_ref, rows, heads)
        for key_rows, value_rows in shards_here:
            total, weighted = add_shard(queries, best, key_rows, value_rows, total, weighted)
        good = (total < total_limit).reshape(total.shape[0] // 8, 8, HD)
        trusted = trusted & jnp.all(good, axis=0)
        finish(rows, total, weighted)
        out_copy(index, rows).start()
    for index, rows in enumerate(blocks):
        out_copy(index, rows).wait()

    @pl.when(jnp.logical_not(jnp.all(trusted)))
    def exact_maximum():
        size = query_ref.shape[0] // len(blocks)

        def visit(index, unused):
            rows = pl.ds(pl.multiple_of(index * size, size), size)
            queries = stacked(query_ref, rows, heads)
            best = stacked(best_ref, rows, heads)
            weighted = stacked(old_sum_ref, rows, heads)
            total = stacked(old_total_ref, rows, heads)
            for key_rows, value_rows in load(()):
                scores = scores_of(queries, key_rows)
                new_best = jnp.maximum(best, jnp.max(scores, axis=1, keepdims=True))
                factor = jnp.exp2(best - new_best)
                weights = jnp.exp2(scores - widen(new_best, scores.shape[1]))
                result = jnp.dot(
                    weights.astype(jnp.bfloat16), value_rows, preferred_element_type=jnp.float32
                )
                weighted = weighted * factor + result[:, :HD]
                total = total * factor + result[:, HD:]
                best = new_best
            finish(rows, total, weighted)
            copy = out_copy(index, rows)
            copy.start()
            copy.wait()
            return unused

        lax.fori_loop(0, len(blocks), visit, 0)


def shards(queries, suffix_kv, prompt_kv, lengths):
    slots, width = queries.shape
    heads = width // HD
    loop_size = lax.axis_size("loop")
    own = prompt_kv[:, 0, :]
    suffix = suffix_kv[:, 0, :]
    shard_rows = own.shape[0]

    gathered = lax.all_gather(own, "loop", axis=0, tiled=False)
    in_hbm = pl.BlockSpec(memory_space=pltpu.HBM)
    in_vmem = pl.BlockSpec(memory_space=pltpu.VMEM)
    state = jax.ShapeDtypeStruct((slots, width), jnp.float32)

    def cost(keys):
        return pl.CostEstimate(
            flops=slots * heads * keys * HD * 4,
            bytes_accessed=slots * width * 14,
            transcendentals=slots * heads * keys,
        )

    best, total, weighted, queries = pl.pallas_call(
        local_stage,
        name="local_stage",
        out_shape=[state] * 3 + [jax.ShapeDtypeStruct((slots, width), queries.dtype)],
        in_specs=[in_hbm] * 4,
        out_specs=[in_vmem] * 4,
        scratch_shapes=[
            pltpu.SMEM(lengths.shape, lengths.dtype),
            pltpu.VMEM(suffix.shape, suffix.dtype),
            pltpu.VMEM(own.shape, own.dtype),
            pltpu.SemaphoreType.DMA((3,)),
            pltpu.SemaphoreType.DMA((slots // BLK,)),
        ],
        compiler_params=pltpu.CompilerParams(vmem_limit_bytes=24 * 2**20),
        cost_estimate=cost(shard_rows + MAXLEN),
    )(*(pltpu.with_memory_space_constraint(x, pltpu.HBM) for x in (lengths, queries, suffix, own)))
    return pl.pallas_call(
        late_stage,
        name="late_stage",
        out_shape=jax.ShapeDtypeStruct((slots, width), jnp.bfloat16),
        in_specs=[in_vmem] * 5,
        out_specs=in_hbm,
        scratch_shapes=[
            pltpu.VMEM((slots, width), jnp.bfloat16),
            pltpu.SemaphoreType.DMA((len(row_blocks(slots)),)),
        ],
        compiler_params=pltpu.CompilerParams(vmem_limit_bytes=32 * 2**20),
        cost_estimate=cost(shard_rows * (loop_size - 1)),
    )(queries, best, total, weighted, gathered)


def solution(mesh):
    placed = (
        P(("groups", "loop"), ("heads", "pair")),
        P(("groups", "loop"), "heads", None),
        P(("groups", "loop"), "heads", None),
        P("groups"),
    )
    return jax.shard_map(
        shards,
        mesh=mesh,
        in_specs=placed,
        out_specs=P(("groups", "loop"), ("heads", "pair")),
        check_vma=False,
    )
```

```python
import functools
import math

import jax
import jax.numpy as jnp
from jax import lax
from jax.experimental import pallas as pl
from jax.experimental.pallas import tpu as pltpu
from jax.sharding import PartitionSpec as P

HD = 128
AG_DEV = 2
MAXLEN = 320
BLK = 128

masked_score = -1e30
empty_best = 1e30
total_limit = 2.0**100
score_scale = math.log2(math.e) / math.sqrt(HD)


def scores_of(query_rows, key_rows):
    return (
        lax.dot_general(
            query_rows, key_rows, (((1,), (1,)), ((), ())), preferred_element_type=jnp.float32
        )
        * score_scale
    )


def with_ones(value_rows):
    return jnp.concatenate([value_rows, jnp.ones_like(value_rows)], axis=1)


def stacked(ref, rows, head_count):
    return jnp.concatenate([ref[rows, h * HD : (h + 1) * HD] for h in range(head_count)], axis=0)


def unstack(ref, rows, head_count, value):
    count = value.shape[0] // head_count
    for h in range(head_count):
        ref[rows, h * HD : (h + 1) * HD] = value[h * count : (h + 1) * count]


def widen(row_value, width):
    return jnp.concatenate([row_value] * (width // HD), axis=1)


def load_stage(
    lengths_hbm,
    query_hbm,
    suffix_hbm,
    own_hbm,
    query_ref,
    suffix_ref,
    own_ref,
    half_ref,
    first_ref,
    lengths_ref,
    sems,
):
    half_rows = half_ref.shape[0]
    half_start = pl.multiple_of(lax.axis_index("pair") * half_rows, half_rows)
    copies = [
        pltpu.make_async_copy(source, target, sems.at[i])
        for i, (source, target) in enumerate(
            [
                (lengths_hbm, lengths_ref),
                (own_hbm.at[pl.ds(half_start, half_rows)], half_ref),
                (own_hbm, own_ref),
                (suffix_hbm, suffix_ref),
                (query_hbm, query_ref),
            ]
        )
    ]
    for copy in copies:
        copy.start()
    copies[0].wait()
    slots = query_ref.shape[0]
    position = lax.axis_index("loop")
    row_at = lax.broadcasted_iota(jnp.int32, first_ref.shape, 0)
    first = jnp.zeros_like(row_at)
    agent_end = 0
    for agent in range(AG_DEV):
        agent_end = agent_end + lengths_ref[position * AG_DEV + agent]
        first = jnp.where(row_at >= agent_end, agent_end if agent + 1 < AG_DEV else slots, first)
    first_ref[...] = first
    for copy in copies[1:]:
        copy.wait()


def local_stage(query_ref, suffix_ref, own_ref, first_ref, best_ref, total_ref, sum_ref):
    slots = query_ref.shape[0]
    heads = query_ref.shape[1] // HD
    own_keys = own_ref[:, :HD]
    own_values = with_ones(own_ref[:, HD:])
    window = BLK * ((MAXLEN + BLK - 2) // BLK) + BLK
    for block in range(slots // BLK):
        stop = (block + 1) * BLK
        start = max(0, stop - window)
        rows = slice(block * BLK, stop)
        row_at = block * BLK + lax.broadcasted_iota(jnp.int32, (BLK, stop - start), 0)
        key_at = start + lax.broadcasted_iota(jnp.int32, (BLK, stop - start), 1)
        first = first_ref[rows]
        allowed = (key_at <= row_at) & (key_at >= widen(first, stop - start))
        queries = stacked(query_ref, rows, heads)
        own_scores = scores_of(queries, own_keys)
        suffix_scores = jnp.where(
            jnp.concatenate([allowed] * heads, axis=0),
            scores_of(queries, suffix_ref[start:stop, :HD]),
            masked_score,
        )
        best = jnp.maximum(
            jnp.max(own_scores, axis=1, keepdims=True),
            jnp.max(suffix_scores, axis=1, keepdims=True),
        )
        own_weights = jnp.exp2(own_scores - best).astype(jnp.bfloat16)
        suffix_weights = jnp.exp2(suffix_scores - best).astype(jnp.bfloat16)
        result = jnp.dot(own_weights, own_values, preferred_element_type=jnp.float32)
        result = result + jnp.dot(
            suffix_weights,
            with_ones(suffix_ref[start:stop, HD:]),
            preferred_element_type=jnp.float32,
        )
        live = jnp.concatenate([first < slots] * heads, axis=0)
        unstack(best_ref, rows, heads, jnp.where(live, best, empty_best))
        unstack(sum_ref, rows, heads, jnp.where(live, result[:, :HD], 0.0))
        unstack(total_ref, rows, heads, jnp.where(live, result[:, HD:], 1.0))


def add_shard(queries, best, key_rows, value_rows, total, weighted):
    scores = scores_of(queries, key_rows)
    weights = jnp.exp2(scores - widen(best, scores.shape[1])).astype(jnp.bfloat16)
    result = jnp.dot(weights, value_rows, preferred_element_type=jnp.float32)
    return total + result[:, HD:], weighted + result[:, :HD]


def row_blocks(count):
    step = next(size for size in (160, 128, count) if count % size == 0)
    return [slice(first, first + step) for first in range(0, count, step)]


def early_stage(*refs):
    query_ref, best_ref, total_ref, sum_ref = refs[:4]
    shard_refs = refs[4:-2]
    total_out, sum_out = refs[-2:]
    heads = query_ref.shape[1] // HD
    shards_here = [(ref[:, :HD], with_ones(ref[:, HD:])) for ref in shard_refs]
    for rows in row_blocks(query_ref.shape[0]):
        queries = stacked(query_ref, rows, heads)
        best = stacked(best_ref, rows, heads)
        total = stacked(total_ref, rows, heads)
        weighted = stacked(sum_ref, rows, heads)
        for key_rows, value_rows in shards_here:
            total, weighted = add_shard(queries, best, key_rows, value_rows, total, weighted)
        unstack(total_out, rows, heads, total)
        unstack(sum_out, rows, heads, weighted)


def late_stage(early_count, late_count, half_count, *refs):
    query_ref, best_ref, old_total_ref, old_sum_ref, total_ref, sum_ref = refs[:6]
    refs = refs[6:]
    half_refs, refs = refs[:half_count], refs[half_count:]
    other_half_refs, refs = refs[:half_count], refs[half_count:]
    early_refs, refs = refs[:early_count], refs[early_count:]
    late_refs, refs = refs[:late_count], refs[late_count:]
    out_hbm, out_ref, out_sems = refs
    heads = query_ref.shape[1] // HD
    blocks = row_blocks(query_ref.shape[0])

    def load(early):
        loaded = [ref[...] for ref in early + late_refs]
        for half_ref, other_ref in zip(half_refs, other_half_refs):
            loaded.append(jnp.concatenate([half_ref[...], other_ref[...]], axis=0))
        return [(shard[:, :HD], with_ones(shard[:, HD:])) for shard in loaded]

    def out_copy(index, rows):
        return pltpu.make_async_copy(out_ref.at[rows], out_hbm.at[rows], out_sems.at[index])

    def finish(rows, total, weighted):
        unstack(out_ref, rows, heads, (weighted / total).astype(jnp.bfloat16))

    trusted = jnp.full((8, HD), True)
    shards_here = load(())
    for index, rows in enumerate(blocks):
        queries = stacked(query_ref, rows, heads)
        best = stacked(best_ref, rows, heads)
        total = stacked(total_ref, rows, heads)
        weighted = stacked(sum_ref, rows, heads)
        for key_rows, value_rows in shards_here:
            total, weighted = add_shard(queries, best, key_rows, value_rows, total, weighted)
        good = (total < total_limit).reshape(total.shape[0] // 8, 8, HD)
        trusted = trusted & jnp.all(good, axis=0)
        finish(rows, total, weighted)
        out_copy(index, rows).start()
    for index, rows in enumerate(blocks):
        out_copy(index, rows).wait()

    @pl.when(jnp.logical_not(jnp.all(trusted)))
    def exact_maximum():
        size = query_ref.shape[0] // len(blocks)

        def visit(index, unused):
            rows = pl.ds(pl.multiple_of(index * size, size), size)
            queries = stacked(query_ref, rows, heads)
            best = stacked(best_ref, rows, heads)
            weighted = stacked(old_sum_ref, rows, heads)
            total = stacked(old_total_ref, rows, heads)
            for key_rows, value_rows in load(early_refs):
                scores = scores_of(queries, key_rows)
                new_best = jnp.maximum(best, jnp.max(scores, axis=1, keepdims=True))
                factor = jnp.exp2(best - new_best)
                weights = jnp.exp2(scores - widen(new_best, scores.shape[1]))
                result = jnp.dot(
                    weights.astype(jnp.bfloat16), value_rows, preferred_element_type=jnp.float32
                )
                weighted = weighted * factor + result[:, :HD]
                total = total * factor + result[:, HD:]
                best = new_best
            finish(rows, total, weighted)
            copy = out_copy(index, rows)
            copy.start()
            copy.wait()
            return unused

        lax.fori_loop(0, len(blocks), visit, 0)


def shards(queries, suffix_kv, prompt_kv, lengths):
    slots, width = queries.shape
    heads = width // HD
    loop_size = lax.axis_size("loop")
    own = prompt_kv[:, 0, :]
    suffix = suffix_kv[:, 0, :]
    shard_rows = own.shape[0]

    def place(loop_index, pair_index):
        return loop_index % loop_size * 2 + pair_index

    in_hbm = pl.BlockSpec(memory_space=pltpu.HBM)
    in_vmem = pl.BlockSpec(memory_space=pltpu.VMEM)
    state = jax.ShapeDtypeStruct((slots, width), jnp.float32)

    def cost(keys):
        return pl.CostEstimate(
            flops=slots * heads * keys * HD * 4,
            bytes_accessed=slots * width * 14,
            transcendentals=slots * heads * keys,
        )

    early = []
    for step in range(1, (loop_size + 1) // 2):
        hops = [(place(i, 0), place(i + step, 0)) for i in range(loop_size)]
        hops += [(place(i, 1), place(i - step, 1)) for i in range(loop_size)]
        early.append(lax.ppermute(own, ("loop", "pair"), hops))
    half_rows = shard_rows // 2
    queries, suffix, own, half, first = pl.pallas_call(
        load_stage,
        name="load_stage",
        out_shape=[
            jax.ShapeDtypeStruct(queries.shape, queries.dtype),
            jax.ShapeDtypeStruct(suffix.shape, suffix.dtype),
            jax.ShapeDtypeStruct(own.shape, own.dtype),
            jax.ShapeDtypeStruct((half_rows, own.shape[1]), own.dtype),
            jax.ShapeDtypeStruct((slots, HD), jnp.int32),
        ],
        in_specs=[in_hbm] * 4,
        out_specs=[in_vmem] * 5,
        scratch_shapes=[
            pltpu.SMEM(lengths.shape, lengths.dtype),
            pltpu.SemaphoreType.DMA((5,)),
        ],
        compiler_params=pltpu.CompilerParams(vmem_limit_bytes=8 * 2**20),
        cost_estimate=pl.CostEstimate(
            flops=0, bytes_accessed=slots * width * 6, transcendentals=0
        ),
    )(*(pltpu.with_memory_space_constraint(x, pltpu.HBM) for x in (lengths, queries, suffix, own)))
    halves = []
    if loop_size % 2 == 0:
        across = [(i, (i + loop_size // 2) % loop_size) for i in range(loop_size)]
        halves.append(lax.ppermute(half, "loop", across))
    best, total, weighted = pl.pallas_call(
        local_stage,
        name="local_stage",
        out_shape=[state] * 3,
        in_specs=[in_vmem] * 4,
        out_specs=[in_vmem] * 3,
        compiler_params=pltpu.CompilerParams(vmem_limit_bytes=24 * 2**20),
        cost_estimate=cost(shard_rows + MAXLEN),
    )(queries, suffix, own, first)
    halves, early, best = lax.optimization_barrier((halves, early, best))
    swap = [(p, p ^ 1) for p in range(2 * loop_size)]
    other_halves = [lax.ppermute(half, ("loop", "pair"), swap) for half in halves]
    late = [lax.ppermute(shard, ("loop", "pair"), swap) for shard in early]
    early_total, early_weighted = total, weighted
    if early:
        early_total, early_weighted = pl.pallas_call(
            early_stage,
            name="early_stage",
            out_shape=[state] * 2,
            in_specs=[in_vmem] * (4 + len(early)),
            out_specs=[in_vmem] * 2,
            compiler_params=pltpu.CompilerParams(vmem_limit_bytes=24 * 2**20),
            cost_estimate=cost(shard_rows * len(early)),
        )(queries, best, total, weighted, *early)
    last_inputs = (queries, best, total, weighted, early_total, early_weighted)
    last_inputs += (*halves, *other_halves, *early, *late)
    return pl.pallas_call(
        functools.partial(late_stage, len(early), len(late), len(halves)),
        name="late_stage",
        out_shape=jax.ShapeDtypeStruct((slots, width), jnp.bfloat16),
        in_specs=[in_vmem] * len(last_inputs),
        out_specs=in_hbm,
        scratch_shapes=[
            pltpu.VMEM((slots, width), jnp.bfloat16),
            pltpu.SemaphoreType.DMA((len(row_blocks(slots)),)),
        ],
        compiler_params=pltpu.CompilerParams(vmem_limit_bytes=32 * 2**20),
        cost_estimate=cost(shard_rows * (len(late) + len(halves))),
    )(*last_inputs)


def solution(mesh):
    placed = (
        P(("groups", "loop"), ("heads", "pair")),
        P(("groups", "loop"), "heads", None),
        P(("groups", "loop"), "heads", None),
        P("groups"),
    )
    return jax.shard_map(
        shards,
        mesh=mesh,
        in_specs=placed,
        out_specs=P(("groups", "loop"), ("heads", "pair")),
        check_vma=False,
    )
```

```python
import functools
import math

import jax
import jax.numpy as jnp
from jax import lax
from jax.experimental import pallas as pl
from jax.experimental.pallas import tpu as pltpu
from jax.sharding import PartitionSpec as P

HD = 128
AG_DEV = 2
MAXLEN = 320
BLK = 128

masked_score = -1e30
empty_best = 1e30
total_limit = 2.0**100
score_scale = math.log2(math.e) / math.sqrt(HD)


def scores_of(query_rows, key_rows):
    return (
        lax.dot_general(
            query_rows, key_rows, (((1,), (1,)), ((), ())), preferred_element_type=jnp.float32
        )
        * score_scale
    )


def with_ones(value_rows):
    return jnp.concatenate([value_rows, jnp.ones_like(value_rows)], axis=1)


def stacked(ref, rows, head_count):
    return jnp.concatenate([ref[rows, h * HD : (h + 1) * HD] for h in range(head_count)], axis=0)


def unstack(ref, rows, head_count, value):
    count = value.shape[0] // head_count
    for h in range(head_count):
        ref[rows, h * HD : (h + 1) * HD] = value[h * count : (h + 1) * count]


def widen(row_value, width):
    return jnp.concatenate([row_value] * (width // HD), axis=1)


def local_stage(
    lengths_hbm,
    query_hbm,
    suffix_hbm,
    own_hbm,
    best_ref,
    total_ref,
    sum_ref,
    query_ref,
    lengths_ref,
    suffix_ref,
    own_ref,
    whole_sems,
    block_sems,
):
    rows_all = query_ref.shape[0]
    heads = query_ref.shape[1] // HD
    blocks = rows_all // BLK
    whole = [
        pltpu.make_async_copy(source, target, whole_sems.at[i])
        for i, (source, target) in enumerate(
            [(lengths_hbm, lengths_ref), (own_hbm, own_ref), (suffix_hbm, suffix_ref)]
        )
    ]
    pieces = [
        pltpu.make_async_copy(
            query_hbm.at[pl.ds(block * BLK, BLK)],
            query_ref.at[pl.ds(block * BLK, BLK)],
            block_sems.at[block],
        )
        for block in range(blocks)
    ]
    for copy in whole + pieces:
        copy.start()
    for copy in whole + pieces:
        copy.wait()
    position = lax.axis_index("loop")
    own_keys = own_ref[:, :HD]
    own_values = with_ones(own_ref[:, HD:])
    window = BLK * ((MAXLEN + BLK - 2) // BLK) + BLK
    for block in range(blocks):
        stop = (block + 1) * BLK
        start = max(0, stop - window)
        rows = slice(block * BLK, stop)
        row_at = block * BLK + lax.broadcasted_iota(jnp.int32, (BLK, stop - start), 0)
        key_at = start + lax.broadcasted_iota(jnp.int32, (BLK, stop - start), 1)
        first = jnp.zeros_like(row_at)
        agent_end = 0
        for agent in range(AG_DEV):
            agent_end = agent_end + lengths_ref[position * AG_DEV + agent]
            first = jnp.where(row_at >= agent_end, agent_end, first)
        allowed = (key_at <= row_at) & (key_at >= first)
        queries = stacked(query_ref, rows, heads)
        own_scores = scores_of(queries, own_keys)
        suffix_scores = jnp.where(
            jnp.concatenate([allowed] * heads, axis=0),
            scores_of(queries, suffix_ref[start:stop, :HD]),
            masked_score,
        )
        best = jnp.maximum(
            jnp.max(own_scores, axis=1, keepdims=True),
            jnp.max(suffix_scores, axis=1, keepdims=True),
        )
        own_weights = jnp.exp2(own_scores - best).astype(jnp.bfloat16)
        suffix_weights = jnp.exp2(suffix_scores - best).astype(jnp.bfloat16)
        result = jnp.dot(own_weights, own_values, preferred_element_type=jnp.float32)
        result = result + jnp.dot(
            suffix_weights,
            with_ones(suffix_ref[start:stop, HD:]),
            preferred_element_type=jnp.float32,
        )
        row_at = block * BLK + lax.broadcasted_iota(jnp.int32, (BLK, HD), 0)
        live = jnp.concatenate([row_at < agent_end] * heads, axis=0)
        unstack(best_ref, rows, heads, jnp.where(live, best, empty_best))
        unstack(sum_ref, rows, heads, jnp.where(live, result[:, :HD], 0.0))
        unstack(total_ref, rows, heads, jnp.where(live, result[:, HD:], 1.0))


def add_shard(queries, best, key_rows, value_rows, total, weighted):
    scores = scores_of(queries, key_rows)
    weights = jnp.exp2(scores - widen(best, scores.shape[1])).astype(jnp.bfloat16)
    result = jnp.dot(weights, value_rows, preferred_element_type=jnp.float32)
    return total + result[:, HD:], weighted + result[:, :HD]


def row_blocks(count):
    step = next(size for size in (160, 128, count) if count % size == 0)
    return [slice(first, first + step) for first in range(0, count, step)]


def add_stage(*refs):
    query_ref, best_ref, total_ref, sum_ref = refs[:4]
    shard_refs = refs[4:-2]
    total_out, sum_out = refs[-2:]
    heads = query_ref.shape[1] // HD
    shards_here = [(ref[:, :HD], with_ones(ref[:, HD:])) for ref in shard_refs]
    for rows in row_blocks(query_ref.shape[0]):
        queries = stacked(query_ref, rows, heads)
        best = stacked(best_ref, rows, heads)
        total = stacked(total_ref, rows, heads)
        weighted = stacked(sum_ref, rows, heads)
        for key_rows, value_rows in shards_here:
            total, weighted = add_shard(queries, best, key_rows, value_rows, total, weighted)
        unstack(total_out, rows, heads, total)
        unstack(sum_out, rows, heads, weighted)


def last_stage(earlier_count, last_count, *refs):
    query_ref, best_ref, old_total_ref, old_sum_ref, total_ref, sum_ref = refs[:6]
    earlier_refs = refs[6 : 6 + earlier_count]
    last_refs = refs[6 + earlier_count : 6 + earlier_count + last_count]
    out_hbm, out_ref, out_sems = refs[6 + earlier_count + last_count :]
    heads = query_ref.shape[1] // HD
    blocks = row_blocks(query_ref.shape[0])

    def load(shard_refs):
        return [(ref[:, :HD], with_ones(ref[:, HD:])) for ref in shard_refs]

    def out_copy(index, rows):
        return pltpu.make_async_copy(out_ref.at[rows], out_hbm.at[rows], out_sems.at[index])

    def finish(rows, total, weighted):
        unstack(out_ref, rows, heads, (weighted / total).astype(jnp.bfloat16))

    trusted = jnp.full((8, HD), True)
    shards_here = load(last_refs)
    for index, rows in enumerate(blocks):
        queries = stacked(query_ref, rows, heads)
        best = stacked(best_ref, rows, heads)
        total = stacked(total_ref, rows, heads)
        weighted = stacked(sum_ref, rows, heads)
        for key_rows, value_rows in shards_here:
            total, weighted = add_shard(queries, best, key_rows, value_rows, total, weighted)
        good = (total < total_limit).reshape(total.shape[0] // 8, 8, HD)
        trusted = trusted & jnp.all(good, axis=0)
        finish(rows, total, weighted)
        out_copy(index, rows).start()
    for index, rows in enumerate(blocks):
        out_copy(index, rows).wait()

    @pl.when(jnp.logical_not(jnp.all(trusted)))
    def exact_maximum():
        size = query_ref.shape[0] // len(blocks)

        def visit(index, unused):
            rows = pl.ds(pl.multiple_of(index * size, size), size)
            queries = stacked(query_ref, rows, heads)
            best = stacked(best_ref, rows, heads)
            weighted = stacked(old_sum_ref, rows, heads)
            total = stacked(old_total_ref, rows, heads)
            for key_rows, value_rows in load(earlier_refs + last_refs):
                scores = scores_of(queries, key_rows)
                new_best = jnp.maximum(best, jnp.max(scores, axis=1, keepdims=True))
                factor = jnp.exp2(best - new_best)
                weights = jnp.exp2(scores - widen(new_best, scores.shape[1]))
                result = jnp.dot(
                    weights.astype(jnp.bfloat16), value_rows, preferred_element_type=jnp.float32
                )
                weighted = weighted * factor + result[:, :HD]
                total = total * factor + result[:, HD:]
                best = new_best
            finish(rows, total, weighted)
            copy = out_copy(index, rows)
            copy.start()
            copy.wait()
            return unused

        lax.fori_loop(0, len(blocks), visit, 0)


def shards(queries, suffix_kv, prompt_kv, lengths):
    slots, width = queries.shape
    heads = width // HD
    loop_size = lax.axis_size("loop")
    own = prompt_kv[:, 0, :]
    suffix = suffix_kv[:, 0, :]
    shard_rows = own.shape[0]

    power_of_two = loop_size & (loop_size - 1) == 0

    def exchange(shard, step_of_core):
        hops = []
        for core, step in enumerate(step_of_core):
            for i in range(loop_size):
                to = i ^ step if power_of_two else (i + step) % loop_size
                hops.append((2 * i + core, 2 * to + core))
        return lax.ppermute(shard, ("loop", "pair"), hops)

    to_both = 1 - loop_size % 2
    early = [exchange(own, (1, 1))] * to_both
    middle = [exchange(own, (step, step + 1)) for step in range(1 + to_both, loop_size, 2)]
    in_hbm = pl.BlockSpec(memory_space=pltpu.HBM)
    in_vmem = pl.BlockSpec(memory_space=pltpu.VMEM)
    state = jax.ShapeDtypeStruct((slots, width), jnp.float32)

    cost = pl.CostEstimate(flops=1, bytes_accessed=1, transcendentals=0)

    best, total, weighted, queries = pl.pallas_call(
        local_stage,
        name="local_stage",
        out_shape=[state] * 3 + [jax.ShapeDtypeStruct((slots, width), queries.dtype)],
        in_specs=[in_hbm] * 4,
        out_specs=[in_vmem] * 4,
        scratch_shapes=[
            pltpu.SMEM(lengths.shape, lengths.dtype),
            pltpu.VMEM(suffix.shape, suffix.dtype),
            pltpu.VMEM(own.shape, own.dtype),
            pltpu.SemaphoreType.DMA((3,)),
            pltpu.SemaphoreType.DMA((slots // BLK,)),
        ],
        compiler_params=pltpu.CompilerParams(vmem_limit_bytes=24 * 2**20),
        cost_estimate=cost,
    )(*(pltpu.with_memory_space_constraint(x, pltpu.HBM) for x in (lengths, queries, suffix, own)))
    def add_shards(total, weighted, shards_now):
        if not shards_now:
            return total, weighted
        return pl.pallas_call(
            add_stage,
            name="add_stage",
            out_shape=[state] * 2,
            in_specs=[in_vmem] * (4 + len(shards_now)),
            out_specs=[in_vmem] * 2,
            compiler_params=pltpu.CompilerParams(vmem_limit_bytes=24 * 2**20),
            cost_estimate=cost,
        )(queries, best, total, weighted, *shards_now)

    new_total, new_weighted = add_shards(total, weighted, early)
    middle, new_total = lax.optimization_barrier((middle, new_total))
    swap = [(p, p ^ 1) for p in range(2 * loop_size)]
    last = [lax.ppermute(shard, ("loop", "pair"), swap) for shard in middle]
    new_total, new_weighted = add_shards(new_total, new_weighted, middle)
    last_inputs = (queries, best, total, weighted, new_total, new_weighted)
    last_inputs += (*early, *middle, *last)
    return pl.pallas_call(
        functools.partial(last_stage, len(early) + len(middle), len(last)),
        name="last_stage",
        out_shape=jax.ShapeDtypeStruct((slots, width), jnp.bfloat16),
        in_specs=[in_vmem] * len(last_inputs),
        out_specs=in_hbm,
        scratch_shapes=[
            pltpu.VMEM((slots, width), jnp.bfloat16),
            pltpu.SemaphoreType.DMA((len(row_blocks(slots)),)),
        ],
        compiler_params=pltpu.CompilerParams(vmem_limit_bytes=32 * 2**20),
        cost_estimate=cost,
    )(*last_inputs)


def solution(mesh):
    placed = (
        P(("groups", "loop"), ("heads", "pair")),
        P(("groups", "loop"), "heads", None),
        P(("groups", "loop"), "heads", None),
        P("groups"),
    )
    return jax.shard_map(
        shards,
        mesh=mesh,
        in_specs=placed,
        out_specs=P(("groups", "loop"), ("heads", "pair")),
        check_vma=False,
    )
```

```python
import functools
import math

import jax
import jax.numpy as jnp
from jax import lax
from jax.experimental import pallas as pl
from jax.experimental.pallas import tpu as pltpu
from jax.sharding import PartitionSpec as P

HD = 128
AG_DEV = 2
MAXLEN = 320
BLK = 128

masked_score = -1e30
empty_best = 1e30
total_limit = 2.0**100
score_scale = math.log2(math.e) / math.sqrt(HD)


def scores_of(query_rows, key_rows):
    return (
        lax.dot_general(
            query_rows, key_rows, (((1,), (1,)), ((), ())), preferred_element_type=jnp.float32
        )
        * score_scale
    )


def with_ones(value_rows):
    return jnp.concatenate([value_rows, jnp.ones_like(value_rows)], axis=1)


def stacked(ref, rows, head_count):
    return jnp.concatenate([ref[rows, h * HD : (h + 1) * HD] for h in range(head_count)], axis=0)


def unstack(ref, rows, head_count, value):
    count = value.shape[0] // head_count
    for h in range(head_count):
        ref[rows, h * HD : (h + 1) * HD] = value[h * count : (h + 1) * count]


def widen(row_value, width):
    return jnp.concatenate([row_value] * (width // HD), axis=1)


def local_stage(
    lengths_hbm,
    query_hbm,
    suffix_hbm,
    own_hbm,
    best_ref,
    total_ref,
    sum_ref,
    query_ref,
    lengths_ref,
    suffix_ref,
    own_ref,
    whole_sems,
    block_sems,
):
    rows_all = query_ref.shape[0]
    heads = query_ref.shape[1] // HD
    blocks = rows_all // BLK
    whole = [
        pltpu.make_async_copy(source, target, whole_sems.at[i])
        for i, (source, target) in enumerate(
            [(lengths_hbm, lengths_ref), (own_hbm, own_ref), (suffix_hbm, suffix_ref)]
        )
    ]
    pieces = [
        pltpu.make_async_copy(
            query_hbm.at[pl.ds(block * BLK, BLK)],
            query_ref.at[pl.ds(block * BLK, BLK)],
            block_sems.at[block],
        )
        for block in range(blocks)
    ]
    for copy in whole + pieces:
        copy.start()
    for copy in whole + pieces:
        copy.wait()
    position = lax.axis_index("loop")
    own_keys = own_ref[:, :HD]
    own_values = with_ones(own_ref[:, HD:])
    window = BLK * ((MAXLEN + BLK - 2) // BLK) + BLK
    for block in range(blocks):
        stop = (block + 1) * BLK
        start = max(0, stop - window)
        rows = slice(block * BLK, stop)
        row_at = block * BLK + lax.broadcasted_iota(jnp.int32, (BLK, stop - start), 0)
        key_at = start + lax.broadcasted_iota(jnp.int32, (BLK, stop - start), 1)
        first = jnp.zeros_like(row_at)
        agent_end = 0
        for agent in range(AG_DEV):
            agent_end = agent_end + lengths_ref[position * AG_DEV + agent]
            first = jnp.where(row_at >= agent_end, agent_end, first)
        allowed = (key_at <= row_at) & (key_at >= first)
        queries = stacked(query_ref, rows, heads)
        own_scores = scores_of(queries, own_keys)
        suffix_scores = jnp.where(
            jnp.concatenate([allowed] * heads, axis=0),
            scores_of(queries, suffix_ref[start:stop, :HD]),
            masked_score,
        )
        best = jnp.maximum(
            jnp.max(own_scores, axis=1, keepdims=True),
            jnp.max(suffix_scores, axis=1, keepdims=True),
        )
        own_weights = jnp.exp2(own_scores - best).astype(jnp.bfloat16)
        suffix_weights = jnp.exp2(suffix_scores - best).astype(jnp.bfloat16)
        result = jnp.dot(own_weights, own_values, preferred_element_type=jnp.float32)
        result = result + jnp.dot(
            suffix_weights,
            with_ones(suffix_ref[start:stop, HD:]),
            preferred_element_type=jnp.float32,
        )
        row_at = block * BLK + lax.broadcasted_iota(jnp.int32, (BLK, HD), 0)
        live = jnp.concatenate([row_at < agent_end] * heads, axis=0)
        unstack(best_ref, rows, heads, jnp.where(live, best, empty_best))
        unstack(sum_ref, rows, heads, jnp.where(live, result[:, :HD], 0.0))
        unstack(total_ref, rows, heads, jnp.where(live, result[:, HD:], 1.0))


def add_shard(queries, best, key_rows, value_rows, total, weighted):
    scores = scores_of(queries, key_rows)
    weights = jnp.exp2(scores - widen(best, scores.shape[1])).astype(jnp.bfloat16)
    result = jnp.dot(weights, value_rows, preferred_element_type=jnp.float32)
    return total + result[:, HD:], weighted + result[:, :HD]


def row_blocks(count):
    step = next(size for size in (160, 128, count) if count % size == 0)
    return [slice(first, first + step) for first in range(0, count, step)]


def add_stage(*refs):
    query_ref, best_ref, total_ref, sum_ref = refs[:4]
    shard_refs = refs[4:-2]
    total_out, sum_out = refs[-2:]
    heads = query_ref.shape[1] // HD
    shards_here = [(ref[:, :HD], with_ones(ref[:, HD:])) for ref in shard_refs]
    for rows in row_blocks(query_ref.shape[0]):
        queries = stacked(query_ref, rows, heads)
        best = stacked(best_ref, rows, heads)
        total = stacked(total_ref, rows, heads)
        weighted = stacked(sum_ref, rows, heads)
        for key_rows, value_rows in shards_here:
            total, weighted = add_shard(queries, best, key_rows, value_rows, total, weighted)
        unstack(total_out, rows, heads, total)
        unstack(sum_out, rows, heads, weighted)


def last_stage(earlier_count, last_count, *refs):
    query_ref, best_ref, old_total_ref, old_sum_ref, total_ref, sum_ref = refs[:6]
    earlier_refs = refs[6 : 6 + earlier_count]
    last_refs = refs[6 + earlier_count : 6 + earlier_count + last_count]
    out_hbm, out_ref, out_sems = refs[6 + earlier_count + last_count :]
    heads = query_ref.shape[1] // HD
    blocks = row_blocks(query_ref.shape[0])

    def load(shard_refs):
        return [(ref[:, :HD], with_ones(ref[:, HD:])) for ref in shard_refs]

    def out_copy(index, rows):
        return pltpu.make_async_copy(out_ref.at[rows], out_hbm.at[rows], out_sems.at[index])

    def finish(rows, total, weighted):
        unstack(out_ref, rows, heads, (weighted / total).astype(jnp.bfloat16))

    trusted = jnp.full((8, HD), True)
    shards_here = load(last_refs)
    for index, rows in enumerate(blocks):
        queries = stacked(query_ref, rows, heads)
        best = stacked(best_ref, rows, heads)
        total = stacked(total_ref, rows, heads)
        weighted = stacked(sum_ref, rows, heads)
        for key_rows, value_rows in shards_here:
            total, weighted = add_shard(queries, best, key_rows, value_rows, total, weighted)
        good = (total < total_limit).reshape(total.shape[0] // 8, 8, HD)
        trusted = trusted & jnp.all(good, axis=0)
        finish(rows, total, weighted)
        out_copy(index, rows).start()
    for index, rows in enumerate(blocks):
        out_copy(index, rows).wait()

    @pl.when(jnp.logical_not(jnp.all(trusted)))
    def exact_maximum():
        size = query_ref.shape[0] // len(blocks)

        def visit(index, unused):
            rows = pl.ds(pl.multiple_of(index * size, size), size)
            queries = stacked(query_ref, rows, heads)
            best = stacked(best_ref, rows, heads)
            weighted = stacked(old_sum_ref, rows, heads)
            total = stacked(old_total_ref, rows, heads)
            for key_rows, value_rows in load(earlier_refs + last_refs):
                scores = scores_of(queries, key_rows)
                new_best = jnp.maximum(best, jnp.max(scores, axis=1, keepdims=True))
                factor = jnp.exp2(best - new_best)
                weights = jnp.exp2(scores - widen(new_best, scores.shape[1]))
                result = jnp.dot(
                    weights.astype(jnp.bfloat16), value_rows, preferred_element_type=jnp.float32
                )
                weighted = weighted * factor + result[:, :HD]
                total = total * factor + result[:, HD:]
                best = new_best
            finish(rows, total, weighted)
            copy = out_copy(index, rows)
            copy.start()
            copy.wait()
            return unused

        lax.fori_loop(0, len(blocks), visit, 0)


def shards(queries, suffix_kv, prompt_kv, lengths):
    slots, width = queries.shape
    heads = width // HD
    loop_size = lax.axis_size("loop")
    own = prompt_kv[:, 0, :]
    suffix = suffix_kv[:, 0, :]
    shard_rows = own.shape[0]

    power_of_two = loop_size & (loop_size - 1) == 0

    def exchange(shard, step_of_core):
        hops = []
        for core, step in enumerate(step_of_core):
            for i in range(loop_size):
                to = i ^ step if power_of_two else (i + step) % loop_size
                hops.append((2 * i + core, 2 * to + core))
        return lax.ppermute(shard, ("loop", "pair"), hops)

    to_both = 1 - loop_size % 2
    early = [exchange(own, (1, 1))] * to_both
    middle = [exchange(own, (step, step + 1)) for step in range(1 + to_both, loop_size, 2)]
    in_hbm = pl.BlockSpec(memory_space=pltpu.HBM)
    in_vmem = pl.BlockSpec(memory_space=pltpu.VMEM)
    state = jax.ShapeDtypeStruct((slots, width), jnp.float32)

    cost = pl.CostEstimate(flops=1, bytes_accessed=1, transcendentals=0)

    best, total, weighted, queries = pl.pallas_call(
        local_stage,
        name="local_stage",
        out_shape=[state] * 3 + [jax.ShapeDtypeStruct((slots, width), queries.dtype)],
        in_specs=[in_hbm] * 4,
        out_specs=[in_vmem] * 4,
        scratch_shapes=[
            pltpu.SMEM(lengths.shape, lengths.dtype),
            pltpu.VMEM(suffix.shape, suffix.dtype),
            pltpu.VMEM(own.shape, own.dtype),
            pltpu.SemaphoreType.DMA((3,)),
            pltpu.SemaphoreType.DMA((slots // BLK,)),
        ],
        compiler_params=pltpu.CompilerParams(vmem_limit_bytes=24 * 2**20),
        cost_estimate=cost,
    )(*(pltpu.with_memory_space_constraint(x, pltpu.HBM) for x in (lengths, queries, suffix, own)))
    def add_shards(total, weighted, shards_now):
        if not shards_now:
            return total, weighted
        return pl.pallas_call(
            add_stage,
            name="add_stage",
            out_shape=[state] * 2,
            in_specs=[in_vmem] * (4 + len(shards_now)),
            out_specs=[in_vmem] * 2,
            compiler_params=pltpu.CompilerParams(vmem_limit_bytes=24 * 2**20),
            cost_estimate=cost,
        )(queries, best, total, weighted, *shards_now)

    middle, best = lax.optimization_barrier((middle, best))
    swap = [(p, p ^ 1) for p in range(2 * loop_size)]
    last = [lax.ppermute(shard, ("loop", "pair"), swap) for shard in middle]
    new_total, new_weighted = add_shards(total, weighted, middle + early)
    last_inputs = (queries, best, total, weighted, new_total, new_weighted)
    last_inputs += (*middle, *early, *last)
    return pl.pallas_call(
        functools.partial(last_stage, len(early) + len(middle), len(last)),
        name="last_stage",
        out_shape=jax.ShapeDtypeStruct((slots, width), jnp.bfloat16),
        in_specs=[in_vmem] * len(last_inputs),
        out_specs=in_hbm,
        scratch_shapes=[
            pltpu.VMEM((slots, width), jnp.bfloat16),
            pltpu.SemaphoreType.DMA((len(row_blocks(slots)),)),
        ],
        compiler_params=pltpu.CompilerParams(vmem_limit_bytes=32 * 2**20),
        cost_estimate=cost,
    )(*last_inputs)


def solution(mesh):
    placed = (
        P(("groups", "loop"), ("heads", "pair")),
        P(("groups", "loop"), "heads", None),
        P(("groups", "loop"), "heads", None),
        P("groups"),
    )
    return jax.shard_map(
        shards,
        mesh=mesh,
        in_specs=placed,
        out_specs=P(("groups", "loop"), ("heads", "pair")),
        check_vma=False,
    )
```

```python
import functools
import math

import jax
import jax.numpy as jnp
from jax import lax
from jax.experimental import pallas as pl
from jax.experimental.pallas import tpu as pltpu
from jax.sharding import PartitionSpec as P

HD = 128
AG_DEV = 2
MAXLEN = 320
BLK = 128

masked_score = -1e30
empty_best = 1e30
total_limit = 2.0**100
score_scale = math.log2(math.e) / math.sqrt(HD)


def scores_of(query_rows, key_rows):
    return (
        lax.dot_general(
            query_rows, key_rows, (((1,), (1,)), ((), ())), preferred_element_type=jnp.float32
        )
        * score_scale
    )


def with_ones(value_rows):
    return jnp.concatenate([value_rows, jnp.ones_like(value_rows)], axis=1)


def stacked(ref, rows, head_count):
    return jnp.concatenate([ref[rows, h * HD : (h + 1) * HD] for h in range(head_count)], axis=0)


def unstack(ref, rows, head_count, value):
    count = value.shape[0] // head_count
    for h in range(head_count):
        ref[rows, h * HD : (h + 1) * HD] = value[h * count : (h + 1) * count]


def widen(row_value, width):
    return jnp.concatenate([row_value] * (width // HD), axis=1)


def local_stage(
    lengths_hbm,
    query_hbm,
    suffix_hbm,
    own_hbm,
    best_ref,
    total_ref,
    sum_ref,
    query_ref,
    lengths_ref,
    suffix_ref,
    own_ref,
    whole_sems,
    block_sems,
):
    rows_all = query_ref.shape[0]
    heads = query_ref.shape[1] // HD
    blocks = rows_all // BLK
    whole = [
        pltpu.make_async_copy(source, target, whole_sems.at[i])
        for i, (source, target) in enumerate(
            [(lengths_hbm, lengths_ref), (own_hbm, own_ref), (suffix_hbm, suffix_ref)]
        )
    ]
    pieces = [
        pltpu.make_async_copy(
            query_hbm.at[pl.ds(block * BLK, BLK)],
            query_ref.at[pl.ds(block * BLK, BLK)],
            block_sems.at[block],
        )
        for block in range(blocks)
    ]
    for copy in whole + pieces:
        copy.start()
    for copy in whole + pieces:
        copy.wait()
    position = lax.axis_index("loop")
    own_keys = own_ref[:, :HD]
    own_values = with_ones(own_ref[:, HD:])
    window = BLK * ((MAXLEN + BLK - 2) // BLK) + BLK
    for block in range(blocks):
        stop = (block + 1) * BLK
        start = max(0, stop - window)
        rows = slice(block * BLK, stop)
        row_at = block * BLK + lax.broadcasted_iota(jnp.int32, (BLK, stop - start), 0)
        key_at = start + lax.broadcasted_iota(jnp.int32, (BLK, stop - start), 1)
        first = jnp.zeros_like(row_at)
        agent_end = 0
        for agent in range(AG_DEV):
            agent_end = agent_end + lengths_ref[position * AG_DEV + agent]
            first = jnp.where(row_at >= agent_end, agent_end, first)
        allowed = (key_at <= row_at) & (key_at >= first)
        queries = stacked(query_ref, rows, heads)
        own_scores = scores_of(queries, own_keys)
        suffix_scores = jnp.where(
            jnp.concatenate([allowed] * heads, axis=0),
            scores_of(queries, suffix_ref[start:stop, :HD]),
            masked_score,
        )
        best = jnp.maximum(
            jnp.max(own_scores, axis=1, keepdims=True),
            jnp.max(suffix_scores, axis=1, keepdims=True),
        )
        own_weights = jnp.exp2(own_scores - best).astype(jnp.bfloat16)
        suffix_weights = jnp.exp2(suffix_scores - best).astype(jnp.bfloat16)
        result = jnp.dot(own_weights, own_values, preferred_element_type=jnp.float32)
        result = result + jnp.dot(
            suffix_weights,
            with_ones(suffix_ref[start:stop, HD:]),
            preferred_element_type=jnp.float32,
        )
        row_at = block * BLK + lax.broadcasted_iota(jnp.int32, (BLK, HD), 0)
        live = jnp.concatenate([row_at < agent_end] * heads, axis=0)
        unstack(best_ref, rows, heads, jnp.where(live, best, empty_best))
        unstack(sum_ref, rows, heads, jnp.where(live, result[:, :HD], 0.0))
        unstack(total_ref, rows, heads, jnp.where(live, result[:, HD:], 1.0))


def add_shard(queries, best, key_rows, value_rows, total, weighted):
    scores = scores_of(queries, key_rows)
    weights = jnp.exp2(scores - widen(best, scores.shape[1])).astype(jnp.bfloat16)
    result = jnp.dot(weights, value_rows, preferred_element_type=jnp.float32)
    return total + result[:, HD:], weighted + result[:, :HD]


def row_blocks(count):
    step = next(size for size in (160, 128, count) if count % size == 0)
    return [slice(first, first + step) for first in range(0, count, step)]


def add_stage(*refs):
    query_ref, best_ref, total_ref, sum_ref = refs[:4]
    shard_refs = refs[4:-2]
    total_out, sum_out = refs[-2:]
    heads = query_ref.shape[1] // HD
    shards_here = [(ref[:, :HD], with_ones(ref[:, HD:])) for ref in shard_refs]
    for rows in row_blocks(query_ref.shape[0]):
        queries = stacked(query_ref, rows, heads)
        best = stacked(best_ref, rows, heads)
        total = stacked(total_ref, rows, heads)
        weighted = stacked(sum_ref, rows, heads)
        for key_rows, value_rows in shards_here:
            total, weighted = add_shard(queries, best, key_rows, value_rows, total, weighted)
        unstack(total_out, rows, heads, total)
        unstack(sum_out, rows, heads, weighted)


def last_stage(earlier_count, last_count, *refs):
    query_ref, best_ref, old_total_ref, old_sum_ref, total_ref, sum_ref = refs[:6]
    earlier_refs = refs[6 : 6 + earlier_count]
    last_refs = refs[6 + earlier_count : 6 + earlier_count + last_count]
    out_hbm, out_ref, out_sems = refs[6 + earlier_count + last_count :]
    heads = query_ref.shape[1] // HD
    blocks = row_blocks(query_ref.shape[0])

    def load(shard_refs):
        return [(ref[:, :HD], with_ones(ref[:, HD:])) for ref in shard_refs]

    def out_copy(index, rows):
        return pltpu.make_async_copy(out_ref.at[rows], out_hbm.at[rows], out_sems.at[index])

    def finish(rows, total, weighted):
        unstack(out_ref, rows, heads, (weighted / total).astype(jnp.bfloat16))

    trusted = jnp.full((8, HD), True)
    shards_here = load(last_refs)
    for index, rows in enumerate(blocks):
        queries = stacked(query_ref, rows, heads)
        best = stacked(best_ref, rows, heads)
        total = stacked(total_ref, rows, heads)
        weighted = stacked(sum_ref, rows, heads)
        for key_rows, value_rows in shards_here:
            total, weighted = add_shard(queries, best, key_rows, value_rows, total, weighted)
        good = (total < total_limit).reshape(total.shape[0] // 8, 8, HD)
        trusted = trusted & jnp.all(good, axis=0)
        finish(rows, total, weighted)
        out_copy(index, rows).start()
    for index, rows in enumerate(blocks):
        out_copy(index, rows).wait()

    @pl.when(jnp.logical_not(jnp.all(trusted)))
    def exact_maximum():
        size = query_ref.shape[0] // len(blocks)

        def visit(index, unused):
            rows = pl.ds(pl.multiple_of(index * size, size), size)
            queries = stacked(query_ref, rows, heads)
            best = stacked(best_ref, rows, heads)
            weighted = stacked(old_sum_ref, rows, heads)
            total = stacked(old_total_ref, rows, heads)
            for key_rows, value_rows in load(earlier_refs + last_refs):
                scores = scores_of(queries, key_rows)
                new_best = jnp.maximum(best, jnp.max(scores, axis=1, keepdims=True))
                factor = jnp.exp2(best - new_best)
                weights = jnp.exp2(scores - widen(new_best, scores.shape[1]))
                result = jnp.dot(
                    weights.astype(jnp.bfloat16), value_rows, preferred_element_type=jnp.float32
                )
                weighted = weighted * factor + result[:, :HD]
                total = total * factor + result[:, HD:]
                best = new_best
            finish(rows, total, weighted)
            copy = out_copy(index, rows)
            copy.start()
            copy.wait()
            return unused

        lax.fori_loop(0, len(blocks), visit, 0)


def shards(queries, suffix_kv, prompt_kv, lengths):
    slots, width = queries.shape
    heads = width // HD
    loop_size = lax.axis_size("loop")
    own = prompt_kv[:, 0, :]
    suffix = suffix_kv[:, 0, :]
    shard_rows = own.shape[0]

    power_of_two = loop_size & (loop_size - 1) == 0

    def exchange(shard, step_of_core):
        hops = []
        for core, step in enumerate(step_of_core):
            for i in range(loop_size):
                to = i ^ step if power_of_two else (i + step) % loop_size
                hops.append((2 * i + core, 2 * to + core))
        return lax.ppermute(shard, ("loop", "pair"), hops)

    to_both = 1 - loop_size % 2
    both = [exchange(own, (1, 1))] * to_both
    middle = [exchange(own, (step, step + 1)) for step in range(1 + to_both, loop_size, 2)]
    in_hbm = pl.BlockSpec(memory_space=pltpu.HBM)
    in_vmem = pl.BlockSpec(memory_space=pltpu.VMEM)
    state = jax.ShapeDtypeStruct((slots, width), jnp.float32)

    cost = pl.CostEstimate(flops=1, bytes_accessed=1, transcendentals=0)

    best, total, weighted, queries = pl.pallas_call(
        local_stage,
        name="local_stage",
        out_shape=[state] * 3 + [jax.ShapeDtypeStruct((slots, width), queries.dtype)],
        in_specs=[in_hbm] * 4,
        out_specs=[in_vmem] * 4,
        scratch_shapes=[
            pltpu.SMEM(lengths.shape, lengths.dtype),
            pltpu.VMEM(suffix.shape, suffix.dtype),
            pltpu.VMEM(own.shape, own.dtype),
            pltpu.SemaphoreType.DMA((3,)),
            pltpu.SemaphoreType.DMA((slots // BLK,)),
        ],
        compiler_params=pltpu.CompilerParams(vmem_limit_bytes=24 * 2**20),
        cost_estimate=cost,
    )(*(pltpu.with_memory_space_constraint(x, pltpu.HBM) for x in (lengths, queries, suffix, own)))
    def add_shards(total, weighted, shards_now):
        if not shards_now:
            return total, weighted
        return pl.pallas_call(
            add_stage,
            name="add_stage",
            out_shape=[state] * 2,
            in_specs=[in_vmem] * (4 + len(shards_now)),
            out_specs=[in_vmem] * 2,
            compiler_params=pltpu.CompilerParams(vmem_limit_bytes=24 * 2**20),
            cost_estimate=cost,
        )(queries, best, total, weighted, *shards_now)

    middle, best = lax.optimization_barrier((middle, best))
    swap = [(p, p ^ 1) for p in range(2 * loop_size)]
    last = [lax.ppermute(shard, ("loop", "pair"), swap) for shard in middle]
    new_total, new_weighted = add_shards(total, weighted, middle)
    last_inputs = (queries, best, total, weighted, new_total, new_weighted)
    last_inputs += (*middle, *last, *both)
    return pl.pallas_call(
        functools.partial(last_stage, len(middle), len(last) + len(both)),
        name="last_stage",
        out_shape=jax.ShapeDtypeStruct((slots, width), jnp.bfloat16),
        in_specs=[in_vmem] * len(last_inputs),
        out_specs=in_hbm,
        scratch_shapes=[
            pltpu.VMEM((slots, width), jnp.bfloat16),
            pltpu.SemaphoreType.DMA((len(row_blocks(slots)),)),
        ],
        compiler_params=pltpu.CompilerParams(vmem_limit_bytes=32 * 2**20),
        cost_estimate=cost,
    )(*last_inputs)


def solution(mesh):
    placed = (
        P(("groups", "loop"), ("heads", "pair")),
        P(("groups", "loop"), "heads", None),
        P(("groups", "loop"), "heads", None),
        P("groups"),
    )
    return jax.shard_map(
        shards,
        mesh=mesh,
        in_specs=placed,
        out_specs=P(("groups", "loop"), ("heads", "pair")),
        check_vma=False,
    )
```

```python
import functools
import math

import jax
import jax.numpy as jnp
from jax import lax
from jax.experimental import pallas as pl
from jax.experimental.pallas import tpu as pltpu
from jax.sharding import PartitionSpec as P

HD = 128
AG_DEV = 2
MAXLEN = 320
BLK = 128

masked_score = -1e30
empty_best = 1e30
total_limit = 2.0**100
score_scale = math.log2(math.e) / math.sqrt(HD)


def scores_of(query_rows, key_rows):
    return (
        lax.dot_general(
            query_rows, key_rows, (((1,), (1,)), ((), ())), preferred_element_type=jnp.float32
        )
        * score_scale
    )


def with_ones(value_rows):
    return jnp.concatenate([value_rows, jnp.ones_like(value_rows)], axis=1)


def stacked(ref, rows, head_count):
    return jnp.concatenate([ref[rows, h * HD : (h + 1) * HD] for h in range(head_count)], axis=0)


def unstack(ref, rows, head_count, value):
    count = value.shape[0] // head_count
    for h in range(head_count):
        ref[rows, h * HD : (h + 1) * HD] = value[h * count : (h + 1) * count]


def widen(row_value, width):
    return jnp.concatenate([row_value] * (width // HD), axis=1)


def local_stage(
    lengths_hbm,
    query_hbm,
    suffix_hbm,
    own_hbm,
    best_ref,
    total_ref,
    sum_ref,
    query_ref,
    lengths_ref,
    suffix_ref,
    own_ref,
    whole_sems,
    block_sems,
):
    rows_all = query_ref.shape[0]
    heads = query_ref.shape[1] // HD
    blocks = rows_all // BLK
    whole = [
        pltpu.make_async_copy(source, target, whole_sems.at[i])
        for i, (source, target) in enumerate(
            [(lengths_hbm, lengths_ref), (own_hbm, own_ref), (suffix_hbm, suffix_ref)]
        )
    ]
    pieces = [
        pltpu.make_async_copy(
            query_hbm.at[pl.ds(block * BLK, BLK)],
            query_ref.at[pl.ds(block * BLK, BLK)],
            block_sems.at[block],
        )
        for block in range(blocks)
    ]
    for copy in whole + pieces:
        copy.start()
    for copy in whole + pieces:
        copy.wait()
    position = lax.axis_index("loop")
    window = BLK * ((MAXLEN + BLK - 2) // BLK) + BLK
    for block in range(blocks):
        stop = (block + 1) * BLK
        start = max(0, stop - window)
        rows = slice(block * BLK, stop)
        row_at = block * BLK + lax.broadcasted_iota(jnp.int32, (BLK, stop - start), 0)
        key_at = start + lax.broadcasted_iota(jnp.int32, (BLK, stop - start), 1)
        first = jnp.zeros_like(row_at)
        agent_end = 0
        for agent in range(AG_DEV):
            agent_end = agent_end + lengths_ref[position * AG_DEV + agent]
            first = jnp.where(row_at >= agent_end, agent_end, first)
        allowed = (key_at <= row_at) & (key_at >= first)
        queries = stacked(query_ref, rows, heads)
        shard = jnp.concatenate([own_ref[...], suffix_ref[start:stop]], axis=0)
        scores = scores_of(queries, shard[:, :HD])
        own_scores = scores[:, : own_ref.shape[0]]
        suffix_scores = jnp.where(
            jnp.concatenate([allowed] * heads, axis=0), scores[:, own_ref.shape[0] :], masked_score
        )
        scores = jnp.concatenate([own_scores, suffix_scores], axis=1)
        best = jnp.max(scores, axis=1, keepdims=True)
        weights = jnp.exp2(scores - best).astype(jnp.bfloat16)
        result = jnp.dot(weights, with_ones(shard[:, HD:]), preferred_element_type=jnp.float32)
        row_at = block * BLK + lax.broadcasted_iota(jnp.int32, (BLK, HD), 0)
        live = jnp.concatenate([row_at < agent_end] * heads, axis=0)
        unstack(best_ref, rows, heads, jnp.where(live, best, empty_best))
        unstack(sum_ref, rows, heads, jnp.where(live, result[:, :HD], 0.0))
        unstack(total_ref, rows, heads, jnp.where(live, result[:, HD:], 1.0))


def add_shard(queries, best, key_rows, value_rows, total, weighted):
    scores = scores_of(queries, key_rows)
    weights = jnp.exp2(scores - widen(best, scores.shape[1])).astype(jnp.bfloat16)
    result = jnp.dot(weights, value_rows, preferred_element_type=jnp.float32)
    return total + result[:, HD:], weighted + result[:, :HD]


def row_blocks(count, largest):
    step = next(size for size in (largest, 128, 16, count) if count % size == 0)
    return [slice(first, first + step) for first in range(0, count, step)]


def add_stage(*refs):
    query_ref, best_ref, total_ref, sum_ref = refs[:4]
    shard_refs = refs[4:-2]
    total_out, sum_out = refs[-2:]
    heads = query_ref.shape[1] // HD
    shards_here = [(ref[:, :HD], with_ones(ref[:, HD:])) for ref in shard_refs]
    for rows in row_blocks(query_ref.shape[0], 80):
        queries = stacked(query_ref, rows, heads)
        best = stacked(best_ref, rows, heads)
        total = stacked(total_ref, rows, heads)
        weighted = stacked(sum_ref, rows, heads)
        for key_rows, value_rows in shards_here:
            total, weighted = add_shard(queries, best, key_rows, value_rows, total, weighted)
        unstack(total_out, rows, heads, total)
        unstack(sum_out, rows, heads, weighted)


def last_stage(earlier_count, last_count, *refs):
    query_ref, best_ref, old_total_ref, old_sum_ref, total_ref, sum_ref = refs[:6]
    earlier_refs = refs[6 : 6 + earlier_count]
    last_refs = refs[6 + earlier_count : 6 + earlier_count + last_count]
    out_hbm, out_ref, out_sems = refs[6 + earlier_count + last_count :]
    heads = query_ref.shape[1] // HD
    blocks = row_blocks(query_ref.shape[0], 160)

    def out_copy(index, rows):
        return pltpu.make_async_copy(out_ref.at[rows], out_hbm.at[rows], out_sems.at[index])

    def finish(rows, total, weighted):
        unstack(out_ref, rows, heads, (weighted / total).astype(jnp.bfloat16))

    trusted = jnp.full((8, HD), True)
    shard = jnp.concatenate([ref[...] for ref in last_refs], axis=0)
    key_rows, value_rows = shard[:, :HD], with_ones(shard[:, HD:])
    for index, rows in enumerate(blocks):
        queries = stacked(query_ref, rows, heads)
        best = stacked(best_ref, rows, heads)
        total = stacked(total_ref, rows, heads)
        weighted = stacked(sum_ref, rows, heads)
        total, weighted = add_shard(queries, best, key_rows, value_rows, total, weighted)
        good = (total < total_limit).reshape(total.shape[0] // 8, 8, HD)
        trusted = trusted & jnp.all(good, axis=0)
        finish(rows, total, weighted)
        out_copy(index, rows).start()
    for index, rows in enumerate(blocks):
        out_copy(index, rows).wait()

    @pl.when(jnp.logical_not(jnp.all(trusted)))
    def exact_maximum():
        size = query_ref.shape[0] // len(blocks)

        def visit(index, unused):
            rows = pl.ds(pl.multiple_of(index * size, size), size)
            queries = stacked(query_ref, rows, heads)
            best = stacked(best_ref, rows, heads)
            weighted = stacked(old_sum_ref, rows, heads)
            total = stacked(old_total_ref, rows, heads)
            for shard_ref in earlier_refs + last_refs:
                key_rows, value_rows = shard_ref[:, :HD], with_ones(shard_ref[:, HD:])
                scores = scores_of(queries, key_rows)
                new_best = jnp.maximum(best, jnp.max(scores, axis=1, keepdims=True))
                factor = jnp.exp2(best - new_best)
                weights = jnp.exp2(scores - widen(new_best, scores.shape[1]))
                result = jnp.dot(
                    weights.astype(jnp.bfloat16), value_rows, preferred_element_type=jnp.float32
                )
                weighted = weighted * factor + result[:, :HD]
                total = total * factor + result[:, HD:]
                best = new_best
            finish(rows, total, weighted)
            copy = out_copy(index, rows)
            copy.start()
            copy.wait()
            return unused

        lax.fori_loop(0, len(blocks), visit, 0)


def shards(queries, suffix_kv, prompt_kv, lengths):
    slots, width = queries.shape
    heads = width // HD
    loop_size = lax.axis_size("loop")
    own = prompt_kv[:, 0, :]
    suffix = suffix_kv[:, 0, :]
    shard_rows = own.shape[0]

    power_of_two = loop_size & (loop_size - 1) == 0

    def exchange(shard, step_of_core):
        hops = []
        for core, step in enumerate(step_of_core):
            for i in range(loop_size):
                to = i ^ step if power_of_two else (i + step) % loop_size
                hops.append((2 * i + core, 2 * to + core))
        return lax.ppermute(shard, ("loop", "pair"), hops)

    to_both = 1 - loop_size % 2
    both = [exchange(own, (1, 1))] * to_both
    middle = [exchange(own, (step, step + 1)) for step in range(1 + to_both, loop_size, 2)]
    in_hbm = pl.BlockSpec(memory_space=pltpu.HBM)
    in_vmem = pl.BlockSpec(memory_space=pltpu.VMEM)
    state = jax.ShapeDtypeStruct((slots, width), jnp.float32)

    cost = pl.CostEstimate(flops=1, bytes_accessed=1, transcendentals=0)

    best, total, weighted, queries = pl.pallas_call(
        local_stage,
        name="local_stage",
        out_shape=[state] * 3 + [jax.ShapeDtypeStruct((slots, width), queries.dtype)],
        in_specs=[in_hbm] * 4,
        out_specs=[in_vmem] * 4,
        scratch_shapes=[
            pltpu.SMEM(lengths.shape, lengths.dtype),
            pltpu.VMEM(suffix.shape, suffix.dtype),
            pltpu.VMEM(own.shape, own.dtype),
            pltpu.SemaphoreType.DMA((3,)),
            pltpu.SemaphoreType.DMA((slots // BLK,)),
        ],
        compiler_params=pltpu.CompilerParams(vmem_limit_bytes=24 * 2**20),
        cost_estimate=cost,
    )(*(pltpu.with_memory_space_constraint(x, pltpu.HBM) for x in (lengths, queries, suffix, own)))
    def add_shards(total, weighted, shards_now):
        if not shards_now:
            return total, weighted
        return pl.pallas_call(
            add_stage,
            name="add_stage",
            out_shape=[state] * 2,
            in_specs=[in_vmem] * (4 + len(shards_now)),
            out_specs=[in_vmem] * 2,
            compiler_params=pltpu.CompilerParams(vmem_limit_bytes=24 * 2**20),
            cost_estimate=cost,
        )(queries, best, total, weighted, *shards_now)

    middle, best = lax.optimization_barrier((middle, best))
    swap = [(p, p ^ 1) for p in range(2 * loop_size)]
    last = [lax.ppermute(shard, ("loop", "pair"), swap) for shard in middle]
    new_total, new_weighted = add_shards(total, weighted, middle)
    last_inputs = (queries, best, total, weighted, new_total, new_weighted)
    last_inputs += (*middle, *last, *both)
    return pl.pallas_call(
        functools.partial(last_stage, len(middle), len(last) + len(both)),
        name="last_stage",
        out_shape=jax.ShapeDtypeStruct((slots, width), jnp.bfloat16),
        in_specs=[in_vmem] * len(last_inputs),
        out_specs=in_hbm,
        scratch_shapes=[
            pltpu.VMEM((slots, width), jnp.bfloat16),
            pltpu.SemaphoreType.DMA((len(row_blocks(slots, 160)),)),
        ],
        compiler_params=pltpu.CompilerParams(vmem_limit_bytes=32 * 2**20),
        cost_estimate=cost,
    )(*last_inputs)


def solution(mesh):
    placed = (
        P(("groups", "loop"), ("heads", "pair")),
        P(("groups", "loop"), "heads", None),
        P(("groups", "loop"), "heads", None),
        P("groups"),
    )
    return jax.shard_map(
        shards,
        mesh=mesh,
        in_specs=placed,
        out_specs=P(("groups", "loop"), ("heads", "pair")),
        check_vma=False,
    )
```

```python
import functools
import math

import jax
import jax.numpy as jnp
from jax import lax
from jax.experimental import pallas as pl
from jax.experimental.pallas import tpu as pltpu
from jax.sharding import PartitionSpec as P

HD = 128
AG_DEV = 2
MAXLEN = 320
BLK = 128

masked_score = -1e30
empty_best = 1e30
total_limit = 2.0**100
score_scale = math.log2(math.e) / math.sqrt(HD)


def scores_of(query_rows, key_rows):
    return (
        lax.dot_general(
            query_rows, key_rows, (((1,), (1,)), ((), ())), preferred_element_type=jnp.float32
        )
        * score_scale
    )


def with_ones(value_rows):
    return jnp.concatenate([value_rows, jnp.ones_like(value_rows)], axis=1)


def stacked(ref, rows, head_count):
    return jnp.concatenate([ref[rows, h * HD : (h + 1) * HD] for h in range(head_count)], axis=0)


def unstack(ref, rows, head_count, value):
    count = value.shape[0] // head_count
    for h in range(head_count):
        ref[rows, h * HD : (h + 1) * HD] = value[h * count : (h + 1) * count]


def widen(row_value, width):
    return jnp.concatenate([row_value] * (width // HD), axis=1)


def local_stage(
    lengths_hbm,
    query_hbm,
    suffix_hbm,
    own_hbm,
    best_ref,
    total_ref,
    sum_ref,
    query_ref,
    wide_ref,
    lengths_ref,
    suffix_ref,
    own_ref,
    whole_sems,
    block_sems,
):
    rows_all = query_ref.shape[0]
    heads = query_ref.shape[1] // HD
    blocks = rows_all // BLK
    whole = [
        pltpu.make_async_copy(source, target, whole_sems.at[i])
        for i, (source, target) in enumerate(
            [(lengths_hbm, lengths_ref), (own_hbm, own_ref), (suffix_hbm, suffix_ref)]
        )
    ]
    pieces = [
        pltpu.make_async_copy(
            query_hbm.at[pl.ds(block * BLK, BLK)],
            query_ref.at[pl.ds(block * BLK, BLK)],
            block_sems.at[block],
        )
        for block in range(blocks)
    ]
    for copy in whole + pieces:
        copy.start()
    for copy in whole + pieces:
        copy.wait()
    position = lax.axis_index("loop")
    window = BLK * ((MAXLEN + BLK - 2) // BLK) + BLK
    for block in range(blocks):
        stop = (block + 1) * BLK
        start = max(0, stop - window)
        rows = slice(block * BLK, stop)
        row_at = block * BLK + lax.broadcasted_iota(jnp.int32, (BLK, stop - start), 0)
        key_at = start + lax.broadcasted_iota(jnp.int32, (BLK, stop - start), 1)
        first = jnp.zeros_like(row_at)
        agent_end = 0
        for agent in range(AG_DEV):
            agent_end = agent_end + lengths_ref[position * AG_DEV + agent]
            first = jnp.where(row_at >= agent_end, agent_end, first)
        allowed = (key_at <= row_at) & (key_at >= first)
        queries = stacked(query_ref, rows, heads)
        shard = jnp.concatenate([own_ref[...], suffix_ref[start:stop]], axis=0)
        scores = scores_of(queries, shard[:, :HD])
        own_scores = scores[:, : own_ref.shape[0]]
        suffix_scores = jnp.where(
            jnp.concatenate([allowed] * heads, axis=0), scores[:, own_ref.shape[0] :], masked_score
        )
        scores = jnp.concatenate([own_scores, suffix_scores], axis=1)
        best = jnp.max(scores, axis=1, keepdims=True) / score_scale
        best = best.astype(jnp.bfloat16).astype(jnp.float32)
        weights = jnp.exp2(scores - best * score_scale).astype(jnp.bfloat16)
        result = jnp.dot(weights, with_ones(shard[:, HD:]), preferred_element_type=jnp.float32)
        row_at = block * BLK + lax.broadcasted_iota(jnp.int32, (BLK, HD), 0)
        live = jnp.concatenate([row_at < agent_end] * heads, axis=0)
        best = jnp.where(live, best, empty_best)
        unstack(best_ref, rows, heads, best * score_scale)
        lane = lax.broadcasted_iota(jnp.int32, best.shape, 1)
        point = jnp.where(lane == 0, -best, 0.0).astype(jnp.bfloat16)
        for h in range(heads):
            wide_ref[rows, 2 * h * HD : (2 * h + 1) * HD] = queries[h * BLK : (h + 1) * BLK]
            wide_ref[rows, (2 * h + 1) * HD : (2 * h + 2) * HD] = point[h * BLK : (h + 1) * BLK]
        unstack(sum_ref, rows, heads, jnp.where(live, result[:, :HD], 0.0))
        unstack(total_ref, rows, heads, jnp.where(live, result[:, HD:], 1.0))


def add_shard(queries, best, key_rows, value_rows, total, weighted):
    scores = scores_of(queries, key_rows)
    weights = jnp.exp2(scores - widen(best, scores.shape[1])).astype(jnp.bfloat16)
    result = jnp.dot(weights, value_rows, preferred_element_type=jnp.float32)
    return total + result[:, HD:], weighted + result[:, :HD]


def row_blocks(count, largest):
    step = next(size for size in (largest, 128, 16, count) if count % size == 0)
    return [slice(first, first + step) for first in range(0, count, step)]


def add_stage(*refs):
    wide_ref, total_ref, sum_ref = refs[:3]
    shard_refs = refs[3:-2]
    total_out, sum_out = refs[-2:]
    heads = sum_ref.shape[1] // HD
    shard = jnp.concatenate([ref[...] for ref in shard_refs], axis=0)
    key_rows, value_rows = with_ones(shard[:, :HD]), with_ones(shard[:, HD:])
    for rows in row_blocks(wide_ref.shape[0], 160):
        queries = jnp.concatenate(
            [wide_ref[rows, 2 * h * HD : (2 * h + 2) * HD] for h in range(heads)], axis=0
        )
        weights = jnp.exp2(scores_of(queries, key_rows)).astype(jnp.bfloat16)
        result = jnp.dot(weights, value_rows, preferred_element_type=jnp.float32)
        unstack(total_out, rows, heads, stacked(total_ref, rows, heads) + result[:, HD:])
        unstack(sum_out, rows, heads, stacked(sum_ref, rows, heads) + result[:, :HD])


def last_stage(earlier_count, last_count, *refs):
    query_ref, best_ref, old_total_ref, old_sum_ref, total_ref, sum_ref = refs[:6]
    earlier_refs = refs[6 : 6 + earlier_count]
    last_refs = refs[6 + earlier_count : 6 + earlier_count + last_count]
    out_hbm, out_ref, out_sems = refs[6 + earlier_count + last_count :]
    heads = query_ref.shape[1] // HD
    blocks = row_blocks(query_ref.shape[0], 160)

    def out_copy(index, rows):
        return pltpu.make_async_copy(out_ref.at[rows], out_hbm.at[rows], out_sems.at[index])

    def finish(rows, total, weighted):
        unstack(out_ref, rows, heads, (weighted / total).astype(jnp.bfloat16))

    trusted = jnp.full((8, HD), True)
    shard = jnp.concatenate([ref[...] for ref in last_refs], axis=0)
    key_rows, value_rows = shard[:, :HD], with_ones(shard[:, HD:])
    for index, rows in enumerate(blocks):
        queries = stacked(query_ref, rows, heads)
        best = stacked(best_ref, rows, heads)
        total = stacked(total_ref, rows, heads)
        weighted = stacked(sum_ref, rows, heads)
        total, weighted = add_shard(queries, best, key_rows, value_rows, total, weighted)
        good = (total < total_limit).reshape(total.shape[0] // 8, 8, HD)
        trusted = trusted & jnp.all(good, axis=0)
        finish(rows, total, weighted)
        out_copy(index, rows).start()
    for index, rows in enumerate(blocks):
        out_copy(index, rows).wait()

    @pl.when(jnp.logical_not(jnp.all(trusted)))
    def exact_maximum():
        size = query_ref.shape[0] // len(blocks)

        def visit(index, unused):
            rows = pl.ds(pl.multiple_of(index * size, size), size)
            queries = stacked(query_ref, rows, heads)
            best = stacked(best_ref, rows, heads)
            weighted = stacked(old_sum_ref, rows, heads)
            total = stacked(old_total_ref, rows, heads)
            for shard_ref in earlier_refs + last_refs:
                key_rows, value_rows = shard_ref[:, :HD], with_ones(shard_ref[:, HD:])
                scores = scores_of(queries, key_rows)
                new_best = jnp.maximum(best, jnp.max(scores, axis=1, keepdims=True))
                factor = jnp.exp2(best - new_best)
                weights = jnp.exp2(scores - widen(new_best, scores.shape[1]))
                result = jnp.dot(
                    weights.astype(jnp.bfloat16), value_rows, preferred_element_type=jnp.float32
                )
                weighted = weighted * factor + result[:, :HD]
                total = total * factor + result[:, HD:]
                best = new_best
            finish(rows, total, weighted)
            copy = out_copy(index, rows)
            copy.start()
            copy.wait()
            return unused

        lax.fori_loop(0, len(blocks), visit, 0)


def shards(queries, suffix_kv, prompt_kv, lengths):
    slots, width = queries.shape
    heads = width // HD
    loop_size = lax.axis_size("loop")
    own = prompt_kv[:, 0, :]
    suffix = suffix_kv[:, 0, :]
    shard_rows = own.shape[0]

    power_of_two = loop_size & (loop_size - 1) == 0

    def exchange(shard, step_of_core):
        hops = []
        for core, step in enumerate(step_of_core):
            for i in range(loop_size):
                to = i ^ step if power_of_two else (i + step) % loop_size
                hops.append((2 * i + core, 2 * to + core))
        return lax.ppermute(shard, ("loop", "pair"), hops)

    to_both = 1 - loop_size % 2
    both = [exchange(own, (1, 1))] * to_both
    middle = [exchange(own, (step, step + 1)) for step in range(1 + to_both, loop_size, 2)]
    in_hbm = pl.BlockSpec(memory_space=pltpu.HBM)
    in_vmem = pl.BlockSpec(memory_space=pltpu.VMEM)
    state = jax.ShapeDtypeStruct((slots, width), jnp.float32)

    cost = pl.CostEstimate(flops=1, bytes_accessed=1, transcendentals=0)

    best, total, weighted, queries, wide = pl.pallas_call(
        local_stage,
        name="local_stage",
        out_shape=[state] * 3
        + [
            jax.ShapeDtypeStruct((slots, width), queries.dtype),
            jax.ShapeDtypeStruct((slots, 2 * width), queries.dtype),
        ],
        in_specs=[in_hbm] * 4,
        out_specs=[in_vmem] * 5,
        scratch_shapes=[
            pltpu.SMEM(lengths.shape, lengths.dtype),
            pltpu.VMEM(suffix.shape, suffix.dtype),
            pltpu.VMEM(own.shape, own.dtype),
            pltpu.SemaphoreType.DMA((3,)),
            pltpu.SemaphoreType.DMA((slots // BLK,)),
        ],
        compiler_params=pltpu.CompilerParams(vmem_limit_bytes=24 * 2**20),
        cost_estimate=cost,
    )(*(pltpu.with_memory_space_constraint(x, pltpu.HBM) for x in (lengths, queries, suffix, own)))
    def add_shards(total, weighted, shards_now):
        if not shards_now:
            return total, weighted
        return pl.pallas_call(
            add_stage,
            name="add_stage",
            out_shape=[state] * 2,
            in_specs=[in_vmem] * (3 + len(shards_now)),
            out_specs=[in_vmem] * 2,
            compiler_params=pltpu.CompilerParams(vmem_limit_bytes=24 * 2**20),
            cost_estimate=cost,
        )(wide, total, weighted, *shards_now)

    middle, best = lax.optimization_barrier((middle, best))
    swap = [(p, p ^ 1) for p in range(2 * loop_size)]
    last = [lax.ppermute(shard, ("loop", "pair"), swap) for shard in middle]
    new_total, new_weighted = add_shards(total, weighted, middle)
    last_inputs = (queries, best, total, weighted, new_total, new_weighted)
    last_inputs += (*middle, *last, *both)
    return pl.pallas_call(
        functools.partial(last_stage, len(middle), len(last) + len(both)),
        name="last_stage",
        out_shape=jax.ShapeDtypeStruct((slots, width), jnp.bfloat16),
        in_specs=[in_vmem] * len(last_inputs),
        out_specs=in_hbm,
        scratch_shapes=[
            pltpu.VMEM((slots, width), jnp.bfloat16),
            pltpu.SemaphoreType.DMA((len(row_blocks(slots, 160)),)),
        ],
        compiler_params=pltpu.CompilerParams(vmem_limit_bytes=32 * 2**20),
        cost_estimate=cost,
    )(*last_inputs)


def solution(mesh):
    placed = (
        P(("groups", "loop"), ("heads", "pair")),
        P(("groups", "loop"), "heads", None),
        P(("groups", "loop"), "heads", None),
        P("groups"),
    )
    return jax.shard_map(
        shards,
        mesh=mesh,
        in_specs=placed,
        out_specs=P(("groups", "loop"), ("heads", "pair")),
        check_vma=False,
    )
```

```python
import functools
import math

import jax
import jax.numpy as jnp
from jax import lax
from jax.experimental import pallas as pl
from jax.experimental.pallas import tpu as pltpu
from jax.sharding import PartitionSpec as P

HD = 128
AG_DEV = 2
MAXLEN = 320
BLK = 128

masked_score = -1e30
empty_best = 1e30
total_limit = 2.0**100
score_scale = math.log2(math.e) / math.sqrt(HD)


def scores_of(query_rows, key_rows):
    return (
        lax.dot_general(
            query_rows, key_rows, (((1,), (1,)), ((), ())), preferred_element_type=jnp.float32
        )
        * score_scale
    )


def with_ones(value_rows):
    return jnp.concatenate([value_rows, jnp.ones_like(value_rows)], axis=1)


def stacked(ref, rows, head_count):
    return jnp.concatenate([ref[rows, h * HD : (h + 1) * HD] for h in range(head_count)], axis=0)


def unstack(ref, rows, head_count, value):
    count = value.shape[0] // head_count
    for h in range(head_count):
        ref[rows, h * HD : (h + 1) * HD] = value[h * count : (h + 1) * count]


def widen(row_value, width):
    return jnp.concatenate([row_value] * (width // HD), axis=1)


def local_stage(
    lengths_hbm,
    query_hbm,
    suffix_hbm,
    own_hbm,
    best_ref,
    total_ref,
    sum_ref,
    query_ref,
    lengths_ref,
    suffix_ref,
    own_ref,
    whole_sems,
    block_sems,
):
    rows_all = query_ref.shape[0]
    heads = query_ref.shape[1] // HD
    blocks = rows_all // BLK
    whole = [
        pltpu.make_async_copy(source, target, whole_sems.at[i])
        for i, (source, target) in enumerate(
            [(lengths_hbm, lengths_ref), (own_hbm, own_ref), (suffix_hbm, suffix_ref)]
        )
    ]
    pieces = [
        pltpu.make_async_copy(
            query_hbm.at[pl.ds(block * BLK, BLK)],
            query_ref.at[pl.ds(block * BLK, BLK)],
            block_sems.at[block],
        )
        for block in range(blocks)
    ]
    for copy in whole + pieces:
        copy.start()
    for copy in whole + pieces:
        copy.wait()
    position = lax.axis_index("loop")
    window = BLK * ((MAXLEN + BLK - 2) // BLK) + BLK
    for block in range(blocks):
        stop = (block + 1) * BLK
        start = max(0, stop - window)
        rows = slice(block * BLK, stop)
        row_at = block * BLK + lax.broadcasted_iota(jnp.int32, (BLK, stop - start), 0)
        key_at = start + lax.broadcasted_iota(jnp.int32, (BLK, stop - start), 1)
        first = jnp.zeros_like(row_at)
        agent_end = 0
        for agent in range(AG_DEV):
            agent_end = agent_end + lengths_ref[position * AG_DEV + agent]
            first = jnp.where(row_at >= agent_end, agent_end, first)
        allowed = (key_at <= row_at) & (key_at >= first)
        queries = stacked(query_ref, rows, heads)
        shard = jnp.concatenate([own_ref[...], suffix_ref[start:stop]], axis=0)
        scores = scores_of(queries, shard[:, :HD])
        own_scores = scores[:, : own_ref.shape[0]]
        suffix_scores = jnp.where(
            jnp.concatenate([allowed] * heads, axis=0), scores[:, own_ref.shape[0] :], masked_score
        )
        scores = jnp.concatenate([own_scores, suffix_scores], axis=1)
        best = jnp.max(scores, axis=1, keepdims=True)
        weights = jnp.exp2(scores - best).astype(jnp.bfloat16)
        result = jnp.dot(weights, with_ones(shard[:, HD:]), preferred_element_type=jnp.float32)
        row_at = block * BLK + lax.broadcasted_iota(jnp.int32, (BLK, HD), 0)
        live = jnp.concatenate([row_at < agent_end] * heads, axis=0)
        unstack(best_ref, rows, heads, jnp.where(live, best, empty_best))
        unstack(sum_ref, rows, heads, jnp.where(live, result[:, :HD], 0.0))
        unstack(total_ref, rows, heads, jnp.where(live, result[:, HD:], 1.0))


def staged(blocks, start, finish):
    coming = start(blocks[0])
    for index, rows in enumerate(blocks):
        now = coming
        if index + 1 < len(blocks):
            coming = start(blocks[index + 1])
        finish(index, rows, now)


def row_blocks(count, largest):
    step = next(size for size in (largest, 128, 16, count) if count % size == 0)
    return [slice(first, first + step) for first in range(0, count, step)]


def add_stage(*refs):
    query_ref, best_ref, total_ref, sum_ref = refs[:4]
    shard_refs = refs[4:-2]
    total_out, sum_out = refs[-2:]
    heads = query_ref.shape[1] // HD
    shard = jnp.concatenate([ref[...] for ref in shard_refs], axis=0)
    key_rows, value_rows = shard[:, :HD], with_ones(shard[:, HD:])

    def start(rows):
        return scores_of(stacked(query_ref, rows, heads), key_rows)

    def finish(index, rows, scores):
        best = stacked(best_ref, rows, heads)
        weights = jnp.exp2(scores - widen(best, scores.shape[1])).astype(jnp.bfloat16)
        result = jnp.dot(weights, value_rows, preferred_element_type=jnp.float32)
        unstack(total_out, rows, heads, stacked(total_ref, rows, heads) + result[:, HD:])
        unstack(sum_out, rows, heads, stacked(sum_ref, rows, heads) + result[:, :HD])

    staged(row_blocks(query_ref.shape[0], 80), start, finish)


def last_stage(earlier_count, last_count, *refs):
    query_ref, best_ref, old_total_ref, old_sum_ref, total_ref, sum_ref = refs[:6]
    earlier_refs = refs[6 : 6 + earlier_count]
    last_refs = refs[6 + earlier_count : 6 + earlier_count + last_count]
    out_hbm, out_ref, out_sems = refs[6 + earlier_count + last_count :]
    heads = query_ref.shape[1] // HD
    blocks = row_blocks(query_ref.shape[0], 80)

    def out_copy(index, rows):
        return pltpu.make_async_copy(out_ref.at[rows], out_hbm.at[rows], out_sems.at[index])

    def write(rows, total, weighted):
        unstack(out_ref, rows, heads, (weighted / total).astype(jnp.bfloat16))

    shard = jnp.concatenate([ref[...] for ref in last_refs], axis=0)
    trusted = [jnp.full((8, HD), True)]

    def start(rows):
        return scores_of(stacked(query_ref, rows, heads), shard[:, :HD])

    def finish(index, rows, scores):
        best = stacked(best_ref, rows, heads)
        weights = jnp.exp2(scores - widen(best, scores.shape[1]))
        lanes = sum(weights[:, i : i + HD] for i in range(0, scores.shape[1], HD))
        total = stacked(total_ref, rows, heads) + jnp.sum(lanes, axis=1, keepdims=True)
        weighted = stacked(sum_ref, rows, heads) + jnp.dot(
            weights.astype(jnp.bfloat16), shard[:, HD:], preferred_element_type=jnp.float32
        )
        good = (total < total_limit).reshape(total.shape[0] // 8, 8, HD)
        trusted[0] = trusted[0] & jnp.all(good, axis=0)
        write(rows, total, weighted)
        out_copy(index, rows).start()

    staged(blocks, start, finish)
    for index, rows in enumerate(blocks):
        out_copy(index, rows).wait()

    @pl.when(jnp.logical_not(jnp.all(trusted[0])))
    def exact_maximum():
        size = query_ref.shape[0] // len(blocks)

        def visit(index, unused):
            rows = pl.ds(pl.multiple_of(index * size, size), size)
            queries = stacked(query_ref, rows, heads)
            best = stacked(best_ref, rows, heads)
            weighted = stacked(old_sum_ref, rows, heads)
            total = stacked(old_total_ref, rows, heads)
            for shard_ref in earlier_refs + last_refs:
                key_rows, value_rows = shard_ref[:, :HD], with_ones(shard_ref[:, HD:])
                scores = scores_of(queries, key_rows)
                new_best = jnp.maximum(best, jnp.max(scores, axis=1, keepdims=True))
                factor = jnp.exp2(best - new_best)
                weights = jnp.exp2(scores - widen(new_best, scores.shape[1]))
                result = jnp.dot(
                    weights.astype(jnp.bfloat16), value_rows, preferred_element_type=jnp.float32
                )
                weighted = weighted * factor + result[:, :HD]
                total = total * factor + result[:, HD:]
                best = new_best
            write(rows, total, weighted)
            copy = out_copy(index, rows)
            copy.start()
            copy.wait()
            return unused

        lax.fori_loop(0, len(blocks), visit, 0)


def shards(queries, suffix_kv, prompt_kv, lengths):
    slots, width = queries.shape
    heads = width // HD
    loop_size = lax.axis_size("loop")
    own = prompt_kv[:, 0, :]
    suffix = suffix_kv[:, 0, :]
    shard_rows = own.shape[0]

    power_of_two = loop_size & (loop_size - 1) == 0

    def exchange(shard, step_of_core):
        hops = []
        for core, step in enumerate(step_of_core):
            for i in range(loop_size):
                to = i ^ step if power_of_two else (i + step) % loop_size
                hops.append((2 * i + core, 2 * to + core))
        return lax.ppermute(shard, ("loop", "pair"), hops)

    to_both = 1 - loop_size % 2
    both = [exchange(own, (1, 1))] * to_both
    middle = [exchange(own, (step, step + 1)) for step in range(1 + to_both, loop_size, 2)]
    in_hbm = pl.BlockSpec(memory_space=pltpu.HBM)
    in_vmem = pl.BlockSpec(memory_space=pltpu.VMEM)
    state = jax.ShapeDtypeStruct((slots, width), jnp.float32)

    cost = pl.CostEstimate(flops=1, bytes_accessed=1, transcendentals=0)

    best, total, weighted, queries = pl.pallas_call(
        local_stage,
        name="local_stage",
        out_shape=[state] * 3 + [jax.ShapeDtypeStruct((slots, width), queries.dtype)],
        in_specs=[in_hbm] * 4,
        out_specs=[in_vmem] * 4,
        scratch_shapes=[
            pltpu.SMEM(lengths.shape, lengths.dtype),
            pltpu.VMEM(suffix.shape, suffix.dtype),
            pltpu.VMEM(own.shape, own.dtype),
            pltpu.SemaphoreType.DMA((3,)),
            pltpu.SemaphoreType.DMA((slots // BLK,)),
        ],
        compiler_params=pltpu.CompilerParams(vmem_limit_bytes=24 * 2**20),
        cost_estimate=cost,
    )(*(pltpu.with_memory_space_constraint(x, pltpu.HBM) for x in (lengths, queries, suffix, own)))
    def add_shards(total, weighted, shards_now):
        if not shards_now:
            return total, weighted
        return pl.pallas_call(
            add_stage,
            name="add_stage",
            out_shape=[state] * 2,
            in_specs=[in_vmem] * (4 + len(shards_now)),
            out_specs=[in_vmem] * 2,
            compiler_params=pltpu.CompilerParams(vmem_limit_bytes=24 * 2**20),
            cost_estimate=cost,
        )(queries, best, total, weighted, *shards_now)

    middle, best = lax.optimization_barrier((middle, best))
    swap = [(p, p ^ 1) for p in range(2 * loop_size)]
    last = [lax.ppermute(shard, ("loop", "pair"), swap) for shard in middle]
    new_total, new_weighted = add_shards(total, weighted, middle)
    last_inputs = (queries, best, total, weighted, new_total, new_weighted)
    last_inputs += (*middle, *last, *both)
    return pl.pallas_call(
        functools.partial(last_stage, len(middle), len(last) + len(both)),
        name="last_stage",
        out_shape=jax.ShapeDtypeStruct((slots, width), jnp.bfloat16),
        in_specs=[in_vmem] * len(last_inputs),
        out_specs=in_hbm,
        scratch_shapes=[
            pltpu.VMEM((slots, width), jnp.bfloat16),
            pltpu.SemaphoreType.DMA((len(row_blocks(slots, 80)),)),
        ],
        compiler_params=pltpu.CompilerParams(vmem_limit_bytes=32 * 2**20),
        cost_estimate=cost,
    )(*last_inputs)


def solution(mesh):
    placed = (
        P(("groups", "loop"), ("heads", "pair")),
        P(("groups", "loop"), "heads", None),
        P(("groups", "loop"), "heads", None),
        P("groups"),
    )
    return jax.shard_map(
        shards,
        mesh=mesh,
        in_specs=placed,
        out_specs=P(("groups", "loop"), ("heads", "pair")),
        check_vma=False,
    )
```

```python
import functools
import math

import jax
import jax.numpy as jnp
from jax import lax
from jax.experimental import pallas as pl
from jax.experimental.pallas import tpu as pltpu
from jax.sharding import PartitionSpec as P

HD = 128
AG_DEV = 2
MAXLEN = 320
BLK = 128

masked_score = -1e30
empty_best = 1e30
total_limit = 2.0**100
score_scale = math.log2(math.e) / math.sqrt(HD)


def scores_of(query_rows, key_rows):
    return (
        lax.dot_general(
            query_rows, key_rows, (((1,), (1,)), ((), ())), preferred_element_type=jnp.float32
        )
        * score_scale
    )


def with_ones(value_rows):
    return jnp.concatenate([value_rows, jnp.ones_like(value_rows)], axis=1)


def stacked(ref, rows, head_count):
    return jnp.concatenate([ref[rows, h * HD : (h + 1) * HD] for h in range(head_count)], axis=0)


def unstack(ref, rows, head_count, value):
    count = value.shape[0] // head_count
    for h in range(head_count):
        ref[rows, h * HD : (h + 1) * HD] = value[h * count : (h + 1) * count]


def widen(row_value, width):
    return jnp.concatenate([row_value] * (width // HD), axis=1)


def local_stage(
    lengths_hbm,
    query_hbm,
    suffix_hbm,
    own_hbm,
    best_ref,
    total_ref,
    sum_ref,
    query_ref,
    lengths_ref,
    suffix_ref,
    own_ref,
    whole_sems,
    block_sems,
):
    rows_all = query_ref.shape[0]
    heads = query_ref.shape[1] // HD
    blocks = rows_all // BLK
    whole = [
        pltpu.make_async_copy(source, target, whole_sems.at[i])
        for i, (source, target) in enumerate(
            [(lengths_hbm, lengths_ref), (own_hbm, own_ref), (suffix_hbm, suffix_ref)]
        )
    ]
    pieces = [
        pltpu.make_async_copy(
            query_hbm.at[pl.ds(block * BLK, BLK)],
            query_ref.at[pl.ds(block * BLK, BLK)],
            block_sems.at[block],
        )
        for block in range(blocks)
    ]
    for copy in whole + pieces:
        copy.start()
    for copy in whole + pieces:
        copy.wait()
    position = lax.axis_index("loop")
    window = BLK * ((MAXLEN + BLK - 2) // BLK) + BLK
    for block in range(blocks):
        stop = (block + 1) * BLK
        start = max(0, stop - window)
        rows = slice(block * BLK, stop)
        row_at = block * BLK + lax.broadcasted_iota(jnp.int32, (BLK, stop - start), 0)
        key_at = start + lax.broadcasted_iota(jnp.int32, (BLK, stop - start), 1)
        first = jnp.zeros_like(row_at)
        agent_end = 0
        for agent in range(AG_DEV):
            agent_end = agent_end + lengths_ref[position * AG_DEV + agent]
            first = jnp.where(row_at >= agent_end, agent_end, first)
        allowed = (key_at <= row_at) & (key_at >= first)
        queries = stacked(query_ref, rows, heads)
        shard = jnp.concatenate([own_ref[...], suffix_ref[start:stop]], axis=0)
        scores = scores_of(queries, shard[:, :HD])
        own_scores = scores[:, : own_ref.shape[0]]
        suffix_scores = jnp.where(
            jnp.concatenate([allowed] * heads, axis=0), scores[:, own_ref.shape[0] :], masked_score
        )
        scores = jnp.concatenate([own_scores, suffix_scores], axis=1)
        best = jnp.max(scores, axis=1, keepdims=True)
        weights = jnp.exp2(scores - best).astype(jnp.bfloat16)
        result = jnp.dot(weights, with_ones(shard[:, HD:]), preferred_element_type=jnp.float32)
        row_at = block * BLK + lax.broadcasted_iota(jnp.int32, (BLK, HD), 0)
        live = jnp.concatenate([row_at < agent_end] * heads, axis=0)
        unstack(best_ref, rows, heads, jnp.where(live, best, empty_best))
        unstack(sum_ref, rows, heads, jnp.where(live, result[:, :HD], 0.0))
        unstack(total_ref, rows, heads, jnp.where(live, result[:, HD:], 1.0))


def staged(blocks, start, finish):
    coming = start(blocks[0])
    for index, rows in enumerate(blocks):
        now = coming
        if index + 1 < len(blocks):
            coming = start(blocks[index + 1])
        finish(index, rows, now)


def row_blocks(count, largest):
    step = next(size for size in (largest, 128, 16, count) if count % size == 0)
    return [slice(first, first + step) for first in range(0, count, step)]


def add_stage(*refs):
    query_ref, best_ref, total_ref, sum_ref = refs[:4]
    shard_refs = refs[4:-2]
    total_out, sum_out = refs[-2:]
    heads = query_ref.shape[1] // HD
    shard = jnp.concatenate([ref[...] for ref in shard_refs], axis=0)
    key_rows, value_rows = shard[:, :HD], with_ones(shard[:, HD:])

    def start(rows):
        return scores_of(stacked(query_ref, rows, heads), key_rows)

    def finish(index, rows, scores):
        best = stacked(best_ref, rows, heads)
        weights = jnp.exp2(scores - widen(best, scores.shape[1])).astype(jnp.bfloat16)
        result = jnp.dot(weights, value_rows, preferred_element_type=jnp.float32)
        unstack(total_out, rows, heads, stacked(total_ref, rows, heads) + result[:, HD:])
        unstack(sum_out, rows, heads, stacked(sum_ref, rows, heads) + result[:, :HD])

    staged(row_blocks(query_ref.shape[0], 80), start, finish)


def last_stage(far_count, near_count, *refs):
    query_ref, best_ref, old_total_ref, old_sum_ref, total_ref, sum_ref = refs[:6]
    refs = refs[6:]
    far_refs, refs = refs[:far_count], refs[far_count:]
    swapped_refs, refs = refs[:far_count], refs[far_count:]
    by_swap_refs, refs = refs[:near_count], refs[near_count:]
    direct_refs, refs = refs[:near_count], refs[near_count:]
    out_hbm, out_ref, out_sems = refs
    heads = query_ref.shape[1] // HD
    blocks = row_blocks(query_ref.shape[0], 80)

    def out_copy(index, rows):
        return pltpu.make_async_copy(out_ref.at[rows], out_hbm.at[rows], out_sems.at[index])

    def write(rows, total, weighted):
        unstack(out_ref, rows, heads, (weighted / total).astype(jnp.bfloat16))

    is_direct = lax.axis_index("pair") == 1

    def last_shards():
        shards_here = [ref[...] for ref in swapped_refs]
        for by_swap, direct in zip(by_swap_refs, direct_refs):
            shards_here.append(jnp.where(is_direct, direct[...], by_swap[...]))
        return shards_here

    shard = jnp.concatenate(last_shards(), axis=0)
    trusted = [jnp.full((8, HD), True)]

    def start(rows):
        return scores_of(stacked(query_ref, rows, heads), shard[:, :HD])

    def finish(index, rows, scores):
        best = stacked(best_ref, rows, heads)
        weights = jnp.exp2(scores - widen(best, scores.shape[1]))
        lanes = sum(weights[:, i : i + HD] for i in range(0, scores.shape[1], HD))
        total = stacked(total_ref, rows, heads) + jnp.sum(lanes, axis=1, keepdims=True)
        weighted = stacked(sum_ref, rows, heads) + jnp.dot(
            weights.astype(jnp.bfloat16), shard[:, HD:], preferred_element_type=jnp.float32
        )
        good = (total < total_limit).reshape(total.shape[0] // 8, 8, HD)
        trusted[0] = trusted[0] & jnp.all(good, axis=0)
        write(rows, total, weighted)
        out_copy(index, rows).start()

    staged(blocks, start, finish)
    is_trusted = jnp.all(trusted[0])
    for index, rows in enumerate(blocks):
        out_copy(index, rows).wait()

    @pl.when(jnp.logical_not(is_trusted))
    def exact_maximum():
        size = query_ref.shape[0] // len(blocks)

        def visit(index, unused):
            rows = pl.ds(pl.multiple_of(index * size, size), size)
            queries = stacked(query_ref, rows, heads)
            best = stacked(best_ref, rows, heads)
            weighted = stacked(old_sum_ref, rows, heads)
            total = stacked(old_total_ref, rows, heads)
            for shard in [ref[...] for ref in far_refs] + last_shards():
                key_rows, value_rows = shard[:, :HD], with_ones(shard[:, HD:])
                scores = scores_of(queries, key_rows)
                new_best = jnp.maximum(best, jnp.max(scores, axis=1, keepdims=True))
                factor = jnp.exp2(best - new_best)
                weights = jnp.exp2(scores - widen(new_best, scores.shape[1]))
                result = jnp.dot(
                    weights.astype(jnp.bfloat16), value_rows, preferred_element_type=jnp.float32
                )
                weighted = weighted * factor + result[:, :HD]
                total = total * factor + result[:, HD:]
                best = new_best
            write(rows, total, weighted)
            copy = out_copy(index, rows)
            copy.start()
            copy.wait()
            return unused

        lax.fori_loop(0, len(blocks), visit, 0)


def shards(queries, suffix_kv, prompt_kv, lengths):
    slots, width = queries.shape
    heads = width // HD
    loop_size = lax.axis_size("loop")
    own = prompt_kv[:, 0, :]
    suffix = suffix_kv[:, 0, :]
    shard_rows = own.shape[0]

    power_of_two = loop_size & (loop_size - 1) == 0

    def partner(i, step):
        return i ^ step if power_of_two else (i + step) % loop_size

    single = [1] * (1 - loop_size % 2)
    single_hops = [
        hop
        for i in range(loop_size)
        for hop in ((2 * i, 2 * partner(i, 1) + 1), (2 * i + 1, 2 * i))
    ]
    near = [lax.ppermute(own, ("loop", "pair"), single_hops) for step in single]
    far = []
    for step in range(1 + len(single), loop_size, 2):
        hops = [
            (2 * i + core, 2 * partner(i, step + core) + core)
            for core in range(2)
            for i in range(loop_size)
        ]
        far.append(lax.ppermute(own, ("loop", "pair"), hops))
    in_hbm = pl.BlockSpec(memory_space=pltpu.HBM)
    in_vmem = pl.BlockSpec(memory_space=pltpu.VMEM)
    state = jax.ShapeDtypeStruct((slots, width), jnp.float32)

    cost = pl.CostEstimate(flops=1, bytes_accessed=1, transcendentals=0)

    best, total, weighted, queries = pl.pallas_call(
        local_stage,
        name="local_stage",
        out_shape=[state] * 3 + [jax.ShapeDtypeStruct((slots, width), queries.dtype)],
        in_specs=[in_hbm] * 4,
        out_specs=[in_vmem] * 4,
        scratch_shapes=[
            pltpu.SMEM(lengths.shape, lengths.dtype),
            pltpu.VMEM(suffix.shape, suffix.dtype),
            pltpu.VMEM(own.shape, own.dtype),
            pltpu.SemaphoreType.DMA((3,)),
            pltpu.SemaphoreType.DMA((slots // BLK,)),
        ],
        compiler_params=pltpu.CompilerParams(vmem_limit_bytes=24 * 2**20),
        cost_estimate=cost,
    )(*(pltpu.with_memory_space_constraint(x, pltpu.HBM) for x in (lengths, queries, suffix, own)))
    def add_shards(total, weighted, shards_now):
        if not shards_now:
            return total, weighted
        return pl.pallas_call(
            add_stage,
            name="add_stage",
            out_shape=[state] * 2,
            in_specs=[in_vmem] * (4 + len(shards_now)),
            out_specs=[in_vmem] * 2,
            compiler_params=pltpu.CompilerParams(vmem_limit_bytes=24 * 2**20),
            cost_estimate=cost,
        )(queries, best, total, weighted, *shards_now)

    near, far, best = lax.optimization_barrier((near, far, best))
    swap = [(p, p ^ 1) for p in range(2 * loop_size)]
    far_swapped = [lax.ppermute(shard, ("loop", "pair"), swap) for shard in far]
    near_swapped = [lax.ppermute(shard, ("loop", "pair"), swap) for shard in near]
    new_total, new_weighted = add_shards(total, weighted, far)
    last_inputs = (queries, best, total, weighted, new_total, new_weighted)
    last_inputs += (*far, *far_swapped, *near_swapped, *near)
    return pl.pallas_call(
        functools.partial(last_stage, len(far), len(near)),
        name="last_stage",
        out_shape=jax.ShapeDtypeStruct((slots, width), jnp.bfloat16),
        in_specs=[in_vmem] * len(last_inputs),
        out_specs=in_hbm,
        scratch_shapes=[
            pltpu.VMEM((slots, width), jnp.bfloat16),
            pltpu.SemaphoreType.DMA((len(row_blocks(slots, 80)),)),
        ],
        compiler_params=pltpu.CompilerParams(vmem_limit_bytes=32 * 2**20),
        cost_estimate=cost,
    )(*last_inputs)


def solution(mesh):
    placed = (
        P(("groups", "loop"), ("heads", "pair")),
        P(("groups", "loop"), "heads", None),
        P(("groups", "loop"), "heads", None),
        P("groups"),
    )
    return jax.shard_map(
        shards,
        mesh=mesh,
        in_specs=placed,
        out_specs=P(("groups", "loop"), ("heads", "pair")),
        check_vma=False,
    )
```

```python
import functools
import math

import jax
import jax.numpy as jnp
from jax import lax
from jax.experimental import pallas as pl
from jax.experimental.pallas import tpu as pltpu
from jax.sharding import PartitionSpec as P

HD = 128
AG_DEV = 2
MAXLEN = 320
BLK = 128

masked_score = -1e30
empty_best = 1e30
total_limit = 2.0**100
score_scale = math.log2(math.e) / math.sqrt(HD)


def scores_of(query_rows, key_rows):
    return (
        lax.dot_general(
            query_rows, key_rows, (((1,), (1,)), ((), ())), preferred_element_type=jnp.float32
        )
        * score_scale
    )


def with_ones(value_rows):
    return jnp.concatenate([value_rows, jnp.ones_like(value_rows)], axis=1)


def stacked(ref, rows, head_count):
    return jnp.concatenate([ref[rows, h * HD : (h + 1) * HD] for h in range(head_count)], axis=0)


def unstack(ref, rows, head_count, value):
    count = value.shape[0] // head_count
    for h in range(head_count):
        ref[rows, h * HD : (h + 1) * HD] = value[h * count : (h + 1) * count]


def widen(row_value, width):
    return jnp.concatenate([row_value] * (width // HD), axis=1)


def local_stage(
    lengths_hbm,
    query_hbm,
    suffix_hbm,
    own_hbm,
    best_ref,
    total_ref,
    sum_ref,
    query_ref,
    lengths_ref,
    suffix_ref,
    own_ref,
    whole_sems,
    block_sems,
):
    rows_all = query_ref.shape[0]
    heads = query_ref.shape[1] // HD
    blocks = rows_all // BLK
    whole = [
        pltpu.make_async_copy(source, target, whole_sems.at[i])
        for i, (source, target) in enumerate(
            [(lengths_hbm, lengths_ref), (own_hbm, own_ref), (suffix_hbm, suffix_ref)]
        )
    ]
    pieces = [
        pltpu.make_async_copy(
            query_hbm.at[pl.ds(block * BLK, BLK)],
            query_ref.at[pl.ds(block * BLK, BLK)],
            block_sems.at[block],
        )
        for block in range(blocks)
    ]
    for copy in whole + pieces:
        copy.start()
    for copy in whole + pieces:
        copy.wait()
    position = lax.axis_index("loop")
    window = BLK * ((MAXLEN + BLK - 2) // BLK) + BLK
    for block in range(blocks):
        stop = (block + 1) * BLK
        start = max(0, stop - window)
        rows = slice(block * BLK, stop)
        row_at = block * BLK + lax.broadcasted_iota(jnp.int32, (BLK, stop - start), 0)
        key_at = start + lax.broadcasted_iota(jnp.int32, (BLK, stop - start), 1)
        first = jnp.zeros_like(row_at)
        agent_end = 0
        for agent in range(AG_DEV):
            agent_end = agent_end + lengths_ref[position * AG_DEV + agent]
            first = jnp.where(row_at >= agent_end, agent_end, first)
        allowed = (key_at <= row_at) & (key_at >= first)
        queries = stacked(query_ref, rows, heads)
        shard = jnp.concatenate([own_ref[...], suffix_ref[start:stop]], axis=0)
        scores = scores_of(queries, shard[:, :HD])
        own_scores = scores[:, : own_ref.shape[0]]
        suffix_scores = jnp.where(
            jnp.concatenate([allowed] * heads, axis=0), scores[:, own_ref.shape[0] :], masked_score
        )
        scores = jnp.concatenate([own_scores, suffix_scores], axis=1)
        best = jnp.max(scores, axis=1, keepdims=True)
        weights = jnp.exp2(scores - best).astype(jnp.bfloat16)
        result = jnp.dot(weights, with_ones(shard[:, HD:]), preferred_element_type=jnp.float32)
        row_at = block * BLK + lax.broadcasted_iota(jnp.int32, (BLK, HD), 0)
        live = jnp.concatenate([row_at < agent_end] * heads, axis=0)
        unstack(best_ref, rows, heads, jnp.where(live, best, empty_best))
        unstack(sum_ref, rows, heads, jnp.where(live, result[:, :HD], 0.0))
        unstack(total_ref, rows, heads, jnp.where(live, result[:, HD:], 1.0))


def staged(blocks, start, finish):
    coming = start(blocks[0])
    for index, rows in enumerate(blocks):
        now = coming
        if index + 1 < len(blocks):
            coming = start(blocks[index + 1])
        finish(index, rows, now)


def row_blocks(count, largest):
    step = next(size for size in (largest, 128, 16, count) if count % size == 0)
    return [slice(first, first + step) for first in range(0, count, step)]


def add_stage(*refs):
    query_ref, best_ref, total_ref, sum_ref = refs[:4]
    shard_refs = refs[4:-2]
    total_out, sum_out = refs[-2:]
    heads = query_ref.shape[1] // HD
    shard = jnp.concatenate([ref[...] for ref in shard_refs], axis=0)
    key_rows, value_rows = shard[:, :HD], with_ones(shard[:, HD:])

    def start(rows):
        return scores_of(stacked(query_ref, rows, heads), key_rows)

    def finish(index, rows, scores):
        best = stacked(best_ref, rows, heads)
        weights = jnp.exp2(scores - widen(best, scores.shape[1])).astype(jnp.bfloat16)
        result = jnp.dot(weights, value_rows, preferred_element_type=jnp.float32)
        unstack(total_out, rows, heads, stacked(total_ref, rows, heads) + result[:, HD:])
        unstack(sum_out, rows, heads, stacked(sum_ref, rows, heads) + result[:, :HD])

    staged(row_blocks(query_ref.shape[0], 80), start, finish)


def last_stage(paired_count, single_count, *refs):
    query_ref, best_ref, old_total_ref, old_sum_ref, total_ref, sum_ref = refs[:6]
    refs = refs[6:]
    paired_refs, refs = refs[:paired_count], refs[paired_count:]
    swapped_refs, refs = refs[:paired_count], refs[paired_count:]
    by_swap_refs, refs = refs[:single_count], refs[single_count:]
    direct_refs, refs = refs[:single_count], refs[single_count:]
    out_hbm, out_ref, out_sems = refs
    heads = query_ref.shape[1] // HD
    blocks = row_blocks(query_ref.shape[0], 80)

    def out_copy(index, rows):
        return pltpu.make_async_copy(out_ref.at[rows], out_hbm.at[rows], out_sems.at[index])

    def write(rows, total, weighted):
        unstack(out_ref, rows, heads, (weighted / total).astype(jnp.bfloat16))

    is_direct = lax.axis_index("pair") == 0

    def last_shards():
        shards_here = [ref[...] for ref in swapped_refs]
        for by_swap, direct in zip(by_swap_refs, direct_refs):
            shards_here.append(jnp.where(is_direct, direct[...], by_swap[...]))
        return shards_here

    shard = jnp.concatenate(last_shards(), axis=0)
    trusted = [jnp.full((8, HD), True)]

    def start(rows):
        return scores_of(stacked(query_ref, rows, heads), shard[:, :HD])

    def finish(index, rows, scores):
        best = stacked(best_ref, rows, heads)
        weights = jnp.exp2(scores - widen(best, scores.shape[1]))
        lanes = sum(weights[:, i : i + HD] for i in range(0, scores.shape[1], HD))
        total = stacked(total_ref, rows, heads) + jnp.sum(lanes, axis=1, keepdims=True)
        weighted = stacked(sum_ref, rows, heads) + jnp.dot(
            weights.astype(jnp.bfloat16), shard[:, HD:], preferred_element_type=jnp.float32
        )
        good = (total < total_limit).reshape(total.shape[0] // 8, 8, HD)
        trusted[0] = trusted[0] & jnp.all(good, axis=0)
        write(rows, total, weighted)
        out_copy(index, rows).start()

    staged(blocks, start, finish)
    is_trusted = jnp.all(trusted[0])
    for index, rows in enumerate(blocks):
        out_copy(index, rows).wait()

    @pl.when(jnp.logical_not(is_trusted))
    def exact_maximum():
        size = query_ref.shape[0] // len(blocks)

        def visit(index, unused):
            rows = pl.ds(pl.multiple_of(index * size, size), size)
            queries = stacked(query_ref, rows, heads)
            best = stacked(best_ref, rows, heads)
            weighted = stacked(old_sum_ref, rows, heads)
            total = stacked(old_total_ref, rows, heads)
            for shard in [ref[...] for ref in paired_refs] + last_shards():
                key_rows, value_rows = shard[:, :HD], with_ones(shard[:, HD:])
                scores = scores_of(queries, key_rows)
                new_best = jnp.maximum(best, jnp.max(scores, axis=1, keepdims=True))
                factor = jnp.exp2(best - new_best)
                weights = jnp.exp2(scores - widen(new_best, scores.shape[1]))
                result = jnp.dot(
                    weights.astype(jnp.bfloat16), value_rows, preferred_element_type=jnp.float32
                )
                weighted = weighted * factor + result[:, :HD]
                total = total * factor + result[:, HD:]
                best = new_best
            write(rows, total, weighted)
            copy = out_copy(index, rows)
            copy.start()
            copy.wait()
            return unused

        lax.fori_loop(0, len(blocks), visit, 0)


def shards(queries, suffix_kv, prompt_kv, lengths):
    slots, width = queries.shape
    heads = width // HD
    loop_size = lax.axis_size("loop")
    own = prompt_kv[:, 0, :]
    suffix = suffix_kv[:, 0, :]
    shard_rows = own.shape[0]

    power_of_two = loop_size & (loop_size - 1) == 0

    def partner(i, step):
        return i ^ step if power_of_two else (i + step) % loop_size

    paired = []
    for step in range(1, loop_size - 1, 2):
        hops = [
            hop
            for i in range(loop_size)
            for hop in (
                (2 * i, 2 * partner(i, step) + 1),
                (2 * i + 1, 2 * partner(i, step + 1)),
            )
        ]
        paired.append(lax.ppermute(own, ("loop", "pair"), hops))
    single = []
    if loop_size % 2 == 0:
        hops = [
            hop
            for i in range(loop_size)
            for hop in ((2 * i, 2 * i + 1), (2 * i + 1, 2 * partner(i, loop_size - 1)))
        ]
        single.append(lax.ppermute(own, ("loop", "pair"), hops))
    in_hbm = pl.BlockSpec(memory_space=pltpu.HBM)
    in_vmem = pl.BlockSpec(memory_space=pltpu.VMEM)
    state = jax.ShapeDtypeStruct((slots, width), jnp.float32)

    cost = pl.CostEstimate(flops=1, bytes_accessed=1, transcendentals=0)

    best, total, weighted, queries = pl.pallas_call(
        local_stage,
        name="local_stage",
        out_shape=[state] * 3 + [jax.ShapeDtypeStruct((slots, width), queries.dtype)],
        in_specs=[in_hbm] * 4,
        out_specs=[in_vmem] * 4,
        scratch_shapes=[
            pltpu.SMEM(lengths.shape, lengths.dtype),
            pltpu.VMEM(suffix.shape, suffix.dtype),
            pltpu.VMEM(own.shape, own.dtype),
            pltpu.SemaphoreType.DMA((3,)),
            pltpu.SemaphoreType.DMA((slots // BLK,)),
        ],
        compiler_params=pltpu.CompilerParams(vmem_limit_bytes=24 * 2**20),
        cost_estimate=cost,
    )(*(pltpu.with_memory_space_constraint(x, pltpu.HBM) for x in (lengths, queries, suffix, own)))
    def add_shards(total, weighted, shards_now):
        if not shards_now:
            return total, weighted
        return pl.pallas_call(
            add_stage,
            name="add_stage",
            out_shape=[state] * 2,
            in_specs=[in_vmem] * (4 + len(shards_now)),
            out_specs=[in_vmem] * 2,
            compiler_params=pltpu.CompilerParams(vmem_limit_bytes=24 * 2**20),
            cost_estimate=cost,
        )(queries, best, total, weighted, *shards_now)

    single, paired, best = lax.optimization_barrier((single, paired, best))
    swap = [(p, p ^ 1) for p in range(2 * loop_size)]
    paired_swapped = [lax.ppermute(shard, ("loop", "pair"), swap) for shard in paired]
    single_swapped = [lax.ppermute(shard, ("loop", "pair"), swap) for shard in single]
    new_total, new_weighted = add_shards(total, weighted, paired)
    last_inputs = (queries, best, total, weighted, new_total, new_weighted)
    last_inputs += (*paired, *paired_swapped, *single_swapped, *single)
    return pl.pallas_call(
        functools.partial(last_stage, len(paired), len(single)),
        name="last_stage",
        out_shape=jax.ShapeDtypeStruct((slots, width), jnp.bfloat16),
        in_specs=[in_vmem] * len(last_inputs),
        out_specs=in_hbm,
        scratch_shapes=[
            pltpu.VMEM((slots, width), jnp.bfloat16),
            pltpu.SemaphoreType.DMA((len(row_blocks(slots, 80)),)),
        ],
        compiler_params=pltpu.CompilerParams(vmem_limit_bytes=32 * 2**20),
        cost_estimate=cost,
    )(*last_inputs)


def solution(mesh):
    placed = (
        P(("groups", "loop"), ("heads", "pair")),
        P(("groups", "loop"), "heads", None),
        P(("groups", "loop"), "heads", None),
        P("groups"),
    )
    return jax.shard_map(
        shards,
        mesh=mesh,
        in_specs=placed,
        out_specs=P(("groups", "loop"), ("heads", "pair")),
        check_vma=False,
    )
```

```python
import functools
import math

import jax
import jax.numpy as jnp
from jax import lax
from jax.experimental import pallas as pl
from jax.experimental.pallas import tpu as pltpu
from jax.sharding import PartitionSpec as P

HD = 128
AG_DEV = 2
MAXLEN = 320
BLK = 128

masked_score = -1e30
empty_best = 1e30
total_limit = 2.0**100
score_scale = math.log2(math.e) / math.sqrt(HD)


def scores_of(query_rows, key_rows):
    return (
        lax.dot_general(
            query_rows, key_rows, (((1,), (1,)), ((), ())), preferred_element_type=jnp.float32
        )
        * score_scale
    )


def with_ones(value_rows):
    return jnp.concatenate([value_rows, jnp.ones_like(value_rows)], axis=1)


def stacked(ref, rows, head_count):
    return jnp.concatenate([ref[rows, h * HD : (h + 1) * HD] for h in range(head_count)], axis=0)


def unstack(ref, rows, head_count, value):
    count = value.shape[0] // head_count
    for h in range(head_count):
        ref[rows, h * HD : (h + 1) * HD] = value[h * count : (h + 1) * count]


def widen(row_value, width):
    return jnp.concatenate([row_value] * (width // HD), axis=1)


def local_stage(
    lengths_hbm,
    query_hbm,
    suffix_hbm,
    own_hbm,
    best_ref,
    total_ref,
    sum_ref,
    query_ref,
    lengths_ref,
    suffix_ref,
    own_ref,
    whole_sems,
    block_sems,
):
    rows_all = query_ref.shape[0]
    heads = query_ref.shape[1] // HD
    blocks = rows_all // BLK
    whole = [
        pltpu.make_async_copy(source, target, whole_sems.at[i])
        for i, (source, target) in enumerate(
            [(lengths_hbm, lengths_ref), (own_hbm, own_ref), (suffix_hbm, suffix_ref)]
        )
    ]
    pieces = [
        pltpu.make_async_copy(
            query_hbm.at[pl.ds(block * BLK, BLK)],
            query_ref.at[pl.ds(block * BLK, BLK)],
            block_sems.at[block],
        )
        for block in range(blocks)
    ]
    for copy in whole + pieces:
        copy.start()
    for copy in whole + pieces:
        copy.wait()
    position = lax.axis_index("loop")
    window = BLK * ((MAXLEN + BLK - 2) // BLK) + BLK
    for block in range(blocks):
        stop = (block + 1) * BLK
        start = max(0, stop - window)
        rows = slice(block * BLK, stop)
        row_at = block * BLK + lax.broadcasted_iota(jnp.int32, (BLK, stop - start), 0)
        key_at = start + lax.broadcasted_iota(jnp.int32, (BLK, stop - start), 1)
        first = jnp.zeros_like(row_at)
        agent_end = 0
        for agent in range(AG_DEV):
            agent_end = agent_end + lengths_ref[position * AG_DEV + agent]
            first = jnp.where(row_at >= agent_end, agent_end, first)
        allowed = (key_at <= row_at) & (key_at >= first)
        queries = stacked(query_ref, rows, heads)
        shard = jnp.concatenate([own_ref[...], suffix_ref[start:stop]], axis=0)
        scores = scores_of(queries, shard[:, :HD])
        own_scores = scores[:, : own_ref.shape[0]]
        suffix_scores = jnp.where(
            jnp.concatenate([allowed] * heads, axis=0), scores[:, own_ref.shape[0] :], masked_score
        )
        scores = jnp.concatenate([own_scores, suffix_scores], axis=1)
        best = jnp.max(scores, axis=1, keepdims=True)
        weights = jnp.exp2(scores - best).astype(jnp.bfloat16)
        result = jnp.dot(weights, with_ones(shard[:, HD:]), preferred_element_type=jnp.float32)
        row_at = block * BLK + lax.broadcasted_iota(jnp.int32, (BLK, HD), 0)
        live = jnp.concatenate([row_at < agent_end] * heads, axis=0)
        unstack(best_ref, rows, heads, jnp.where(live, best, empty_best))
        unstack(sum_ref, rows, heads, jnp.where(live, result[:, :HD], 0.0))
        unstack(total_ref, rows, heads, jnp.where(live, result[:, HD:], 1.0))


def staged(blocks, start, finish):
    coming = start(blocks[0])
    for index, rows in enumerate(blocks):
        now = coming
        if index + 1 < len(blocks):
            coming = start(blocks[index + 1])
        finish(index, rows, now)


def row_blocks(count, largest):
    step = next(size for size in (largest, 128, 16, count) if count % size == 0)
    return [slice(first, first + step) for first in range(0, count, step)]


def add_stage(*refs):
    query_ref, best_ref, total_ref, sum_ref = refs[:4]
    shard_refs = refs[4:-2]
    total_out, sum_out = refs[-2:]
    heads = query_ref.shape[1] // HD
    shard = jnp.concatenate([ref[...] for ref in shard_refs], axis=0)
    key_rows, value_rows = shard[:, :HD], with_ones(shard[:, HD:])

    def start(rows):
        return scores_of(stacked(query_ref, rows, heads), key_rows)

    def finish(index, rows, scores):
        best = stacked(best_ref, rows, heads)
        weights = jnp.exp2(scores - widen(best, scores.shape[1])).astype(jnp.bfloat16)
        result = jnp.dot(weights, value_rows, preferred_element_type=jnp.float32)
        unstack(total_out, rows, heads, stacked(total_ref, rows, heads) + result[:, HD:])
        unstack(sum_out, rows, heads, stacked(sum_ref, rows, heads) + result[:, :HD])

    staged(row_blocks(query_ref.shape[0], 80), start, finish)


def last_stage(paired_count, single_count, *refs):
    query_ref, best_ref, old_total_ref, old_sum_ref, total_ref, sum_ref = refs[:6]
    refs = refs[6:]
    paired_refs, refs = refs[:paired_count], refs[paired_count:]
    swapped_refs, refs = refs[:paired_count], refs[paired_count:]
    by_swap_refs, refs = refs[:single_count], refs[single_count:]
    direct_refs, refs = refs[:single_count], refs[single_count:]
    out_hbm, out_ref, out_sems = refs
    heads = query_ref.shape[1] // HD
    blocks = row_blocks(query_ref.shape[0], 80)

    def out_copy(index, rows):
        return pltpu.make_async_copy(out_ref.at[rows], out_hbm.at[rows], out_sems.at[index])

    def write(rows, total, weighted):
        unstack(out_ref, rows, heads, (weighted / total).astype(jnp.bfloat16))

    is_direct = lax.axis_index("pair") == 0

    def last_shards():
        return [
            jnp.where(is_direct, direct[...], by_swap[...])
            for by_swap, direct in zip(by_swap_refs, direct_refs)
        ]

    shard = jnp.concatenate(last_shards(), axis=0)
    trusted = [jnp.full((8, HD), True)]

    def start(rows):
        return scores_of(stacked(query_ref, rows, heads), shard[:, :HD])

    def finish(index, rows, scores):
        best = stacked(best_ref, rows, heads)
        weights = jnp.exp2(scores - widen(best, scores.shape[1]))
        lanes = sum(weights[:, i : i + HD] for i in range(0, scores.shape[1], HD))
        total = stacked(total_ref, rows, heads) + jnp.sum(lanes, axis=1, keepdims=True)
        weighted = stacked(sum_ref, rows, heads) + jnp.dot(
            weights.astype(jnp.bfloat16), shard[:, HD:], preferred_element_type=jnp.float32
        )
        good = (total < total_limit).reshape(total.shape[0] // 8, 8, HD)
        trusted[0] = trusted[0] & jnp.all(good, axis=0)
        write(rows, total, weighted)
        out_copy(index, rows).start()

    staged(blocks, start, finish)
    is_trusted = jnp.all(trusted[0])
    for index, rows in enumerate(blocks):
        out_copy(index, rows).wait()

    @pl.when(jnp.logical_not(is_trusted))
    def exact_maximum():
        size = query_ref.shape[0] // len(blocks)

        def visit(index, unused):
            rows = pl.ds(pl.multiple_of(index * size, size), size)
            queries = stacked(query_ref, rows, heads)
            best = stacked(best_ref, rows, heads)
            weighted = stacked(old_sum_ref, rows, heads)
            total = stacked(old_total_ref, rows, heads)
            for shard in [ref[...] for ref in paired_refs + swapped_refs] + last_shards():
                key_rows, value_rows = shard[:, :HD], with_ones(shard[:, HD:])
                scores = scores_of(queries, key_rows)
                new_best = jnp.maximum(best, jnp.max(scores, axis=1, keepdims=True))
                factor = jnp.exp2(best - new_best)
                weights = jnp.exp2(scores - widen(new_best, scores.shape[1]))
                result = jnp.dot(
                    weights.astype(jnp.bfloat16), value_rows, preferred_element_type=jnp.float32
                )
                weighted = weighted * factor + result[:, :HD]
                total = total * factor + result[:, HD:]
                best = new_best
            write(rows, total, weighted)
            copy = out_copy(index, rows)
            copy.start()
            copy.wait()
            return unused

        lax.fori_loop(0, len(blocks), visit, 0)


def shards(queries, suffix_kv, prompt_kv, lengths):
    slots, width = queries.shape
    heads = width // HD
    loop_size = lax.axis_size("loop")
    own = prompt_kv[:, 0, :]
    suffix = suffix_kv[:, 0, :]
    shard_rows = own.shape[0]

    power_of_two = loop_size & (loop_size - 1) == 0

    def partner(i, step):
        return i ^ step if power_of_two else (i + step) % loop_size

    paired = []
    for step in range(1, loop_size - 1, 2):
        hops = [
            hop
            for i in range(loop_size)
            for hop in (
                (2 * i, 2 * partner(i, step) + 1),
                (2 * i + 1, 2 * partner(i, step + 1)),
            )
        ]
        paired.append(lax.ppermute(own, ("loop", "pair"), hops))
    single = []
    if loop_size % 2 == 0:
        hops = [
            hop
            for i in range(loop_size)
            for hop in ((2 * i, 2 * i + 1), (2 * i + 1, 2 * partner(i, loop_size - 1)))
        ]
        single.append(lax.ppermute(own, ("loop", "pair"), hops))
    in_hbm = pl.BlockSpec(memory_space=pltpu.HBM)
    in_vmem = pl.BlockSpec(memory_space=pltpu.VMEM)
    state = jax.ShapeDtypeStruct((slots, width), jnp.float32)

    cost = pl.CostEstimate(flops=1, bytes_accessed=1, transcendentals=0)

    best, total, weighted, queries = pl.pallas_call(
        local_stage,
        name="local_stage",
        out_shape=[state] * 3 + [jax.ShapeDtypeStruct((slots, width), queries.dtype)],
        in_specs=[in_hbm] * 4,
        out_specs=[in_vmem] * 4,
        scratch_shapes=[
            pltpu.SMEM(lengths.shape, lengths.dtype),
            pltpu.VMEM(suffix.shape, suffix.dtype),
            pltpu.VMEM(own.shape, own.dtype),
            pltpu.SemaphoreType.DMA((3,)),
            pltpu.SemaphoreType.DMA((slots // BLK,)),
        ],
        compiler_params=pltpu.CompilerParams(vmem_limit_bytes=24 * 2**20),
        cost_estimate=cost,
    )(*(pltpu.with_memory_space_constraint(x, pltpu.HBM) for x in (lengths, queries, suffix, own)))
    def add_shards(total, weighted, shards_now):
        if not shards_now:
            return total, weighted
        return pl.pallas_call(
            add_stage,
            name="add_stage",
            out_shape=[state] * 2,
            in_specs=[in_vmem] * (4 + len(shards_now)),
            out_specs=[in_vmem] * 2,
            compiler_params=pltpu.CompilerParams(vmem_limit_bytes=24 * 2**20),
            cost_estimate=cost,
        )(queries, best, total, weighted, *shards_now)

    swap = [(p, p ^ 1) for p in range(2 * loop_size)]

    def swapped(shards_now):
        return [lax.ppermute(shard, ("loop", "pair"), swap) for shard in shards_now]

    paired, best = lax.optimization_barrier((paired, best))
    paired_swapped = swapped(paired)
    new_total, new_weighted = add_shards(total, weighted, paired)
    single, new_total = lax.optimization_barrier((single, new_total))
    single_swapped = swapped(single)
    if not single:
        single = single_swapped = [paired_swapped.pop()]
    new_total, new_weighted = add_shards(new_total, new_weighted, paired_swapped)
    last_inputs = (queries, best, total, weighted, new_total, new_weighted)
    last_inputs += (*paired, *paired_swapped, *single_swapped, *single)
    return pl.pallas_call(
        functools.partial(last_stage, len(paired), len(single)),
        name="last_stage",
        out_shape=jax.ShapeDtypeStruct((slots, width), jnp.bfloat16),
        in_specs=[in_vmem] * len(last_inputs),
        out_specs=in_hbm,
        scratch_shapes=[
            pltpu.VMEM((slots, width), jnp.bfloat16),
            pltpu.SemaphoreType.DMA((len(row_blocks(slots, 80)),)),
        ],
        compiler_params=pltpu.CompilerParams(vmem_limit_bytes=32 * 2**20),
        cost_estimate=cost,
    )(*last_inputs)


def solution(mesh):
    placed = (
        P(("groups", "loop"), ("heads", "pair")),
        P(("groups", "loop"), "heads", None),
        P(("groups", "loop"), "heads", None),
        P("groups"),
    )
    return jax.shard_map(
        shards,
        mesh=mesh,
        in_specs=placed,
        out_specs=P(("groups", "loop"), ("heads", "pair")),
        check_vma=False,
    )
```

```python
import functools
import math

import jax
import jax.numpy as jnp
from jax import lax
from jax.experimental import pallas as pl
from jax.experimental.pallas import tpu as pltpu
from jax.sharding import PartitionSpec as P

HD = 128
AG_DEV = 2
MAXLEN = 320
BLK = 128

masked_score = -1e30
empty_best = 1e30
total_limit = 2.0**100
score_scale = math.log2(math.e) / math.sqrt(HD)


def scores_of(query_rows, key_rows):
    return (
        lax.dot_general(
            query_rows, key_rows, (((1,), (1,)), ((), ())), preferred_element_type=jnp.float32
        )
        * score_scale
    )


def with_ones(value_rows):
    return jnp.concatenate([value_rows, jnp.ones_like(value_rows)], axis=1)


def stacked(ref, rows, head_count):
    return jnp.concatenate([ref[rows, h * HD : (h + 1) * HD] for h in range(head_count)], axis=0)


def unstack(ref, rows, head_count, value):
    count = value.shape[0] // head_count
    for h in range(head_count):
        ref[rows, h * HD : (h + 1) * HD] = value[h * count : (h + 1) * count]


def widen(row_value, width):
    return jnp.concatenate([row_value] * (width // HD), axis=1)


def local_stage(
    lengths_hbm,
    query_hbm,
    suffix_hbm,
    own_hbm,
    best_ref,
    total_ref,
    sum_ref,
    query_ref,
    lengths_ref,
    suffix_ref,
    own_ref,
    whole_sems,
    block_sems,
):
    rows_all = query_ref.shape[0]
    heads = query_ref.shape[1] // HD
    blocks = rows_all // BLK
    whole = [
        pltpu.make_async_copy(source, target, whole_sems.at[i])
        for i, (source, target) in enumerate(
            [(lengths_hbm, lengths_ref), (own_hbm, own_ref), (suffix_hbm, suffix_ref)]
        )
    ]
    pieces = [
        pltpu.make_async_copy(
            query_hbm.at[pl.ds(block * BLK, BLK)],
            query_ref.at[pl.ds(block * BLK, BLK)],
            block_sems.at[block],
        )
        for block in range(blocks)
    ]
    for copy in whole + pieces:
        copy.start()
    for copy in whole + pieces:
        copy.wait()
    position = lax.axis_index("loop")
    window = BLK * ((MAXLEN + BLK - 2) // BLK) + BLK
    for block in range(blocks):
        stop = (block + 1) * BLK
        start = max(0, stop - window)
        rows = slice(block * BLK, stop)
        row_at = block * BLK + lax.broadcasted_iota(jnp.int32, (BLK, stop - start), 0)
        key_at = start + lax.broadcasted_iota(jnp.int32, (BLK, stop - start), 1)
        first = jnp.zeros_like(row_at)
        agent_end = 0
        for agent in range(AG_DEV):
            agent_end = agent_end + lengths_ref[position * AG_DEV + agent]
            first = jnp.where(row_at >= agent_end, agent_end, first)
        allowed = (key_at <= row_at) & (key_at >= first)
        queries = stacked(query_ref, rows, heads)
        shard = jnp.concatenate([own_ref[...], suffix_ref[start:stop]], axis=0)
        scores = scores_of(queries, shard[:, :HD])
        own_scores = scores[:, : own_ref.shape[0]]
        suffix_scores = jnp.where(
            jnp.concatenate([allowed] * heads, axis=0), scores[:, own_ref.shape[0] :], masked_score
        )
        scores = jnp.concatenate([own_scores, suffix_scores], axis=1)
        best = jnp.max(scores, axis=1, keepdims=True)
        weights = jnp.exp2(scores - best).astype(jnp.bfloat16)
        result = jnp.dot(weights, with_ones(shard[:, HD:]), preferred_element_type=jnp.float32)
        row_at = block * BLK + lax.broadcasted_iota(jnp.int32, (BLK, HD), 0)
        live = jnp.concatenate([row_at < agent_end] * heads, axis=0)
        unstack(best_ref, rows, heads, jnp.where(live, best, empty_best))
        unstack(sum_ref, rows, heads, jnp.where(live, result[:, :HD], 0.0))
        unstack(total_ref, rows, heads, jnp.where(live, result[:, HD:], 1.0))


def staged(blocks, start, finish):
    coming = start(blocks[0])
    for index, rows in enumerate(blocks):
        now = coming
        if index + 1 < len(blocks):
            coming = start(blocks[index + 1])
        finish(index, rows, now)


def row_blocks(count, largest):
    step = next(size for size in (largest, 128, 16, count) if count % size == 0)
    return [slice(first, first + step) for first in range(0, count, step)]


def add_stage(*refs):
    query_ref, best_ref, total_ref, sum_ref = refs[:4]
    shard_refs = refs[4:-2]
    total_out, sum_out = refs[-2:]
    heads = query_ref.shape[1] // HD
    shard = jnp.concatenate([ref[...] for ref in shard_refs], axis=0)
    key_rows, value_rows = shard[:, :HD], with_ones(shard[:, HD:])

    def start(rows):
        return scores_of(stacked(query_ref, rows, heads), key_rows)

    def finish(index, rows, scores):
        best = stacked(best_ref, rows, heads)
        weights = jnp.exp2(scores - widen(best, scores.shape[1])).astype(jnp.bfloat16)
        result = jnp.dot(weights, value_rows, preferred_element_type=jnp.float32)
        unstack(total_out, rows, heads, stacked(total_ref, rows, heads) + result[:, HD:])
        unstack(sum_out, rows, heads, stacked(sum_ref, rows, heads) + result[:, :HD])

    staged(row_blocks(query_ref.shape[0], 80), start, finish)


def last_stage(paired_count, single_count, *refs):
    query_ref, best_ref, old_total_ref, old_sum_ref, total_ref, sum_ref = refs[:6]
    refs = refs[6:]
    paired_refs, refs = refs[:paired_count], refs[paired_count:]
    swapped_refs, refs = refs[:paired_count], refs[paired_count:]
    by_swap_refs, refs = refs[:single_count], refs[single_count:]
    direct_refs, refs = refs[:single_count], refs[single_count:]
    out_hbm, out_ref, out_sems = refs
    heads = query_ref.shape[1] // HD
    blocks = row_blocks(query_ref.shape[0], 80)

    def out_copy(index, rows):
        return pltpu.make_async_copy(out_ref.at[rows], out_hbm.at[rows], out_sems.at[index])

    def write(rows, total, weighted):
        unstack(out_ref, rows, heads, (weighted / total).astype(jnp.bfloat16))

    is_direct = lax.axis_index("pair") == 0

    def last_shards():
        return [
            jnp.where(is_direct, direct[...], by_swap[...])
            for by_swap, direct in zip(by_swap_refs, direct_refs)
        ]

    shard = jnp.concatenate(last_shards(), axis=0)
    trusted = [jnp.full((8, HD), True)]

    def start(rows):
        return scores_of(stacked(query_ref, rows, heads), shard[:, :HD])

    def finish(index, rows, scores):
        best = stacked(best_ref, rows, heads)
        weights = jnp.exp2(scores - widen(best, scores.shape[1]))
        lanes = sum(weights[:, i : i + HD] for i in range(0, scores.shape[1], HD))
        total = stacked(total_ref, rows, heads) + jnp.sum(lanes, axis=1, keepdims=True)
        weighted = stacked(sum_ref, rows, heads) + jnp.dot(
            weights.astype(jnp.bfloat16), shard[:, HD:], preferred_element_type=jnp.float32
        )
        good = (total < total_limit).reshape(total.shape[0] // 8, 8, HD)
        trusted[0] = trusted[0] & jnp.all(good, axis=0)
        write(rows, total, weighted)
        out_copy(index, rows).start()

    staged(blocks, start, finish)
    is_trusted = jnp.all(trusted[0])
    for index, rows in enumerate(blocks):
        out_copy(index, rows).wait()

    @pl.when(jnp.logical_not(is_trusted))
    def exact_maximum():
        size = query_ref.shape[0] // len(blocks)

        def visit(index, unused):
            rows = pl.ds(pl.multiple_of(index * size, size), size)
            queries = stacked(query_ref, rows, heads)
            best = stacked(best_ref, rows, heads)
            weighted = stacked(old_sum_ref, rows, heads)
            total = stacked(old_total_ref, rows, heads)
            for shard in [ref[...] for ref in paired_refs + swapped_refs] + last_shards():
                key_rows, value_rows = shard[:, :HD], with_ones(shard[:, HD:])
                scores = scores_of(queries, key_rows)
                new_best = jnp.maximum(best, jnp.max(scores, axis=1, keepdims=True))
                factor = jnp.exp2(best - new_best)
                weights = jnp.exp2(scores - widen(new_best, scores.shape[1]))
                result = jnp.dot(
                    weights.astype(jnp.bfloat16), value_rows, preferred_element_type=jnp.float32
                )
                weighted = weighted * factor + result[:, :HD]
                total = total * factor + result[:, HD:]
                best = new_best
            write(rows, total, weighted)
            copy = out_copy(index, rows)
            copy.start()
            copy.wait()
            return unused

        lax.fori_loop(0, len(blocks), visit, 0)


def shards(queries, suffix_kv, prompt_kv, lengths):
    slots, width = queries.shape
    heads = width // HD
    loop_size = lax.axis_size("loop")
    own = prompt_kv[:, 0, :]
    suffix = suffix_kv[:, 0, :]
    shard_rows = own.shape[0]

    power_of_two = loop_size & (loop_size - 1) == 0

    def partner(i, step):
        return i ^ step if power_of_two else (i + step) % loop_size

    paired = []
    for step in range(1, (loop_size + 1) // 2):
        hops = [
            hop
            for i in range(loop_size)
            for hop in (
                (2 * i, 2 * partner(i, step) + 1),
                (2 * i + 1, 2 * partner(i, loop_size - step)),
            )
        ]
        paired.append(lax.ppermute(own, ("loop", "pair"), hops))
    single = []
    if loop_size % 2 == 0:
        hops = [
            hop
            for i in range(loop_size)
            for hop in ((2 * i, 2 * i + 1), (2 * i + 1, 2 * partner(i, loop_size // 2)))
        ]
        single.append(lax.ppermute(own, ("loop", "pair"), hops))
    in_hbm = pl.BlockSpec(memory_space=pltpu.HBM)
    in_vmem = pl.BlockSpec(memory_space=pltpu.VMEM)
    state = jax.ShapeDtypeStruct((slots, width), jnp.float32)

    cost = pl.CostEstimate(flops=1, bytes_accessed=1, transcendentals=0)

    best, total, weighted, queries = pl.pallas_call(
        local_stage,
        name="local_stage",
        out_shape=[state] * 3 + [jax.ShapeDtypeStruct((slots, width), queries.dtype)],
        in_specs=[in_hbm] * 4,
        out_specs=[in_vmem] * 4,
        scratch_shapes=[
            pltpu.SMEM(lengths.shape, lengths.dtype),
            pltpu.VMEM(suffix.shape, suffix.dtype),
            pltpu.VMEM(own.shape, own.dtype),
            pltpu.SemaphoreType.DMA((3,)),
            pltpu.SemaphoreType.DMA((slots // BLK,)),
        ],
        compiler_params=pltpu.CompilerParams(vmem_limit_bytes=24 * 2**20),
        cost_estimate=cost,
    )(*(pltpu.with_memory_space_constraint(x, pltpu.HBM) for x in (lengths, queries, suffix, own)))
    def add_shards(total, weighted, shards_now):
        if not shards_now:
            return total, weighted
        return pl.pallas_call(
            add_stage,
            name="add_stage",
            out_shape=[state] * 2,
            in_specs=[in_vmem] * (4 + len(shards_now)),
            out_specs=[in_vmem] * 2,
            compiler_params=pltpu.CompilerParams(vmem_limit_bytes=24 * 2**20),
            cost_estimate=cost,
        )(queries, best, total, weighted, *shards_now)

    swap = [(p, p ^ 1) for p in range(2 * loop_size)]

    def swapped(shards_now):
        return [lax.ppermute(shard, ("loop", "pair"), swap) for shard in shards_now]

    paired, best = lax.optimization_barrier((paired, best))
    paired_swapped = swapped(paired)
    new_total, new_weighted = add_shards(total, weighted, paired)
    single, new_total = lax.optimization_barrier((single, new_total))
    single_swapped = swapped(single)
    if not single:
        single = single_swapped = [paired_swapped.pop()]
    new_total, new_weighted = add_shards(new_total, new_weighted, paired_swapped)
    last_inputs = (queries, best, total, weighted, new_total, new_weighted)
    last_inputs += (*paired, *paired_swapped, *single_swapped, *single)
    return pl.pallas_call(
        functools.partial(last_stage, len(paired), len(single)),
        name="last_stage",
        out_shape=jax.ShapeDtypeStruct((slots, width), jnp.bfloat16),
        in_specs=[in_vmem] * len(last_inputs),
        out_specs=in_hbm,
        scratch_shapes=[
            pltpu.VMEM((slots, width), jnp.bfloat16),
            pltpu.SemaphoreType.DMA((len(row_blocks(slots, 80)),)),
        ],
        compiler_params=pltpu.CompilerParams(vmem_limit_bytes=32 * 2**20),
        cost_estimate=cost,
    )(*last_inputs)


def solution(mesh):
    placed = (
        P(("groups", "loop"), ("heads", "pair")),
        P(("groups", "loop"), "heads", None),
        P(("groups", "loop"), "heads", None),
        P("groups"),
    )
    return jax.shard_map(
        shards,
        mesh=mesh,
        in_specs=placed,
        out_specs=P(("groups", "loop"), ("heads", "pair")),
        check_vma=False,
    )
```

```python
import functools
import math

import jax
import jax.numpy as jnp
from jax import lax
from jax.experimental import pallas as pl
from jax.experimental.pallas import tpu as pltpu
from jax.sharding import PartitionSpec as P

HD = 128
AG_DEV = 2
MAXLEN = 320
BLK = 128
FOUR = 4

masked_score = -1e30
empty_best = 1e30
total_limit = 2.0**100
score_scale = math.log2(math.e) / math.sqrt(HD)


def scores_of(query_rows, key_rows):
    return (
        lax.dot_general(
            query_rows, key_rows, (((1,), (1,)), ((), ())), preferred_element_type=jnp.float32
        )
        * score_scale
    )


def with_ones(value_rows):
    return jnp.concatenate([value_rows, jnp.ones_like(value_rows)], axis=1)


def stacked(ref, rows, head_count):
    return jnp.concatenate([ref[rows, h * HD : (h + 1) * HD] for h in range(head_count)], axis=0)


def unstack(ref, rows, head_count, value):
    count = value.shape[0] // head_count
    for h in range(head_count):
        ref[rows, h * HD : (h + 1) * HD] = value[h * count : (h + 1) * count]


def widen(row_value, width):
    return jnp.concatenate([row_value] * (width // HD), axis=1)


def local_stage(
    lengths_hbm,
    query_hbm,
    suffix_hbm,
    own_hbm,
    best_ref,
    total_ref,
    sum_ref,
    query_ref,
    lengths_ref,
    suffix_ref,
    own_ref,
    whole_sems,
    block_sems,
):
    rows_all = query_ref.shape[0]
    heads = query_ref.shape[1] // HD
    blocks = rows_all // BLK
    whole = [
        pltpu.make_async_copy(source, target, whole_sems.at[i])
        for i, (source, target) in enumerate(
            [(lengths_hbm, lengths_ref), (own_hbm, own_ref), (suffix_hbm, suffix_ref)]
        )
    ]
    pieces = [
        pltpu.make_async_copy(
            query_hbm.at[pl.ds(block * BLK, BLK)],
            query_ref.at[pl.ds(block * BLK, BLK)],
            block_sems.at[block],
        )
        for block in range(blocks)
    ]
    for copy in whole + pieces:
        copy.start()
    for copy in whole + pieces:
        copy.wait()
    position = lax.axis_index("loop")
    window = BLK * ((MAXLEN + BLK - 2) // BLK) + BLK
    for block in range(blocks):
        stop = (block + 1) * BLK
        start = max(0, stop - window)
        rows = slice(block * BLK, stop)
        row_at = block * BLK + lax.broadcasted_iota(jnp.int32, (BLK, stop - start), 0)
        key_at = start + lax.broadcasted_iota(jnp.int32, (BLK, stop - start), 1)
        first = jnp.zeros_like(row_at)
        agent_end = 0
        for agent in range(AG_DEV):
            agent_end = agent_end + lengths_ref[position * AG_DEV + agent]
            first = jnp.where(row_at >= agent_end, agent_end, first)
        allowed = (key_at <= row_at) & (key_at >= first)
        queries = stacked(query_ref, rows, heads)
        shard = jnp.concatenate([own_ref[...], suffix_ref[start:stop]], axis=0)
        scores = scores_of(queries, shard[:, :HD])
        own_scores = scores[:, : own_ref.shape[0]]
        suffix_scores = jnp.where(
            jnp.concatenate([allowed] * heads, axis=0), scores[:, own_ref.shape[0] :], masked_score
        )
        scores = jnp.concatenate([own_scores, suffix_scores], axis=1)
        best = jnp.max(scores, axis=1, keepdims=True)
        weights = jnp.exp2(scores - best).astype(jnp.bfloat16)
        result = jnp.dot(weights, with_ones(shard[:, HD:]), preferred_element_type=jnp.float32)
        row_at = block * BLK + lax.broadcasted_iota(jnp.int32, (BLK, HD), 0)
        live = jnp.concatenate([row_at < agent_end] * heads, axis=0)
        unstack(best_ref, rows, heads, jnp.where(live, best, empty_best))
        unstack(sum_ref, rows, heads, jnp.where(live, result[:, :HD], 0.0))
        unstack(total_ref, rows, heads, jnp.where(live, result[:, HD:], 1.0))


def staged(blocks, start, finish):
    coming = start(blocks[0])
    for index, rows in enumerate(blocks):
        now = coming
        if index + 1 < len(blocks):
            coming = start(blocks[index + 1])
        finish(index, rows, now)


def row_blocks(count, largest):
    step = next(size for size in (largest, 128, 16, count) if count % size == 0)
    return [slice(first, first + step) for first in range(0, count, step)]


def place():
    return lax.rem(lax.axis_index("loop"), FOUR), lax.axis_index("pair")


def penalty(is_there):
    return jnp.where(is_there, 0.0, empty_best)


def add_stage(by_swap, *refs):
    query_ref, best_ref, total_ref, sum_ref = refs[:4]
    shard_refs = refs[4:-2]
    total_out, sum_out = refs[-2:]
    heads = query_ref.shape[1] // HD
    shard = jnp.concatenate([ref[...] for ref in shard_refs], axis=0)
    key_rows, value_rows = shard[:, :HD], with_ones(shard[:, HD:])
    extra = None
    if by_swap is not None:
        position, core = place()
        extra = penalty((position != 1) | (core == int(by_swap)))

    def start(rows):
        return scores_of(stacked(query_ref, rows, heads), key_rows)

    def finish(index, rows, scores):
        best = stacked(best_ref, rows, heads)
        if extra is None:
            points = widen(best, scores.shape[1])
        else:
            held = shard_refs[-1].shape[0]
            points = [best] * ((scores.shape[1] - held) // HD) + [best + extra] * (held // HD)
            points = jnp.concatenate(points, axis=1)
        weights = jnp.exp2(scores - points).astype(jnp.bfloat16)
        result = jnp.dot(weights, value_rows, preferred_element_type=jnp.float32)
        unstack(total_out, rows, heads, stacked(total_ref, rows, heads) + result[:, HD:])
        unstack(sum_out, rows, heads, stacked(sum_ref, rows, heads) + result[:, :HD])

    staged(row_blocks(query_ref.shape[0], 80), start, finish)


def last_stage(routed, *refs):
    query_ref, best_ref, old_total_ref, old_sum_ref, total_ref, sum_ref = refs[:6]
    earlier_refs, refs = refs[6:-6], refs[-6:]
    direct_ref, swapped_ref, out_hbm, out_ref, trusted_ref, out_sems = refs
    heads = query_ref.shape[1] // HD
    blocks = row_blocks(query_ref.shape[0], 80)
    position, core = place()
    takes_both = (position == 1) & routed

    def out_copy(index, rows):
        return pltpu.make_async_copy(out_ref.at[rows], out_hbm.at[rows], out_sems.at[index])

    def write(rows, total, weighted):
        unstack(out_ref, rows, heads, (weighted / total).astype(jnp.bfloat16))

    def process(shard):
        trusted = [jnp.full((8, HD), True)]

        def start(rows):
            return scores_of(stacked(query_ref, rows, heads), shard[:, :HD])

        def finish(index, rows, scores):
            best = stacked(best_ref, rows, heads)
            weights = jnp.exp2(scores - widen(best, scores.shape[1]))
            lanes = sum(weights[:, i : i + HD] for i in range(0, scores.shape[1], HD))
            total = stacked(total_ref, rows, heads) + jnp.sum(lanes, axis=1, keepdims=True)
            weighted = stacked(sum_ref, rows, heads) + jnp.dot(
                weights.astype(jnp.bfloat16), shard[:, HD:], preferred_element_type=jnp.float32
            )
            good = (total < total_limit).reshape(total.shape[0] // 8, 8, HD)
            trusted[0] = trusted[0] & jnp.all(good, axis=0)
            write(rows, total, weighted)
            out_copy(index, rows).start()

        staged(blocks, start, finish)
        trusted_ref[0] = jnp.all(trusted[0]).astype(jnp.int32)
        for index, rows in enumerate(blocks):
            out_copy(index, rows).wait()

    @pl.when(jnp.logical_not(takes_both))
    def one_shard():
        process(jnp.where(core == 0, direct_ref[...], swapped_ref[...]))

    @pl.when(takes_both)
    def two_shards():
        process(jnp.concatenate([direct_ref[...], swapped_ref[...]], axis=0))

    @pl.when(trusted_ref[0] == 0)
    def exact_maximum():
        size = query_ref.shape[0] // len(blocks)
        counted = [(ref, 0.0) for ref in earlier_refs]
        if routed:
            counted[-2:] = [
                (ref, penalty((position != 1) | (core == by_swap)))
                for by_swap, ref in enumerate(earlier_refs[-2:])
            ]
        counted += [
            (ref, penalty(takes_both | (core == by_swap)))
            for by_swap, ref in enumerate([direct_ref, swapped_ref])
        ]

        def visit(index, unused):
            rows = pl.ds(pl.multiple_of(index * size, size), size)
            queries = stacked(query_ref, rows, heads)
            best = stacked(best_ref, rows, heads)
            weighted = stacked(old_sum_ref, rows, heads)
            total = stacked(old_total_ref, rows, heads)
            for shard_ref, extra in counted:
                key_rows, value_rows = shard_ref[:, :HD], with_ones(shard_ref[:, HD:])
                scores = scores_of(queries, key_rows) - extra
                new_best = jnp.maximum(best, jnp.max(scores, axis=1, keepdims=True))
                factor = jnp.exp2(best - new_best)
                weights = jnp.exp2(scores - widen(new_best, scores.shape[1]))
                result = jnp.dot(
                    weights.astype(jnp.bfloat16), value_rows, preferred_element_type=jnp.float32
                )
                weighted = weighted * factor + result[:, :HD]
                total = total * factor + result[:, HD:]
                best = new_best
            write(rows, total, weighted)
            copy = out_copy(index, rows)
            copy.start()
            copy.wait()
            return unused

        lax.fori_loop(0, len(blocks), visit, 0)


def shards(queries, suffix_kv, prompt_kv, lengths):
    slots, width = queries.shape
    heads = width // HD
    loop_size = lax.axis_size("loop")
    own = prompt_kv[:, 0, :]
    suffix = suffix_kv[:, 0, :]
    shard_rows = own.shape[0]

    routed = loop_size >= FOUR and loop_size & (loop_size - 1) == 0

    def send(shard, route):
        hops = []
        for i in range(loop_size):
            for core in range(2):
                to, to_core = route(i, core)
                hops.append((2 * i + core, 2 * to + to_core))
        return lax.ppermute(shard, ("loop", "pair"), hops)

    def first_route(i, core):
        position, base = i % FOUR, i - i % FOUR
        if core == 0:
            return {0: (i + 1, 0), 1: (i, 1)}.get(position, (i ^ 1, 1))
        return {2: (base, 0), 3: (base, 1)}.get(position, (i ^ 3, 0))

    def second_route(i, core):
        position, base = i % FOUR, i - i % FOUR
        if core == 0:
            return (base, 0) if position == 1 else (i, 1)
        return {2: (base + 1, 0), 3: (base + 1, 1)}.get(position, (i ^ 2, 0))

    if routed:
        early = [
            send(own, lambda i, core, step=step: (i ^ (step + core), 1 - core))
            for step in range(FOUR, loop_size, 2)
        ]
        early.append(send(own, first_route))
        final = send(own, second_route)
    else:
        early = [
            send(own, lambda i, core, step=step: ((i + step) % loop_size, core))
            for step in range(1, loop_size)
        ]
        final = early.pop()
    in_hbm = pl.BlockSpec(memory_space=pltpu.HBM)
    in_vmem = pl.BlockSpec(memory_space=pltpu.VMEM)
    state = jax.ShapeDtypeStruct((slots, width), jnp.float32)

    cost = pl.CostEstimate(flops=1, bytes_accessed=1, transcendentals=0)

    best, total, weighted, queries = pl.pallas_call(
        local_stage,
        name="local_stage",
        out_shape=[state] * 3 + [jax.ShapeDtypeStruct((slots, width), queries.dtype)],
        in_specs=[in_hbm] * 4,
        out_specs=[in_vmem] * 4,
        scratch_shapes=[
            pltpu.SMEM(lengths.shape, lengths.dtype),
            pltpu.VMEM(suffix.shape, suffix.dtype),
            pltpu.VMEM(own.shape, own.dtype),
            pltpu.SemaphoreType.DMA((3,)),
            pltpu.SemaphoreType.DMA((slots // BLK,)),
        ],
        compiler_params=pltpu.CompilerParams(vmem_limit_bytes=24 * 2**20),
        cost_estimate=cost,
    )(*(pltpu.with_memory_space_constraint(x, pltpu.HBM) for x in (lengths, queries, suffix, own)))
    def add_shards(total, weighted, shards_now, by_swap):
        if not shards_now:
            return total, weighted
        return pl.pallas_call(
            functools.partial(add_stage, by_swap if routed else None),
            name="add_stage",
            out_shape=[state] * 2,
            in_specs=[in_vmem] * (4 + len(shards_now)),
            out_specs=[in_vmem] * 2,
            compiler_params=pltpu.CompilerParams(vmem_limit_bytes=24 * 2**20),
            cost_estimate=cost,
        )(queries, best, total, weighted, *shards_now)

    def swapped(shard):
        return send(shard, lambda i, core: (i, 1 - core))

    early, best = lax.optimization_barrier((early, best))
    early_swapped = [swapped(shard) for shard in early] if routed else []
    new_total, new_weighted = add_shards(total, weighted, early, False)
    final, new_total = lax.optimization_barrier((final, new_total))
    final_swapped = swapped(final) if routed else final
    new_total, new_weighted = add_shards(new_total, new_weighted, early_swapped, True)
    last_inputs = (queries, best, total, weighted, new_total, new_weighted)
    last_inputs += (*early[:-1], *early_swapped[:-1], *early[-1:], *early_swapped[-1:])
    last_inputs += (final, final_swapped)
    return pl.pallas_call(
        functools.partial(last_stage, routed),
        name="last_stage",
        out_shape=jax.ShapeDtypeStruct((slots, width), jnp.bfloat16),
        in_specs=[in_vmem] * len(last_inputs),
        out_specs=in_hbm,
        scratch_shapes=[
            pltpu.VMEM((slots, width), jnp.bfloat16),
            pltpu.SMEM((1,), jnp.int32),
            pltpu.SemaphoreType.DMA((len(row_blocks(slots, 80)),)),
        ],
        compiler_params=pltpu.CompilerParams(vmem_limit_bytes=32 * 2**20),
        cost_estimate=cost,
    )(*last_inputs)


def solution(mesh):
    placed = (
        P(("groups", "loop"), ("heads", "pair")),
        P(("groups", "loop"), "heads", None),
        P(("groups", "loop"), "heads", None),
        P("groups"),
    )
    return jax.shard_map(
        shards,
        mesh=mesh,
        in_specs=placed,
        out_specs=P(("groups", "loop"), ("heads", "pair")),
        check_vma=False,
    )
```

```python
import functools
import math

import jax
import jax.numpy as jnp
from jax import lax
from jax.experimental import pallas as pl
from jax.experimental.pallas import tpu as pltpu
from jax.sharding import PartitionSpec as P

HD = 128
AG_DEV = 2
MAXLEN = 320
BLK = 128
FOUR = 4

masked_score = -1e30
empty_best = 1e30
total_limit = 2.0**100
score_scale = math.log2(math.e) / math.sqrt(HD)


def scores_of(query_rows, key_rows):
    return (
        lax.dot_general(
            query_rows, key_rows, (((1,), (1,)), ((), ())), preferred_element_type=jnp.float32
        )
        * score_scale
    )


def with_ones(value_rows):
    return jnp.concatenate([value_rows, jnp.ones_like(value_rows)], axis=1)


def stacked(ref, rows, head_count):
    return jnp.concatenate([ref[rows, h * HD : (h + 1) * HD] for h in range(head_count)], axis=0)


def unstack(ref, rows, head_count, value):
    count = value.shape[0] // head_count
    for h in range(head_count):
        ref[rows, h * HD : (h + 1) * HD] = value[h * count : (h + 1) * count]


def widen(row_value, width):
    return jnp.concatenate([row_value] * (width // HD), axis=1)


def load_blocks(count):
    return [pl.ds(first, BLK) for first in range(0, count, BLK)]


def load_stage(
    lengths_hbm,
    query_hbm,
    suffix_hbm,
    own_hbm,
    query_ref,
    suffix_ref,
    own_ref,
    first_ref,
    lengths_ref,
    sems,
):
    pairs = [(lengths_hbm, lengths_ref), (own_hbm, own_ref)]
    for source, target in ((query_hbm, query_ref), (suffix_hbm, suffix_ref)):
        for rows in load_blocks(target.shape[0]):
            pairs.append((source.at[rows], target.at[rows]))
    copies = [
        pltpu.make_async_copy(source, target, sems.at[i])
        for i, (source, target) in enumerate(pairs)
    ]
    for copy in copies:
        copy.start()
    copies[0].wait()
    slots = query_ref.shape[0]
    position = lax.axis_index("loop")
    row_at = lax.broadcasted_iota(jnp.int32, first_ref.shape, 0)
    first = jnp.zeros_like(row_at)
    agent_end = 0
    for agent in range(AG_DEV):
        agent_end = agent_end + lengths_ref[position * AG_DEV + agent]
        first = jnp.where(row_at >= agent_end, agent_end if agent + 1 < AG_DEV else slots, first)
    first_ref[...] = first
    for copy in copies[1:]:
        copy.wait()


def local_stage(query_ref, suffix_ref, own_ref, first_ref, best_ref, total_ref, sum_ref):
    slots = query_ref.shape[0]
    heads = query_ref.shape[1] // HD
    own_keys = own_ref[:, :HD]
    own_values = with_ones(own_ref[:, HD:])
    window = BLK * ((MAXLEN + BLK - 2) // BLK) + BLK
    for block in range(slots // BLK):
        stop = (block + 1) * BLK
        start = max(0, stop - window)
        rows = slice(block * BLK, stop)
        row_at = block * BLK + lax.broadcasted_iota(jnp.int32, (BLK, stop - start), 0)
        key_at = start + lax.broadcasted_iota(jnp.int32, (BLK, stop - start), 1)
        first = first_ref[rows]
        allowed = (key_at <= row_at) & (key_at >= widen(first, stop - start))
        queries = stacked(query_ref, rows, heads)
        own_scores = scores_of(queries, own_keys)
        suffix_scores = jnp.where(
            jnp.concatenate([allowed] * heads, axis=0),
            scores_of(queries, suffix_ref[start:stop, :HD]),
            masked_score,
        )
        best = jnp.maximum(
            jnp.max(own_scores, axis=1, keepdims=True),
            jnp.max(suffix_scores, axis=1, keepdims=True),
        )
        own_weights = jnp.exp2(own_scores - best).astype(jnp.bfloat16)
        suffix_weights = jnp.exp2(suffix_scores - best).astype(jnp.bfloat16)
        result = jnp.dot(own_weights, own_values, preferred_element_type=jnp.float32)
        result = result + jnp.dot(
            suffix_weights,
            with_ones(suffix_ref[start:stop, HD:]),
            preferred_element_type=jnp.float32,
        )
        live = jnp.concatenate([first < slots] * heads, axis=0)
        unstack(best_ref, rows, heads, jnp.where(live, best, empty_best))
        unstack(sum_ref, rows, heads, jnp.where(live, result[:, :HD], 0.0))
        unstack(total_ref, rows, heads, jnp.where(live, result[:, HD:], 1.0))


def staged(blocks, start, finish):
    coming = start(blocks[0])
    for index, rows in enumerate(blocks):
        now = coming
        if index + 1 < len(blocks):
            coming = start(blocks[index + 1])
        finish(index, rows, now)


def row_blocks(count, largest):
    step = next(size for size in (largest, 128, 16, count) if count % size == 0)
    return [slice(first, first + step) for first in range(0, count, step)]


def place():
    return lax.rem(lax.axis_index("loop"), 2) == 1, lax.axis_index("pair")


def penalty(is_there):
    return jnp.where(is_there, 0.0, empty_best)


def add_stage(by_swap, *refs):
    query_ref, best_ref, total_ref, sum_ref = refs[:4]
    shard_refs = refs[4:-2]
    total_out, sum_out = refs[-2:]
    heads = query_ref.shape[1] // HD
    shard = jnp.concatenate([ref[...] for ref in shard_refs], axis=0)
    key_rows, value_rows = shard[:, :HD], with_ones(shard[:, HD:])
    extra = None
    if by_swap is not None:
        is_odd, core = place()
        extra = penalty(jnp.logical_not(is_odd) | (core == int(by_swap)))

    def start(rows):
        return scores_of(stacked(query_ref, rows, heads), key_rows)

    def finish(index, rows, scores):
        best = stacked(best_ref, rows, heads)
        if extra is None:
            points = widen(best, scores.shape[1])
        else:
            held = shard_refs[-1].shape[0]
            points = [best] * ((scores.shape[1] - held) // HD) + [best + extra] * (held // HD)
            points = jnp.concatenate(points, axis=1)
        weights = jnp.exp2(scores - points).astype(jnp.bfloat16)
        result = jnp.dot(weights, value_rows, preferred_element_type=jnp.float32)
        unstack(total_out, rows, heads, stacked(total_ref, rows, heads) + result[:, HD:])
        unstack(sum_out, rows, heads, stacked(sum_ref, rows, heads) + result[:, :HD])

    staged(row_blocks(query_ref.shape[0], 80), start, finish)


def last_stage(routed, *refs):
    query_ref, best_ref, old_total_ref, old_sum_ref, total_ref, sum_ref = refs[:6]
    earlier_refs, refs = refs[6:-6], refs[-6:]
    direct_ref, swapped_ref, out_hbm, out_ref, trusted_ref, out_sems = refs
    heads = query_ref.shape[1] // HD
    blocks = row_blocks(query_ref.shape[0], 80)
    is_odd, core = place()
    takes_both = is_odd & routed

    def out_copy(index, rows):
        return pltpu.make_async_copy(out_ref.at[rows], out_hbm.at[rows], out_sems.at[index])

    def write(rows, total, weighted):
        unstack(out_ref, rows, heads, (weighted / total).astype(jnp.bfloat16))

    def process(shard):
        trusted = [jnp.full((8, HD), True)]

        def start(rows):
            return scores_of(stacked(query_ref, rows, heads), shard[:, :HD])

        def finish(index, rows, scores):
            best = stacked(best_ref, rows, heads)
            weights = jnp.exp2(scores - widen(best, scores.shape[1]))
            lanes = sum(weights[:, i : i + HD] for i in range(0, scores.shape[1], HD))
            total = stacked(total_ref, rows, heads) + jnp.sum(lanes, axis=1, keepdims=True)
            weighted = stacked(sum_ref, rows, heads) + jnp.dot(
                weights.astype(jnp.bfloat16), shard[:, HD:], preferred_element_type=jnp.float32
            )
            good = (total < total_limit).reshape(total.shape[0] // 8, 8, HD)
            trusted[0] = trusted[0] & jnp.all(good, axis=0)
            write(rows, total, weighted)
            out_copy(index, rows).start()

        staged(blocks, start, finish)
        trusted_ref[0] = jnp.all(trusted[0]).astype(jnp.int32)
        for index, rows in enumerate(blocks):
            out_copy(index, rows).wait()

    @pl.when(jnp.logical_not(takes_both))
    def one_shard():
        process(jnp.where(core == 0, direct_ref[...], swapped_ref[...]))

    @pl.when(takes_both)
    def two_shards():
        process(jnp.concatenate([direct_ref[...], swapped_ref[...]], axis=0))

    @pl.when(trusted_ref[0] == 0)
    def exact_maximum():
        size = query_ref.shape[0] // len(blocks)
        counted = [(ref, 0.0) for ref in earlier_refs]
        if routed:
            counted[-2:] = [
                (ref, penalty(jnp.logical_not(is_odd) | (core == by_swap)))
                for by_swap, ref in enumerate(earlier_refs[-2:])
            ]
        counted += [
            (ref, penalty(takes_both | (core == by_swap)))
            for by_swap, ref in enumerate([direct_ref, swapped_ref])
        ]

        def visit(index, unused):
            rows = pl.ds(pl.multiple_of(index * size, size), size)
            queries = stacked(query_ref, rows, heads)
            best = stacked(best_ref, rows, heads)
            weighted = stacked(old_sum_ref, rows, heads)
            total = stacked(old_total_ref, rows, heads)
            for shard_ref, extra in counted:
                key_rows, value_rows = shard_ref[:, :HD], with_ones(shard_ref[:, HD:])
                scores = scores_of(queries, key_rows) - extra
                new_best = jnp.maximum(best, jnp.max(scores, axis=1, keepdims=True))
                factor = jnp.exp2(best - new_best)
                weights = jnp.exp2(scores - widen(new_best, scores.shape[1]))
                result = jnp.dot(
                    weights.astype(jnp.bfloat16), value_rows, preferred_element_type=jnp.float32
                )
                weighted = weighted * factor + result[:, :HD]
                total = total * factor + result[:, HD:]
                best = new_best
            write(rows, total, weighted)
            copy = out_copy(index, rows)
            copy.start()
            copy.wait()
            return unused

        lax.fori_loop(0, len(blocks), visit, 0)


def shards(queries, suffix_kv, prompt_kv, lengths):
    slots, width = queries.shape
    heads = width // HD
    loop_size = lax.axis_size("loop")
    own = prompt_kv[:, 0, :]
    suffix = suffix_kv[:, 0, :]
    shard_rows = own.shape[0]

    routed = loop_size >= FOUR and loop_size & (loop_size - 1) == 0

    def send(shard, route):
        hops = []
        for i in range(loop_size):
            for core in range(2):
                to, to_core = route(i, core)
                hops.append((2 * i + core, 2 * to + to_core))
        return lax.ppermute(shard, ("loop", "pair"), hops)

    def first_route(i, core):
        if core == 1:
            return (i ^ 2) & ~1, i & 1
        return (i, 1) if i & 1 else (i + 1, 0)

    def second_route(i, core):
        if core == 1:
            return (i ^ 2) | 1, i & 1
        return (i - 1, 0) if i & 1 else (i, 1)

    early = []
    if routed:
        early = [
            send(own, lambda i, core, step=step: (i ^ (step + core), 1 - core))
            for step in range(FOUR, loop_size, 2)
        ]
        early.append(send(own, first_route))
    in_hbm = pl.BlockSpec(memory_space=pltpu.HBM)
    in_vmem = pl.BlockSpec(memory_space=pltpu.VMEM)
    state = jax.ShapeDtypeStruct((slots, width), jnp.float32)

    cost = pl.CostEstimate(flops=1, bytes_accessed=1, transcendentals=0)

    queries, suffix, own, first = pl.pallas_call(
        load_stage,
        name="load_stage",
        out_shape=[
            jax.ShapeDtypeStruct(queries.shape, queries.dtype),
            jax.ShapeDtypeStruct(suffix.shape, suffix.dtype),
            jax.ShapeDtypeStruct(own.shape, own.dtype),
            jax.ShapeDtypeStruct((slots, HD), jnp.int32),
        ],
        in_specs=[in_hbm] * 4,
        out_specs=[in_vmem] * 4,
        scratch_shapes=[
            pltpu.SMEM(lengths.shape, lengths.dtype),
            pltpu.SemaphoreType.DMA((2 + 2 * len(load_blocks(slots)),)),
        ],
        compiler_params=pltpu.CompilerParams(vmem_limit_bytes=8 * 2**20),
        cost_estimate=cost,
    )(*(pltpu.with_memory_space_constraint(x, pltpu.HBM) for x in (lengths, queries, suffix, own)))
    if routed:
        final = send(own, second_route)
    else:
        early = [
            send(own, lambda i, core, step=step: ((i + step) % loop_size, core))
            for step in range(1, loop_size)
        ]
        final = early.pop()
    best, total, weighted = pl.pallas_call(
        local_stage,
        name="local_stage",
        out_shape=[state] * 3,
        in_specs=[in_vmem] * 4,
        out_specs=[in_vmem] * 3,
        compiler_params=pltpu.CompilerParams(vmem_limit_bytes=24 * 2**20),
        cost_estimate=cost,
    )(queries, suffix, own, first)

    def add_shards(total, weighted, shards_now, by_swap):
        if not shards_now:
            return total, weighted
        return pl.pallas_call(
            functools.partial(add_stage, by_swap if routed else None),
            name="add_stage",
            out_shape=[state] * 2,
            in_specs=[in_vmem] * (4 + len(shards_now)),
            out_specs=[in_vmem] * 2,
            compiler_params=pltpu.CompilerParams(vmem_limit_bytes=24 * 2**20),
            cost_estimate=cost,
        )(queries, best, total, weighted, *shards_now)

    def swapped(shard):
        return send(shard, lambda i, core: (i, 1 - core))

    early, best = lax.optimization_barrier((early, best))
    early_swapped = [swapped(shard) for shard in early] if routed else []
    new_total, new_weighted = add_shards(total, weighted, early, False)
    final, new_total = lax.optimization_barrier((final, new_total))
    final_swapped = swapped(final) if routed else final
    new_total, new_weighted = add_shards(new_total, new_weighted, early_swapped, True)
    last_inputs = (queries, best, total, weighted, new_total, new_weighted)
    last_inputs += (*early[:-1], *early_swapped[:-1], *early[-1:], *early_swapped[-1:])
    last_inputs += (final, final_swapped)
    return pl.pallas_call(
        functools.partial(last_stage, routed),
        name="last_stage",
        out_shape=jax.ShapeDtypeStruct((slots, width), jnp.bfloat16),
        in_specs=[in_vmem] * len(last_inputs),
        out_specs=in_hbm,
        scratch_shapes=[
            pltpu.VMEM((slots, width), jnp.bfloat16),
            pltpu.SMEM((1,), jnp.int32),
            pltpu.SemaphoreType.DMA((len(row_blocks(slots, 80)),)),
        ],
        compiler_params=pltpu.CompilerParams(vmem_limit_bytes=32 * 2**20),
        cost_estimate=cost,
    )(*last_inputs)


def solution(mesh):
    placed = (
        P(("groups", "loop"), ("heads", "pair")),
        P(("groups", "loop"), "heads", None),
        P(("groups", "loop"), "heads", None),
        P("groups"),
    )
    return jax.shard_map(
        shards,
        mesh=mesh,
        in_specs=placed,
        out_specs=P(("groups", "loop"), ("heads", "pair")),
        check_vma=False,
    )
```

```python
import functools
import math

import jax
import jax.numpy as jnp
from jax import lax
from jax.experimental import pallas as pl
from jax.experimental.pallas import tpu as pltpu
from jax.sharding import PartitionSpec as P

HD = 128
AG_DEV = 2
MAXLEN = 320
BLK = 128
FOUR = 4

masked_score = -1e30
empty_best = 1e30
total_limit = 2.0**100
score_scale = math.log2(math.e) / math.sqrt(HD)


def scores_of(query_rows, key_rows):
    return (
        lax.dot_general(
            query_rows, key_rows, (((1,), (1,)), ((), ())), preferred_element_type=jnp.float32
        )
        * score_scale
    )


def with_ones(value_rows):
    return jnp.concatenate([value_rows, jnp.ones_like(value_rows)], axis=1)


def stacked(ref, rows, head_count):
    return jnp.concatenate([ref[rows, h * HD : (h + 1) * HD] for h in range(head_count)], axis=0)


def unstack(ref, rows, head_count, value):
    count = value.shape[0] // head_count
    for h in range(head_count):
        ref[rows, h * HD : (h + 1) * HD] = value[h * count : (h + 1) * count]


def widen(row_value, width):
    return jnp.concatenate([row_value] * (width // HD), axis=1)


def local_stage(
    lengths_hbm,
    query_hbm,
    suffix_hbm,
    own_hbm,
    best_ref,
    total_ref,
    sum_ref,
    query_ref,
    lengths_ref,
    suffix_ref,
    own_ref,
    whole_sems,
    block_sems,
):
    rows_all = query_ref.shape[0]
    heads = query_ref.shape[1] // HD
    blocks = rows_all // BLK
    whole = [
        pltpu.make_async_copy(source, target, whole_sems.at[i])
        for i, (source, target) in enumerate(
            [(lengths_hbm, lengths_ref), (own_hbm, own_ref), (suffix_hbm, suffix_ref)]
        )
    ]
    pieces = [
        pltpu.make_async_copy(
            query_hbm.at[pl.ds(block * BLK, BLK)],
            query_ref.at[pl.ds(block * BLK, BLK)],
            block_sems.at[block],
        )
        for block in range(blocks)
    ]
    for copy in whole + pieces:
        copy.start()
    for copy in whole + pieces:
        copy.wait()
    position = lax.axis_index("loop")
    window = BLK * ((MAXLEN + BLK - 2) // BLK) + BLK
    for block in range(blocks):
        stop = (block + 1) * BLK
        start = max(0, stop - window)
        rows = slice(block * BLK, stop)
        row_at = block * BLK + lax.broadcasted_iota(jnp.int32, (BLK, stop - start), 0)
        key_at = start + lax.broadcasted_iota(jnp.int32, (BLK, stop - start), 1)
        first = jnp.zeros_like(row_at)
        agent_end = 0
        for agent in range(AG_DEV):
            agent_end = agent_end + lengths_ref[position * AG_DEV + agent]
            first = jnp.where(row_at >= agent_end, agent_end, first)
        allowed = (key_at <= row_at) & (key_at >= first)
        queries = stacked(query_ref, rows, heads)
        shard = jnp.concatenate([own_ref[...], suffix_ref[start:stop]], axis=0)
        scores = scores_of(queries, shard[:, :HD])
        own_scores = scores[:, : own_ref.shape[0]]
        suffix_scores = jnp.where(
            jnp.concatenate([allowed] * heads, axis=0), scores[:, own_ref.shape[0] :], masked_score
        )
        scores = jnp.concatenate([own_scores, suffix_scores], axis=1)
        best = jnp.max(scores, axis=1, keepdims=True)
        weights = jnp.exp2(scores - best).astype(jnp.bfloat16)
        result = jnp.dot(weights, with_ones(shard[:, HD:]), preferred_element_type=jnp.float32)
        row_at = block * BLK + lax.broadcasted_iota(jnp.int32, (BLK, HD), 0)
        live = jnp.concatenate([row_at < agent_end] * heads, axis=0)
        unstack(best_ref, rows, heads, jnp.where(live, best, empty_best))
        unstack(sum_ref, rows, heads, jnp.where(live, result[:, :HD], 0.0))
        unstack(total_ref, rows, heads, jnp.where(live, result[:, HD:], 1.0))


def staged(blocks, start, finish):
    coming = start(blocks[0])
    for index, rows in enumerate(blocks):
        now = coming
        if index + 1 < len(blocks):
            coming = start(blocks[index + 1])
        finish(index, rows, now)


def row_blocks(count, largest):
    step = next(size for size in (largest, 128, 16, count) if count % size == 0)
    return [slice(first, first + step) for first in range(0, count, step)]


def place():
    return lax.rem(lax.axis_index("loop"), FOUR), lax.axis_index("pair")


def penalty(is_there):
    return jnp.where(is_there, 0.0, empty_best)


def add_stage(by_swap, *refs):
    query_ref, best_ref, total_ref, sum_ref = refs[:4]
    shard_refs = refs[4:-2]
    total_out, sum_out = refs[-2:]
    heads = query_ref.shape[1] // HD
    shard = jnp.concatenate([ref[...] for ref in shard_refs], axis=0)
    key_rows, value_rows = shard[:, :HD], with_ones(shard[:, HD:])
    extra = None
    if by_swap is not None:
        position, core = place()
        extra = penalty((position != 1) | (core == int(by_swap)))

    def start(rows):
        return scores_of(stacked(query_ref, rows, heads), key_rows)

    def finish(index, rows, scores):
        best = stacked(best_ref, rows, heads)
        if extra is None:
            points = widen(best, scores.shape[1])
        else:
            held = shard_refs[-1].shape[0]
            points = [best] * ((scores.shape[1] - held) // HD) + [best + extra] * (held // HD)
            points = jnp.concatenate(points, axis=1)
        weights = jnp.exp2(scores - points).astype(jnp.bfloat16)
        result = jnp.dot(weights, value_rows, preferred_element_type=jnp.float32)
        unstack(total_out, rows, heads, stacked(total_ref, rows, heads) + result[:, HD:])
        unstack(sum_out, rows, heads, stacked(sum_ref, rows, heads) + result[:, :HD])

    staged(row_blocks(query_ref.shape[0], 80), start, finish)


def last_stage(routed, *refs):
    query_ref, best_ref, old_total_ref, old_sum_ref, total_ref, sum_ref = refs[:6]
    earlier_refs, refs = refs[6:-6], refs[-6:]
    direct_ref, swapped_ref, out_hbm, out_ref, trusted_ref, out_sems = refs
    heads = query_ref.shape[1] // HD
    blocks = row_blocks(query_ref.shape[0], 80)
    position, core = place()
    takes_both = (position == 1) & routed
    is_direct = core == jnp.where(position == 0, 0, 1)

    def out_copy(index, rows):
        return pltpu.make_async_copy(out_ref.at[rows], out_hbm.at[rows], out_sems.at[index])

    def write(rows, total, weighted):
        unstack(out_ref, rows, heads, (weighted / total).astype(jnp.bfloat16))

    def process(shard):
        trusted = [jnp.full((8, HD), True)]

        def start(rows):
            return scores_of(stacked(query_ref, rows, heads), shard[:, :HD])

        def finish(index, rows, scores):
            best = stacked(best_ref, rows, heads)
            weights = jnp.exp2(scores - widen(best, scores.shape[1]))
            lanes = sum(weights[:, i : i + HD] for i in range(0, scores.shape[1], HD))
            total = stacked(total_ref, rows, heads) + jnp.sum(lanes, axis=1, keepdims=True)
            weighted = stacked(sum_ref, rows, heads) + jnp.dot(
                weights.astype(jnp.bfloat16), shard[:, HD:], preferred_element_type=jnp.float32
            )
            good = (total < total_limit).reshape(total.shape[0] // 8, 8, HD)
            trusted[0] = trusted[0] & jnp.all(good, axis=0)
            write(rows, total, weighted)
            out_copy(index, rows).start()

        staged(blocks, start, finish)
        trusted_ref[0] = jnp.all(trusted[0]).astype(jnp.int32)
        for index, rows in enumerate(blocks):
            out_copy(index, rows).wait()

    @pl.when(jnp.logical_not(takes_both))
    def one_shard():
        process(jnp.where(is_direct, direct_ref[...], swapped_ref[...]))

    @pl.when(takes_both)
    def two_shards():
        process(jnp.concatenate([direct_ref[...], swapped_ref[...]], axis=0))

    @pl.when(trusted_ref[0] == 0)
    def exact_maximum():
        size = query_ref.shape[0] // len(blocks)
        counted = [(ref, 0.0) for ref in earlier_refs]
        if routed:
            counted[-2:] = [
                (ref, penalty((position != 1) | (core == by_swap)))
                for by_swap, ref in enumerate(earlier_refs[-2:])
            ]
        counted += [
            (direct_ref, penalty(takes_both | is_direct)),
            (swapped_ref, penalty(takes_both | jnp.logical_not(is_direct))),
        ]

        def visit(index, unused):
            rows = pl.ds(pl.multiple_of(index * size, size), size)
            queries = stacked(query_ref, rows, heads)
            best = stacked(best_ref, rows, heads)
            weighted = stacked(old_sum_ref, rows, heads)
            total = stacked(old_total_ref, rows, heads)
            for shard_ref, extra in counted:
                key_rows, value_rows = shard_ref[:, :HD], with_ones(shard_ref[:, HD:])
                scores = scores_of(queries, key_rows) - extra
                new_best = jnp.maximum(best, jnp.max(scores, axis=1, keepdims=True))
                factor = jnp.exp2(best - new_best)
                weights = jnp.exp2(scores - widen(new_best, scores.shape[1]))
                result = jnp.dot(
                    weights.astype(jnp.bfloat16), value_rows, preferred_element_type=jnp.float32
                )
                weighted = weighted * factor + result[:, :HD]
                total = total * factor + result[:, HD:]
                best = new_best
            write(rows, total, weighted)
            copy = out_copy(index, rows)
            copy.start()
            copy.wait()
            return unused

        lax.fori_loop(0, len(blocks), visit, 0)


def shards(queries, suffix_kv, prompt_kv, lengths):
    slots, width = queries.shape
    heads = width // HD
    loop_size = lax.axis_size("loop")
    own = prompt_kv[:, 0, :]
    suffix = suffix_kv[:, 0, :]
    shard_rows = own.shape[0]

    routed = loop_size >= FOUR and loop_size & (loop_size - 1) == 0

    def send(shard, route):
        hops = []
        for i in range(loop_size):
            for core in range(2):
                to, to_core = route(i, core)
                hops.append((2 * i + core, 2 * to + to_core))
        return lax.ppermute(shard, ("loop", "pair"), hops)

    def first_route(i, core):
        base = i - i % FOUR
        to, to_core = [((1, 0), (3, 1)), ((1, 1), (2, 0)), ((3, 0), (0, 0)), ((2, 1), (0, 1))][
            i % FOUR
        ][core]
        return base + to, to_core

    def second_route(i, core):
        base = i - i % FOUR
        to, to_core = [((0, 1), (2, 1)), ((0, 0), (3, 1)), ((3, 0), (1, 0)), ((2, 0), (1, 1))][
            i % FOUR
        ][core]
        return base + to, to_core

    if routed:
        early = [
            send(own, lambda i, core, step=step: (i ^ (step + core), 1 - core))
            for step in range(FOUR, loop_size, 2)
        ]
        early.append(send(own, first_route))
        final = send(own, second_route)
    else:
        early = [
            send(own, lambda i, core, step=step: ((i + step) % loop_size, core))
            for step in range(1, loop_size)
        ]
        final = early.pop()
    in_hbm = pl.BlockSpec(memory_space=pltpu.HBM)
    in_vmem = pl.BlockSpec(memory_space=pltpu.VMEM)
    state = jax.ShapeDtypeStruct((slots, width), jnp.float32)

    cost = pl.CostEstimate(flops=1, bytes_accessed=1, transcendentals=0)

    best, total, weighted, queries = pl.pallas_call(
        local_stage,
        name="local_stage",
        out_shape=[state] * 3 + [jax.ShapeDtypeStruct((slots, width), queries.dtype)],
        in_specs=[in_hbm] * 4,
        out_specs=[in_vmem] * 4,
        scratch_shapes=[
            pltpu.SMEM(lengths.shape, lengths.dtype),
            pltpu.VMEM(suffix.shape, suffix.dtype),
            pltpu.VMEM(own.shape, own.dtype),
            pltpu.SemaphoreType.DMA((3,)),
            pltpu.SemaphoreType.DMA((slots // BLK,)),
        ],
        compiler_params=pltpu.CompilerParams(vmem_limit_bytes=24 * 2**20),
        cost_estimate=cost,
    )(*(pltpu.with_memory_space_constraint(x, pltpu.HBM) for x in (lengths, queries, suffix, own)))
    def add_shards(total, weighted, shards_now, by_swap):
        if not shards_now:
            return total, weighted
        return pl.pallas_call(
            functools.partial(add_stage, by_swap if routed else None),
            name="add_stage",
            out_shape=[state] * 2,
            in_specs=[in_vmem] * (4 + len(shards_now)),
            out_specs=[in_vmem] * 2,
            compiler_params=pltpu.CompilerParams(vmem_limit_bytes=24 * 2**20),
            cost_estimate=cost,
        )(queries, best, total, weighted, *shards_now)

    def swapped(shard):
        return send(shard, lambda i, core: (i, 1 - core))

    early, best = lax.optimization_barrier((early, best))
    early_swapped = [swapped(shard) for shard in early] if routed else []
    new_total, new_weighted = add_shards(total, weighted, early, False)
    final, new_total = lax.optimization_barrier((final, new_total))
    final_swapped = swapped(final) if routed else final
    new_total, new_weighted = add_shards(new_total, new_weighted, early_swapped, True)
    last_inputs = (queries, best, total, weighted, new_total, new_weighted)
    last_inputs += (*early[:-1], *early_swapped[:-1], *early[-1:], *early_swapped[-1:])
    last_inputs += (final, final_swapped)
    return pl.pallas_call(
        functools.partial(last_stage, routed),
        name="last_stage",
        out_shape=jax.ShapeDtypeStruct((slots, width), jnp.bfloat16),
        in_specs=[in_vmem] * len(last_inputs),
        out_specs=in_hbm,
        scratch_shapes=[
            pltpu.VMEM((slots, width), jnp.bfloat16),
            pltpu.SMEM((1,), jnp.int32),
            pltpu.SemaphoreType.DMA((len(row_blocks(slots, 80)),)),
        ],
        compiler_params=pltpu.CompilerParams(vmem_limit_bytes=32 * 2**20),
        cost_estimate=cost,
    )(*last_inputs)


def solution(mesh):
    placed = (
        P(("groups", "loop"), ("heads", "pair")),
        P(("groups", "loop"), "heads", None),
        P(("groups", "loop"), "heads", None),
        P("groups"),
    )
    return jax.shard_map(
        shards,
        mesh=mesh,
        in_specs=placed,
        out_specs=P(("groups", "loop"), ("heads", "pair")),
        check_vma=False,
    )
```

```python
import functools
import math

import jax
import jax.numpy as jnp
from jax import lax
from jax.experimental import pallas as pl
from jax.experimental.pallas import tpu as pltpu
from jax.sharding import PartitionSpec as P

HD = 128
AG_DEV = 2
MINLEN = 128
MAXLEN = 320
BLK = 128
FOUR = 4

masked_score = -1e30
empty_best = 1e30
total_limit = 2.0**100
score_scale = math.log2(math.e) / math.sqrt(HD)


def scores_of(query_rows, key_rows):
    return (
        lax.dot_general(
            query_rows, key_rows, (((1,), (1,)), ((), ())), preferred_element_type=jnp.float32
        )
        * score_scale
    )


def with_ones(value_rows):
    return jnp.concatenate([value_rows, jnp.ones_like(value_rows)], axis=1)


def stacked(ref, rows, head_count):
    return jnp.concatenate([ref[rows, h * HD : (h + 1) * HD] for h in range(head_count)], axis=0)


def unstack(ref, rows, head_count, value):
    count = value.shape[0] // head_count
    for h in range(head_count):
        ref[rows, h * HD : (h + 1) * HD] = value[h * count : (h + 1) * count]


def widen(row_value, width):
    return jnp.concatenate([row_value] * (width // HD), axis=1)


def local_stage(
    lengths_hbm,
    query_hbm,
    suffix_hbm,
    own_hbm,
    best_ref,
    total_ref,
    sum_ref,
    query_ref,
    lengths_ref,
    suffix_ref,
    own_ref,
    whole_sems,
    block_sems,
):
    rows_all = query_ref.shape[0]
    heads = query_ref.shape[1] // HD
    blocks = rows_all // BLK
    whole = [
        pltpu.make_async_copy(source, target, whole_sems.at[i])
        for i, (source, target) in enumerate(
            [(lengths_hbm, lengths_ref), (own_hbm, own_ref), (suffix_hbm, suffix_ref)]
        )
    ]
    pieces = [
        pltpu.make_async_copy(
            query_hbm.at[pl.ds(block * BLK, BLK)],
            query_ref.at[pl.ds(block * BLK, BLK)],
            block_sems.at[block],
        )
        for block in range(blocks)
    ]
    for copy in whole + pieces:
        copy.start()
    for copy in whole + pieces:
        copy.wait()
    position = lax.axis_index("loop")
    window = BLK * ((MAXLEN + BLK - 2) // BLK) + BLK
    for block in range(blocks):
        stop = (block + 1) * BLK
        start = max(0, stop - window, MINLEN // BLK * BLK if block * BLK >= MAXLEN else 0)
        rows = slice(block * BLK, stop)
        row_at = block * BLK + lax.broadcasted_iota(jnp.int32, (BLK, stop - start), 0)
        key_at = start + lax.broadcasted_iota(jnp.int32, (BLK, stop - start), 1)
        first = jnp.zeros_like(row_at)
        agent_end = 0
        for agent in range(AG_DEV):
            agent_end = agent_end + lengths_ref[position * AG_DEV + agent]
            first = jnp.where(row_at >= agent_end, agent_end, first)
        allowed = (key_at <= row_at) & (key_at >= first)
        queries = stacked(query_ref, rows, heads)
        shard = jnp.concatenate([own_ref[...], suffix_ref[start:stop]], axis=0)
        scores = scores_of(queries, shard[:, :HD])
        own_scores = scores[:, : own_ref.shape[0]]
        suffix_scores = jnp.where(
            jnp.concatenate([allowed] * heads, axis=0), scores[:, own_ref.shape[0] :], masked_score
        )
        scores = jnp.concatenate([own_scores, suffix_scores], axis=1)
        best = jnp.max(scores, axis=1, keepdims=True)
        weights = jnp.exp2(scores - best).astype(jnp.bfloat16)
        result = jnp.dot(weights, with_ones(shard[:, HD:]), preferred_element_type=jnp.float32)
        row_at = block * BLK + lax.broadcasted_iota(jnp.int32, (BLK, HD), 0)
        live = jnp.concatenate([row_at < agent_end] * heads, axis=0)
        unstack(best_ref, rows, heads, jnp.where(live, best, empty_best))
        unstack(sum_ref, rows, heads, jnp.where(live, result[:, :HD], 0.0))
        unstack(total_ref, rows, heads, jnp.where(live, result[:, HD:], 1.0))


def staged(blocks, start, finish):
    coming = start(blocks[0])
    for index, rows in enumerate(blocks):
        now = coming
        if index + 1 < len(blocks):
            coming = start(blocks[index + 1])
        finish(index, rows, now)


def row_blocks(count, largest):
    step = next(size for size in (largest, 128, 16, count) if count % size == 0)
    return [slice(first, first + step) for first in range(0, count, step)]


def place():
    return lax.rem(lax.axis_index("loop"), FOUR), lax.axis_index("pair")


def penalty(is_there):
    return jnp.where(is_there, 0.0, empty_best)


def add_stage(by_swap, *refs):
    query_ref, best_ref, total_ref, sum_ref = refs[:4]
    shard_refs = refs[4:-2]
    total_out, sum_out = refs[-2:]
    heads = query_ref.shape[1] // HD
    shard = jnp.concatenate([ref[...] for ref in shard_refs], axis=0)
    key_rows, value_rows = shard[:, :HD], with_ones(shard[:, HD:])
    extra = None
    if by_swap is not None:
        position, core = place()
        extra = penalty((position != 1) | (core == int(by_swap)))

    def start(rows):
        return scores_of(stacked(query_ref, rows, heads), key_rows)

    def finish(index, rows, scores):
        best = stacked(best_ref, rows, heads)
        if extra is None:
            points = widen(best, scores.shape[1])
        else:
            held = shard_refs[-1].shape[0]
            points = [best] * ((scores.shape[1] - held) // HD) + [best + extra] * (held // HD)
            points = jnp.concatenate(points, axis=1)
        weights = jnp.exp2(scores - points).astype(jnp.bfloat16)
        result = jnp.dot(weights, value_rows, preferred_element_type=jnp.float32)
        unstack(total_out, rows, heads, stacked(total_ref, rows, heads) + result[:, HD:])
        unstack(sum_out, rows, heads, stacked(sum_ref, rows, heads) + result[:, :HD])

    staged(row_blocks(query_ref.shape[0], 80), start, finish)


def last_stage(routed, *refs):
    query_ref, best_ref, old_total_ref, old_sum_ref, total_ref, sum_ref = refs[:6]
    earlier_refs, refs = refs[6:-6], refs[-6:]
    direct_ref, swapped_ref, out_hbm, out_ref, trusted_ref, out_sems = refs
    heads = query_ref.shape[1] // HD
    blocks = row_blocks(query_ref.shape[0], 80)
    position, core = place()
    takes_both = (position == 1) & routed
    is_direct = core == jnp.where(position == 0, 0, 1)

    def out_copy(index, rows):
        return pltpu.make_async_copy(out_ref.at[rows], out_hbm.at[rows], out_sems.at[index])

    def write(rows, total, weighted):
        unstack(out_ref, rows, heads, (weighted / total).astype(jnp.bfloat16))

    def process(shard):
        trusted = [jnp.full((8, HD), True)]

        def start(rows):
            return scores_of(stacked(query_ref, rows, heads), shard[:, :HD])

        def finish(index, rows, scores):
            best = stacked(best_ref, rows, heads)
            weights = jnp.exp2(scores - widen(best, scores.shape[1]))
            lanes = sum(weights[:, i : i + HD] for i in range(0, scores.shape[1], HD))
            total = stacked(total_ref, rows, heads) + jnp.sum(lanes, axis=1, keepdims=True)
            weighted = stacked(sum_ref, rows, heads) + jnp.dot(
                weights.astype(jnp.bfloat16), shard[:, HD:], preferred_element_type=jnp.float32
            )
            good = (total < total_limit).reshape(total.shape[0] // 8, 8, HD)
            trusted[0] = trusted[0] & jnp.all(good, axis=0)
            write(rows, total, weighted)
            out_copy(index, rows).start()

        staged(blocks, start, finish)
        trusted_ref[0] = jnp.all(trusted[0]).astype(jnp.int32)
        for index, rows in enumerate(blocks):
            out_copy(index, rows).wait()

    @pl.when(jnp.logical_not(takes_both))
    def one_shard():
        process(jnp.where(is_direct, direct_ref[...], swapped_ref[...]))

    @pl.when(takes_both)
    def two_shards():
        process(jnp.concatenate([direct_ref[...], swapped_ref[...]], axis=0))

    @pl.when(trusted_ref[0] == 0)
    def exact_maximum():
        size = query_ref.shape[0] // len(blocks)
        counted = [(ref, 0.0) for ref in earlier_refs]
        if routed:
            counted[-2:] = [
                (ref, penalty((position != 1) | (core == by_swap)))
                for by_swap, ref in enumerate(earlier_refs[-2:])
            ]
        counted += [
            (direct_ref, penalty(takes_both | is_direct)),
            (swapped_ref, penalty(takes_both | jnp.logical_not(is_direct))),
        ]

        def visit(index, unused):
            rows = pl.ds(pl.multiple_of(index * size, size), size)
            queries = stacked(query_ref, rows, heads)
            best = stacked(best_ref, rows, heads)
            weighted = stacked(old_sum_ref, rows, heads)
            total = stacked(old_total_ref, rows, heads)
            for shard_ref, extra in counted:
                key_rows, value_rows = shard_ref[:, :HD], with_ones(shard_ref[:, HD:])
                scores = scores_of(queries, key_rows) - extra
                new_best = jnp.maximum(best, jnp.max(scores, axis=1, keepdims=True))
                factor = jnp.exp2(best - new_best)
                weights = jnp.exp2(scores - widen(new_best, scores.shape[1]))
                result = jnp.dot(
                    weights.astype(jnp.bfloat16), value_rows, preferred_element_type=jnp.float32
                )
                weighted = weighted * factor + result[:, :HD]
                total = total * factor + result[:, HD:]
                best = new_best
            write(rows, total, weighted)
            copy = out_copy(index, rows)
            copy.start()
            copy.wait()
            return unused

        lax.fori_loop(0, len(blocks), visit, 0)


def shards(queries, suffix_kv, prompt_kv, lengths):
    slots, width = queries.shape
    heads = width // HD
    loop_size = lax.axis_size("loop")
    own = prompt_kv[:, 0, :]
    suffix = suffix_kv[:, 0, :]
    shard_rows = own.shape[0]

    routed = loop_size >= FOUR and loop_size & (loop_size - 1) == 0

    def send(shard, route):
        hops = []
        for i in range(loop_size):
            for core in range(2):
                goal = route(i, core)
                if goal is not None:
                    hops.append((2 * i + core, 2 * goal[0] + goal[1]))
        return lax.ppermute(shard, ("loop", "pair"), hops)

    def first_route(i, core):
        base = i - i % FOUR
        to, to_core = [((1, 0), (3, 1)), ((1, 1), (2, 0)), ((3, 0), (0, 0)), ((2, 1), (0, 1))][
            i % FOUR
        ][core]
        return base + to, to_core

    def second_route(i, core):
        base = i - i % FOUR
        to, to_core = [((0, 1), (2, 1)), ((0, 0), (3, 1)), (None, (1, 0)), (None, (1, 1))][
            i % FOUR
        ][core] or (None, None)
        return None if to is None else (base + to, to_core)

    if routed:
        early = [
            send(own, lambda i, core, step=step: (i ^ (step + core), 1 - core))
            for step in range(FOUR, loop_size, 2)
        ]
        early.append(send(own, first_route))
        final = send(own, second_route)
    else:
        early = [
            send(own, lambda i, core, step=step: ((i + step) % loop_size, core))
            for step in range(1, loop_size)
        ]
        final = early.pop()
    in_hbm = pl.BlockSpec(memory_space=pltpu.HBM)
    in_vmem = pl.BlockSpec(memory_space=pltpu.VMEM)
    state = jax.ShapeDtypeStruct((slots, width), jnp.float32)

    cost = pl.CostEstimate(flops=1, bytes_accessed=1, transcendentals=0)

    best, total, weighted, queries = pl.pallas_call(
        local_stage,
        name="local_stage",
        out_shape=[state] * 3 + [jax.ShapeDtypeStruct((slots, width), queries.dtype)],
        in_specs=[in_hbm] * 4,
        out_specs=[in_vmem] * 4,
        scratch_shapes=[
            pltpu.SMEM(lengths.shape, lengths.dtype),
            pltpu.VMEM(suffix.shape, suffix.dtype),
            pltpu.VMEM(own.shape, own.dtype),
            pltpu.SemaphoreType.DMA((3,)),
            pltpu.SemaphoreType.DMA((slots // BLK,)),
        ],
        compiler_params=pltpu.CompilerParams(vmem_limit_bytes=24 * 2**20),
        cost_estimate=cost,
    )(*(pltpu.with_memory_space_constraint(x, pltpu.HBM) for x in (lengths, queries, suffix, own)))
    def add_shards(total, weighted, shards_now, by_swap):
        if not shards_now:
            return total, weighted
        return pl.pallas_call(
            functools.partial(add_stage, by_swap if routed else None),
            name="add_stage",
            out_shape=[state] * 2,
            in_specs=[in_vmem] * (4 + len(shards_now)),
            out_specs=[in_vmem] * 2,
            compiler_params=pltpu.CompilerParams(vmem_limit_bytes=24 * 2**20),
            cost_estimate=cost,
        )(queries, best, total, weighted, *shards_now)

    def swapped(shard):
        return send(shard, lambda i, core: (i, 1 - core))

    early, best = lax.optimization_barrier((early, best))
    early_swapped = [swapped(shard) for shard in early] if routed else []
    new_total, new_weighted = add_shards(total, weighted, early, False)
    final, new_total = lax.optimization_barrier((final, new_total))
    final_swapped = swapped(final) if routed else final
    new_total, new_weighted = add_shards(new_total, new_weighted, early_swapped, True)
    last_inputs = (queries, best, total, weighted, new_total, new_weighted)
    last_inputs += (*early[:-1], *early_swapped[:-1], *early[-1:], *early_swapped[-1:])
    last_inputs += (final, final_swapped)
    return pl.pallas_call(
        functools.partial(last_stage, routed),
        name="last_stage",
        out_shape=jax.ShapeDtypeStruct((slots, width), jnp.bfloat16),
        in_specs=[in_vmem] * len(last_inputs),
        out_specs=in_hbm,
        scratch_shapes=[
            pltpu.VMEM((slots, width), jnp.bfloat16),
            pltpu.SMEM((1,), jnp.int32),
            pltpu.SemaphoreType.DMA((len(row_blocks(slots, 80)),)),
        ],
        compiler_params=pltpu.CompilerParams(vmem_limit_bytes=32 * 2**20),
        cost_estimate=cost,
    )(*last_inputs)


def solution(mesh):
    placed = (
        P(("groups", "loop"), ("heads", "pair")),
        P(("groups", "loop"), "heads", None),
        P(("groups", "loop"), "heads", None),
        P("groups"),
    )
    return jax.shard_map(
        shards,
        mesh=mesh,
        in_specs=placed,
        out_specs=P(("groups", "loop"), ("heads", "pair")),
        check_vma=False,
    )
```

```python
import functools
import math

import jax
import jax.numpy as jnp
from jax import lax
from jax.experimental import pallas as pl
from jax.experimental.pallas import tpu as pltpu
from jax.sharding import PartitionSpec as P

HD = 128
AG_DEV = 2
MAXLEN = 320
BLK = 128
FOUR = 4

masked_score = -1e30
empty_best = 1e30
total_limit = 2.0**100
score_scale = math.log2(math.e) / math.sqrt(HD)


def scores_of(query_rows, key_rows):
    return (
        lax.dot_general(
            query_rows, key_rows, (((1,), (1,)), ((), ())), preferred_element_type=jnp.float32
        )
        * score_scale
    )


def with_ones(value_rows):
    return jnp.concatenate([value_rows, jnp.ones_like(value_rows)], axis=1)


def stacked(ref, rows, head_count):
    return jnp.concatenate([ref[rows, h * HD : (h + 1) * HD] for h in range(head_count)], axis=0)


def unstack(ref, rows, head_count, value):
    count = value.shape[0] // head_count
    for h in range(head_count):
        ref[rows, h * HD : (h + 1) * HD] = value[h * count : (h + 1) * count]


def widen(row_value, width):
    return jnp.concatenate([row_value] * (width // HD), axis=1)


def local_stage(
    lengths_hbm,
    query_hbm,
    suffix_hbm,
    own_hbm,
    best_ref,
    total_ref,
    sum_ref,
    query_ref,
    lengths_ref,
    suffix_ref,
    own_ref,
    whole_sems,
    block_sems,
):
    rows_all = query_ref.shape[0]
    heads = query_ref.shape[1] // HD
    blocks = rows_all // BLK
    whole = [
        pltpu.make_async_copy(source, target, whole_sems.at[i])
        for i, (source, target) in enumerate(
            [(lengths_hbm, lengths_ref), (own_hbm, own_ref), (suffix_hbm, suffix_ref)]
        )
    ]
    pieces = [
        pltpu.make_async_copy(
            query_hbm.at[pl.ds(block * BLK, BLK)],
            query_ref.at[pl.ds(block * BLK, BLK)],
            block_sems.at[block],
        )
        for block in range(blocks)
    ]
    for copy in whole + pieces:
        copy.start()
    for copy in whole + pieces:
        copy.wait()
    position = lax.axis_index("loop")
    window = BLK * ((MAXLEN + BLK - 2) // BLK) + BLK
    for block in range(blocks):
        stop = (block + 1) * BLK
        start = max(0, stop - window)
        rows = slice(block * BLK, stop)
        row_at = block * BLK + lax.broadcasted_iota(jnp.int32, (BLK, stop - start), 0)
        key_at = start + lax.broadcasted_iota(jnp.int32, (BLK, stop - start), 1)
        first = jnp.zeros_like(row_at)
        agent_end = 0
        for agent in range(AG_DEV):
            agent_end = agent_end + lengths_ref[position * AG_DEV + agent]
            first = jnp.where(row_at >= agent_end, agent_end, first)
        allowed = (key_at <= row_at) & (key_at >= first)
        queries = stacked(query_ref, rows, heads)
        shard = jnp.concatenate([own_ref[...], suffix_ref[start:stop]], axis=0)
        scores = scores_of(queries, shard[:, :HD])
        own_scores = scores[:, : own_ref.shape[0]]
        suffix_scores = jnp.where(
            jnp.concatenate([allowed] * heads, axis=0), scores[:, own_ref.shape[0] :], masked_score
        )
        scores = jnp.concatenate([own_scores, suffix_scores], axis=1)
        best = jnp.max(scores, axis=1, keepdims=True)
        weights = jnp.exp2(scores - best).astype(jnp.bfloat16)
        result = jnp.dot(weights, with_ones(shard[:, HD:]), preferred_element_type=jnp.float32)
        row_at = block * BLK + lax.broadcasted_iota(jnp.int32, (BLK, HD), 0)
        live = jnp.concatenate([row_at < agent_end] * heads, axis=0)
        unstack(best_ref, rows, heads, jnp.where(live, best, empty_best))
        unstack(sum_ref, rows, heads, jnp.where(live, result[:, :HD], 0.0))
        unstack(total_ref, rows, heads, jnp.where(live, result[:, HD:], 1.0))


def staged(blocks, start, finish):
    coming = start(blocks[0])
    for index, rows in enumerate(blocks):
        now = coming
        if index + 1 < len(blocks):
            coming = start(blocks[index + 1])
        finish(index, rows, now)


def row_blocks(count, largest):
    step = next(size for size in (largest, 128, 16, count) if count % size == 0)
    return [slice(first, first + step) for first in range(0, count, step)]


def place():
    return lax.rem(lax.axis_index("loop"), FOUR), lax.axis_index("pair")


def penalty(is_there):
    return jnp.where(is_there, 0.0, empty_best)


def add_stage(by_swap, *refs):
    query_ref, best_ref, total_ref, sum_ref = refs[:4]
    shard_refs = refs[4:-2]
    total_out, sum_out = refs[-2:]
    heads = query_ref.shape[1] // HD
    shard = jnp.concatenate([ref[...] for ref in shard_refs], axis=0)
    key_rows, value_rows = shard[:, :HD], with_ones(shard[:, HD:])
    extra = None
    if by_swap is not None:
        position, core = place()
        extra = penalty((position != 1) | (core == int(by_swap)))

    def start(rows):
        return scores_of(stacked(query_ref, rows, heads), key_rows)

    def finish(index, rows, scores):
        best = stacked(best_ref, rows, heads)
        if extra is None:
            points = widen(best, scores.shape[1])
        else:
            held = shard_refs[-1].shape[0]
            points = [best] * ((scores.shape[1] - held) // HD) + [best + extra] * (held // HD)
            points = jnp.concatenate(points, axis=1)
        weights = jnp.exp2(scores - points).astype(jnp.bfloat16)
        result = jnp.dot(weights, value_rows, preferred_element_type=jnp.float32)
        unstack(total_out, rows, heads, stacked(total_ref, rows, heads) + result[:, HD:])
        unstack(sum_out, rows, heads, stacked(sum_ref, rows, heads) + result[:, :HD])

    staged(row_blocks(query_ref.shape[0], 80), start, finish)


def last_stage(routed, *refs):
    query_ref, best_ref, old_total_ref, old_sum_ref, total_ref, sum_ref = refs[:6]
    earlier_refs, refs = refs[6:-6], refs[-6:]
    direct_ref, swapped_ref, out_hbm, out_ref, trusted_ref, out_sems = refs
    heads = query_ref.shape[1] // HD
    blocks = row_blocks(query_ref.shape[0], 80)
    position, core = place()
    takes_both = (position == 1) & routed
    is_direct = core == jnp.where(position == 0, 0, 1)

    def out_copy(index, rows):
        return pltpu.make_async_copy(out_ref.at[rows], out_hbm.at[rows], out_sems.at[index])

    def write(rows, total, weighted):
        inverse = pl.reciprocal(total, approx=True)
        inverse = inverse * (2.0 - total * inverse)
        unstack(out_ref, rows, heads, (weighted * inverse).astype(jnp.bfloat16))

    def process(shard):
        trusted = [jnp.full((8, HD), True)]
        key_rows, value_rows = shard[:, :HD], with_ones(shard[:, HD:])

        def start(rows):
            return scores_of(stacked(query_ref, rows, heads), key_rows)

        def finish(index, rows, scores):
            best = stacked(best_ref, rows, heads)
            weights = jnp.exp2(scores - widen(best, scores.shape[1])).astype(jnp.bfloat16)
            result = jnp.dot(weights, value_rows, preferred_element_type=jnp.float32)
            total = stacked(total_ref, rows, heads) + result[:, HD:]
            weighted = stacked(sum_ref, rows, heads) + result[:, :HD]
            good = (total < total_limit).reshape(total.shape[0] // 8, 8, HD)
            trusted[0] = trusted[0] & jnp.all(good, axis=0)
            write(rows, total, weighted)
            out_copy(index, rows).start()

        staged(blocks, start, finish)
        trusted_ref[0] = jnp.all(trusted[0]).astype(jnp.int32)
        for index, rows in enumerate(blocks):
            out_copy(index, rows).wait()

    @pl.when(jnp.logical_not(takes_both))
    def one_shard():
        process(jnp.where(is_direct, direct_ref[...], swapped_ref[...]))

    @pl.when(takes_both)
    def two_shards():
        process(jnp.concatenate([direct_ref[...], swapped_ref[...]], axis=0))

    @pl.when(trusted_ref[0] == 0)
    def exact_maximum():
        size = query_ref.shape[0] // len(blocks)
        counted = [(ref, 0.0) for ref in earlier_refs]
        if routed:
            counted[-2:] = [
                (ref, penalty((position != 1) | (core == by_swap)))
                for by_swap, ref in enumerate(earlier_refs[-2:])
            ]
        counted += [
            (direct_ref, penalty(takes_both | is_direct)),
            (swapped_ref, penalty(takes_both | jnp.logical_not(is_direct))),
        ]

        def visit(index, unused):
            rows = pl.ds(pl.multiple_of(index * size, size), size)
            queries = stacked(query_ref, rows, heads)
            best = stacked(best_ref, rows, heads)
            weighted = stacked(old_sum_ref, rows, heads)
            total = stacked(old_total_ref, rows, heads)
            for shard_ref, extra in counted:
                key_rows, value_rows = shard_ref[:, :HD], with_ones(shard_ref[:, HD:])
                scores = scores_of(queries, key_rows) - extra
                new_best = jnp.maximum(best, jnp.max(scores, axis=1, keepdims=True))
                factor = jnp.exp2(best - new_best)
                weights = jnp.exp2(scores - widen(new_best, scores.shape[1]))
                result = jnp.dot(
                    weights.astype(jnp.bfloat16), value_rows, preferred_element_type=jnp.float32
                )
                weighted = weighted * factor + result[:, :HD]
                total = total * factor + result[:, HD:]
                best = new_best
            write(rows, total, weighted)
            copy = out_copy(index, rows)
            copy.start()
            copy.wait()
            return unused

        lax.fori_loop(0, len(blocks), visit, 0)


def shards(queries, suffix_kv, prompt_kv, lengths):
    slots, width = queries.shape
    heads = width // HD
    loop_size = lax.axis_size("loop")
    own = prompt_kv[:, 0, :]
    suffix = suffix_kv[:, 0, :]
    shard_rows = own.shape[0]

    routed = loop_size >= FOUR and loop_size & (loop_size - 1) == 0

    def send(shard, route):
        hops = []
        for i in range(loop_size):
            for core in range(2):
                to, to_core = route(i, core)
                hops.append((2 * i + core, 2 * to + to_core))
        return lax.ppermute(shard, ("loop", "pair"), hops)

    def first_route(i, core):
        base = i - i % FOUR
        to, to_core = [((1, 0), (3, 1)), ((1, 1), (2, 0)), ((3, 0), (0, 0)), ((2, 1), (0, 1))][
            i % FOUR
        ][core]
        return base + to, to_core

    def second_route(i, core):
        base = i - i % FOUR
        to, to_core = [((0, 1), (2, 1)), ((0, 0), (3, 1)), ((3, 0), (1, 0)), ((2, 0), (1, 1))][
            i % FOUR
        ][core]
        return base + to, to_core

    if routed:
        early = [
            send(own, lambda i, core, step=step: (i ^ (step + core), 1 - core))
            for step in range(FOUR, loop_size, 2)
        ]
        early.append(send(own, first_route))
        final = send(own, second_route)
    else:
        early = [
            send(own, lambda i, core, step=step: ((i + step) % loop_size, core))
            for step in range(1, loop_size)
        ]
        final = early.pop()
    in_hbm = pl.BlockSpec(memory_space=pltpu.HBM)
    in_vmem = pl.BlockSpec(memory_space=pltpu.VMEM)
    state = jax.ShapeDtypeStruct((slots, width), jnp.float32)

    cost = pl.CostEstimate(flops=1, bytes_accessed=1, transcendentals=0)

    best, total, weighted, queries = pl.pallas_call(
        local_stage,
        name="local_stage",
        out_shape=[state] * 3 + [jax.ShapeDtypeStruct((slots, width), queries.dtype)],
        in_specs=[in_hbm] * 4,
        out_specs=[in_vmem] * 4,
        scratch_shapes=[
            pltpu.SMEM(lengths.shape, lengths.dtype),
            pltpu.VMEM(suffix.shape, suffix.dtype),
            pltpu.VMEM(own.shape, own.dtype),
            pltpu.SemaphoreType.DMA((3,)),
            pltpu.SemaphoreType.DMA((slots // BLK,)),
        ],
        compiler_params=pltpu.CompilerParams(vmem_limit_bytes=24 * 2**20),
        cost_estimate=cost,
    )(*(pltpu.with_memory_space_constraint(x, pltpu.HBM) for x in (lengths, queries, suffix, own)))
    def add_shards(total, weighted, shards_now, by_swap):
        if not shards_now:
            return total, weighted
        return pl.pallas_call(
            functools.partial(add_stage, by_swap if routed else None),
            name="add_stage",
            out_shape=[state] * 2,
            in_specs=[in_vmem] * (4 + len(shards_now)),
            out_specs=[in_vmem] * 2,
            compiler_params=pltpu.CompilerParams(vmem_limit_bytes=24 * 2**20),
            cost_estimate=cost,
        )(queries, best, total, weighted, *shards_now)

    def swapped(shard):
        return send(shard, lambda i, core: (i, 1 - core))

    early, best = lax.optimization_barrier((early, best))
    early_swapped = [swapped(shard) for shard in early] if routed else []
    new_total, new_weighted = add_shards(total, weighted, early, False)
    final, new_total = lax.optimization_barrier((final, new_total))
    final_swapped = swapped(final) if routed else final
    new_total, new_weighted = add_shards(new_total, new_weighted, early_swapped, True)
    last_inputs = (queries, best, total, weighted, new_total, new_weighted)
    last_inputs += (*early[:-1], *early_swapped[:-1], *early[-1:], *early_swapped[-1:])
    last_inputs += (final, final_swapped)
    return pl.pallas_call(
        functools.partial(last_stage, routed),
        name="last_stage",
        out_shape=jax.ShapeDtypeStruct((slots, width), jnp.bfloat16),
        in_specs=[in_vmem] * len(last_inputs),
        out_specs=in_hbm,
        scratch_shapes=[
            pltpu.VMEM((slots, width), jnp.bfloat16),
            pltpu.SMEM((1,), jnp.int32),
            pltpu.SemaphoreType.DMA((len(row_blocks(slots, 80)),)),
        ],
        compiler_params=pltpu.CompilerParams(vmem_limit_bytes=32 * 2**20),
        cost_estimate=cost,
    )(*last_inputs)


def solution(mesh):
    placed = (
        P(("groups", "loop"), ("heads", "pair")),
        P(("groups", "loop"), "heads", None),
        P(("groups", "loop"), "heads", None),
        P("groups"),
    )
    return jax.shard_map(
        shards,
        mesh=mesh,
        in_specs=placed,
        out_specs=P(("groups", "loop"), ("heads", "pair")),
        check_vma=False,
    )
```

```python
import functools
import math

import jax
import jax.numpy as jnp
from jax import lax
from jax.experimental import pallas as pl
from jax.experimental.pallas import tpu as pltpu
from jax.sharding import PartitionSpec as P

HD = 128
AG_DEV = 2
MAXLEN = 320
BLK = 128
FOUR = 4

masked_score = -1e30
empty_best = 1e30
total_limit = 2.0**100
score_scale = math.log2(math.e) / math.sqrt(HD)


def scores_of(query_rows, key_rows):
    return (
        lax.dot_general(
            query_rows, key_rows, (((1,), (1,)), ((), ())), preferred_element_type=jnp.float32
        )
        * score_scale
    )


def with_ones(value_rows):
    return jnp.concatenate([value_rows, jnp.ones_like(value_rows)], axis=1)


def stacked(ref, rows, head_count):
    return jnp.concatenate([ref[rows, h * HD : (h + 1) * HD] for h in range(head_count)], axis=0)


def unstack(ref, rows, head_count, value):
    count = value.shape[0] // head_count
    for h in range(head_count):
        ref[rows, h * HD : (h + 1) * HD] = value[h * count : (h + 1) * count]


def widen(row_value, width):
    return jnp.concatenate([row_value] * (width // HD), axis=1)


def place():
    return lax.rem(lax.axis_index("loop"), FOUR), lax.axis_index("pair")


def load_blocks(count):
    return [pl.ds(first, BLK) for first in range(0, count, BLK)]


def load(
    lengths_hbm,
    query_hbm,
    suffix_hbm,
    own_hbm,
    query_ref,
    suffix_ref,
    own_ref,
    first_ref,
    lengths_ref,
    sems,
):
    pairs = [(lengths_hbm, lengths_ref), (own_hbm, own_ref)]
    for source, target in ((query_hbm, query_ref), (suffix_hbm, suffix_ref)):
        for rows in load_blocks(target.shape[0]):
            pairs.append((source.at[rows], target.at[rows]))
    copies = [
        pltpu.make_async_copy(source, target, sems.at[i])
        for i, (source, target) in enumerate(pairs)
    ]
    for copy in copies:
        copy.start()
    copies[0].wait()
    slots = query_ref.shape[0]
    position = lax.axis_index("loop")
    row_at = lax.broadcasted_iota(jnp.int32, first_ref.shape, 0)
    first = jnp.zeros_like(row_at)
    agent_end = 0
    for agent in range(AG_DEV):
        agent_end = agent_end + lengths_ref[position * AG_DEV + agent]
        first = jnp.where(row_at >= agent_end, agent_end if agent + 1 < AG_DEV else slots, first)
    first_ref[...] = first
    for copy in copies[1:]:
        copy.wait()


def prelude_stage(*refs):
    @pl.when(place()[0] == 0)
    def ahead():
        load(*refs)


def local_stage(*refs):
    sources, (best_ref, total_ref, sum_ref), loaded, scratch = (
        refs[:4],
        refs[8:11],
        refs[11:15],
        refs[15:],
    )
    query_ref, suffix_ref, own_ref, first_ref = loaded

    @pl.when(place()[0] != 0)
    def now():
        load(*sources, *loaded, *scratch)

    slots = query_ref.shape[0]
    heads = query_ref.shape[1] // HD
    own_keys = own_ref[:, :HD]
    own_values = with_ones(own_ref[:, HD:])
    window = BLK * ((MAXLEN + BLK - 2) // BLK) + BLK
    for block in range(slots // BLK):
        stop = (block + 1) * BLK
        start = max(0, stop - window)
        rows = slice(block * BLK, stop)
        row_at = block * BLK + lax.broadcasted_iota(jnp.int32, (BLK, stop - start), 0)
        key_at = start + lax.broadcasted_iota(jnp.int32, (BLK, stop - start), 1)
        first = first_ref[rows]
        allowed = (key_at <= row_at) & (key_at >= widen(first, stop - start))
        queries = stacked(query_ref, rows, heads)
        own_scores = scores_of(queries, own_keys)
        suffix_scores = jnp.where(
            jnp.concatenate([allowed] * heads, axis=0),
            scores_of(queries, suffix_ref[start:stop, :HD]),
            masked_score,
        )
        best = jnp.maximum(
            jnp.max(own_scores, axis=1, keepdims=True),
            jnp.max(suffix_scores, axis=1, keepdims=True),
        )
        own_weights = jnp.exp2(own_scores - best).astype(jnp.bfloat16)
        suffix_weights = jnp.exp2(suffix_scores - best).astype(jnp.bfloat16)
        result = jnp.dot(own_weights, own_values, preferred_element_type=jnp.float32)
        result = result + jnp.dot(
            suffix_weights,
            with_ones(suffix_ref[start:stop, HD:]),
            preferred_element_type=jnp.float32,
        )
        live = jnp.concatenate([first < slots] * heads, axis=0)
        unstack(best_ref, rows, heads, jnp.where(live, best, empty_best))
        unstack(sum_ref, rows, heads, jnp.where(live, result[:, :HD], 0.0))
        unstack(total_ref, rows, heads, jnp.where(live, result[:, HD:], 1.0))


def staged(blocks, start, finish):
    coming = start(blocks[0])
    for index, rows in enumerate(blocks):
        now = coming
        if index + 1 < len(blocks):
            coming = start(blocks[index + 1])
        finish(index, rows, now)


def row_blocks(count, largest):
    step = next(size for size in (largest, 128, 16, count) if count % size == 0)
    return [slice(first, first + step) for first in range(0, count, step)]


def penalty(is_there):
    return jnp.where(is_there, 0.0, empty_best)


def add_stage(by_swap, *refs):
    query_ref, best_ref, total_ref, sum_ref = refs[:4]
    shard_refs = refs[4:-2]
    total_out, sum_out = refs[-2:]
    heads = query_ref.shape[1] // HD
    shard = jnp.concatenate([ref[...] for ref in shard_refs], axis=0)
    key_rows, value_rows = shard[:, :HD], with_ones(shard[:, HD:])
    extra = None
    if by_swap is not None:
        position, core = place()
        extra = penalty((position != 1) | (core == int(by_swap)))

    def start(rows):
        return scores_of(stacked(query_ref, rows, heads), key_rows)

    def finish(index, rows, scores):
        best = stacked(best_ref, rows, heads)
        if extra is None:
            points = widen(best, scores.shape[1])
        else:
            held = shard_refs[-1].shape[0]
            points = [best] * ((scores.shape[1] - held) // HD) + [best + extra] * (held // HD)
            points = jnp.concatenate(points, axis=1)
        weights = jnp.exp2(scores - points).astype(jnp.bfloat16)
        result = jnp.dot(weights, value_rows, preferred_element_type=jnp.float32)
        unstack(total_out, rows, heads, stacked(total_ref, rows, heads) + result[:, HD:])
        unstack(sum_out, rows, heads, stacked(sum_ref, rows, heads) + result[:, :HD])

    staged(row_blocks(query_ref.shape[0], 80), start, finish)


def last_stage(routed, *refs):
    query_ref, best_ref, old_total_ref, old_sum_ref, total_ref, sum_ref = refs[:6]
    earlier_refs, refs = refs[6:-6], refs[-6:]
    direct_ref, swapped_ref, out_hbm, out_ref, trusted_ref, out_sems = refs
    heads = query_ref.shape[1] // HD
    blocks = row_blocks(query_ref.shape[0], 80)
    position, core = place()
    takes_both = (position == 1) & routed
    is_direct = core == 0

    def out_copy(index, rows):
        return pltpu.make_async_copy(out_ref.at[rows], out_hbm.at[rows], out_sems.at[index])

    def write(rows, total, weighted):
        inverse = pl.reciprocal(total, approx=True)
        inverse = inverse * (2.0 - total * inverse)
        unstack(out_ref, rows, heads, (weighted * inverse).astype(jnp.bfloat16))

    def process(shard):
        trusted = [jnp.full((8, HD), True)]
        key_rows, value_rows = shard[:, :HD], with_ones(shard[:, HD:])

        def start(rows):
            return scores_of(stacked(query_ref, rows, heads), key_rows)

        def finish(index, rows, scores):
            best = stacked(best_ref, rows, heads)
            weights = jnp.exp2(scores - widen(best, scores.shape[1])).astype(jnp.bfloat16)
            result = jnp.dot(weights, value_rows, preferred_element_type=jnp.float32)
            total = stacked(total_ref, rows, heads) + result[:, HD:]
            weighted = stacked(sum_ref, rows, heads) + result[:, :HD]
            good = (total < total_limit).reshape(total.shape[0] // 8, 8, HD)
            trusted[0] = trusted[0] & jnp.all(good, axis=0)
            write(rows, total, weighted)
            out_copy(index, rows).start()

        staged(blocks, start, finish)
        trusted_ref[0] = jnp.all(trusted[0]).astype(jnp.int32)
        for index, rows in enumerate(blocks):
            out_copy(index, rows).wait()

    @pl.when(jnp.logical_not(takes_both))
    def one_shard():
        process(jnp.where(is_direct, direct_ref[...], swapped_ref[...]))

    @pl.when(takes_both)
    def two_shards():
        process(jnp.concatenate([direct_ref[...], swapped_ref[...]], axis=0))

    @pl.when(trusted_ref[0] == 0)
    def exact_maximum():
        size = query_ref.shape[0] // len(blocks)
        counted = [(ref, 0.0) for ref in earlier_refs]
        if routed:
            counted[-2:] = [
                (ref, penalty((position != 1) | (core == by_swap)))
                for by_swap, ref in enumerate(earlier_refs[-2:])
            ]
        counted += [
            (direct_ref, penalty(takes_both | is_direct)),
            (swapped_ref, penalty(takes_both | jnp.logical_not(is_direct))),
        ]

        def visit(index, unused):
            rows = pl.ds(pl.multiple_of(index * size, size), size)
            queries = stacked(query_ref, rows, heads)
            best = stacked(best_ref, rows, heads)
            weighted = stacked(old_sum_ref, rows, heads)
            total = stacked(old_total_ref, rows, heads)
            for shard_ref, extra in counted:
                key_rows, value_rows = shard_ref[:, :HD], with_ones(shard_ref[:, HD:])
                scores = scores_of(queries, key_rows) - extra
                new_best = jnp.maximum(best, jnp.max(scores, axis=1, keepdims=True))
                factor = jnp.exp2(best - new_best)
                weights = jnp.exp2(scores - widen(new_best, scores.shape[1]))
                result = jnp.dot(
                    weights.astype(jnp.bfloat16), value_rows, preferred_element_type=jnp.float32
                )
                weighted = weighted * factor + result[:, :HD]
                total = total * factor + result[:, HD:]
                best = new_best
            write(rows, total, weighted)
            copy = out_copy(index, rows)
            copy.start()
            copy.wait()
            return unused

        lax.fori_loop(0, len(blocks), visit, 0)


def shards(queries, suffix_kv, prompt_kv, lengths):
    slots, width = queries.shape
    heads = width // HD
    loop_size = lax.axis_size("loop")
    own = prompt_kv[:, 0, :]
    suffix = suffix_kv[:, 0, :]
    shard_rows = own.shape[0]

    in_hbm = pl.BlockSpec(memory_space=pltpu.HBM)
    in_vmem = pl.BlockSpec(memory_space=pltpu.VMEM)
    state = jax.ShapeDtypeStruct((slots, width), jnp.float32)

    cost = pl.CostEstimate(flops=1, bytes_accessed=1, transcendentals=0)

    routed = loop_size >= FOUR and loop_size & (loop_size - 1) == 0

    def send(shard, route):
        hops = []
        for i in range(loop_size):
            for core in range(2):
                to, to_core = route(i, core)
                hops.append((2 * i + core, 2 * to + to_core))
        return lax.ppermute(shard, ("loop", "pair"), hops)

    def first_route(i, core):
        base = i - i % FOUR
        to, to_core = [((1, 0), (3, 1)), ((1, 1), (2, 0)), ((3, 0), (0, 0)), ((2, 1), (0, 1))][
            i % FOUR
        ][core]
        return base + to, to_core

    def second_route(i, core):
        base = i - i % FOUR
        to, to_core = [((0, 1), (2, 0)), ((0, 0), (3, 0)), ((2, 1), (1, 0)), ((3, 1), (1, 1))][
            i % FOUR
        ][core]
        return base + to, to_core

    hbm = [pltpu.with_memory_space_constraint(x, pltpu.HBM) for x in (lengths, queries, suffix, own)]
    buffers = [
        jax.ShapeDtypeStruct(queries.shape, queries.dtype),
        jax.ShapeDtypeStruct(suffix.shape, suffix.dtype),
        jax.ShapeDtypeStruct(own.shape, own.dtype),
        jax.ShapeDtypeStruct((slots, HD), jnp.int32),
    ]
    load_scratch = [
        pltpu.SMEM(lengths.shape, lengths.dtype),
        pltpu.SemaphoreType.DMA((2 + 2 * len(load_blocks(slots)),)),
    ]
    loaded = pl.pallas_call(
        prelude_stage,
        name="prelude_stage",
        out_shape=buffers,
        in_specs=[in_hbm] * 4,
        out_specs=[in_vmem] * 4,
        scratch_shapes=load_scratch,
        compiler_params=pltpu.CompilerParams(vmem_limit_bytes=8 * 2**20),
        cost_estimate=cost,
    )(*hbm)
    own, loaded = lax.optimization_barrier((own, loaded))
    if routed:
        early = [
            send(own, lambda i, core, step=step: (i ^ (step + core), 1 - core))
            for step in range(FOUR, loop_size, 2)
        ]
        early.append(send(own, first_route))
        final = send(own, second_route)
    else:
        early = [
            send(own, lambda i, core, step=step: ((i + step) % loop_size, core))
            for step in range(1, loop_size)
        ]
        final = early.pop()
    best, total, weighted, queries, *unused = pl.pallas_call(
        local_stage,
        name="local_stage",
        out_shape=[state] * 3 + buffers,
        in_specs=[in_hbm] * 4 + [in_vmem] * 4,
        out_specs=[in_vmem] * 7,
        scratch_shapes=load_scratch,
        input_output_aliases={4 + i: 3 + i for i in range(4)},
        compiler_params=pltpu.CompilerParams(vmem_limit_bytes=24 * 2**20),
        cost_estimate=cost,
    )(*hbm, *loaded)

    def add_shards(total, weighted, shards_now, by_swap):
        if not shards_now:
            return total, weighted
        return pl.pallas_call(
            functools.partial(add_stage, by_swap if routed else None),
            name="add_stage",
            out_shape=[state] * 2,
            in_specs=[in_vmem] * (4 + len(shards_now)),
            out_specs=[in_vmem] * 2,
            compiler_params=pltpu.CompilerParams(vmem_limit_bytes=24 * 2**20),
            cost_estimate=cost,
        )(queries, best, total, weighted, *shards_now)

    def swapped(shard):
        return send(shard, lambda i, core: (i, 1 - core))

    early, best = lax.optimization_barrier((early, best))
    early_swapped = [swapped(shard) for shard in early] if routed else []
    new_total, new_weighted = add_shards(total, weighted, early, False)
    final, new_total = lax.optimization_barrier((final, new_total))
    final_swapped = swapped(final) if routed else final
    new_total, new_weighted = add_shards(new_total, new_weighted, early_swapped, True)
    last_inputs = (queries, best, total, weighted, new_total, new_weighted)
    last_inputs += (*early[:-1], *early_swapped[:-1], *early[-1:], *early_swapped[-1:])
    last_inputs += (final, final_swapped)
    return pl.pallas_call(
        functools.partial(last_stage, routed),
        name="last_stage",
        out_shape=jax.ShapeDtypeStruct((slots, width), jnp.bfloat16),
        in_specs=[in_vmem] * len(last_inputs),
        out_specs=in_hbm,
        scratch_shapes=[
            pltpu.VMEM((slots, width), jnp.bfloat16),
            pltpu.SMEM((1,), jnp.int32),
            pltpu.SemaphoreType.DMA((len(row_blocks(slots, 80)),)),
        ],
        compiler_params=pltpu.CompilerParams(vmem_limit_bytes=32 * 2**20),
        cost_estimate=cost,
    )(*last_inputs)


def solution(mesh):
    placed = (
        P(("groups", "loop"), ("heads", "pair")),
        P(("groups", "loop"), "heads", None),
        P(("groups", "loop"), "heads", None),
        P("groups"),
    )
    return jax.shard_map(
        shards,
        mesh=mesh,
        in_specs=placed,
        out_specs=P(("groups", "loop"), ("heads", "pair")),
        check_vma=False,
    )
```

```python
import functools
import math

import jax
import jax.numpy as jnp
from jax import lax
from jax.experimental import pallas as pl
from jax.experimental.pallas import tpu as pltpu
from jax.sharding import PartitionSpec as P

HD = 128
AG_DEV = 2
MAXLEN = 320
BLK = 128
FOUR = 4

masked_score = -1e30
empty_best = 1e30
total_limit = 2.0**100
score_scale = math.log2(math.e) / math.sqrt(HD)


def scores_of(query_rows, key_rows):
    return (
        lax.dot_general(
            query_rows, key_rows, (((1,), (1,)), ((), ())), preferred_element_type=jnp.float32
        )
        * score_scale
    )


def with_ones(value_rows):
    return jnp.concatenate([value_rows, jnp.ones_like(value_rows)], axis=1)


def stacked(ref, rows, head_count):
    return jnp.concatenate([ref[rows, h * HD : (h + 1) * HD] for h in range(head_count)], axis=0)


def unstack(ref, rows, head_count, value):
    count = value.shape[0] // head_count
    for h in range(head_count):
        ref[rows, h * HD : (h + 1) * HD] = value[h * count : (h + 1) * count]


def widen(row_value, width):
    return jnp.concatenate([row_value] * (width // HD), axis=1)


def place():
    return lax.rem(lax.axis_index("loop"), FOUR), lax.axis_index("pair")


def load_blocks(count):
    return [pl.ds(first, BLK) for first in range(0, count, BLK)]


def load(
    lengths_hbm,
    query_hbm,
    suffix_hbm,
    own_hbm,
    query_ref,
    suffix_ref,
    own_ref,
    first_ref,
    lengths_ref,
    sems,
):
    pairs = [(lengths_hbm, lengths_ref), (own_hbm, own_ref)]
    for source, target in ((query_hbm, query_ref), (suffix_hbm, suffix_ref)):
        for rows in load_blocks(target.shape[0]):
            pairs.append((source.at[rows], target.at[rows]))
    copies = [
        pltpu.make_async_copy(source, target, sems.at[i])
        for i, (source, target) in enumerate(pairs)
    ]
    for copy in copies:
        copy.start()
    copies[0].wait()
    slots = query_ref.shape[0]
    position = lax.axis_index("loop")
    row_at = lax.broadcasted_iota(jnp.int32, first_ref.shape, 0)
    first = jnp.zeros_like(row_at)
    agent_end = 0
    for agent in range(AG_DEV):
        agent_end = agent_end + lengths_ref[position * AG_DEV + agent]
        first = jnp.where(row_at >= agent_end, agent_end if agent + 1 < AG_DEV else slots, first)
    first_ref[...] = first
    for copy in copies[1:]:
        copy.wait()


def prelude_stage(*refs):
    @pl.when(is_first_chip())
    def ahead():
        load(*refs)


def local_stage(*refs):
    sources, (best_ref, total_ref, sum_ref), loaded, scratch = (
        refs[:4],
        refs[8:11],
        refs[11:15],
        refs[15:],
    )
    query_ref, suffix_ref, own_ref, first_ref = loaded

    @pl.when(jnp.logical_not(is_first_chip()))
    def now():
        load(*sources, *loaded, *scratch)

    slots = query_ref.shape[0]
    heads = query_ref.shape[1] // HD
    own_keys = own_ref[:, :HD]
    own_values = with_ones(own_ref[:, HD:])
    window = BLK * ((MAXLEN + BLK - 2) // BLK) + BLK
    for block in range(slots // BLK):
        stop = (block + 1) * BLK
        start = max(0, stop - window)
        rows = slice(block * BLK, stop)
        row_at = block * BLK + lax.broadcasted_iota(jnp.int32, (BLK, stop - start), 0)
        key_at = start + lax.broadcasted_iota(jnp.int32, (BLK, stop - start), 1)
        first = first_ref[rows]
        allowed = (key_at <= row_at) & (key_at >= widen(first, stop - start))
        queries = stacked(query_ref, rows, heads)
        own_scores = scores_of(queries, own_keys)
        suffix_scores = jnp.where(
            jnp.concatenate([allowed] * heads, axis=0),
            scores_of(queries, suffix_ref[start:stop, :HD]),
            masked_score,
        )
        best = jnp.maximum(
            jnp.max(own_scores, axis=1, keepdims=True),
            jnp.max(suffix_scores, axis=1, keepdims=True),
        )
        own_weights = jnp.exp2(own_scores - best).astype(jnp.bfloat16)
        suffix_weights = jnp.exp2(suffix_scores - best).astype(jnp.bfloat16)
        result = jnp.dot(own_weights, own_values, preferred_element_type=jnp.float32)
        result = result + jnp.dot(
            suffix_weights,
            with_ones(suffix_ref[start:stop, HD:]),
            preferred_element_type=jnp.float32,
        )
        live = jnp.concatenate([first < slots] * heads, axis=0)
        unstack(best_ref, rows, heads, jnp.where(live, best, empty_best))
        unstack(sum_ref, rows, heads, jnp.where(live, result[:, :HD], 0.0))
        unstack(total_ref, rows, heads, jnp.where(live, result[:, HD:], 1.0))


def staged(blocks, start, finish):
    coming = start(blocks[0])
    for index, rows in enumerate(blocks):
        now = coming
        if index + 1 < len(blocks):
            coming = start(blocks[index + 1])
        finish(index, rows, now)


def row_blocks(count, largest):
    step = next(size for size in (largest, 128, 16, count) if count % size == 0)
    return [slice(first, first + step) for first in range(0, count, step)]


def is_first_chip():
    return lax.axis_index("groups") + lax.axis_index("loop") + lax.axis_index("heads") == 0


def penalty(is_there):
    return jnp.where(is_there, 0.0, empty_best)


def add_stage(by_swap, *refs):
    query_ref, best_ref, total_ref, sum_ref = refs[:4]
    shard_refs = refs[4:-2]
    total_out, sum_out = refs[-2:]
    heads = query_ref.shape[1] // HD
    shard = jnp.concatenate([ref[...] for ref in shard_refs], axis=0)
    key_rows, value_rows = shard[:, :HD], with_ones(shard[:, HD:])
    extra = None
    if by_swap is not None:
        position, core = place()
        extra = penalty((position != 1) | (core == int(by_swap)))

    def start(rows):
        return scores_of(stacked(query_ref, rows, heads), key_rows)

    def finish(index, rows, scores):
        best = stacked(best_ref, rows, heads)
        if extra is None:
            points = widen(best, scores.shape[1])
        else:
            held = shard_refs[-1].shape[0]
            points = [best] * ((scores.shape[1] - held) // HD) + [best + extra] * (held // HD)
            points = jnp.concatenate(points, axis=1)
        weights = jnp.exp2(scores - points).astype(jnp.bfloat16)
        result = jnp.dot(weights, value_rows, preferred_element_type=jnp.float32)
        unstack(total_out, rows, heads, stacked(total_ref, rows, heads) + result[:, HD:])
        unstack(sum_out, rows, heads, stacked(sum_ref, rows, heads) + result[:, :HD])

    staged(row_blocks(query_ref.shape[0], 80), start, finish)


def last_stage(routed, *refs):
    query_ref, best_ref, old_total_ref, old_sum_ref, total_ref, sum_ref = refs[:6]
    earlier_refs, refs = refs[6:-6], refs[-6:]
    direct_ref, swapped_ref, out_hbm, out_ref, trusted_ref, out_sems = refs
    heads = query_ref.shape[1] // HD
    blocks = row_blocks(query_ref.shape[0], 80)
    position, core = place()
    takes_both = (position == 1) & routed
    is_direct = core == 0

    def out_copy(index, rows):
        return pltpu.make_async_copy(out_ref.at[rows], out_hbm.at[rows], out_sems.at[index])

    def write(rows, total, weighted):
        inverse = pl.reciprocal(total, approx=True)
        inverse = inverse * (2.0 - total * inverse)
        unstack(out_ref, rows, heads, (weighted * inverse).astype(jnp.bfloat16))

    def process(shard):
        trusted = [jnp.full((8, HD), True)]
        key_rows, value_rows = shard[:, :HD], with_ones(shard[:, HD:])

        def start(rows):
            return scores_of(stacked(query_ref, rows, heads), key_rows)

        def finish(index, rows, scores):
            best = stacked(best_ref, rows, heads)
            weights = jnp.exp2(scores - widen(best, scores.shape[1])).astype(jnp.bfloat16)
            result = jnp.dot(weights, value_rows, preferred_element_type=jnp.float32)
            total = stacked(total_ref, rows, heads) + result[:, HD:]
            weighted = stacked(sum_ref, rows, heads) + result[:, :HD]
            good = (total < total_limit).reshape(total.shape[0] // 8, 8, HD)
            trusted[0] = trusted[0] & jnp.all(good, axis=0)
            write(rows, total, weighted)
            out_copy(index, rows).start()

        staged(blocks, start, finish)
        trusted_ref[0] = jnp.all(trusted[0]).astype(jnp.int32)
        for index, rows in enumerate(blocks):
            out_copy(index, rows).wait()

    @pl.when(jnp.logical_not(takes_both))
    def one_shard():
        process(jnp.where(is_direct, direct_ref[...], swapped_ref[...]))

    @pl.when(takes_both)
    def two_shards():
        process(jnp.concatenate([direct_ref[...], swapped_ref[...]], axis=0))

    @pl.when(trusted_ref[0] == 0)
    def exact_maximum():
        size = query_ref.shape[0] // len(blocks)
        counted = [(ref, 0.0) for ref in earlier_refs]
        if routed:
            counted[-2:] = [
                (ref, penalty((position != 1) | (core == by_swap)))
                for by_swap, ref in enumerate(earlier_refs[-2:])
            ]
        counted += [
            (direct_ref, penalty(takes_both | is_direct)),
            (swapped_ref, penalty(takes_both | jnp.logical_not(is_direct))),
        ]

        def visit(index, unused):
            rows = pl.ds(pl.multiple_of(index * size, size), size)
            queries = stacked(query_ref, rows, heads)
            best = stacked(best_ref, rows, heads)
            weighted = stacked(old_sum_ref, rows, heads)
            total = stacked(old_total_ref, rows, heads)
            for shard_ref, extra in counted:
                key_rows, value_rows = shard_ref[:, :HD], with_ones(shard_ref[:, HD:])
                scores = scores_of(queries, key_rows) - extra
                new_best = jnp.maximum(best, jnp.max(scores, axis=1, keepdims=True))
                factor = jnp.exp2(best - new_best)
                weights = jnp.exp2(scores - widen(new_best, scores.shape[1]))
                result = jnp.dot(
                    weights.astype(jnp.bfloat16), value_rows, preferred_element_type=jnp.float32
                )
                weighted = weighted * factor + result[:, :HD]
                total = total * factor + result[:, HD:]
                best = new_best
            write(rows, total, weighted)
            copy = out_copy(index, rows)
            copy.start()
            copy.wait()
            return unused

        lax.fori_loop(0, len(blocks), visit, 0)


def shards(queries, suffix_kv, prompt_kv, lengths):
    slots, width = queries.shape
    heads = width // HD
    loop_size = lax.axis_size("loop")
    own = prompt_kv[:, 0, :]
    suffix = suffix_kv[:, 0, :]
    shard_rows = own.shape[0]

    in_hbm = pl.BlockSpec(memory_space=pltpu.HBM)
    in_vmem = pl.BlockSpec(memory_space=pltpu.VMEM)
    state = jax.ShapeDtypeStruct((slots, width), jnp.float32)

    cost = pl.CostEstimate(flops=1, bytes_accessed=1, transcendentals=0)

    routed = loop_size >= FOUR and loop_size & (loop_size - 1) == 0

    def send(shard, route):
        hops = []
        for i in range(loop_size):
            for core in range(2):
                to, to_core = route(i, core)
                hops.append((2 * i + core, 2 * to + to_core))
        return lax.ppermute(shard, ("loop", "pair"), hops)

    def first_route(i, core):
        base = i - i % FOUR
        to, to_core = [((1, 0), (3, 1)), ((1, 1), (2, 1)), ((0, 0), (3, 0)), ((2, 0), (0, 1))][
            i % FOUR
        ][core]
        return base + to, to_core

    def second_route(i, core):
        base = i - i % FOUR
        to, to_core = [((0, 1), (2, 0)), ((0, 0), (3, 0)), ((2, 1), (1, 0)), ((3, 1), (1, 1))][
            i % FOUR
        ][core]
        return base + to, to_core

    hbm = [pltpu.with_memory_space_constraint(x, pltpu.HBM) for x in (lengths, queries, suffix, own)]
    buffers = [
        jax.ShapeDtypeStruct(queries.shape, queries.dtype),
        jax.ShapeDtypeStruct(suffix.shape, suffix.dtype),
        jax.ShapeDtypeStruct(own.shape, own.dtype),
        jax.ShapeDtypeStruct((slots, HD), jnp.int32),
    ]
    load_scratch = [
        pltpu.SMEM(lengths.shape, lengths.dtype),
        pltpu.SemaphoreType.DMA((2 + 2 * len(load_blocks(slots)),)),
    ]
    loaded = pl.pallas_call(
        prelude_stage,
        name="prelude_stage",
        out_shape=buffers,
        in_specs=[in_hbm] * 4,
        out_specs=[in_vmem] * 4,
        scratch_shapes=load_scratch,
        compiler_params=pltpu.CompilerParams(vmem_limit_bytes=8 * 2**20),
        cost_estimate=cost,
    )(*hbm)
    own, loaded = lax.optimization_barrier((own, loaded))
    if routed:
        early = [
            send(own, lambda i, core, step=step: (i ^ (step + core), 1 - core))
            for step in range(FOUR, loop_size, 2)
        ]
        early.append(send(own, first_route))
        final = send(own, second_route)
    else:
        early = [
            send(own, lambda i, core, step=step: ((i + step) % loop_size, core))
            for step in range(1, loop_size)
        ]
        final = early.pop()
    best, total, weighted, queries, *unused = pl.pallas_call(
        local_stage,
        name="local_stage",
        out_shape=[state] * 3 + buffers,
        in_specs=[in_hbm] * 4 + [in_vmem] * 4,
        out_specs=[in_vmem] * 7,
        scratch_shapes=load_scratch,
        input_output_aliases={4 + i: 3 + i for i in range(4)},
        compiler_params=pltpu.CompilerParams(vmem_limit_bytes=24 * 2**20),
        cost_estimate=cost,
    )(*hbm, *loaded)

    def add_shards(total, weighted, shards_now, by_swap):
        if not shards_now:
            return total, weighted
        return pl.pallas_call(
            functools.partial(add_stage, by_swap if routed else None),
            name="add_stage",
            out_shape=[state] * 2,
            in_specs=[in_vmem] * (4 + len(shards_now)),
            out_specs=[in_vmem] * 2,
            compiler_params=pltpu.CompilerParams(vmem_limit_bytes=24 * 2**20),
            cost_estimate=cost,
        )(queries, best, total, weighted, *shards_now)

    def swapped(shard):
        return send(shard, lambda i, core: (i, 1 - core))

    early, best = lax.optimization_barrier((early, best))
    early_swapped = [swapped(shard) for shard in early] if routed else []
    new_total, new_weighted = add_shards(total, weighted, early, False)
    final, new_total = lax.optimization_barrier((final, new_total))
    final_swapped = swapped(final) if routed else final
    new_total, new_weighted = add_shards(new_total, new_weighted, early_swapped, True)
    last_inputs = (queries, best, total, weighted, new_total, new_weighted)
    last_inputs += (*early[:-1], *early_swapped[:-1], *early[-1:], *early_swapped[-1:])
    last_inputs += (final, final_swapped)
    return pl.pallas_call(
        functools.partial(last_stage, routed),
        name="last_stage",
        out_shape=jax.ShapeDtypeStruct((slots, width), jnp.bfloat16),
        in_specs=[in_vmem] * len(last_inputs),
        out_specs=in_hbm,
        scratch_shapes=[
            pltpu.VMEM((slots, width), jnp.bfloat16),
            pltpu.SMEM((1,), jnp.int32),
            pltpu.SemaphoreType.DMA((len(row_blocks(slots, 80)),)),
        ],
        compiler_params=pltpu.CompilerParams(vmem_limit_bytes=32 * 2**20),
        cost_estimate=cost,
    )(*last_inputs)


def solution(mesh):
    placed = (
        P(("groups", "loop"), ("heads", "pair")),
        P(("groups", "loop"), "heads", None),
        P(("groups", "loop"), "heads", None),
        P("groups"),
    )
    return jax.shard_map(
        shards,
        mesh=mesh,
        in_specs=placed,
        out_specs=P(("groups", "loop"), ("heads", "pair")),
        check_vma=False,
    )
```

```python
import functools
import math

import jax
import jax.numpy as jnp
from jax import lax
from jax.experimental import pallas as pl
from jax.experimental.pallas import tpu as pltpu
from jax.sharding import PartitionSpec as P

HD = 128
AG_DEV = 2
MAXLEN = 320
BLK = 128
FOUR = 4

masked_score = -1e30
empty_best = 1e30
total_limit = 2.0**100
score_scale = math.log2(math.e) / math.sqrt(HD)


def scores_of(query_rows, key_rows):
    return (
        lax.dot_general(
            query_rows, key_rows, (((1,), (1,)), ((), ())), preferred_element_type=jnp.float32
        )
        * score_scale
    )


def with_ones(value_rows):
    return jnp.concatenate([value_rows, jnp.ones_like(value_rows)], axis=1)


def stacked(ref, rows, head_count):
    return jnp.concatenate([ref[rows, h * HD : (h + 1) * HD] for h in range(head_count)], axis=0)


def unstack(ref, rows, head_count, value):
    count = value.shape[0] // head_count
    for h in range(head_count):
        ref[rows, h * HD : (h + 1) * HD] = value[h * count : (h + 1) * count]


def widen(row_value, width):
    return jnp.concatenate([row_value] * (width // HD), axis=1)


def place():
    return lax.rem(lax.axis_index("loop"), 2) == 1, lax.axis_index("pair")


def load_blocks(count):
    return [pl.ds(first, BLK) for first in range(0, count, BLK)]


def load(
    lengths_hbm,
    query_hbm,
    suffix_hbm,
    own_hbm,
    query_ref,
    suffix_ref,
    own_ref,
    first_ref,
    lengths_ref,
    sems,
):
    pairs = [(lengths_hbm, lengths_ref), (own_hbm, own_ref)]
    for source, target in ((query_hbm, query_ref), (suffix_hbm, suffix_ref)):
        for rows in load_blocks(target.shape[0]):
            pairs.append((source.at[rows], target.at[rows]))
    copies = [
        pltpu.make_async_copy(source, target, sems.at[i])
        for i, (source, target) in enumerate(pairs)
    ]
    for copy in copies:
        copy.start()
    copies[0].wait()
    slots = query_ref.shape[0]
    position = lax.axis_index("loop")
    row_at = lax.broadcasted_iota(jnp.int32, first_ref.shape, 0)
    first = jnp.zeros_like(row_at)
    agent_end = 0
    for agent in range(AG_DEV):
        agent_end = agent_end + lengths_ref[position * AG_DEV + agent]
        first = jnp.where(row_at >= agent_end, agent_end if agent + 1 < AG_DEV else slots, first)
    first_ref[...] = first
    for copy in copies[1:]:
        copy.wait()


def prelude_stage(*refs):
    @pl.when(is_first_chip())
    def ahead():
        load(*refs)


def local_stage(*refs):
    sources, (best_ref, total_ref, sum_ref), loaded, scratch = (
        refs[:4],
        refs[8:11],
        refs[11:15],
        refs[15:],
    )
    query_ref, suffix_ref, own_ref, first_ref = loaded

    @pl.when(jnp.logical_not(is_first_chip()))
    def now():
        load(*sources, *loaded, *scratch)

    slots = query_ref.shape[0]
    heads = query_ref.shape[1] // HD
    own_keys = own_ref[:, :HD]
    own_values = with_ones(own_ref[:, HD:])
    window = BLK * ((MAXLEN + BLK - 2) // BLK) + BLK
    for block in range(slots // BLK):
        stop = (block + 1) * BLK
        start = max(0, stop - window)
        rows = slice(block * BLK, stop)
        row_at = block * BLK + lax.broadcasted_iota(jnp.int32, (BLK, stop - start), 0)
        key_at = start + lax.broadcasted_iota(jnp.int32, (BLK, stop - start), 1)
        first = first_ref[rows]
        allowed = (key_at <= row_at) & (key_at >= widen(first, stop - start))
        queries = stacked(query_ref, rows, heads)
        own_scores = scores_of(queries, own_keys)
        suffix_scores = jnp.where(
            jnp.concatenate([allowed] * heads, axis=0),
            scores_of(queries, suffix_ref[start:stop, :HD]),
            masked_score,
        )
        best = jnp.maximum(
            jnp.max(own_scores, axis=1, keepdims=True),
            jnp.max(suffix_scores, axis=1, keepdims=True),
        )
        own_weights = jnp.exp2(own_scores - best).astype(jnp.bfloat16)
        suffix_weights = jnp.exp2(suffix_scores - best).astype(jnp.bfloat16)
        result = jnp.dot(own_weights, own_values, preferred_element_type=jnp.float32)
        result = result + jnp.dot(
            suffix_weights,
            with_ones(suffix_ref[start:stop, HD:]),
            preferred_element_type=jnp.float32,
        )
        live = jnp.concatenate([first < slots] * heads, axis=0)
        unstack(best_ref, rows, heads, jnp.where(live, best, empty_best))
        unstack(sum_ref, rows, heads, jnp.where(live, result[:, :HD], 0.0))
        unstack(total_ref, rows, heads, jnp.where(live, result[:, HD:], 1.0))


def staged(blocks, start, finish):
    coming = start(blocks[0])
    for index, rows in enumerate(blocks):
        now = coming
        if index + 1 < len(blocks):
            coming = start(blocks[index + 1])
        finish(index, rows, now)


def row_blocks(count, largest):
    step = next(size for size in (largest, 128, 16, count) if count % size == 0)
    return [slice(first, first + step) for first in range(0, count, step)]


def is_first_chip():
    return lax.axis_index("groups") + lax.axis_index("loop") + lax.axis_index("heads") == 0


def penalty(is_there):
    return jnp.where(is_there, 0.0, empty_best)


def add_stage(by_swap, *refs):
    query_ref, best_ref, total_ref, sum_ref = refs[:4]
    shard_refs = refs[4:-2]
    total_out, sum_out = refs[-2:]
    heads = query_ref.shape[1] // HD
    shard = jnp.concatenate([ref[...] for ref in shard_refs], axis=0)
    key_rows, value_rows = shard[:, :HD], with_ones(shard[:, HD:])
    extra = None
    if by_swap is not None:
        is_odd, core = place()
        extra = penalty(jnp.logical_not(is_odd) | (core == int(by_swap)))

    def start(rows):
        return scores_of(stacked(query_ref, rows, heads), key_rows)

    def finish(index, rows, scores):
        best = stacked(best_ref, rows, heads)
        if extra is None:
            points = widen(best, scores.shape[1])
        else:
            held = shard_refs[-1].shape[0]
            points = [best] * ((scores.shape[1] - held) // HD) + [best + extra] * (held // HD)
            points = jnp.concatenate(points, axis=1)
        weights = jnp.exp2(scores - points).astype(jnp.bfloat16)
        result = jnp.dot(weights, value_rows, preferred_element_type=jnp.float32)
        unstack(total_out, rows, heads, stacked(total_ref, rows, heads) + result[:, HD:])
        unstack(sum_out, rows, heads, stacked(sum_ref, rows, heads) + result[:, :HD])

    staged(row_blocks(query_ref.shape[0], 80), start, finish)


def last_stage(routed, *refs):
    query_ref, best_ref, old_total_ref, old_sum_ref, total_ref, sum_ref = refs[:6]
    earlier_refs, refs = refs[6:-6], refs[-6:]
    direct_ref, swapped_ref, out_hbm, out_ref, trusted_ref, out_sems = refs
    heads = query_ref.shape[1] // HD
    blocks = row_blocks(query_ref.shape[0], 80)
    is_odd, core = place()
    takes_both = is_odd & routed
    is_direct = core == 0

    def out_copy(index, rows):
        return pltpu.make_async_copy(out_ref.at[rows], out_hbm.at[rows], out_sems.at[index])

    def write(rows, total, weighted):
        inverse = pl.reciprocal(total, approx=True)
        inverse = inverse * (2.0 - total * inverse)
        unstack(out_ref, rows, heads, (weighted * inverse).astype(jnp.bfloat16))

    def process(shard):
        trusted = [jnp.full((8, HD), True)]
        key_rows, value_rows = shard[:, :HD], with_ones(shard[:, HD:])

        def start(rows):
            return scores_of(stacked(query_ref, rows, heads), key_rows)

        def finish(index, rows, scores):
            best = stacked(best_ref, rows, heads)
            weights = jnp.exp2(scores - widen(best, scores.shape[1])).astype(jnp.bfloat16)
            result = jnp.dot(weights, value_rows, preferred_element_type=jnp.float32)
            total = stacked(total_ref, rows, heads) + result[:, HD:]
            weighted = stacked(sum_ref, rows, heads) + result[:, :HD]
            good = (total < total_limit).reshape(total.shape[0] // 8, 8, HD)
            trusted[0] = trusted[0] & jnp.all(good, axis=0)
            write(rows, total, weighted)
            out_copy(index, rows).start()

        staged(blocks, start, finish)
        trusted_ref[0] = jnp.all(trusted[0]).astype(jnp.int32)
        for index, rows in enumerate(blocks):
            out_copy(index, rows).wait()

    @pl.when(jnp.logical_not(takes_both))
    def one_shard():
        process(jnp.where(is_direct, direct_ref[...], swapped_ref[...]))

    @pl.when(takes_both)
    def two_shards():
        process(jnp.concatenate([direct_ref[...], swapped_ref[...]], axis=0))

    @pl.when(trusted_ref[0] == 0)
    def exact_maximum():
        size = query_ref.shape[0] // len(blocks)
        counted = [(ref, 0.0) for ref in earlier_refs]
        if routed:
            counted[-2:] = [
                (ref, penalty(jnp.logical_not(is_odd) | (core == by_swap)))
                for by_swap, ref in enumerate(earlier_refs[-2:])
            ]
        counted += [
            (direct_ref, penalty(takes_both | is_direct)),
            (swapped_ref, penalty(takes_both | jnp.logical_not(is_direct))),
        ]

        def visit(index, unused):
            rows = pl.ds(pl.multiple_of(index * size, size), size)
            queries = stacked(query_ref, rows, heads)
            best = stacked(best_ref, rows, heads)
            weighted = stacked(old_sum_ref, rows, heads)
            total = stacked(old_total_ref, rows, heads)
            for shard_ref, extra in counted:
                key_rows, value_rows = shard_ref[:, :HD], with_ones(shard_ref[:, HD:])
                scores = scores_of(queries, key_rows) - extra
                new_best = jnp.maximum(best, jnp.max(scores, axis=1, keepdims=True))
                factor = jnp.exp2(best - new_best)
                weights = jnp.exp2(scores - widen(new_best, scores.shape[1]))
                result = jnp.dot(
                    weights.astype(jnp.bfloat16), value_rows, preferred_element_type=jnp.float32
                )
                weighted = weighted * factor + result[:, :HD]
                total = total * factor + result[:, HD:]
                best = new_best
            write(rows, total, weighted)
            copy = out_copy(index, rows)
            copy.start()
            copy.wait()
            return unused

        lax.fori_loop(0, len(blocks), visit, 0)


def shards(queries, suffix_kv, prompt_kv, lengths):
    slots, width = queries.shape
    heads = width // HD
    loop_size = lax.axis_size("loop")
    own = prompt_kv[:, 0, :]
    suffix = suffix_kv[:, 0, :]
    shard_rows = own.shape[0]

    in_hbm = pl.BlockSpec(memory_space=pltpu.HBM)
    in_vmem = pl.BlockSpec(memory_space=pltpu.VMEM)
    state = jax.ShapeDtypeStruct((slots, width), jnp.float32)

    cost = pl.CostEstimate(flops=1, bytes_accessed=1, transcendentals=0)

    routed = loop_size >= FOUR and loop_size & (loop_size - 1) == 0

    def send(shard, route):
        hops = []
        for i in range(loop_size):
            for core in range(2):
                to, to_core = route(i, core)
                hops.append((2 * i + core, 2 * to + to_core))
        return lax.ppermute(shard, ("loop", "pair"), hops)

    def first_route(i, core):
        if core == 1:
            return (i ^ 2) & ~1, i & 1
        return (i, 1) if i & 1 else (i + 1, 0)

    def second_route(i, core):
        if core == 1:
            return (i ^ 2) | 1, 1 - i & 1
        return (i - 1, 0) if i & 1 else (i, 1)

    hbm = [pltpu.with_memory_space_constraint(x, pltpu.HBM) for x in (lengths, queries, suffix, own)]
    buffers = [
        jax.ShapeDtypeStruct(queries.shape, queries.dtype),
        jax.ShapeDtypeStruct(suffix.shape, suffix.dtype),
        jax.ShapeDtypeStruct(own.shape, own.dtype),
        jax.ShapeDtypeStruct((slots, HD), jnp.int32),
    ]
    load_scratch = [
        pltpu.SMEM(lengths.shape, lengths.dtype),
        pltpu.SemaphoreType.DMA((2 + 2 * len(load_blocks(slots)),)),
    ]
    loaded = pl.pallas_call(
        prelude_stage,
        name="prelude_stage",
        out_shape=buffers,
        in_specs=[in_hbm] * 4,
        out_specs=[in_vmem] * 4,
        scratch_shapes=load_scratch,
        compiler_params=pltpu.CompilerParams(vmem_limit_bytes=8 * 2**20),
        cost_estimate=cost,
    )(*hbm)
    own, loaded = lax.optimization_barrier((own, loaded))
    if routed:
        early = [
            send(own, lambda i, core, step=step: (i ^ (step + core), 1 - core))
            for step in range(FOUR, loop_size, 2)
        ]
        early.append(send(own, first_route))
        final = send(own, second_route)
    else:
        early = [
            send(own, lambda i, core, step=step: ((i + step) % loop_size, core))
            for step in range(1, loop_size)
        ]
        final = early.pop()
    best, total, weighted, queries, *unused = pl.pallas_call(
        local_stage,
        name="local_stage",
        out_shape=[state] * 3 + buffers,
        in_specs=[in_hbm] * 4 + [in_vmem] * 4,
        out_specs=[in_vmem] * 7,
        scratch_shapes=load_scratch,
        input_output_aliases={4 + i: 3 + i for i in range(4)},
        compiler_params=pltpu.CompilerParams(vmem_limit_bytes=24 * 2**20),
        cost_estimate=cost,
    )(*hbm, *loaded)

    def add_shards(total, weighted, shards_now, by_swap):
        if not shards_now:
            return total, weighted
        return pl.pallas_call(
            functools.partial(add_stage, by_swap if routed else None),
            name="add_stage",
            out_shape=[state] * 2,
            in_specs=[in_vmem] * (4 + len(shards_now)),
            out_specs=[in_vmem] * 2,
            compiler_params=pltpu.CompilerParams(vmem_limit_bytes=24 * 2**20),
            cost_estimate=cost,
        )(queries, best, total, weighted, *shards_now)

    def swapped(shard):
        return send(shard, lambda i, core: (i, 1 - core))

    early, best = lax.optimization_barrier((early, best))
    early_swapped = [swapped(shard) for shard in early] if routed else []
    new_total, new_weighted = add_shards(total, weighted, early, False)
    final, new_total = lax.optimization_barrier((final, new_total))
    final_swapped = swapped(final) if routed else final
    new_total, new_weighted = add_shards(new_total, new_weighted, early_swapped, True)
    last_inputs = (queries, best, total, weighted, new_total, new_weighted)
    last_inputs += (*early[:-1], *early_swapped[:-1], *early[-1:], *early_swapped[-1:])
    last_inputs += (final, final_swapped)
    return pl.pallas_call(
        functools.partial(last_stage, routed),
        name="last_stage",
        out_shape=jax.ShapeDtypeStruct((slots, width), jnp.bfloat16),
        in_specs=[in_vmem] * len(last_inputs),
        out_specs=in_hbm,
        scratch_shapes=[
            pltpu.VMEM((slots, width), jnp.bfloat16),
            pltpu.SMEM((1,), jnp.int32),
            pltpu.SemaphoreType.DMA((len(row_blocks(slots, 80)),)),
        ],
        compiler_params=pltpu.CompilerParams(vmem_limit_bytes=32 * 2**20),
        cost_estimate=cost,
    )(*last_inputs)


def solution(mesh):
    placed = (
        P(("groups", "loop"), ("heads", "pair")),
        P(("groups", "loop"), "heads", None),
        P(("groups", "loop"), "heads", None),
        P("groups"),
    )
    return jax.shard_map(
        shards,
        mesh=mesh,
        in_specs=placed,
        out_specs=P(("groups", "loop"), ("heads", "pair")),
        check_vma=False,
    )
```

```python
import functools
import math

import jax
import jax.numpy as jnp
from jax import lax
from jax.experimental import pallas as pl
from jax.experimental.pallas import tpu as pltpu
from jax.sharding import PartitionSpec as P

HD = 128
AG_DEV = 2
MAXLEN = 320
BLK = 128
FOUR = 4

masked_score = -1e30
empty_best = 1e30
total_limit = 2.0**100
score_scale = math.log2(math.e) / math.sqrt(HD)


def scores_of(query_rows, key_rows):
    return (
        lax.dot_general(
            query_rows, key_rows, (((1,), (1,)), ((), ())), preferred_element_type=jnp.float32
        )
        * score_scale
    )


def with_ones(value_rows):
    return jnp.concatenate([value_rows, jnp.ones_like(value_rows)], axis=1)


def stacked(ref, rows, head_count):
    return jnp.concatenate([ref[rows, h * HD : (h + 1) * HD] for h in range(head_count)], axis=0)


def unstack(ref, rows, head_count, value):
    count = value.shape[0] // head_count
    for h in range(head_count):
        ref[rows, h * HD : (h + 1) * HD] = value[h * count : (h + 1) * count]


def widen(row_value, width):
    return jnp.concatenate([row_value] * (width // HD), axis=1)


def place():
    return lax.rem(lax.axis_index("loop"), 2) == 1, lax.axis_index("pair")


def load_blocks(count):
    return [pl.ds(first, BLK) for first in range(0, count, BLK)]


def load(
    lengths_hbm,
    query_hbm,
    suffix_hbm,
    own_hbm,
    query_ref,
    suffix_ref,
    own_ref,
    first_ref,
    lengths_ref,
    sems,
):
    pairs = [(lengths_hbm, lengths_ref), (own_hbm, own_ref)]
    for source, target in ((query_hbm, query_ref), (suffix_hbm, suffix_ref)):
        for rows in load_blocks(target.shape[0]):
            pairs.append((source.at[rows], target.at[rows]))
    copies = [
        pltpu.make_async_copy(source, target, sems.at[i])
        for i, (source, target) in enumerate(pairs)
    ]
    for copy in copies:
        copy.start()
    copies[0].wait()
    slots = query_ref.shape[0]
    position = lax.axis_index("loop")
    row_at = lax.broadcasted_iota(jnp.int32, first_ref.shape, 0)
    first = jnp.zeros_like(row_at)
    agent_end = 0
    for agent in range(AG_DEV):
        agent_end = agent_end + lengths_ref[position * AG_DEV + agent]
        first = jnp.where(row_at >= agent_end, agent_end if agent + 1 < AG_DEV else slots, first)
    first_ref[...] = first
    for copy in copies[1:]:
        copy.wait()


def loads_first():
    axes = ("groups", "loop", "heads")
    return sum(lax.axis_index(axis) for axis in axes) == 0


def loads_last():
    return lax.rem(lax.axis_index("loop"), FOUR) == FOUR - 1


def load_ahead_stage(*refs):
    @pl.when(loads_first())
    def load_now():
        load(*refs)


def load_between_stage(*refs):
    @pl.when(jnp.logical_not(loads_first() | loads_last()))
    def load_now():
        load(*refs[:4], *refs[8:])


def local_stage(*refs):
    sources, (best_ref, total_ref, sum_ref), loaded, scratch = (
        refs[:4],
        refs[8:11],
        refs[11:15],
        refs[15:],
    )
    query_ref, suffix_ref, own_ref, first_ref = loaded

    @pl.when(loads_last() & jnp.logical_not(loads_first()))
    def load_now():
        load(*sources, *loaded, *scratch)

    slots = query_ref.shape[0]
    heads = query_ref.shape[1] // HD
    own_keys = own_ref[:, :HD]
    own_values = with_ones(own_ref[:, HD:])
    window = BLK * ((MAXLEN + BLK - 2) // BLK) + BLK
    for block in range(slots // BLK):
        stop = (block + 1) * BLK
        start = max(0, stop - window)
        rows = slice(block * BLK, stop)
        row_at = block * BLK + lax.broadcasted_iota(jnp.int32, (BLK, stop - start), 0)
        key_at = start + lax.broadcasted_iota(jnp.int32, (BLK, stop - start), 1)
        first = first_ref[rows]
        allowed = (key_at <= row_at) & (key_at >= widen(first, stop - start))
        queries = stacked(query_ref, rows, heads)
        own_scores = scores_of(queries, own_keys)
        suffix_scores = jnp.where(
            jnp.concatenate([allowed] * heads, axis=0),
            scores_of(queries, suffix_ref[start:stop, :HD]),
            masked_score,
        )
        best = jnp.maximum(
            jnp.max(own_scores, axis=1, keepdims=True),
            jnp.max(suffix_scores, axis=1, keepdims=True),
        )
        own_weights = jnp.exp2(own_scores - best).astype(jnp.bfloat16)
        suffix_weights = jnp.exp2(suffix_scores - best).astype(jnp.bfloat16)
        result = jnp.dot(own_weights, own_values, preferred_element_type=jnp.float32)
        result = result + jnp.dot(
            suffix_weights,
            with_ones(suffix_ref[start:stop, HD:]),
            preferred_element_type=jnp.float32,
        )
        live = jnp.concatenate([first < slots] * heads, axis=0)
        unstack(best_ref, rows, heads, jnp.where(live, best, empty_best))
        unstack(sum_ref, rows, heads, jnp.where(live, result[:, :HD], 0.0))
        unstack(total_ref, rows, heads, jnp.where(live, result[:, HD:], 1.0))


def staged(blocks, start, finish):
    coming = start(blocks[0])
    for index, rows in enumerate(blocks):
        now = coming
        if index + 1 < len(blocks):
            coming = start(blocks[index + 1])
        finish(index, rows, now)


def row_blocks(count, largest):
    step = next(size for size in (largest, 128, 16, count) if count % size == 0)
    return [slice(first, first + step) for first in range(0, count, step)]


def penalty(is_there):
    return jnp.where(is_there, 0.0, empty_best)


def add_stage(by_swap, *refs):
    query_ref, best_ref, total_ref, sum_ref = refs[:4]
    shard_refs = refs[4:-2]
    total_out, sum_out = refs[-2:]
    heads = query_ref.shape[1] // HD
    shard = jnp.concatenate([ref[...] for ref in shard_refs], axis=0)
    key_rows, value_rows = shard[:, :HD], with_ones(shard[:, HD:])
    extra = None
    if by_swap is not None:
        is_odd, core = place()
        extra = penalty(jnp.logical_not(is_odd) | (core == int(by_swap)))

    def start(rows):
        return scores_of(stacked(query_ref, rows, heads), key_rows)

    def finish(index, rows, scores):
        best = stacked(best_ref, rows, heads)
        if extra is None:
            points = widen(best, scores.shape[1])
        else:
            held = shard_refs[-1].shape[0]
            points = [best] * ((scores.shape[1] - held) // HD) + [best + extra] * (held // HD)
            points = jnp.concatenate(points, axis=1)
        weights = jnp.exp2(scores - points).astype(jnp.bfloat16)
        result = jnp.dot(weights, value_rows, preferred_element_type=jnp.float32)
        unstack(total_out, rows, heads, stacked(total_ref, rows, heads) + result[:, HD:])
        unstack(sum_out, rows, heads, stacked(sum_ref, rows, heads) + result[:, :HD])

    staged(row_blocks(query_ref.shape[0], 80), start, finish)


def last_stage(routed, *refs):
    query_ref, best_ref, old_total_ref, old_sum_ref, total_ref, sum_ref = refs[:6]
    earlier_refs, refs = refs[6:-6], refs[-6:]
    direct_ref, swapped_ref, out_hbm, out_ref, trusted_ref, out_sems = refs
    heads = query_ref.shape[1] // HD
    blocks = row_blocks(query_ref.shape[0], 80)
    is_odd, core = place()
    takes_both = is_odd & routed
    is_direct = core == 0

    def out_copy(index, rows):
        return pltpu.make_async_copy(out_ref.at[rows], out_hbm.at[rows], out_sems.at[index])

    def write(rows, total, weighted):
        inverse = pl.reciprocal(total, approx=True)
        inverse = inverse * (2.0 - total * inverse)
        unstack(out_ref, rows, heads, (weighted * inverse).astype(jnp.bfloat16))

    def process(shard):
        trusted = [jnp.full((8, HD), True)]
        key_rows, value_rows = shard[:, :HD], with_ones(shard[:, HD:])

        def start(rows):
            return scores_of(stacked(query_ref, rows, heads), key_rows)

        def finish(index, rows, scores):
            best = stacked(best_ref, rows, heads)
            weights = jnp.exp2(scores - widen(best, scores.shape[1])).astype(jnp.bfloat16)
            result = jnp.dot(weights, value_rows, preferred_element_type=jnp.float32)
            total = stacked(total_ref, rows, heads) + result[:, HD:]
            weighted = stacked(sum_ref, rows, heads) + result[:, :HD]
            good = (total < total_limit).reshape(total.shape[0] // 8, 8, HD)
            trusted[0] = trusted[0] & jnp.all(good, axis=0)
            write(rows, total, weighted)
            out_copy(index, rows).start()

        staged(blocks, start, finish)
        trusted_ref[0] = jnp.all(trusted[0]).astype(jnp.int32)
        for index, rows in enumerate(blocks):
            out_copy(index, rows).wait()

    @pl.when(jnp.logical_not(takes_both))
    def one_shard():
        process(jnp.where(is_direct, direct_ref[...], swapped_ref[...]))

    @pl.when(takes_both)
    def two_shards():
        process(jnp.concatenate([direct_ref[...], swapped_ref[...]], axis=0))

    @pl.when(trusted_ref[0] == 0)
    def exact_maximum():
        size = query_ref.shape[0] // len(blocks)
        counted = [(ref, 0.0) for ref in earlier_refs]
        if routed:
            counted[-2:] = [
                (ref, penalty(jnp.logical_not(is_odd) | (core == by_swap)))
                for by_swap, ref in enumerate(earlier_refs[-2:])
            ]
        counted += [
            (direct_ref, penalty(takes_both | is_direct)),
            (swapped_ref, penalty(takes_both | jnp.logical_not(is_direct))),
        ]

        def visit(index, unused):
            rows = pl.ds(pl.multiple_of(index * size, size), size)
            queries = stacked(query_ref, rows, heads)
            best = stacked(best_ref, rows, heads)
            weighted = stacked(old_sum_ref, rows, heads)
            total = stacked(old_total_ref, rows, heads)
            for shard_ref, extra in counted:
                key_rows, value_rows = shard_ref[:, :HD], with_ones(shard_ref[:, HD:])
                scores = scores_of(queries, key_rows) - extra
                new_best = jnp.maximum(best, jnp.max(scores, axis=1, keepdims=True))
                factor = jnp.exp2(best - new_best)
                weights = jnp.exp2(scores - widen(new_best, scores.shape[1]))
                result = jnp.dot(
                    weights.astype(jnp.bfloat16), value_rows, preferred_element_type=jnp.float32
                )
                weighted = weighted * factor + result[:, :HD]
                total = total * factor + result[:, HD:]
                best = new_best
            write(rows, total, weighted)
            copy = out_copy(index, rows)
            copy.start()
            copy.wait()
            return unused

        lax.fori_loop(0, len(blocks), visit, 0)


def shards(queries, suffix_kv, prompt_kv, lengths):
    slots, width = queries.shape
    heads = width // HD
    loop_size = lax.axis_size("loop")
    own = prompt_kv[:, 0, :]
    suffix = suffix_kv[:, 0, :]
    shard_rows = own.shape[0]

    in_hbm = pl.BlockSpec(memory_space=pltpu.HBM)
    in_vmem = pl.BlockSpec(memory_space=pltpu.VMEM)
    state = jax.ShapeDtypeStruct((slots, width), jnp.float32)

    cost = pl.CostEstimate(flops=1, bytes_accessed=1, transcendentals=0)

    routed = loop_size >= FOUR and loop_size & (loop_size - 1) == 0

    def send(shard, route):
        hops = []
        for i in range(loop_size):
            for core in range(2):
                to, to_core = route(i, core)
                hops.append((2 * i + core, 2 * to + to_core))
        return lax.ppermute(shard, ("loop", "pair"), hops)

    def first_route(i, core):
        if core == 1:
            return (i ^ 2) & ~1, i & 1
        return (i, 1) if i & 1 else (i + 1, 0)

    def second_route(i, core):
        if core == 1:
            return (i ^ 2) | 1, 1 - i & 1
        return (i - 1, 0) if i & 1 else (i, 1)

    hbm = [pltpu.with_memory_space_constraint(x, pltpu.HBM) for x in (lengths, queries, suffix, own)]
    buffers = [
        jax.ShapeDtypeStruct(queries.shape, queries.dtype),
        jax.ShapeDtypeStruct(suffix.shape, suffix.dtype),
        jax.ShapeDtypeStruct(own.shape, own.dtype),
        jax.ShapeDtypeStruct((slots, HD), jnp.int32),
    ]
    load_scratch = [
        pltpu.SMEM(lengths.shape, lengths.dtype),
        pltpu.SemaphoreType.DMA((2 + 2 * len(load_blocks(slots)),)),
    ]
    loaded = pl.pallas_call(
        load_ahead_stage,
        name="load_ahead_stage",
        out_shape=buffers,
        in_specs=[in_hbm] * 4,
        out_specs=[in_vmem] * 4,
        scratch_shapes=load_scratch,
        compiler_params=pltpu.CompilerParams(vmem_limit_bytes=8 * 2**20),
        cost_estimate=cost,
    )(*hbm)
    own, loaded = lax.optimization_barrier((own, loaded))
    if routed:
        early = [
            send(own, lambda i, core, step=step: (i ^ (step + core), 1 - core))
            for step in range(FOUR, loop_size, 2)
        ]
        early.append(send(own, first_route))
    loaded = pl.pallas_call(
        load_between_stage,
        name="load_between_stage",
        out_shape=buffers,
        in_specs=[in_hbm] * 4 + [in_vmem] * 4,
        out_specs=[in_vmem] * 4,
        scratch_shapes=load_scratch,
        input_output_aliases={4 + i: i for i in range(4)},
        compiler_params=pltpu.CompilerParams(vmem_limit_bytes=8 * 2**20),
        cost_estimate=cost,
    )(*hbm, *loaded)
    own, loaded = lax.optimization_barrier((own, loaded))
    if routed:
        final = send(own, second_route)
    else:
        early = [
            send(own, lambda i, core, step=step: ((i + step) % loop_size, core))
            for step in range(1, loop_size)
        ]
        final = early.pop()
    best, total, weighted, queries, *unused = pl.pallas_call(
        local_stage,
        name="local_stage",
        out_shape=[state] * 3 + buffers,
        in_specs=[in_hbm] * 4 + [in_vmem] * 4,
        out_specs=[in_vmem] * 7,
        scratch_shapes=load_scratch,
        input_output_aliases={4 + i: 3 + i for i in range(4)},
        compiler_params=pltpu.CompilerParams(vmem_limit_bytes=24 * 2**20),
        cost_estimate=cost,
    )(*hbm, *loaded)

    def add_shards(total, weighted, shards_now, by_swap):
        if not shards_now:
            return total, weighted
        return pl.pallas_call(
            functools.partial(add_stage, by_swap if routed else None),
            name="add_stage",
            out_shape=[state] * 2,
            in_specs=[in_vmem] * (4 + len(shards_now)),
            out_specs=[in_vmem] * 2,
            compiler_params=pltpu.CompilerParams(vmem_limit_bytes=24 * 2**20),
            cost_estimate=cost,
        )(queries, best, total, weighted, *shards_now)

    def swapped(shard):
        return send(shard, lambda i, core: (i, 1 - core))

    early, best = lax.optimization_barrier((early, best))
    early_swapped = [swapped(shard) for shard in early] if routed else []
    new_total, new_weighted = add_shards(total, weighted, early, False)
    final, new_total = lax.optimization_barrier((final, new_total))
    final_swapped = swapped(final) if routed else final
    new_total, new_weighted = add_shards(new_total, new_weighted, early_swapped, True)
    last_inputs = (queries, best, total, weighted, new_total, new_weighted)
    last_inputs += (*early[:-1], *early_swapped[:-1], *early[-1:], *early_swapped[-1:])
    last_inputs += (final, final_swapped)
    return pl.pallas_call(
        functools.partial(last_stage, routed),
        name="last_stage",
        out_shape=jax.ShapeDtypeStruct((slots, width), jnp.bfloat16),
        in_specs=[in_vmem] * len(last_inputs),
        out_specs=in_hbm,
        scratch_shapes=[
            pltpu.VMEM((slots, width), jnp.bfloat16),
            pltpu.SMEM((1,), jnp.int32),
            pltpu.SemaphoreType.DMA((len(row_blocks(slots, 80)),)),
        ],
        compiler_params=pltpu.CompilerParams(vmem_limit_bytes=32 * 2**20),
        cost_estimate=cost,
    )(*last_inputs)


def solution(mesh):
    placed = (
        P(("groups", "loop"), ("heads", "pair")),
        P(("groups", "loop"), "heads", None),
        P(("groups", "loop"), "heads", None),
        P("groups"),
    )
    return jax.shard_map(
        shards,
        mesh=mesh,
        in_specs=placed,
        out_specs=P(("groups", "loop"), ("heads", "pair")),
        check_vma=False,
    )
```

```python
import functools
import math

import jax
import jax.numpy as jnp
from jax import lax
from jax.experimental import pallas as pl
from jax.experimental.pallas import tpu as pltpu
from jax.sharding import PartitionSpec as P

HD = 128
AG_DEV = 2
MAXLEN = 320
BLK = 128
FOUR = 4

masked_score = -1e30
empty_best = 1e30
total_limit = 2.0**100
score_scale = math.log2(math.e) / math.sqrt(HD)


def scores_of(query_rows, key_rows):
    return (
        lax.dot_general(
            query_rows, key_rows, (((1,), (1,)), ((), ())), preferred_element_type=jnp.float32
        )
        * score_scale
    )


def with_ones(value_rows):
    return jnp.concatenate([value_rows, jnp.ones_like(value_rows)], axis=1)


def stacked(ref, rows, head_count):
    return jnp.concatenate([ref[rows, h * HD : (h + 1) * HD] for h in range(head_count)], axis=0)


def unstack(ref, rows, head_count, value):
    count = value.shape[0] // head_count
    for h in range(head_count):
        ref[rows, h * HD : (h + 1) * HD] = value[h * count : (h + 1) * count]


def widen(row_value, width):
    return jnp.concatenate([row_value] * (width // HD), axis=1)


def place():
    return lax.rem(lax.axis_index("loop"), 2) == 1, lax.axis_index("pair")


def load_blocks(count):
    return [pl.ds(first, BLK) for first in range(0, count, BLK)]


def load(
    lengths_hbm,
    query_hbm,
    suffix_hbm,
    own_hbm,
    query_ref,
    suffix_ref,
    own_ref,
    first_ref,
    lengths_ref,
    sems,
):
    pairs = [(lengths_hbm, lengths_ref), (own_hbm, own_ref)]
    for source, target in ((query_hbm, query_ref), (suffix_hbm, suffix_ref)):
        for rows in load_blocks(target.shape[0]):
            pairs.append((source.at[rows], target.at[rows]))
    copies = [
        pltpu.make_async_copy(source, target, sems.at[i])
        for i, (source, target) in enumerate(pairs)
    ]
    for copy in copies:
        copy.start()
    copies[0].wait()
    slots = query_ref.shape[0]
    position = lax.axis_index("loop")
    row_at = lax.broadcasted_iota(jnp.int32, first_ref.shape, 0)
    first = jnp.zeros_like(row_at)
    agent_end = 0
    for agent in range(AG_DEV):
        agent_end = agent_end + lengths_ref[position * AG_DEV + agent]
        first = jnp.where(row_at >= agent_end, agent_end if agent + 1 < AG_DEV else slots, first)
    first_ref[...] = first
    for copy in copies[1:]:
        copy.wait()


def prelude_stage(*refs):
    @pl.when(is_first_chip())
    def ahead():
        load(*refs)


def local_stage(*refs):
    sources, (best_ref, total_ref, sum_ref), loaded, scratch = (
        refs[:4],
        refs[8:11],
        refs[11:15],
        refs[15:],
    )
    query_ref, suffix_ref, own_ref, first_ref = loaded

    @pl.when(jnp.logical_not(is_first_chip()))
    def now():
        load(*sources, *loaded, *scratch)

    slots = query_ref.shape[0]
    heads = query_ref.shape[1] // HD
    own_keys = own_ref[:, :HD]
    own_values = with_ones(own_ref[:, HD:])
    window = BLK * ((MAXLEN + BLK - 2) // BLK) + BLK
    for block in range(slots // BLK):
        stop = (block + 1) * BLK
        start = max(0, stop - window)
        rows = slice(block * BLK, stop)
        row_at = block * BLK + lax.broadcasted_iota(jnp.int32, (BLK, stop - start), 0)
        key_at = start + lax.broadcasted_iota(jnp.int32, (BLK, stop - start), 1)
        first = first_ref[rows]
        allowed = (key_at <= row_at) & (key_at >= widen(first, stop - start))
        queries = stacked(query_ref, rows, heads)
        own_scores = scores_of(queries, own_keys)
        suffix_scores = jnp.where(
            jnp.concatenate([allowed] * heads, axis=0),
            scores_of(queries, suffix_ref[start:stop, :HD]),
            masked_score,
        )
        best = jnp.maximum(
            jnp.max(own_scores, axis=1, keepdims=True),
            jnp.max(suffix_scores, axis=1, keepdims=True),
        )
        own_weights = jnp.exp2(own_scores - best).astype(jnp.bfloat16)
        suffix_weights = jnp.exp2(suffix_scores - best).astype(jnp.bfloat16)
        result = jnp.dot(own_weights, own_values, preferred_element_type=jnp.float32)
        result = result + jnp.dot(
            suffix_weights,
            with_ones(suffix_ref[start:stop, HD:]),
            preferred_element_type=jnp.float32,
        )
        live = jnp.concatenate([first < slots] * heads, axis=0)
        unstack(best_ref, rows, heads, jnp.where(live, best, empty_best))
        unstack(sum_ref, rows, heads, jnp.where(live, result[:, :HD], 0.0))
        unstack(total_ref, rows, heads, jnp.where(live, result[:, HD:], 1.0))


def staged(blocks, start, finish):
    coming = start(blocks[0])
    for index, rows in enumerate(blocks):
        now = coming
        if index + 1 < len(blocks):
            coming = start(blocks[index + 1])
        finish(index, rows, now)


def row_blocks(count, largest):
    step = next(size for size in (largest, 128, 16, count) if count % size == 0)
    return [slice(first, first + step) for first in range(0, count, step)]


def is_first_chip():
    return lax.axis_index("groups") + lax.axis_index("loop") + lax.axis_index("heads") == 0


def penalty(is_there):
    return jnp.where(is_there, 0.0, empty_best)


def add_stage(by_swap, *refs):
    query_ref, best_ref, total_ref, sum_ref = refs[:4]
    shard_refs = refs[4:-2]
    total_out, sum_out = refs[-2:]
    heads = query_ref.shape[1] // HD
    shard = jnp.concatenate([ref[...] for ref in shard_refs], axis=0)
    key_rows, value_rows = shard[:, :HD], with_ones(shard[:, HD:])
    extra = None
    if by_swap is not None:
        is_odd, core = place()
        extra = penalty(jnp.logical_not(is_odd) | (core == int(by_swap)))

    def start(rows):
        return scores_of(stacked(query_ref, rows, heads), key_rows)

    def finish(index, rows, scores):
        best = stacked(best_ref, rows, heads)
        if extra is None:
            points = widen(best, scores.shape[1])
        else:
            held = shard_refs[-1].shape[0]
            points = [best] * ((scores.shape[1] - held) // HD) + [best + extra] * (held // HD)
            points = jnp.concatenate(points, axis=1)
        weights = jnp.exp2(scores - points).astype(jnp.bfloat16)
        result = jnp.dot(weights, value_rows, preferred_element_type=jnp.float32)
        unstack(total_out, rows, heads, stacked(total_ref, rows, heads) + result[:, HD:])
        unstack(sum_out, rows, heads, stacked(sum_ref, rows, heads) + result[:, :HD])

    staged(row_blocks(query_ref.shape[0], 80), start, finish)


def last_stage(routed, *refs):
    query_ref, best_ref, old_total_ref, old_sum_ref, total_ref, sum_ref = refs[:6]
    earlier_refs, refs = refs[6:-6], refs[-6:]
    direct_ref, swapped_ref, out_hbm, out_ref, trusted_ref, out_sems = refs
    heads = query_ref.shape[1] // HD
    blocks = row_blocks(query_ref.shape[0], 80)
    is_odd, core = place()
    takes_both = is_odd & routed
    is_direct = core == 0

    def out_copy(index, rows):
        return pltpu.make_async_copy(out_ref.at[rows], out_hbm.at[rows], out_sems.at[index])

    def write(rows, total, weighted):
        inverse = pl.reciprocal(total, approx=True)
        inverse = inverse * (2.0 - total * inverse)
        unstack(out_ref, rows, heads, (weighted * inverse).astype(jnp.bfloat16))

    def process(shard):
        trusted = [jnp.full((8, HD), True)]
        key_rows, value_rows = shard[:, :HD], with_ones(shard[:, HD:])

        def start(rows):
            return scores_of(stacked(query_ref, rows, heads), key_rows)

        def finish(index, rows, scores):
            best = stacked(best_ref, rows, heads)
            weights = jnp.exp2(scores - widen(best, scores.shape[1])).astype(jnp.bfloat16)
            result = jnp.dot(weights, value_rows, preferred_element_type=jnp.float32)
            total = stacked(total_ref, rows, heads) + result[:, HD:]
            weighted = stacked(sum_ref, rows, heads) + result[:, :HD]
            good = (total < total_limit).reshape(total.shape[0] // 8, 8, HD)
            trusted[0] = trusted[0] & jnp.all(good, axis=0)
            write(rows, total, weighted)
            out_copy(index, rows).start()

        staged(blocks, start, finish)
        trusted_ref[0] = jnp.all(trusted[0]).astype(jnp.int32)
        for index, rows in enumerate(blocks):
            out_copy(index, rows).wait()

    @pl.when(jnp.logical_not(takes_both))
    def one_shard():
        process(jnp.where(is_direct, direct_ref[...], swapped_ref[...]))

    @pl.when(takes_both)
    def two_shards():
        process(jnp.concatenate([direct_ref[...], swapped_ref[...]], axis=0))

    @pl.when(trusted_ref[0] == 0)
    def exact_maximum():
        size = query_ref.shape[0] // len(blocks)
        counted = [(ref, 0.0) for ref in earlier_refs]
        if routed:
            counted[-2:] = [
                (ref, penalty(jnp.logical_not(is_odd) | (core == by_swap)))
                for by_swap, ref in enumerate(earlier_refs[-2:])
            ]
        counted += [
            (direct_ref, penalty(takes_both | is_direct)),
            (swapped_ref, penalty(takes_both | jnp.logical_not(is_direct))),
        ]

        def visit(index, unused):
            rows = pl.ds(pl.multiple_of(index * size, size), size)
            queries = stacked(query_ref, rows, heads)
            best = stacked(best_ref, rows, heads)
            weighted = stacked(old_sum_ref, rows, heads)
            total = stacked(old_total_ref, rows, heads)
            for shard_ref, extra in counted:
                key_rows, value_rows = shard_ref[:, :HD], with_ones(shard_ref[:, HD:])
                scores = scores_of(queries, key_rows) - extra
                new_best = jnp.maximum(best, jnp.max(scores, axis=1, keepdims=True))
                factor = jnp.exp2(best - new_best)
                weights = jnp.exp2(scores - widen(new_best, scores.shape[1]))
                result = jnp.dot(
                    weights.astype(jnp.bfloat16), value_rows, preferred_element_type=jnp.float32
                )
                weighted = weighted * factor + result[:, :HD]
                total = total * factor + result[:, HD:]
                best = new_best
            write(rows, total, weighted)
            copy = out_copy(index, rows)
            copy.start()
            copy.wait()
            return unused

        lax.fori_loop(0, len(blocks), visit, 0)


def shards(queries, suffix_kv, prompt_kv, lengths):
    slots, width = queries.shape
    heads = width // HD
    loop_size = lax.axis_size("loop")
    own = prompt_kv[:, 0, :]
    suffix = suffix_kv[:, 0, :]
    shard_rows = own.shape[0]

    in_hbm = pl.BlockSpec(memory_space=pltpu.HBM)
    in_vmem = pl.BlockSpec(memory_space=pltpu.VMEM)
    state = jax.ShapeDtypeStruct((slots, width), jnp.float32)

    cost = pl.CostEstimate(flops=1, bytes_accessed=1, transcendentals=0)

    routed = loop_size >= FOUR and loop_size & (loop_size - 1) == 0

    def send(shard, route):
        hops = []
        for i in range(loop_size):
            for core in range(2):
                to, to_core = route(i, core)
                hops.append((2 * i + core, 2 * to + to_core))
        return lax.ppermute(shard, ("loop", "pair"), hops)

    def far_core(i):
        return 1 ^ (i & 1) ^ (i >> 1 & 1)

    def first_route(i, core):
        if core == 1:
            return (i ^ 2) & ~1, far_core(i)
        return (i, 1) if i & 1 else (i + 1, 0)

    def second_route(i, core):
        if core == 1:
            return (i ^ 2) | 1, far_core(i)
        return (i - 1, 0) if i & 1 else (i, 1)

    hbm = [pltpu.with_memory_space_constraint(x, pltpu.HBM) for x in (lengths, queries, suffix, own)]
    buffers = [
        jax.ShapeDtypeStruct(queries.shape, queries.dtype),
        jax.ShapeDtypeStruct(suffix.shape, suffix.dtype),
        jax.ShapeDtypeStruct(own.shape, own.dtype),
        jax.ShapeDtypeStruct((slots, HD), jnp.int32),
    ]
    load_scratch = [
        pltpu.SMEM(lengths.shape, lengths.dtype),
        pltpu.SemaphoreType.DMA((2 + 2 * len(load_blocks(slots)),)),
    ]
    loaded = pl.pallas_call(
        prelude_stage,
        name="prelude_stage",
        out_shape=buffers,
        in_specs=[in_hbm] * 4,
        out_specs=[in_vmem] * 4,
        scratch_shapes=load_scratch,
        compiler_params=pltpu.CompilerParams(vmem_limit_bytes=8 * 2**20),
        cost_estimate=cost,
    )(*hbm)
    own, loaded = lax.optimization_barrier((own, loaded))
    if routed:
        early = [
            send(own, lambda i, core, step=step: (i ^ (step + core), 1 - core))
            for step in range(FOUR, loop_size, 2)
        ]
        early.append(send(own, first_route))
        final = send(own, second_route)
    else:
        early = [
            send(own, lambda i, core, step=step: ((i + step) % loop_size, core))
            for step in range(1, loop_size)
        ]
        final = early.pop()
    best, total, weighted, queries, *unused = pl.pallas_call(
        local_stage,
        name="local_stage",
        out_shape=[state] * 3 + buffers,
        in_specs=[in_hbm] * 4 + [in_vmem] * 4,
        out_specs=[in_vmem] * 7,
        scratch_shapes=load_scratch,
        input_output_aliases={4 + i: 3 + i for i in range(4)},
        compiler_params=pltpu.CompilerParams(vmem_limit_bytes=24 * 2**20),
        cost_estimate=cost,
    )(*hbm, *loaded)

    def add_shards(total, weighted, shards_now, by_swap):
        if not shards_now:
            return total, weighted
        return pl.pallas_call(
            functools.partial(add_stage, by_swap if routed else None),
            name="add_stage",
            out_shape=[state] * 2,
            in_specs=[in_vmem] * (4 + len(shards_now)),
            out_specs=[in_vmem] * 2,
            compiler_params=pltpu.CompilerParams(vmem_limit_bytes=24 * 2**20),
            cost_estimate=cost,
        )(queries, best, total, weighted, *shards_now)

    def swapped(shard):
        return send(shard, lambda i, core: (i, 1 - core))

    early, best = lax.optimization_barrier((early, best))
    early_swapped = [swapped(shard) for shard in early] if routed else []
    new_total, new_weighted = add_shards(total, weighted, early, False)
    final, new_total = lax.optimization_barrier((final, new_total))
    final_swapped = swapped(final) if routed else final
    new_total, new_weighted = add_shards(new_total, new_weighted, early_swapped, True)
    last_inputs = (queries, best, total, weighted, new_total, new_weighted)
    last_inputs += (*early[:-1], *early_swapped[:-1], *early[-1:], *early_swapped[-1:])
    last_inputs += (final, final_swapped)
    return pl.pallas_call(
        functools.partial(last_stage, routed),
        name="last_stage",
        out_shape=jax.ShapeDtypeStruct((slots, width), jnp.bfloat16),
        in_specs=[in_vmem] * len(last_inputs),
        out_specs=in_hbm,
        scratch_shapes=[
            pltpu.VMEM((slots, width), jnp.bfloat16),
            pltpu.SMEM((1,), jnp.int32),
            pltpu.SemaphoreType.DMA((len(row_blocks(slots, 80)),)),
        ],
        compiler_params=pltpu.CompilerParams(vmem_limit_bytes=32 * 2**20),
        cost_estimate=cost,
    )(*last_inputs)


def solution(mesh):
    placed = (
        P(("groups", "loop"), ("heads", "pair")),
        P(("groups", "loop"), "heads", None),
        P(("groups", "loop"), "heads", None),
        P("groups"),
    )
    return jax.shard_map(
        shards,
        mesh=mesh,
        in_specs=placed,
        out_specs=P(("groups", "loop"), ("heads", "pair")),
        check_vma=False,
    )
```

```python
import functools
import math

import jax
import jax.numpy as jnp
from jax import lax
from jax.experimental import pallas as pl
from jax.experimental.pallas import tpu as pltpu
from jax.sharding import PartitionSpec as P

HD = 128
AG_DEV = 2
MAXLEN = 320
BLK = 128
FOUR = 4

masked_score = -1e30
empty_best = 1e30
total_limit = 2.0**100
score_scale = math.log2(math.e) / math.sqrt(HD)


def scores_of(query_rows, key_rows):
    return (
        lax.dot_general(
            query_rows, key_rows, (((1,), (1,)), ((), ())), preferred_element_type=jnp.float32
        )
        * score_scale
    )


def with_ones(value_rows):
    return jnp.concatenate([value_rows, jnp.ones_like(value_rows)], axis=1)


def stacked(ref, rows, head_count):
    return jnp.concatenate([ref[rows, h * HD : (h + 1) * HD] for h in range(head_count)], axis=0)


def unstack(ref, rows, head_count, value):
    count = value.shape[0] // head_count
    for h in range(head_count):
        ref[rows, h * HD : (h + 1) * HD] = value[h * count : (h + 1) * count]


def widen(row_value, width):
    return jnp.concatenate([row_value] * (width // HD), axis=1)


def place():
    return lax.rem(lax.axis_index("loop"), FOUR), lax.axis_index("pair")


def load_blocks(count):
    return [pl.ds(first, BLK) for first in range(0, count, BLK)]


def load(
    lengths_hbm,
    query_hbm,
    suffix_hbm,
    own_hbm,
    query_ref,
    suffix_ref,
    own_ref,
    first_ref,
    lengths_ref,
    sems,
):
    pairs = [(lengths_hbm, lengths_ref), (own_hbm, own_ref)]
    for source, target in ((query_hbm, query_ref), (suffix_hbm, suffix_ref)):
        for rows in load_blocks(target.shape[0]):
            pairs.append((source.at[rows], target.at[rows]))
    copies = [
        pltpu.make_async_copy(source, target, sems.at[i])
        for i, (source, target) in enumerate(pairs)
    ]
    for copy in copies:
        copy.start()
    copies[0].wait()
    slots = query_ref.shape[0]
    position = lax.axis_index("loop")
    row_at = lax.broadcasted_iota(jnp.int32, first_ref.shape, 0)
    first = jnp.zeros_like(row_at)
    agent_end = 0
    for agent in range(AG_DEV):
        agent_end = agent_end + lengths_ref[position * AG_DEV + agent]
        first = jnp.where(row_at >= agent_end, agent_end if agent + 1 < AG_DEV else slots, first)
    first_ref[...] = first
    for copy in copies[1:]:
        copy.wait()


def prelude_stage(*refs):
    @pl.when(is_first_chip())
    def ahead():
        load(*refs)


def local_stage(*refs):
    sources, (best_ref, total_ref, sum_ref), loaded, scratch = (
        refs[:4],
        refs[8:11],
        refs[11:15],
        refs[15:],
    )
    query_ref, suffix_ref, own_ref, first_ref = loaded

    @pl.when(jnp.logical_not(is_first_chip()))
    def now():
        load(*sources, *loaded, *scratch)

    slots = query_ref.shape[0]
    heads = query_ref.shape[1] // HD
    own_keys = own_ref[:, :HD]
    own_values = with_ones(own_ref[:, HD:])
    window = BLK * ((MAXLEN + BLK - 2) // BLK) + BLK
    for block in range(slots // BLK):
        stop = (block + 1) * BLK
        start = max(0, stop - window)
        rows = slice(block * BLK, stop)
        row_at = block * BLK + lax.broadcasted_iota(jnp.int32, (BLK, stop - start), 0)
        key_at = start + lax.broadcasted_iota(jnp.int32, (BLK, stop - start), 1)
        first = first_ref[rows]
        allowed = (key_at <= row_at) & (key_at >= widen(first, stop - start))
        queries = stacked(query_ref, rows, heads)
        own_scores = scores_of(queries, own_keys)
        suffix_scores = jnp.where(
            jnp.concatenate([allowed] * heads, axis=0),
            scores_of(queries, suffix_ref[start:stop, :HD]),
            masked_score,
        )
        best = jnp.maximum(
            jnp.max(own_scores, axis=1, keepdims=True),
            jnp.max(suffix_scores, axis=1, keepdims=True),
        )
        own_weights = jnp.exp2(own_scores - best).astype(jnp.bfloat16)
        suffix_weights = jnp.exp2(suffix_scores - best).astype(jnp.bfloat16)
        result = jnp.dot(own_weights, own_values, preferred_element_type=jnp.float32)
        result = result + jnp.dot(
            suffix_weights,
            with_ones(suffix_ref[start:stop, HD:]),
            preferred_element_type=jnp.float32,
        )
        live = jnp.concatenate([first < slots] * heads, axis=0)
        unstack(best_ref, rows, heads, jnp.where(live, best, empty_best))
        unstack(sum_ref, rows, heads, jnp.where(live, result[:, :HD], 0.0))
        unstack(total_ref, rows, heads, jnp.where(live, result[:, HD:], 1.0))


def staged(blocks, start, finish):
    coming = start(blocks[0])
    for index, rows in enumerate(blocks):
        now = coming
        if index + 1 < len(blocks):
            coming = start(blocks[index + 1])
        finish(index, rows, now)


def row_blocks(count, largest):
    step = next(size for size in (largest, 128, 16, count) if count % size == 0)
    return [slice(first, first + step) for first in range(0, count, step)]


def is_first_chip():
    return lax.axis_index("groups") + lax.axis_index("loop") + lax.axis_index("heads") == 0


def penalty(is_there):
    return jnp.where(is_there, 0.0, empty_best)


def add_stage(by_swap, *refs):
    query_ref, best_ref, total_ref, sum_ref = refs[:4]
    shard_refs = refs[4:-2]
    total_out, sum_out = refs[-2:]
    heads = query_ref.shape[1] // HD
    shard = jnp.concatenate([ref[...] for ref in shard_refs], axis=0)
    key_rows, value_rows = shard[:, :HD], with_ones(shard[:, HD:])
    extra = None
    if by_swap is not None:
        position, core = place()
        extra = penalty((position != 1) | (core == int(by_swap)))

    def start(rows):
        return scores_of(stacked(query_ref, rows, heads), key_rows)

    def finish(index, rows, scores):
        best = stacked(best_ref, rows, heads)
        if extra is None:
            points = widen(best, scores.shape[1])
        else:
            held = shard_refs[-1].shape[0]
            points = [best] * ((scores.shape[1] - held) // HD) + [best + extra] * (held // HD)
            points = jnp.concatenate(points, axis=1)
        weights = jnp.exp2(scores - points).astype(jnp.bfloat16)
        result = jnp.dot(weights, value_rows, preferred_element_type=jnp.float32)
        unstack(total_out, rows, heads, stacked(total_ref, rows, heads) + result[:, HD:])
        unstack(sum_out, rows, heads, stacked(sum_ref, rows, heads) + result[:, :HD])

    staged(row_blocks(query_ref.shape[0], 80), start, finish)


def last_stage(routed, *refs):
    query_ref, best_ref, old_total_ref, old_sum_ref, total_ref, sum_ref = refs[:6]
    earlier_refs, refs = refs[6:-6], refs[-6:]
    direct_ref, swapped_ref, out_hbm, out_ref, trusted_ref, out_sems = refs
    heads = query_ref.shape[1] // HD
    blocks = row_blocks(query_ref.shape[0], 80)
    position, core = place()
    takes_both = (position == 1) & routed
    is_direct = core == jnp.where(position == 0, 0, 1)

    def out_copy(index, rows):
        return pltpu.make_async_copy(out_ref.at[rows], out_hbm.at[rows], out_sems.at[index])

    def write(rows, total, weighted):
        inverse = pl.reciprocal(total, approx=True)
        inverse = inverse * (2.0 - total * inverse)
        unstack(out_ref, rows, heads, (weighted * inverse).astype(jnp.bfloat16))

    def process(shard):
        trusted = [jnp.full((8, HD), True)]
        key_rows, value_rows = shard[:, :HD], with_ones(shard[:, HD:])

        def start(rows):
            return scores_of(stacked(query_ref, rows, heads), key_rows)

        def finish(index, rows, scores):
            best = stacked(best_ref, rows, heads)
            weights = jnp.exp2(scores - widen(best, scores.shape[1])).astype(jnp.bfloat16)
            result = jnp.dot(weights, value_rows, preferred_element_type=jnp.float32)
            total = stacked(total_ref, rows, heads) + result[:, HD:]
            weighted = stacked(sum_ref, rows, heads) + result[:, :HD]
            good = (total < total_limit).reshape(total.shape[0] // 8, 8, HD)
            trusted[0] = trusted[0] & jnp.all(good, axis=0)
            write(rows, total, weighted)
            out_copy(index, rows).start()

        staged(blocks, start, finish)
        trusted_ref[0] = jnp.all(trusted[0]).astype(jnp.int32)
        for index, rows in enumerate(blocks):
            out_copy(index, rows).wait()

    @pl.when(jnp.logical_not(takes_both))
    def one_shard():
        process(jnp.where(is_direct, direct_ref[...], swapped_ref[...]))

    @pl.when(takes_both)
    def two_shards():
        process(jnp.concatenate([direct_ref[...], swapped_ref[...]], axis=0))

    @pl.when(trusted_ref[0] == 0)
    def exact_maximum():
        size = query_ref.shape[0] // len(blocks)
        counted = [(ref, 0.0) for ref in earlier_refs]
        if routed:
            counted[-2:] = [
                (ref, penalty((position != 1) | (core == by_swap)))
                for by_swap, ref in enumerate(earlier_refs[-2:])
            ]
        counted += [
            (direct_ref, penalty(takes_both | is_direct)),
            (swapped_ref, penalty(takes_both | jnp.logical_not(is_direct))),
        ]

        def visit(index, unused):
            rows = pl.ds(pl.multiple_of(index * size, size), size)
            queries = stacked(query_ref, rows, heads)
            best = stacked(best_ref, rows, heads)
            weighted = stacked(old_sum_ref, rows, heads)
            total = stacked(old_total_ref, rows, heads)
            for shard_ref, extra in counted:
                key_rows, value_rows = shard_ref[:, :HD], with_ones(shard_ref[:, HD:])
                scores = scores_of(queries, key_rows) - extra
                new_best = jnp.maximum(best, jnp.max(scores, axis=1, keepdims=True))
                factor = jnp.exp2(best - new_best)
                weights = jnp.exp2(scores - widen(new_best, scores.shape[1]))
                result = jnp.dot(
                    weights.astype(jnp.bfloat16), value_rows, preferred_element_type=jnp.float32
                )
                weighted = weighted * factor + result[:, :HD]
                total = total * factor + result[:, HD:]
                best = new_best
            write(rows, total, weighted)
            copy = out_copy(index, rows)
            copy.start()
            copy.wait()
            return unused

        lax.fori_loop(0, len(blocks), visit, 0)


def shards(queries, suffix_kv, prompt_kv, lengths):
    slots, width = queries.shape
    heads = width // HD
    loop_size = lax.axis_size("loop")
    own = prompt_kv[:, 0, :]
    suffix = suffix_kv[:, 0, :]
    shard_rows = own.shape[0]

    in_hbm = pl.BlockSpec(memory_space=pltpu.HBM)
    in_vmem = pl.BlockSpec(memory_space=pltpu.VMEM)
    state = jax.ShapeDtypeStruct((slots, width), jnp.float32)

    cost = pl.CostEstimate(flops=1, bytes_accessed=1, transcendentals=0)

    routed = loop_size >= FOUR and loop_size & (loop_size - 1) == 0

    def send(shard, route):
        hops = []
        for i in range(loop_size):
            for core in range(2):
                to, to_core = route(i, core)
                hops.append((2 * i + core, 2 * to + to_core))
        return lax.ppermute(shard, ("loop", "pair"), hops)

    def first_route(i, core):
        base = i - i % FOUR
        to, to_core = [((1, 0), (3, 1)), ((1, 1), (2, 0)), ((3, 0), (0, 0)), ((2, 1), (0, 1))][
            i % FOUR
        ][core]
        return base + to, to_core

    def second_route(i, core):
        base = i - i % FOUR
        to, to_core = [((0, 1), (2, 1)), ((0, 0), (3, 1)), ((3, 0), (1, 0)), ((2, 0), (1, 1))][
            i % FOUR
        ][core]
        return base + to, to_core

    hbm = [pltpu.with_memory_space_constraint(x, pltpu.HBM) for x in (lengths, queries, suffix, own)]
    buffers = [
        jax.ShapeDtypeStruct(queries.shape, queries.dtype),
        jax.ShapeDtypeStruct(suffix.shape, suffix.dtype),
        jax.ShapeDtypeStruct(own.shape, own.dtype),
        jax.ShapeDtypeStruct((slots, HD), jnp.int32),
    ]
    load_scratch = [
        pltpu.SMEM(lengths.shape, lengths.dtype),
        pltpu.SemaphoreType.DMA((2 + 2 * len(load_blocks(slots)),)),
    ]
    loaded = pl.pallas_call(
        prelude_stage,
        name="prelude_stage",
        out_shape=buffers,
        in_specs=[in_hbm] * 4,
        out_specs=[in_vmem] * 4,
        scratch_shapes=load_scratch,
        compiler_params=pltpu.CompilerParams(vmem_limit_bytes=8 * 2**20),
        cost_estimate=cost,
    )(*hbm)
    own, loaded = lax.optimization_barrier((own, loaded))
    if routed:
        early = [
            send(own, lambda i, core, step=step: (i ^ (step + core), 1 - core))
            for step in range(FOUR, loop_size, 2)
        ]
        early.append(send(own, first_route))
        final = send(own, second_route)
    else:
        early = [
            send(own, lambda i, core, step=step: ((i + step) % loop_size, core))
            for step in range(1, loop_size)
        ]
        final = early.pop()
    best, total, weighted, queries, *unused = pl.pallas_call(
        local_stage,
        name="local_stage",
        out_shape=[state] * 3 + buffers,
        in_specs=[in_hbm] * 4 + [in_vmem] * 4,
        out_specs=[in_vmem] * 7,
        scratch_shapes=load_scratch,
        input_output_aliases={4 + i: 3 + i for i in range(4)},
        compiler_params=pltpu.CompilerParams(vmem_limit_bytes=24 * 2**20),
        cost_estimate=cost,
    )(*hbm, *loaded)

    def add_shards(total, weighted, shards_now, by_swap):
        if not shards_now:
            return total, weighted
        return pl.pallas_call(
            functools.partial(add_stage, by_swap if routed else None),
            name="add_stage",
            out_shape=[state] * 2,
            in_specs=[in_vmem] * (4 + len(shards_now)),
            out_specs=[in_vmem] * 2,
            compiler_params=pltpu.CompilerParams(vmem_limit_bytes=24 * 2**20),
            cost_estimate=cost,
        )(queries, best, total, weighted, *shards_now)

    def swapped(shard):
        return send(shard, lambda i, core: (i, 1 - core))

    early, best = lax.optimization_barrier((early, best))
    early_swapped = [swapped(shard) for shard in early] if routed else []
    new_total, new_weighted = add_shards(total, weighted, early, False)
    final, new_total = lax.optimization_barrier((final, new_total))
    final_swapped = swapped(final) if routed else final
    new_total, new_weighted = add_shards(new_total, new_weighted, early_swapped, True)
    last_inputs = (queries, best, total, weighted, new_total, new_weighted)
    last_inputs += (*early[:-1], *early_swapped[:-1], *early[-1:], *early_swapped[-1:])
    last_inputs += (final, final_swapped)
    return pl.pallas_call(
        functools.partial(last_stage, routed),
        name="last_stage",
        out_shape=jax.ShapeDtypeStruct((slots, width), jnp.bfloat16),
        in_specs=[in_vmem] * len(last_inputs),
        out_specs=in_hbm,
        scratch_shapes=[
            pltpu.VMEM((slots, width), jnp.bfloat16),
            pltpu.SMEM((1,), jnp.int32),
            pltpu.SemaphoreType.DMA((len(row_blocks(slots, 80)),)),
        ],
        compiler_params=pltpu.CompilerParams(vmem_limit_bytes=32 * 2**20),
        cost_estimate=cost,
    )(*last_inputs)


def solution(mesh):
    placed = (
        P(("groups", "loop"), ("heads", "pair")),
        P(("groups", "loop"), "heads", None),
        P(("groups", "loop"), "heads", None),
        P("groups"),
    )
    return jax.shard_map(
        shards,
        mesh=mesh,
        in_specs=placed,
        out_specs=P(("groups", "loop"), ("heads", "pair")),
        check_vma=False,
    )
```

```python
import functools
import math

import jax
import jax.numpy as jnp
from jax import lax
from jax.experimental import pallas as pl
from jax.experimental.pallas import tpu as pltpu
from jax.sharding import PartitionSpec as P

HD = 128
AG_DEV = 2
MAXLEN = 320
BLK = 128
FOUR = 4

masked_score = -1e30
empty_best = 1e30
total_limit = 2.0**100
score_scale = math.log2(math.e) / math.sqrt(HD)


def scores_of(query_rows, key_rows):
    return (
        lax.dot_general(
            query_rows, key_rows, (((1,), (1,)), ((), ())), preferred_element_type=jnp.float32
        )
        * score_scale
    )


def with_ones(value_rows):
    return jnp.concatenate([value_rows, jnp.ones_like(value_rows)], axis=1)


def stacked(ref, rows, head_count):
    return jnp.concatenate([ref[rows, h * HD : (h + 1) * HD] for h in range(head_count)], axis=0)


def unstack(ref, rows, head_count, value):
    count = value.shape[0] // head_count
    for h in range(head_count):
        ref[rows, h * HD : (h + 1) * HD] = value[h * count : (h + 1) * count]


def widen(row_value, width):
    return jnp.concatenate([row_value] * (width // HD), axis=1)


def place():
    position = lax.rem(lax.axis_index("loop"), FOUR)
    return (position == 1) | (position == 2), lax.axis_index("pair")


def load_blocks(count):
    return [pl.ds(first, BLK) for first in range(0, count, BLK)]


def load(
    lengths_hbm,
    query_hbm,
    suffix_hbm,
    own_hbm,
    query_ref,
    suffix_ref,
    own_ref,
    first_ref,
    lengths_ref,
    sems,
):
    pairs = [(lengths_hbm, lengths_ref), (own_hbm, own_ref)]
    for source, target in ((query_hbm, query_ref), (suffix_hbm, suffix_ref)):
        for rows in load_blocks(target.shape[0]):
            pairs.append((source.at[rows], target.at[rows]))
    copies = [
        pltpu.make_async_copy(source, target, sems.at[i])
        for i, (source, target) in enumerate(pairs)
    ]
    for copy in copies:
        copy.start()
    copies[0].wait()
    slots = query_ref.shape[0]
    position = lax.axis_index("loop")
    row_at = lax.broadcasted_iota(jnp.int32, first_ref.shape, 0)
    first = jnp.zeros_like(row_at)
    agent_end = 0
    for agent in range(AG_DEV):
        agent_end = agent_end + lengths_ref[position * AG_DEV + agent]
        first = jnp.where(row_at >= agent_end, agent_end if agent + 1 < AG_DEV else slots, first)
    first_ref[...] = first
    for copy in copies[1:]:
        copy.wait()


def prelude_stage(*refs):
    @pl.when(is_first_chip())
    def ahead():
        load(*refs)


def local_stage(*refs):
    sources, (best_ref, total_ref, sum_ref), loaded, scratch = (
        refs[:4],
        refs[8:11],
        refs[11:15],
        refs[15:],
    )
    query_ref, suffix_ref, own_ref, first_ref = loaded

    @pl.when(jnp.logical_not(is_first_chip()))
    def now():
        load(*sources, *loaded, *scratch)

    slots = query_ref.shape[0]
    heads = query_ref.shape[1] // HD
    own_keys = own_ref[:, :HD]
    own_values = with_ones(own_ref[:, HD:])
    window = BLK * ((MAXLEN + BLK - 2) // BLK) + BLK
    for block in range(slots // BLK):
        stop = (block + 1) * BLK
        start = max(0, stop - window)
        rows = slice(block * BLK, stop)
        row_at = block * BLK + lax.broadcasted_iota(jnp.int32, (BLK, stop - start), 0)
        key_at = start + lax.broadcasted_iota(jnp.int32, (BLK, stop - start), 1)
        first = first_ref[rows]
        allowed = (key_at <= row_at) & (key_at >= widen(first, stop - start))
        queries = stacked(query_ref, rows, heads)
        own_scores = scores_of(queries, own_keys)
        suffix_scores = jnp.where(
            jnp.concatenate([allowed] * heads, axis=0),
            scores_of(queries, suffix_ref[start:stop, :HD]),
            masked_score,
        )
        best = jnp.maximum(
            jnp.max(own_scores, axis=1, keepdims=True),
            jnp.max(suffix_scores, axis=1, keepdims=True),
        )
        own_weights = jnp.exp2(own_scores - best).astype(jnp.bfloat16)
        suffix_weights = jnp.exp2(suffix_scores - best).astype(jnp.bfloat16)
        result = jnp.dot(own_weights, own_values, preferred_element_type=jnp.float32)
        result = result + jnp.dot(
            suffix_weights,
            with_ones(suffix_ref[start:stop, HD:]),
            preferred_element_type=jnp.float32,
        )
        live = jnp.concatenate([first < slots] * heads, axis=0)
        unstack(best_ref, rows, heads, jnp.where(live, best, empty_best))
        unstack(sum_ref, rows, heads, jnp.where(live, result[:, :HD], 0.0))
        unstack(total_ref, rows, heads, jnp.where(live, result[:, HD:], 1.0))


def staged(blocks, start, finish):
    coming = start(blocks[0])
    for index, rows in enumerate(blocks):
        now = coming
        if index + 1 < len(blocks):
            coming = start(blocks[index + 1])
        finish(index, rows, now)


def row_blocks(count, largest):
    step = next(size for size in (largest, 128, 16, count) if count % size == 0)
    return [slice(first, first + step) for first in range(0, count, step)]


def is_first_chip():
    return lax.axis_index("groups") + lax.axis_index("loop") + lax.axis_index("heads") == 0


def penalty(is_there):
    return jnp.where(is_there, 0.0, empty_best)


def add_stage(by_swap, *refs):
    query_ref, best_ref, total_ref, sum_ref = refs[:4]
    shard_refs = refs[4:-2]
    total_out, sum_out = refs[-2:]
    heads = query_ref.shape[1] // HD
    shard = jnp.concatenate([ref[...] for ref in shard_refs], axis=0)
    key_rows, value_rows = shard[:, :HD], with_ones(shard[:, HD:])
    extra = None
    if by_swap is not None:
        is_middle, core = place()
        extra = penalty(jnp.logical_not(is_middle) | (core == int(by_swap)))

    def start(rows):
        return scores_of(stacked(query_ref, rows, heads), key_rows)

    def finish(index, rows, scores):
        best = stacked(best_ref, rows, heads)
        if extra is None:
            points = widen(best, scores.shape[1])
        else:
            held = shard_refs[-1].shape[0]
            points = [best] * ((scores.shape[1] - held) // HD) + [best + extra] * (held // HD)
            points = jnp.concatenate(points, axis=1)
        weights = jnp.exp2(scores - points).astype(jnp.bfloat16)
        result = jnp.dot(weights, value_rows, preferred_element_type=jnp.float32)
        unstack(total_out, rows, heads, stacked(total_ref, rows, heads) + result[:, HD:])
        unstack(sum_out, rows, heads, stacked(sum_ref, rows, heads) + result[:, :HD])

    staged(row_blocks(query_ref.shape[0], 80), start, finish)


def last_stage(routed, *refs):
    query_ref, best_ref, old_total_ref, old_sum_ref, total_ref, sum_ref = refs[:6]
    earlier_refs, refs = refs[6:-6], refs[-6:]
    direct_ref, swapped_ref, out_hbm, out_ref, trusted_ref, out_sems = refs
    heads = query_ref.shape[1] // HD
    blocks = row_blocks(query_ref.shape[0], 80)
    is_middle, core = place()
    takes_both = is_middle & routed
    is_direct = core == 0

    def out_copy(index, rows):
        return pltpu.make_async_copy(out_ref.at[rows], out_hbm.at[rows], out_sems.at[index])

    def write(rows, total, weighted):
        inverse = pl.reciprocal(total, approx=True)
        inverse = inverse * (2.0 - total * inverse)
        unstack(out_ref, rows, heads, (weighted * inverse).astype(jnp.bfloat16))

    def process(shard):
        trusted = [jnp.full((8, HD), True)]
        key_rows, value_rows = shard[:, :HD], with_ones(shard[:, HD:])

        def start(rows):
            return scores_of(stacked(query_ref, rows, heads), key_rows)

        def finish(index, rows, scores):
            best = stacked(best_ref, rows, heads)
            weights = jnp.exp2(scores - widen(best, scores.shape[1])).astype(jnp.bfloat16)
            result = jnp.dot(weights, value_rows, preferred_element_type=jnp.float32)
            total = stacked(total_ref, rows, heads) + result[:, HD:]
            weighted = stacked(sum_ref, rows, heads) + result[:, :HD]
            good = (total < total_limit).reshape(total.shape[0] // 8, 8, HD)
            trusted[0] = trusted[0] & jnp.all(good, axis=0)
            write(rows, total, weighted)
            out_copy(index, rows).start()

        staged(blocks, start, finish)
        trusted_ref[0] = jnp.all(trusted[0]).astype(jnp.int32)
        for index, rows in enumerate(blocks):
            out_copy(index, rows).wait()

    @pl.when(jnp.logical_not(takes_both))
    def one_shard():
        process(jnp.where(is_direct, direct_ref[...], swapped_ref[...]))

    @pl.when(takes_both)
    def two_shards():
        process(jnp.concatenate([direct_ref[...], swapped_ref[...]], axis=0))

    @pl.when(trusted_ref[0] == 0)
    def exact_maximum():
        size = query_ref.shape[0] // len(blocks)
        counted = [(ref, 0.0) for ref in earlier_refs]
        if routed:
            counted[-2:] = [
                (ref, penalty(jnp.logical_not(is_middle) | (core == by_swap)))
                for by_swap, ref in enumerate(earlier_refs[-2:])
            ]
        counted += [
            (direct_ref, penalty(takes_both | is_direct)),
            (swapped_ref, penalty(takes_both | jnp.logical_not(is_direct))),
        ]

        def visit(index, unused):
            rows = pl.ds(pl.multiple_of(index * size, size), size)
            queries = stacked(query_ref, rows, heads)
            best = stacked(best_ref, rows, heads)
            weighted = stacked(old_sum_ref, rows, heads)
            total = stacked(old_total_ref, rows, heads)
            for shard_ref, extra in counted:
                key_rows, value_rows = shard_ref[:, :HD], with_ones(shard_ref[:, HD:])
                scores = scores_of(queries, key_rows) - extra
                new_best = jnp.maximum(best, jnp.max(scores, axis=1, keepdims=True))
                factor = jnp.exp2(best - new_best)
                weights = jnp.exp2(scores - widen(new_best, scores.shape[1]))
                result = jnp.dot(
                    weights.astype(jnp.bfloat16), value_rows, preferred_element_type=jnp.float32
                )
                weighted = weighted * factor + result[:, :HD]
                total = total * factor + result[:, HD:]
                best = new_best
            write(rows, total, weighted)
            copy = out_copy(index, rows)
            copy.start()
            copy.wait()
            return unused

        lax.fori_loop(0, len(blocks), visit, 0)


def shards(queries, suffix_kv, prompt_kv, lengths):
    slots, width = queries.shape
    heads = width // HD
    loop_size = lax.axis_size("loop")
    own = prompt_kv[:, 0, :]
    suffix = suffix_kv[:, 0, :]
    shard_rows = own.shape[0]

    in_hbm = pl.BlockSpec(memory_space=pltpu.HBM)
    in_vmem = pl.BlockSpec(memory_space=pltpu.VMEM)
    state = jax.ShapeDtypeStruct((slots, width), jnp.float32)

    cost = pl.CostEstimate(flops=1, bytes_accessed=1, transcendentals=0)

    routed = loop_size >= FOUR and loop_size & (loop_size - 1) == 0

    def send(shard, route):
        hops = []
        for i in range(loop_size):
            for core in range(2):
                to, to_core = route(i, core)
                hops.append((2 * i + core, 2 * to + to_core))
        return lax.ppermute(shard, ("loop", "pair"), hops)

    def first_route(i, core):
        base = i - i % FOUR
        to, to_core = [((1, 0), (3, 1)), ((1, 1), (3, 0)), ((2, 1), (0, 0)), ((2, 0), (0, 1))][
            i % FOUR
        ][core]
        return base + to, to_core

    def second_route(i, core):
        base = i - i % FOUR
        to, to_core = [((0, 1), (2, 1)), ((0, 0), (2, 0)), ((3, 0), (1, 0)), ((3, 1), (1, 1))][
            i % FOUR
        ][core]
        return base + to, to_core

    hbm = [pltpu.with_memory_space_constraint(x, pltpu.HBM) for x in (lengths, queries, suffix, own)]
    buffers = [
        jax.ShapeDtypeStruct(queries.shape, queries.dtype),
        jax.ShapeDtypeStruct(suffix.shape, suffix.dtype),
        jax.ShapeDtypeStruct(own.shape, own.dtype),
        jax.ShapeDtypeStruct((slots, HD), jnp.int32),
    ]
    load_scratch = [
        pltpu.SMEM(lengths.shape, lengths.dtype),
        pltpu.SemaphoreType.DMA((2 + 2 * len(load_blocks(slots)),)),
    ]
    loaded = pl.pallas_call(
        prelude_stage,
        name="prelude_stage",
        out_shape=buffers,
        in_specs=[in_hbm] * 4,
        out_specs=[in_vmem] * 4,
        scratch_shapes=load_scratch,
        compiler_params=pltpu.CompilerParams(vmem_limit_bytes=8 * 2**20),
        cost_estimate=cost,
    )(*hbm)
    own, loaded = lax.optimization_barrier((own, loaded))
    if routed:
        early = [
            send(own, lambda i, core, step=step: (i ^ (step + core), 1 - core))
            for step in range(FOUR, loop_size, 2)
        ]
        early.append(send(own, first_route))
        final = send(own, second_route)
    else:
        early = [
            send(own, lambda i, core, step=step: ((i + step) % loop_size, core))
            for step in range(1, loop_size)
        ]
        final = early.pop()
    best, total, weighted, queries, *unused = pl.pallas_call(
        local_stage,
        name="local_stage",
        out_shape=[state] * 3 + buffers,
        in_specs=[in_hbm] * 4 + [in_vmem] * 4,
        out_specs=[in_vmem] * 7,
        scratch_shapes=load_scratch,
        input_output_aliases={4 + i: 3 + i for i in range(4)},
        compiler_params=pltpu.CompilerParams(vmem_limit_bytes=24 * 2**20),
        cost_estimate=cost,
    )(*hbm, *loaded)

    def add_shards(total, weighted, shards_now, by_swap):
        if not shards_now:
            return total, weighted
        return pl.pallas_call(
            functools.partial(add_stage, by_swap if routed else None),
            name="add_stage",
            out_shape=[state] * 2,
            in_specs=[in_vmem] * (4 + len(shards_now)),
            out_specs=[in_vmem] * 2,
            compiler_params=pltpu.CompilerParams(vmem_limit_bytes=24 * 2**20),
            cost_estimate=cost,
        )(queries, best, total, weighted, *shards_now)

    def swapped(shard):
        return send(shard, lambda i, core: (i, 1 - core))

    early, best = lax.optimization_barrier((early, best))
    early_swapped = [swapped(shard) for shard in early] if routed else []
    new_total, new_weighted = add_shards(total, weighted, early, False)
    final, new_total = lax.optimization_barrier((final, new_total))
    final_swapped = swapped(final) if routed else final
    new_total, new_weighted = add_shards(new_total, new_weighted, early_swapped, True)
    last_inputs = (queries, best, total, weighted, new_total, new_weighted)
    last_inputs += (*early[:-1], *early_swapped[:-1], *early[-1:], *early_swapped[-1:])
    last_inputs += (final, final_swapped)
    return pl.pallas_call(
        functools.partial(last_stage, routed),
        name="last_stage",
        out_shape=jax.ShapeDtypeStruct((slots, width), jnp.bfloat16),
        in_specs=[in_vmem] * len(last_inputs),
        out_specs=in_hbm,
        scratch_shapes=[
            pltpu.VMEM((slots, width), jnp.bfloat16),
            pltpu.SMEM((1,), jnp.int32),
            pltpu.SemaphoreType.DMA((len(row_blocks(slots, 80)),)),
        ],
        compiler_params=pltpu.CompilerParams(vmem_limit_bytes=32 * 2**20),
        cost_estimate=cost,
    )(*last_inputs)


def solution(mesh):
    placed = (
        P(("groups", "loop"), ("heads", "pair")),
        P(("groups", "loop"), "heads", None),
        P(("groups", "loop"), "heads", None),
        P("groups"),
    )
    return jax.shard_map(
        shards,
        mesh=mesh,
        in_specs=placed,
        out_specs=P(("groups", "loop"), ("heads", "pair")),
        check_vma=False,
    )
```

```python
import math

import jax
import jax.numpy as jnp
from jax import lax
from jax.experimental import pallas as pl
from jax.experimental.pallas import tpu as pltpu
from jax.sharding import PartitionSpec as P

HD = 128
AG_DEV = 2
MAXLEN = 320
BLK = 128
FOUR = 4

masked_score = -1e30
empty_best = 1e30
total_limit = 2.0**100
score_scale = math.log2(math.e) / math.sqrt(HD)


def scores_of(query_rows, key_rows):
    return (
        lax.dot_general(
            query_rows, key_rows, (((1,), (1,)), ((), ())), preferred_element_type=jnp.float32
        )
        * score_scale
    )


def with_ones(value_rows):
    return jnp.concatenate([value_rows, jnp.ones_like(value_rows)], axis=1)


def stacked(ref, rows, head_count):
    return jnp.concatenate([ref[rows, h * HD : (h + 1) * HD] for h in range(head_count)], axis=0)


def unstack(ref, rows, head_count, value):
    count = value.shape[0] // head_count
    for h in range(head_count):
        ref[rows, h * HD : (h + 1) * HD] = value[h * count : (h + 1) * count]


def widen(row_value, width):
    return jnp.concatenate([row_value] * (width // HD), axis=1)


def load_blocks(count):
    return [pl.ds(first, BLK) for first in range(0, count, BLK)]


def load(
    lengths_hbm,
    query_hbm,
    suffix_hbm,
    own_hbm,
    query_ref,
    suffix_ref,
    own_ref,
    first_ref,
    lengths_ref,
    sems,
):
    pairs = [(lengths_hbm, lengths_ref), (own_hbm, own_ref)]
    for source, target in ((query_hbm, query_ref), (suffix_hbm, suffix_ref)):
        for rows in load_blocks(target.shape[0]):
            pairs.append((source.at[rows], target.at[rows]))
    copies = [
        pltpu.make_async_copy(source, target, sems.at[i])
        for i, (source, target) in enumerate(pairs)
    ]
    for copy in copies:
        copy.start()
    copies[0].wait()
    slots = query_ref.shape[0]
    position = lax.axis_index("loop")
    row_at = lax.broadcasted_iota(jnp.int32, first_ref.shape, 0)
    first = jnp.zeros_like(row_at)
    agent_end = 0
    for agent in range(AG_DEV):
        agent_end = agent_end + lengths_ref[position * AG_DEV + agent]
        first = jnp.where(row_at >= agent_end, agent_end if agent + 1 < AG_DEV else slots, first)
    first_ref[...] = first
    for copy in copies[1:]:
        copy.wait()


def prelude_stage(*refs):
    @pl.when(is_first_chip())
    def ahead():
        load(*refs)


def local_stage(*refs):
    sources, (best_ref, total_ref, sum_ref), loaded, scratch = (
        refs[:4],
        refs[8:11],
        refs[11:15],
        refs[15:],
    )
    query_ref, suffix_ref, own_ref, first_ref = loaded

    @pl.when(jnp.logical_not(is_first_chip()))
    def now():
        load(*sources, *loaded, *scratch)

    slots = query_ref.shape[0]
    heads = query_ref.shape[1] // HD
    own_keys = own_ref[:, :HD]
    own_values = with_ones(own_ref[:, HD:])
    window = BLK * ((MAXLEN + BLK - 2) // BLK) + BLK
    for block in range(slots // BLK):
        stop = (block + 1) * BLK
        start = max(0, stop - window)
        rows = slice(block * BLK, stop)
        row_at = block * BLK + lax.broadcasted_iota(jnp.int32, (BLK, stop - start), 0)
        key_at = start + lax.broadcasted_iota(jnp.int32, (BLK, stop - start), 1)
        first = first_ref[rows]
        allowed = (key_at <= row_at) & (key_at >= widen(first, stop - start))
        queries = stacked(query_ref, rows, heads)
        own_scores = scores_of(queries, own_keys)
        suffix_scores = jnp.where(
            jnp.concatenate([allowed] * heads, axis=0),
            scores_of(queries, suffix_ref[start:stop, :HD]),
            masked_score,
        )
        best = jnp.maximum(
            jnp.max(own_scores, axis=1, keepdims=True),
            jnp.max(suffix_scores, axis=1, keepdims=True),
        )
        own_weights = jnp.exp2(own_scores - best).astype(jnp.bfloat16)
        suffix_weights = jnp.exp2(suffix_scores - best).astype(jnp.bfloat16)
        result = jnp.dot(own_weights, own_values, preferred_element_type=jnp.float32)
        result = result + jnp.dot(
            suffix_weights,
            with_ones(suffix_ref[start:stop, HD:]),
            preferred_element_type=jnp.float32,
        )
        live = jnp.concatenate([first < slots] * heads, axis=0)
        unstack(best_ref, rows, heads, jnp.where(live, best, empty_best))
        unstack(sum_ref, rows, heads, jnp.where(live, result[:, :HD], 0.0))
        unstack(total_ref, rows, heads, jnp.where(live, result[:, HD:], 1.0))


def staged(blocks, start, finish):
    coming = start(blocks[0])
    for index, rows in enumerate(blocks):
        now = coming
        if index + 1 < len(blocks):
            coming = start(blocks[index + 1])
        finish(index, rows, now)


def row_blocks(count, largest):
    step = next(size for size in (largest, 128, 16, count) if count % size == 0)
    return [slice(first, first + step) for first in range(0, count, step)]


def is_first_chip():
    return lax.axis_index("groups") + lax.axis_index("loop") + lax.axis_index("heads") == 0


def add_stage(*refs):
    query_ref, best_ref, total_ref, sum_ref = refs[:4]
    shard_refs = refs[4:-2]
    total_out, sum_out = refs[-2:]
    heads = query_ref.shape[1] // HD
    shard = jnp.concatenate([ref[...] for ref in shard_refs], axis=0)
    key_rows, value_rows = shard[:, :HD], with_ones(shard[:, HD:])

    def start(rows):
        return scores_of(stacked(query_ref, rows, heads), key_rows)

    def finish(index, rows, scores):
        best = stacked(best_ref, rows, heads)
        weights = jnp.exp2(scores - widen(best, scores.shape[1])).astype(jnp.bfloat16)
        result = jnp.dot(weights, value_rows, preferred_element_type=jnp.float32)
        unstack(total_out, rows, heads, stacked(total_ref, rows, heads) + result[:, HD:])
        unstack(sum_out, rows, heads, stacked(sum_ref, rows, heads) + result[:, :HD])

    staged(row_blocks(query_ref.shape[0], 80), start, finish)


def last_stage(*refs):
    query_ref, best_ref, old_total_ref, old_sum_ref, total_ref, sum_ref = refs[:6]
    earlier_refs, refs = refs[6:-5], refs[-5:]
    direct_ref, swapped_ref, out_hbm, out_ref, out_sems = refs
    heads = query_ref.shape[1] // HD
    blocks = row_blocks(query_ref.shape[0], 80)
    position = lax.rem(lax.axis_index("loop"), FOUR)
    is_direct = lax.axis_index("pair") == jnp.where(position == 2, 1, 0)
    last_shard = jnp.where(is_direct, direct_ref[...], swapped_ref[...])

    def out_copy(index, rows):
        return pltpu.make_async_copy(out_ref.at[rows], out_hbm.at[rows], out_sems.at[index])

    def write(rows, total, weighted):
        inverse = pl.reciprocal(total, approx=True)
        inverse = inverse * (2.0 - total * inverse)
        unstack(out_ref, rows, heads, (weighted * inverse).astype(jnp.bfloat16))

    trusted = [jnp.full((8, HD), True)]
    key_rows, value_rows = last_shard[:, :HD], with_ones(last_shard[:, HD:])

    def start(rows):
        return scores_of(stacked(query_ref, rows, heads), key_rows)

    def finish(index, rows, scores):
        best = stacked(best_ref, rows, heads)
        weights = jnp.exp2(scores - widen(best, scores.shape[1])).astype(jnp.bfloat16)
        result = jnp.dot(weights, value_rows, preferred_element_type=jnp.float32)
        total = stacked(total_ref, rows, heads) + result[:, HD:]
        weighted = stacked(sum_ref, rows, heads) + result[:, :HD]
        good = (total < total_limit).reshape(total.shape[0] // 8, 8, HD)
        trusted[0] = trusted[0] & jnp.all(good, axis=0)
        write(rows, total, weighted)
        out_copy(index, rows).start()

    staged(blocks, start, finish)
    is_trusted = jnp.all(trusted[0])
    for index, rows in enumerate(blocks):
        out_copy(index, rows).wait()

    @pl.when(jnp.logical_not(is_trusted))
    def exact_maximum():
        size = query_ref.shape[0] // len(blocks)
        def visit(index, unused):
            rows = pl.ds(pl.multiple_of(index * size, size), size)
            queries = stacked(query_ref, rows, heads)
            best = stacked(best_ref, rows, heads)
            weighted = stacked(old_sum_ref, rows, heads)
            total = stacked(old_total_ref, rows, heads)
            for shard in [ref[...] for ref in earlier_refs] + [last_shard]:
                key_rows, value_rows = shard[:, :HD], with_ones(shard[:, HD:])
                scores = scores_of(queries, key_rows)
                new_best = jnp.maximum(best, jnp.max(scores, axis=1, keepdims=True))
                factor = jnp.exp2(best - new_best)
                weights = jnp.exp2(scores - widen(new_best, scores.shape[1]))
                result = jnp.dot(
                    weights.astype(jnp.bfloat16), value_rows, preferred_element_type=jnp.float32
                )
                weighted = weighted * factor + result[:, :HD]
                total = total * factor + result[:, HD:]
                best = new_best
            write(rows, total, weighted)
            copy = out_copy(index, rows)
            copy.start()
            copy.wait()
            return unused

        lax.fori_loop(0, len(blocks), visit, 0)


def shards(queries, suffix_kv, prompt_kv, lengths):
    slots, width = queries.shape
    heads = width // HD
    loop_size = lax.axis_size("loop")
    own = prompt_kv[:, 0, :]
    suffix = suffix_kv[:, 0, :]
    shard_rows = own.shape[0]

    in_hbm = pl.BlockSpec(memory_space=pltpu.HBM)
    in_vmem = pl.BlockSpec(memory_space=pltpu.VMEM)
    state = jax.ShapeDtypeStruct((slots, width), jnp.float32)

    cost = pl.CostEstimate(flops=1, bytes_accessed=1, transcendentals=0)

    routed = loop_size >= FOUR and loop_size & (loop_size - 1) == 0

    def send(shard, route):
        hops = []
        for i in range(loop_size):
            for core in range(2):
                to, to_core = route(i, core)
                hops.append((2 * i + core, 2 * to + to_core))
        return lax.ppermute(shard, ("loop", "pair"), hops)

    def routed_by(table):
        def route(i, core):
            to, to_core = table[i % FOUR][core]
            return i - i % FOUR + to, to_core

        return route

    first_route = routed_by(
        [((1, 1), (3, 1)), ((3, 0), (2, 0)), ((1, 0), (0, 0)), ((2, 1), (0, 1))]
    )
    second_route = routed_by(
        [((0, 1), (2, 1)), ((1, 1), (0, 0)), ((3, 0), (2, 0)), ((3, 1), (1, 0))]
    )

    hbm = [pltpu.with_memory_space_constraint(x, pltpu.HBM) for x in (lengths, queries, suffix, own)]
    buffers = [
        jax.ShapeDtypeStruct(queries.shape, queries.dtype),
        jax.ShapeDtypeStruct(suffix.shape, suffix.dtype),
        jax.ShapeDtypeStruct(own.shape, own.dtype),
        jax.ShapeDtypeStruct((slots, HD), jnp.int32),
    ]
    load_scratch = [
        pltpu.SMEM(lengths.shape, lengths.dtype),
        pltpu.SemaphoreType.DMA((2 + 2 * len(load_blocks(slots)),)),
    ]
    loaded = pl.pallas_call(
        prelude_stage,
        name="prelude_stage",
        out_shape=buffers,
        in_specs=[in_hbm] * 4,
        out_specs=[in_vmem] * 4,
        scratch_shapes=load_scratch,
        compiler_params=pltpu.CompilerParams(vmem_limit_bytes=8 * 2**20),
        cost_estimate=cost,
    )(*hbm)
    own, loaded = lax.optimization_barrier((own, loaded))
    if routed:
        early = [
            send(own, lambda i, core, step=step: (i ^ (step + core), 1 - core))
            for step in range(FOUR, loop_size, 2)
        ]
        early.append(send(own, first_route))
        final = send(own, second_route)
    else:
        early = [
            send(own, lambda i, core, step=step: ((i + step) % loop_size, core))
            for step in range(1, loop_size)
        ]
        final = early.pop()
    best, total, weighted, queries, *unused = pl.pallas_call(
        local_stage,
        name="local_stage",
        out_shape=[state] * 3 + buffers,
        in_specs=[in_hbm] * 4 + [in_vmem] * 4,
        out_specs=[in_vmem] * 7,
        scratch_shapes=load_scratch,
        input_output_aliases={4 + i: 3 + i for i in range(4)},
        compiler_params=pltpu.CompilerParams(vmem_limit_bytes=24 * 2**20),
        cost_estimate=cost,
    )(*hbm, *loaded)

    def add_shards(total, weighted, shards_now):
        if not shards_now:
            return total, weighted
        return pl.pallas_call(
            add_stage,
            name="add_stage",
            out_shape=[state] * 2,
            in_specs=[in_vmem] * (4 + len(shards_now)),
            out_specs=[in_vmem] * 2,
            compiler_params=pltpu.CompilerParams(vmem_limit_bytes=24 * 2**20),
            cost_estimate=cost,
        )(queries, best, total, weighted, *shards_now)

    def swapped(shard):
        return send(shard, lambda i, core: (i, 1 - core))

    early, best = lax.optimization_barrier((early, best))
    early_swapped = [swapped(shard) for shard in early] if routed else []
    new_total, new_weighted = add_shards(total, weighted, early)
    final, new_total = lax.optimization_barrier((final, new_total))
    final_swapped = swapped(final) if routed else final
    new_total, new_weighted = add_shards(new_total, new_weighted, early_swapped)
    last_inputs = (queries, best, total, weighted, new_total, new_weighted)
    last_inputs += (*early[:-1], *early_swapped[:-1], *early[-1:], *early_swapped[-1:])
    last_inputs += (final, final_swapped)
    return pl.pallas_call(
        last_stage,
        name="last_stage",
        out_shape=jax.ShapeDtypeStruct((slots, width), jnp.bfloat16),
        in_specs=[in_vmem] * len(last_inputs),
        out_specs=in_hbm,
        scratch_shapes=[
            pltpu.VMEM((slots, width), jnp.bfloat16),
            pltpu.SemaphoreType.DMA((len(row_blocks(slots, 80)),)),
        ],
        compiler_params=pltpu.CompilerParams(vmem_limit_bytes=32 * 2**20),
        cost_estimate=cost,
    )(*last_inputs)


def solution(mesh):
    placed = (
        P(("groups", "loop"), ("heads", "pair")),
        P(("groups", "loop"), "heads", None),
        P(("groups", "loop"), "heads", None),
        P("groups"),
    )
    return jax.shard_map(
        shards,
        mesh=mesh,
        in_specs=placed,
        out_specs=P(("groups", "loop"), ("heads", "pair")),
        check_vma=False,
    )
```

```python
import functools
import math

import jax
import jax.numpy as jnp
from jax import lax
from jax.experimental import pallas as pl
from jax.experimental.pallas import tpu as pltpu
from jax.sharding import PartitionSpec as P

HD = 128
AG_DEV = 2
MAXLEN = 320
BLK = 128
FOUR = 4

masked_score = -1e30
empty_best = 1e30
total_limit = 2.0**100
score_scale = math.log2(math.e) / math.sqrt(HD)


def scores_of(query_rows, key_rows):
    return (
        lax.dot_general(
            query_rows, key_rows, (((1,), (1,)), ((), ())), preferred_element_type=jnp.float32
        )
        * score_scale
    )


def with_ones(value_rows):
    return jnp.concatenate([value_rows, jnp.ones_like(value_rows)], axis=1)


def stacked(ref, rows, head_count):
    return jnp.concatenate([ref[rows, h * HD : (h + 1) * HD] for h in range(head_count)], axis=0)


def unstack(ref, rows, head_count, value):
    count = value.shape[0] // head_count
    for h in range(head_count):
        ref[rows, h * HD : (h + 1) * HD] = value[h * count : (h + 1) * count]


def widen(row_value, width):
    return jnp.concatenate([row_value] * (width // HD), axis=1)


def place():
    return lax.rem(lax.axis_index("loop"), FOUR), lax.axis_index("pair")


def load_blocks(count):
    return [pl.ds(first, BLK) for first in range(0, count, BLK)]


def load(
    lengths_hbm,
    query_hbm,
    suffix_hbm,
    own_hbm,
    query_ref,
    suffix_ref,
    own_ref,
    first_ref,
    lengths_ref,
    sems,
):
    pairs = [(lengths_hbm, lengths_ref), (own_hbm, own_ref)]
    for source, target in ((query_hbm, query_ref), (suffix_hbm, suffix_ref)):
        for rows in load_blocks(target.shape[0]):
            pairs.append((source.at[rows], target.at[rows]))
    copies = [
        pltpu.make_async_copy(source, target, sems.at[i])
        for i, (source, target) in enumerate(pairs)
    ]
    for copy in copies:
        copy.start()
    copies[0].wait()
    slots = query_ref.shape[0]
    position = lax.axis_index("loop")
    row_at = lax.broadcasted_iota(jnp.int32, first_ref.shape, 0)
    first = jnp.zeros_like(row_at)
    agent_end = 0
    for agent in range(AG_DEV):
        agent_end = agent_end + lengths_ref[position * AG_DEV + agent]
        first = jnp.where(row_at >= agent_end, agent_end if agent + 1 < AG_DEV else slots, first)
    first_ref[...] = first
    for copy in copies[1:]:
        copy.wait()


def prelude_stage(*refs):
    @pl.when(is_first_chip())
    def ahead():
        load(*refs)


def local_stage(*refs):
    sources, (best_ref, total_ref, sum_ref), loaded, scratch = (
        refs[:4],
        refs[8:11],
        refs[11:15],
        refs[15:],
    )
    query_ref, suffix_ref, own_ref, first_ref = loaded

    @pl.when(jnp.logical_not(is_first_chip()))
    def now():
        load(*sources, *loaded, *scratch)

    slots = query_ref.shape[0]
    heads = query_ref.shape[1] // HD
    own_keys = own_ref[:, :HD]
    own_values = with_ones(own_ref[:, HD:])
    window = BLK * ((MAXLEN + BLK - 2) // BLK) + BLK
    for block in range(slots // BLK):
        stop = (block + 1) * BLK
        start = max(0, stop - window)
        rows = slice(block * BLK, stop)
        row_at = block * BLK + lax.broadcasted_iota(jnp.int32, (BLK, stop - start), 0)
        key_at = start + lax.broadcasted_iota(jnp.int32, (BLK, stop - start), 1)
        first = first_ref[rows]
        allowed = (key_at <= row_at) & (key_at >= widen(first, stop - start))
        queries = stacked(query_ref, rows, heads)
        own_scores = scores_of(queries, own_keys)
        suffix_scores = jnp.where(
            jnp.concatenate([allowed] * heads, axis=0),
            scores_of(queries, suffix_ref[start:stop, :HD]),
            masked_score,
        )
        best = jnp.maximum(
            jnp.max(own_scores, axis=1, keepdims=True),
            jnp.max(suffix_scores, axis=1, keepdims=True),
        )
        own_weights = jnp.exp2(own_scores - best).astype(jnp.bfloat16)
        suffix_weights = jnp.exp2(suffix_scores - best).astype(jnp.bfloat16)
        result = jnp.dot(own_weights, own_values, preferred_element_type=jnp.float32)
        result = result + jnp.dot(
            suffix_weights,
            with_ones(suffix_ref[start:stop, HD:]),
            preferred_element_type=jnp.float32,
        )
        live = jnp.concatenate([first < slots] * heads, axis=0)
        unstack(best_ref, rows, heads, jnp.where(live, best, empty_best))
        unstack(sum_ref, rows, heads, jnp.where(live, result[:, :HD], 0.0))
        unstack(total_ref, rows, heads, jnp.where(live, result[:, HD:], 1.0))


def staged(blocks, start, finish):
    coming = start(blocks[0])
    for index, rows in enumerate(blocks):
        now = coming
        if index + 1 < len(blocks):
            coming = start(blocks[index + 1])
        finish(index, rows, now)


def row_blocks(count, largest):
    step = next(size for size in (largest, 128, 16, count) if count % size == 0)
    return [slice(first, first + step) for first in range(0, count, step)]


def is_first_chip():
    return lax.axis_index("groups") + lax.axis_index("loop") + lax.axis_index("heads") == 0


def penalty(is_there):
    return jnp.where(is_there, 0.0, empty_best)


def add_stage(by_swap, *refs):
    query_ref, best_ref, total_ref, sum_ref = refs[:4]
    shard_refs = refs[4:-2]
    total_out, sum_out = refs[-2:]
    heads = query_ref.shape[1] // HD
    shard = jnp.concatenate([ref[...] for ref in shard_refs], axis=0)
    key_rows, value_rows = shard[:, :HD], with_ones(shard[:, HD:])
    extra = None
    if by_swap is not None:
        position, core = place()
        extra = penalty((position != 1) | (core == int(by_swap)))

    def start(rows):
        return scores_of(stacked(query_ref, rows, heads), key_rows)

    def finish(index, rows, scores):
        best = stacked(best_ref, rows, heads)
        if extra is None:
            points = widen(best, scores.shape[1])
        else:
            held = shard_refs[-1].shape[0]
            points = [best] * ((scores.shape[1] - held) // HD) + [best + extra] * (held // HD)
            points = jnp.concatenate(points, axis=1)
        weights = jnp.exp2(scores - points).astype(jnp.bfloat16)
        result = jnp.dot(weights, value_rows, preferred_element_type=jnp.float32)
        unstack(total_out, rows, heads, stacked(total_ref, rows, heads) + result[:, HD:])
        unstack(sum_out, rows, heads, stacked(sum_ref, rows, heads) + result[:, :HD])

    staged(row_blocks(query_ref.shape[0], 160), start, finish)


def last_stage(routed, *refs):
    query_ref, best_ref, old_total_ref, old_sum_ref, total_ref, sum_ref = refs[:6]
    earlier_refs, refs = refs[6:-6], refs[-6:]
    direct_ref, swapped_ref, out_hbm, out_ref, trusted_ref, out_sems = refs
    heads = query_ref.shape[1] // HD
    blocks = row_blocks(query_ref.shape[0], 160)
    position, core = place()
    takes_both = (position == 1) & routed
    is_direct = core == jnp.where(position == 0, 0, 1)

    def out_copy(index, rows):
        return pltpu.make_async_copy(out_ref.at[rows], out_hbm.at[rows], out_sems.at[index])

    def write(rows, total, weighted):
        inverse = pl.reciprocal(total, approx=True)
        inverse = inverse * (2.0 - total * inverse)
        unstack(out_ref, rows, heads, (weighted * inverse).astype(jnp.bfloat16))

    def process(shard):
        trusted = [jnp.full((8, HD), True)]
        key_rows, value_rows = shard[:, :HD], with_ones(shard[:, HD:])

        def start(rows):
            return scores_of(stacked(query_ref, rows, heads), key_rows)

        def finish(index, rows, scores):
            best = stacked(best_ref, rows, heads)
            weights = jnp.exp2(scores - widen(best, scores.shape[1])).astype(jnp.bfloat16)
            result = jnp.dot(weights, value_rows, preferred_element_type=jnp.float32)
            total = stacked(total_ref, rows, heads) + result[:, HD:]
            weighted = stacked(sum_ref, rows, heads) + result[:, :HD]
            good = (total < total_limit).reshape(total.shape[0] // 8, 8, HD)
            trusted[0] = trusted[0] & jnp.all(good, axis=0)
            write(rows, total, weighted)
            out_copy(index, rows).start()

        staged(blocks, start, finish)
        trusted_ref[0] = jnp.all(trusted[0]).astype(jnp.int32)
        for index, rows in enumerate(blocks):
            out_copy(index, rows).wait()

    @pl.when(jnp.logical_not(takes_both))
    def one_shard():
        process(jnp.where(is_direct, direct_ref[...], swapped_ref[...]))

    @pl.when(takes_both)
    def two_shards():
        process(jnp.concatenate([direct_ref[...], swapped_ref[...]], axis=0))

    @pl.when(trusted_ref[0] == 0)
    def exact_maximum():
        size = query_ref.shape[0] // len(blocks)
        counted = [(ref, 0.0) for ref in earlier_refs]
        if routed:
            counted[-2:] = [
                (ref, penalty((position != 1) | (core == by_swap)))
                for by_swap, ref in enumerate(earlier_refs[-2:])
            ]
        counted += [
            (direct_ref, penalty(takes_both | is_direct)),
            (swapped_ref, penalty(takes_both | jnp.logical_not(is_direct))),
        ]

        def visit(index, unused):
            rows = pl.ds(pl.multiple_of(index * size, size), size)
            queries = stacked(query_ref, rows, heads)
            best = stacked(best_ref, rows, heads)
            weighted = stacked(old_sum_ref, rows, heads)
            total = stacked(old_total_ref, rows, heads)
            for shard_ref, extra in counted:
                key_rows, value_rows = shard_ref[:, :HD], with_ones(shard_ref[:, HD:])
                scores = scores_of(queries, key_rows) - extra
                new_best = jnp.maximum(best, jnp.max(scores, axis=1, keepdims=True))
                factor = jnp.exp2(best - new_best)
                weights = jnp.exp2(scores - widen(new_best, scores.shape[1]))
                result = jnp.dot(
                    weights.astype(jnp.bfloat16), value_rows, preferred_element_type=jnp.float32
                )
                weighted = weighted * factor + result[:, :HD]
                total = total * factor + result[:, HD:]
                best = new_best
            write(rows, total, weighted)
            copy = out_copy(index, rows)
            copy.start()
            copy.wait()
            return unused

        lax.fori_loop(0, len(blocks), visit, 0)


def shards(queries, suffix_kv, prompt_kv, lengths):
    slots, width = queries.shape
    heads = width // HD
    loop_size = lax.axis_size("loop")
    own = prompt_kv[:, 0, :]
    suffix = suffix_kv[:, 0, :]
    shard_rows = own.shape[0]

    in_hbm = pl.BlockSpec(memory_space=pltpu.HBM)
    in_vmem = pl.BlockSpec(memory_space=pltpu.VMEM)
    state = jax.ShapeDtypeStruct((slots, width), jnp.float32)

    cost = pl.CostEstimate(flops=1, bytes_accessed=1, transcendentals=0)

    routed = loop_size >= FOUR and loop_size & (loop_size - 1) == 0

    def send(shard, route):
        hops = []
        for i in range(loop_size):
            for core in range(2):
                to, to_core = route(i, core)
                hops.append((2 * i + core, 2 * to + to_core))
        return lax.ppermute(shard, ("loop", "pair"), hops)

    def first_route(i, core):
        base = i - i % FOUR
        to, to_core = [((1, 0), (3, 1)), ((1, 1), (2, 0)), ((3, 0), (0, 0)), ((2, 1), (0, 1))][
            i % FOUR
        ][core]
        return base + to, to_core

    def second_route(i, core):
        base = i - i % FOUR
        to, to_core = [((0, 1), (2, 1)), ((0, 0), (3, 1)), ((3, 0), (1, 0)), ((2, 0), (1, 1))][
            i % FOUR
        ][core]
        return base + to, to_core

    hbm = [pltpu.with_memory_space_constraint(x, pltpu.HBM) for x in (lengths, queries, suffix, own)]
    buffers = [
        jax.ShapeDtypeStruct(queries.shape, queries.dtype),
        jax.ShapeDtypeStruct(suffix.shape, suffix.dtype),
        jax.ShapeDtypeStruct(own.shape, own.dtype),
        jax.ShapeDtypeStruct((slots, HD), jnp.int32),
    ]
    load_scratch = [
        pltpu.SMEM(lengths.shape, lengths.dtype),
        pltpu.SemaphoreType.DMA((2 + 2 * len(load_blocks(slots)),)),
    ]
    loaded = pl.pallas_call(
        prelude_stage,
        name="prelude_stage",
        out_shape=buffers,
        in_specs=[in_hbm] * 4,
        out_specs=[in_vmem] * 4,
        scratch_shapes=load_scratch,
        compiler_params=pltpu.CompilerParams(vmem_limit_bytes=8 * 2**20),
        cost_estimate=cost,
    )(*hbm)
    own, loaded = lax.optimization_barrier((own, loaded))
    if routed:
        early = [
            send(own, lambda i, core, step=step: (i ^ (step + core), 1 - core))
            for step in range(FOUR, loop_size, 2)
        ]
        early.append(send(own, first_route))
        final = send(own, second_route)
    else:
        early = [
            send(own, lambda i, core, step=step: ((i + step) % loop_size, core))
            for step in range(1, loop_size)
        ]
        final = early.pop()
    best, total, weighted, queries, *unused = pl.pallas_call(
        local_stage,
        name="local_stage",
        out_shape=[state] * 3 + buffers,
        in_specs=[in_hbm] * 4 + [in_vmem] * 4,
        out_specs=[in_vmem] * 7,
        scratch_shapes=load_scratch,
        input_output_aliases={4 + i: 3 + i for i in range(4)},
        compiler_params=pltpu.CompilerParams(vmem_limit_bytes=24 * 2**20),
        cost_estimate=cost,
    )(*hbm, *loaded)

    def add_shards(total, weighted, shards_now, by_swap):
        if not shards_now:
            return total, weighted
        return pl.pallas_call(
            functools.partial(add_stage, by_swap if routed else None),
            name="add_stage",
            out_shape=[state] * 2,
            in_specs=[in_vmem] * (4 + len(shards_now)),
            out_specs=[in_vmem] * 2,
            compiler_params=pltpu.CompilerParams(vmem_limit_bytes=24 * 2**20),
            cost_estimate=cost,
        )(queries, best, total, weighted, *shards_now)

    def swapped(shard):
        return send(shard, lambda i, core: (i, 1 - core))

    early, best = lax.optimization_barrier((early, best))
    early_swapped = [swapped(shard) for shard in early] if routed else []
    new_total, new_weighted = add_shards(total, weighted, early, False)
    final, new_total = lax.optimization_barrier((final, new_total))
    final_swapped = swapped(final) if routed else final
    new_total, new_weighted = add_shards(new_total, new_weighted, early_swapped, True)
    last_inputs = (queries, best, total, weighted, new_total, new_weighted)
    last_inputs += (*early[:-1], *early_swapped[:-1], *early[-1:], *early_swapped[-1:])
    last_inputs += (final, final_swapped)
    return pl.pallas_call(
        functools.partial(last_stage, routed),
        name="last_stage",
        out_shape=jax.ShapeDtypeStruct((slots, width), jnp.bfloat16),
        in_specs=[in_vmem] * len(last_inputs),
        out_specs=in_hbm,
        scratch_shapes=[
            pltpu.VMEM((slots, width), jnp.bfloat16),
            pltpu.SMEM((1,), jnp.int32),
            pltpu.SemaphoreType.DMA((len(row_blocks(slots, 160)),)),
        ],
        compiler_params=pltpu.CompilerParams(vmem_limit_bytes=32 * 2**20),
        cost_estimate=cost,
    )(*last_inputs)


def solution(mesh):
    placed = (
        P(("groups", "loop"), ("heads", "pair")),
        P(("groups", "loop"), "heads", None),
        P(("groups", "loop"), "heads", None),
        P("groups"),
    )
    return jax.shard_map(
        shards,
        mesh=mesh,
        in_specs=placed,
        out_specs=P(("groups", "loop"), ("heads", "pair")),
        check_vma=False,
    )
```

```python
import functools
import math

import jax
import jax.numpy as jnp
from jax import lax
from jax.experimental import pallas as pl
from jax.experimental.pallas import tpu as pltpu
from jax.sharding import PartitionSpec as P

HD = 128
AG_DEV = 2
MAXLEN = 320
BLK = 128
FOUR = 4

masked_score = -1e30
empty_best = 1e30
total_limit = 2.0**100
score_scale = math.log2(math.e) / math.sqrt(HD)


def scores_of(query_rows, key_rows):
    return (
        lax.dot_general(
            query_rows, key_rows, (((1,), (1,)), ((), ())), preferred_element_type=jnp.float32
        )
        * score_scale
    )


def with_ones(value_rows):
    return jnp.concatenate([value_rows, jnp.ones_like(value_rows)], axis=1)


def stacked(ref, rows, head_count):
    return jnp.concatenate([ref[rows, h * HD : (h + 1) * HD] for h in range(head_count)], axis=0)


def unstack(ref, rows, head_count, value):
    count = value.shape[0] // head_count
    for h in range(head_count):
        ref[rows, h * HD : (h + 1) * HD] = value[h * count : (h + 1) * count]


def widen(row_value, width):
    return jnp.concatenate([row_value] * (width // HD), axis=1)


def place():
    return lax.rem(lax.axis_index("loop"), FOUR), lax.axis_index("pair")


def load_blocks(count):
    return [pl.ds(first, BLK) for first in range(0, count, BLK)]


def load(
    lengths_hbm,
    query_hbm,
    suffix_hbm,
    own_hbm,
    query_ref,
    suffix_ref,
    own_ref,
    first_ref,
    lengths_ref,
    sems,
):
    pairs = [(lengths_hbm, lengths_ref), (own_hbm, own_ref)]
    for source, target in ((query_hbm, query_ref), (suffix_hbm, suffix_ref)):
        for rows in load_blocks(target.shape[0]):
            pairs.append((source.at[rows], target.at[rows]))
    copies = [
        pltpu.make_async_copy(source, target, sems.at[i])
        for i, (source, target) in enumerate(pairs)
    ]
    for copy in copies:
        copy.start()
    copies[0].wait()
    slots = query_ref.shape[0]
    position = lax.axis_index("loop")
    row_at = lax.broadcasted_iota(jnp.int32, first_ref.shape, 0)
    first = jnp.zeros_like(row_at)
    agent_end = 0
    for agent in range(AG_DEV):
        agent_end = agent_end + lengths_ref[position * AG_DEV + agent]
        first = jnp.where(row_at >= agent_end, agent_end if agent + 1 < AG_DEV else slots, first)
    first_ref[...] = first
    for copy in copies[1:]:
        copy.wait()


def prelude_stage(*refs):
    @pl.when(is_first_chip())
    def ahead():
        load(*refs)


def local_stage(*refs):
    sources, (best_ref, total_ref, sum_ref), loaded, scratch = (
        refs[:4],
        refs[8:11],
        refs[11:15],
        refs[15:],
    )
    query_ref, suffix_ref, own_ref, first_ref = loaded

    @pl.when(jnp.logical_not(is_first_chip()))
    def now():
        load(*sources, *loaded, *scratch)

    slots = query_ref.shape[0]
    heads = query_ref.shape[1] // HD
    own_keys = own_ref[:, :HD]
    own_values = with_ones(own_ref[:, HD:])
    window = BLK * ((MAXLEN + BLK - 2) // BLK) + BLK
    for block in range(slots // BLK):
        stop = (block + 1) * BLK
        start = max(0, stop - window)
        rows = slice(block * BLK, stop)
        row_at = block * BLK + lax.broadcasted_iota(jnp.int32, (BLK, stop - start), 0)
        key_at = start + lax.broadcasted_iota(jnp.int32, (BLK, stop - start), 1)
        first = first_ref[rows]
        allowed = (key_at <= row_at) & (key_at >= widen(first, stop - start))
        queries = stacked(query_ref, rows, heads)
        own_scores = scores_of(queries, own_keys)
        suffix_scores = jnp.where(
            jnp.concatenate([allowed] * heads, axis=0),
            scores_of(queries, suffix_ref[start:stop, :HD]),
            masked_score,
        )
        best = jnp.maximum(
            jnp.max(own_scores, axis=1, keepdims=True),
            jnp.max(suffix_scores, axis=1, keepdims=True),
        )
        own_weights = jnp.exp2(own_scores - best).astype(jnp.bfloat16)
        suffix_weights = jnp.exp2(suffix_scores - best).astype(jnp.bfloat16)
        result = jnp.dot(own_weights, own_values, preferred_element_type=jnp.float32)
        result = result + jnp.dot(
            suffix_weights,
            with_ones(suffix_ref[start:stop, HD:]),
            preferred_element_type=jnp.float32,
        )
        live = jnp.concatenate([first < slots] * heads, axis=0)
        unstack(best_ref, rows, heads, jnp.where(live, best, empty_best))
        unstack(sum_ref, rows, heads, jnp.where(live, result[:, :HD], 0.0))
        unstack(total_ref, rows, heads, jnp.where(live, result[:, HD:], 1.0))


def staged(blocks, start, finish):
    coming = start(blocks[0])
    for index, rows in enumerate(blocks):
        now = coming
        if index + 1 < len(blocks):
            coming = start(blocks[index + 1])
        finish(index, rows, now)


def row_blocks(count, largest):
    step = next(size for size in (largest, 128, 16, count) if count % size == 0)
    return [slice(first, first + step) for first in range(0, count, step)]


def is_first_chip():
    return lax.axis_index("groups") + lax.axis_index("loop") + lax.axis_index("heads") == 0


def penalty(is_there):
    return jnp.where(is_there, 0.0, empty_best)


def add_stage(by_swap, *refs):
    query_ref, best_ref, total_ref, sum_ref = refs[:4]
    shard_refs = refs[4:-2]
    total_out, sum_out = refs[-2:]
    heads = query_ref.shape[1] // HD
    shard = jnp.concatenate([ref[...] for ref in shard_refs], axis=0)
    key_rows, value_rows = shard[:, :HD], with_ones(shard[:, HD:])
    extra = None
    if by_swap is not None:
        position, core = place()
        extra = penalty((position != 1) | (core == int(by_swap)))

    def start(rows):
        return scores_of(stacked(query_ref, rows, heads), key_rows)

    def finish(index, rows, scores):
        best = stacked(best_ref, rows, heads)
        if extra is None:
            points = widen(best, scores.shape[1])
        else:
            held = shard_refs[-1].shape[0]
            points = [best] * ((scores.shape[1] - held) // HD) + [best + extra] * (held // HD)
            points = jnp.concatenate(points, axis=1)
        weights = jnp.exp2(scores - points).astype(jnp.bfloat16)
        result = jnp.dot(weights, value_rows, preferred_element_type=jnp.float32)
        unstack(total_out, rows, heads, stacked(total_ref, rows, heads) + result[:, HD:])
        unstack(sum_out, rows, heads, stacked(sum_ref, rows, heads) + result[:, :HD])

    staged(row_blocks(query_ref.shape[0], 80), start, finish)


def last_stage(routed, *refs):
    query_ref, best_ref, old_total_ref, old_sum_ref, total_ref, sum_ref = refs[:6]
    earlier_refs, refs = refs[6:-6], refs[-6:]
    direct_ref, swapped_ref, out_hbm, out_ref, trusted_ref, out_sems = refs
    heads = query_ref.shape[1] // HD
    blocks = row_blocks(query_ref.shape[0], 80)
    position, core = place()
    takes_both = (position == 1) & routed
    is_direct = core == jnp.where(position == 0, 0, 1)

    def out_copy(index, rows):
        return pltpu.make_async_copy(out_ref.at[rows], out_hbm.at[rows], out_sems.at[index])

    def write(rows, total, weighted):
        inverse = pl.reciprocal(total, approx=True)
        inverse = inverse * (2.0 - total * inverse)
        unstack(out_ref, rows, heads, (weighted * inverse).astype(jnp.bfloat16))

    def process(shard):
        trusted = [jnp.full((8, HD), True)]
        key_rows, value_rows = shard[:, :HD], with_ones(shard[:, HD:])

        def start(rows):
            return scores_of(stacked(query_ref, rows, heads), key_rows)

        def finish(index, rows, scores):
            best = stacked(best_ref, rows, heads)
            weights = jnp.exp2(scores - widen(best, scores.shape[1])).astype(jnp.bfloat16)
            result = jnp.dot(weights, value_rows, preferred_element_type=jnp.float32)
            total = stacked(total_ref, rows, heads) + result[:, HD:]
            weighted = stacked(sum_ref, rows, heads) + result[:, :HD]
            good = (total < total_limit).reshape(total.shape[0] // 8, 8, HD)
            trusted[0] = trusted[0] & jnp.all(good, axis=0)
            write(rows, total, weighted)
            out_copy(index, rows).start()

        staged(blocks, start, finish)
        trusted_ref[0] = jnp.all(trusted[0]).astype(jnp.int32)
        for index, rows in enumerate(blocks):
            out_copy(index, rows).wait()

    @pl.when(jnp.logical_not(takes_both))
    def one_shard():
        process(jnp.where(is_direct, direct_ref[...], swapped_ref[...]))

    @pl.when(takes_both)
    def two_shards():
        process(jnp.concatenate([direct_ref[...], swapped_ref[...]], axis=0))

    @pl.when(trusted_ref[0] == 0)
    def exact_maximum():
        size = query_ref.shape[0] // len(blocks)
        counted = [(ref, 0.0) for ref in earlier_refs]
        if routed:
            counted[-2:] = [
                (ref, penalty((position != 1) | (core == by_swap)))
                for by_swap, ref in enumerate(earlier_refs[-2:])
            ]
        counted += [
            (direct_ref, penalty(takes_both | is_direct)),
            (swapped_ref, penalty(takes_both | jnp.logical_not(is_direct))),
        ]

        def visit(index, unused):
            rows = pl.ds(pl.multiple_of(index * size, size), size)
            queries = stacked(query_ref, rows, heads)
            best = stacked(best_ref, rows, heads)
            weighted = stacked(old_sum_ref, rows, heads)
            total = stacked(old_total_ref, rows, heads)
            for shard_ref, extra in counted:
                key_rows, value_rows = shard_ref[:, :HD], with_ones(shard_ref[:, HD:])
                scores = scores_of(queries, key_rows) - extra
                new_best = jnp.maximum(best, jnp.max(scores, axis=1, keepdims=True))
                factor = jnp.exp2(best - new_best)
                weights = jnp.exp2(scores - widen(new_best, scores.shape[1]))
                result = jnp.dot(
                    weights.astype(jnp.bfloat16), value_rows, preferred_element_type=jnp.float32
                )
                weighted = weighted * factor + result[:, :HD]
                total = total * factor + result[:, HD:]
                best = new_best
            write(rows, total, weighted)
            copy = out_copy(index, rows)
            copy.start()
            copy.wait()
            return unused

        lax.fori_loop(0, len(blocks), visit, 0)


def shards(queries, suffix_kv, prompt_kv, lengths):
    slots, width = queries.shape
    heads = width // HD
    loop_size = lax.axis_size("loop")
    own = prompt_kv[:, 0, :]
    suffix = suffix_kv[:, 0, :]
    shard_rows = own.shape[0]

    in_hbm = pl.BlockSpec(memory_space=pltpu.HBM)
    in_vmem = pl.BlockSpec(memory_space=pltpu.VMEM)
    state = jax.ShapeDtypeStruct((slots, width), jnp.float32)

    cost = pl.CostEstimate(flops=1, bytes_accessed=1, transcendentals=0)

    routed = loop_size >= FOUR and loop_size & (loop_size - 1) == 0

    def send(shard, route):
        hops = []
        for i in range(loop_size):
            for core in range(2):
                to, to_core = route(i, core)
                hops.append((2 * i + core, 2 * to + to_core))
        return lax.ppermute(shard, ("loop", "pair"), hops)

    def first_route(i, core):
        base = i - i % FOUR
        to, to_core = [((1, 0), (3, 1)), ((1, 1), (2, 1)), ((3, 0), (0, 0)), ((2, 0), (0, 1))][
            i % FOUR
        ][core]
        return base + to, to_core

    def second_route(i, core):
        base = i - i % FOUR
        to, to_core = [((0, 1), (2, 1)), ((0, 0), (3, 1)), ((3, 0), (1, 0)), ((2, 0), (1, 1))][
            i % FOUR
        ][core]
        return base + to, to_core

    hbm = [pltpu.with_memory_space_constraint(x, pltpu.HBM) for x in (lengths, queries, suffix, own)]
    buffers = [
        jax.ShapeDtypeStruct(queries.shape, queries.dtype),
        jax.ShapeDtypeStruct(suffix.shape, suffix.dtype),
        jax.ShapeDtypeStruct(own.shape, own.dtype),
        jax.ShapeDtypeStruct((slots, HD), jnp.int32),
    ]
    load_scratch = [
        pltpu.SMEM(lengths.shape, lengths.dtype),
        pltpu.SemaphoreType.DMA((2 + 2 * len(load_blocks(slots)),)),
    ]
    loaded = pl.pallas_call(
        prelude_stage,
        name="prelude_stage",
        out_shape=buffers,
        in_specs=[in_hbm] * 4,
        out_specs=[in_vmem] * 4,
        scratch_shapes=load_scratch,
        compiler_params=pltpu.CompilerParams(vmem_limit_bytes=8 * 2**20),
        cost_estimate=cost,
    )(*hbm)
    own, loaded = lax.optimization_barrier((own, loaded))
    if routed:
        early = [
            send(own, lambda i, core, step=step: (i ^ (step + core), 1 - core))
            for step in range(FOUR, loop_size, 2)
        ]
        early.append(send(own, first_route))
        final = send(own, second_route)
    else:
        early = [
            send(own, lambda i, core, step=step: ((i + step) % loop_size, core))
            for step in range(1, loop_size)
        ]
        final = early.pop()
    best, total, weighted, queries, *unused = pl.pallas_call(
        local_stage,
        name="local_stage",
        out_shape=[state] * 3 + buffers,
        in_specs=[in_hbm] * 4 + [in_vmem] * 4,
        out_specs=[in_vmem] * 7,
        scratch_shapes=load_scratch,
        input_output_aliases={4 + i: 3 + i for i in range(4)},
        compiler_params=pltpu.CompilerParams(vmem_limit_bytes=24 * 2**20),
        cost_estimate=cost,
    )(*hbm, *loaded)

    def add_shards(total, weighted, shards_now, by_swap):
        if not shards_now:
            return total, weighted
        return pl.pallas_call(
            functools.partial(add_stage, by_swap if routed else None),
            name="add_stage",
            out_shape=[state] * 2,
            in_specs=[in_vmem] * (4 + len(shards_now)),
            out_specs=[in_vmem] * 2,
            compiler_params=pltpu.CompilerParams(vmem_limit_bytes=24 * 2**20),
            cost_estimate=cost,
        )(queries, best, total, weighted, *shards_now)

    def swapped(shard):
        return send(shard, lambda i, core: (i, 1 - core))

    early, best = lax.optimization_barrier((early, best))
    early_swapped = [swapped(shard) for shard in early] if routed else []
    new_total, new_weighted = add_shards(total, weighted, early, False)
    final, new_total = lax.optimization_barrier((final, new_total))
    final_swapped = swapped(final) if routed else final
    new_total, new_weighted = add_shards(new_total, new_weighted, early_swapped, True)
    last_inputs = (queries, best, total, weighted, new_total, new_weighted)
    last_inputs += (*early[:-1], *early_swapped[:-1], *early[-1:], *early_swapped[-1:])
    last_inputs += (final, final_swapped)
    return pl.pallas_call(
        functools.partial(last_stage, routed),
        name="last_stage",
        out_shape=jax.ShapeDtypeStruct((slots, width), jnp.bfloat16),
        in_specs=[in_vmem] * len(last_inputs),
        out_specs=in_hbm,
        scratch_shapes=[
            pltpu.VMEM((slots, width), jnp.bfloat16),
            pltpu.SMEM((1,), jnp.int32),
            pltpu.SemaphoreType.DMA((len(row_blocks(slots, 80)),)),
        ],
        compiler_params=pltpu.CompilerParams(vmem_limit_bytes=32 * 2**20),
        cost_estimate=cost,
    )(*last_inputs)


def solution(mesh):
    placed = (
        P(("groups", "loop"), ("heads", "pair")),
        P(("groups", "loop"), "heads", None),
        P(("groups", "loop"), "heads", None),
        P("groups"),
    )
    return jax.shard_map(
        shards,
        mesh=mesh,
        in_specs=placed,
        out_specs=P(("groups", "loop"), ("heads", "pair")),
        check_vma=False,
    )
```

```python
import functools
import math

import jax
import jax.numpy as jnp
from jax import lax
from jax.experimental import pallas as pl
from jax.experimental.pallas import tpu as pltpu
from jax.sharding import PartitionSpec as P

HD = 128
AG_DEV = 2
MAXLEN = 320
BLK = 128
FOUR = 4

masked_score = -1e30
empty_best = 1e30
total_limit = 2.0**100
score_scale = math.log2(math.e) / math.sqrt(HD)


def scores_of(query_rows, key_rows):
    return (
        lax.dot_general(
            query_rows, key_rows, (((1,), (1,)), ((), ())), preferred_element_type=jnp.float32
        )
        * score_scale
    )


def with_ones(value_rows):
    return jnp.concatenate([value_rows, jnp.ones_like(value_rows)], axis=1)


def stacked(ref, rows, head_count):
    return jnp.concatenate([ref[rows, h * HD : (h + 1) * HD] for h in range(head_count)], axis=0)


def unstack(ref, rows, head_count, value):
    count = value.shape[0] // head_count
    for h in range(head_count):
        ref[rows, h * HD : (h + 1) * HD] = value[h * count : (h + 1) * count]


def widen(row_value, width):
    return jnp.concatenate([row_value] * (width // HD), axis=1)


def place():
    return lax.rem(lax.axis_index("loop"), FOUR), lax.axis_index("pair")


def load_blocks(count):
    return [pl.ds(first, BLK) for first in range(0, count, BLK)]


def load(
    lengths_hbm,
    query_hbm,
    suffix_hbm,
    own_hbm,
    query_ref,
    suffix_ref,
    own_ref,
    first_ref,
    lengths_ref,
    sems,
):
    pairs = [(lengths_hbm, lengths_ref), (own_hbm, own_ref)]
    for source, target in ((query_hbm, query_ref), (suffix_hbm, suffix_ref)):
        for rows in load_blocks(target.shape[0]):
            pairs.append((source.at[rows], target.at[rows]))
    copies = [
        pltpu.make_async_copy(source, target, sems.at[i])
        for i, (source, target) in enumerate(pairs)
    ]
    for copy in copies:
        copy.start()
    copies[0].wait()
    slots = query_ref.shape[0]
    position = lax.axis_index("loop")
    row_at = lax.broadcasted_iota(jnp.int32, first_ref.shape, 0)
    first = jnp.zeros_like(row_at)
    agent_end = 0
    for agent in range(AG_DEV):
        agent_end = agent_end + lengths_ref[position * AG_DEV + agent]
        first = jnp.where(row_at >= agent_end, agent_end if agent + 1 < AG_DEV else slots, first)
    first_ref[...] = first
    for copy in copies[1:]:
        copy.wait()


def prelude_stage(*refs):
    @pl.when(is_first_chip())
    def ahead():
        load(*refs)


def local_stage(*refs):
    sources, (best_ref, total_ref, sum_ref), loaded, scratch = (
        refs[:4],
        refs[8:11],
        refs[11:15],
        refs[15:],
    )
    query_ref, suffix_ref, own_ref, first_ref = loaded

    @pl.when(jnp.logical_not(is_first_chip()))
    def now():
        load(*sources, *loaded, *scratch)

    slots = query_ref.shape[0]
    heads = query_ref.shape[1] // HD
    own_keys = own_ref[:, :HD]
    own_values = with_ones(own_ref[:, HD:])
    window = BLK * ((MAXLEN + BLK - 2) // BLK) + BLK
    for block in range(slots // BLK):
        stop = (block + 1) * BLK
        start = max(0, stop - window)
        rows = slice(block * BLK, stop)
        row_at = block * BLK + lax.broadcasted_iota(jnp.int32, (BLK, stop - start), 0)
        key_at = start + lax.broadcasted_iota(jnp.int32, (BLK, stop - start), 1)
        first = first_ref[rows]
        allowed = (key_at <= row_at) & (key_at >= widen(first, stop - start))
        queries = stacked(query_ref, rows, heads)
        own_scores = scores_of(queries, own_keys)
        suffix_scores = jnp.where(
            jnp.concatenate([allowed] * heads, axis=0),
            scores_of(queries, suffix_ref[start:stop, :HD]),
            masked_score,
        )
        best = jnp.maximum(
            jnp.max(own_scores, axis=1, keepdims=True),
            jnp.max(suffix_scores, axis=1, keepdims=True),
        )
        own_weights = jnp.exp2(own_scores - best).astype(jnp.bfloat16)
        suffix_weights = jnp.exp2(suffix_scores - best).astype(jnp.bfloat16)
        result = jnp.dot(own_weights, own_values, preferred_element_type=jnp.float32)
        result = result + jnp.dot(
            suffix_weights,
            with_ones(suffix_ref[start:stop, HD:]),
            preferred_element_type=jnp.float32,
        )
        live = jnp.concatenate([first < slots] * heads, axis=0)
        unstack(best_ref, rows, heads, jnp.where(live, best, empty_best))
        unstack(sum_ref, rows, heads, jnp.where(live, result[:, :HD], 0.0))
        unstack(total_ref, rows, heads, jnp.where(live, result[:, HD:], 1.0))


def staged(blocks, start, finish):
    coming = start(blocks[0])
    for index, rows in enumerate(blocks):
        now = coming
        if index + 1 < len(blocks):
            coming = start(blocks[index + 1])
        finish(index, rows, now)


def row_blocks(count, largest):
    step = next(size for size in (largest, 128, 16, count) if count % size == 0)
    return [slice(first, first + step) for first in range(0, count, step)]


def is_first_chip():
    return lax.axis_index("groups") + lax.axis_index("loop") + lax.axis_index("heads") == 0


def penalty(is_there):
    return jnp.where(is_there, 0.0, empty_best)


def add_stage(by_swap, *refs):
    query_ref, best_ref, total_ref, sum_ref = refs[:4]
    shard_refs = refs[4:-2]
    total_out, sum_out = refs[-2:]
    heads = query_ref.shape[1] // HD
    shard = jnp.concatenate([ref[...] for ref in shard_refs], axis=0)
    key_rows, value_rows = shard[:, :HD], with_ones(shard[:, HD:])
    extra = None
    if by_swap is not None:
        position, core = place()
        extra = penalty((position == 0) | (core == int(by_swap)))

    def start(rows):
        return scores_of(stacked(query_ref, rows, heads), key_rows)

    def finish(index, rows, scores):
        best = stacked(best_ref, rows, heads)
        if extra is None:
            points = widen(best, scores.shape[1])
        else:
            held = shard_refs[-1].shape[0]
            points = [best] * ((scores.shape[1] - held) // HD) + [best + extra] * (held // HD)
            points = jnp.concatenate(points, axis=1)
        weights = jnp.exp2(scores - points).astype(jnp.bfloat16)
        result = jnp.dot(weights, value_rows, preferred_element_type=jnp.float32)
        unstack(total_out, rows, heads, stacked(total_ref, rows, heads) + result[:, HD:])
        unstack(sum_out, rows, heads, stacked(sum_ref, rows, heads) + result[:, :HD])

    staged(row_blocks(query_ref.shape[0], 80), start, finish)


def last_stage(routed, *refs):
    query_ref, best_ref, old_total_ref, old_sum_ref, total_ref, sum_ref = refs[:6]
    earlier_refs, refs = refs[6:-6], refs[-6:]
    direct_ref, swapped_ref, out_hbm, out_ref, trusted_ref, out_sems = refs
    heads = query_ref.shape[1] // HD
    blocks = row_blocks(query_ref.shape[0], 80)
    position, core = place()
    takes_both = (position != 0) & routed
    is_direct = core == 0

    def out_copy(index, rows):
        return pltpu.make_async_copy(out_ref.at[rows], out_hbm.at[rows], out_sems.at[index])

    def write(rows, total, weighted):
        inverse = pl.reciprocal(total, approx=True)
        inverse = inverse * (2.0 - total * inverse)
        unstack(out_ref, rows, heads, (weighted * inverse).astype(jnp.bfloat16))

    def process(shard):
        trusted = [jnp.full((8, HD), True)]
        key_rows, value_rows = shard[:, :HD], with_ones(shard[:, HD:])

        def start(rows):
            return scores_of(stacked(query_ref, rows, heads), key_rows)

        def finish(index, rows, scores):
            best = stacked(best_ref, rows, heads)
            weights = jnp.exp2(scores - widen(best, scores.shape[1])).astype(jnp.bfloat16)
            result = jnp.dot(weights, value_rows, preferred_element_type=jnp.float32)
            total = stacked(total_ref, rows, heads) + result[:, HD:]
            weighted = stacked(sum_ref, rows, heads) + result[:, :HD]
            good = (total < total_limit).reshape(total.shape[0] // 8, 8, HD)
            trusted[0] = trusted[0] & jnp.all(good, axis=0)
            write(rows, total, weighted)
            out_copy(index, rows).start()

        staged(blocks, start, finish)
        trusted_ref[0] = jnp.all(trusted[0]).astype(jnp.int32)
        for index, rows in enumerate(blocks):
            out_copy(index, rows).wait()

    @pl.when(jnp.logical_not(takes_both))
    def one_shard():
        process(jnp.where(is_direct, direct_ref[...], swapped_ref[...]))

    @pl.when(takes_both)
    def two_shards():
        process(jnp.concatenate([direct_ref[...], swapped_ref[...]], axis=0))

    @pl.when(trusted_ref[0] == 0)
    def exact_maximum():
        size = query_ref.shape[0] // len(blocks)
        counted = [(ref, 0.0) for ref in earlier_refs]
        if routed:
            counted[-2:] = [
                (ref, penalty((position == 0) | (core == by_swap)))
                for by_swap, ref in enumerate(earlier_refs[-2:])
            ]
        counted += [
            (direct_ref, penalty(takes_both | is_direct)),
            (swapped_ref, penalty(takes_both | jnp.logical_not(is_direct))),
        ]

        def visit(index, unused):
            rows = pl.ds(pl.multiple_of(index * size, size), size)
            queries = stacked(query_ref, rows, heads)
            best = stacked(best_ref, rows, heads)
            weighted = stacked(old_sum_ref, rows, heads)
            total = stacked(old_total_ref, rows, heads)
            for shard_ref, extra in counted:
                key_rows, value_rows = shard_ref[:, :HD], with_ones(shard_ref[:, HD:])
                scores = scores_of(queries, key_rows) - extra
                new_best = jnp.maximum(best, jnp.max(scores, axis=1, keepdims=True))
                factor = jnp.exp2(best - new_best)
                weights = jnp.exp2(scores - widen(new_best, scores.shape[1]))
                result = jnp.dot(
                    weights.astype(jnp.bfloat16), value_rows, preferred_element_type=jnp.float32
                )
                weighted = weighted * factor + result[:, :HD]
                total = total * factor + result[:, HD:]
                best = new_best
            write(rows, total, weighted)
            copy = out_copy(index, rows)
            copy.start()
            copy.wait()
            return unused

        lax.fori_loop(0, len(blocks), visit, 0)


def shards(queries, suffix_kv, prompt_kv, lengths):
    slots, width = queries.shape
    heads = width // HD
    loop_size = lax.axis_size("loop")
    own = prompt_kv[:, 0, :]
    suffix = suffix_kv[:, 0, :]
    shard_rows = own.shape[0]

    in_hbm = pl.BlockSpec(memory_space=pltpu.HBM)
    in_vmem = pl.BlockSpec(memory_space=pltpu.VMEM)
    state = jax.ShapeDtypeStruct((slots, width), jnp.float32)

    cost = pl.CostEstimate(flops=1, bytes_accessed=1, transcendentals=0)

    routed = loop_size >= FOUR and loop_size & (loop_size - 1) == 0

    def send(shard, route):
        hops = []
        for i in range(loop_size):
            for core in range(2):
                to, to_core = route(i, core)
                hops.append((2 * i + core, 2 * to + to_core))
        return lax.ppermute(shard, ("loop", "pair"), hops)

    def first_route(i, core):
        base = i - i % FOUR
        to, to_core = [((1, 0), (3, 0)), ((1, 1), (2, 0)), ((2, 1), (0, 0)), ((3, 1), (0, 1))][
            i % FOUR
        ][core]
        return base + to, to_core

    def second_route(i, core):
        base = i - i % FOUR
        to, to_core = [((0, 1), (2, 1)), ((0, 0), (3, 1)), ((3, 0), (1, 0)), ((2, 0), (1, 1))][
            i % FOUR
        ][core]
        return base + to, to_core

    hbm = [pltpu.with_memory_space_constraint(x, pltpu.HBM) for x in (lengths, queries, suffix, own)]
    buffers = [
        jax.ShapeDtypeStruct(queries.shape, queries.dtype),
        jax.ShapeDtypeStruct(suffix.shape, suffix.dtype),
        jax.ShapeDtypeStruct(own.shape, own.dtype),
        jax.ShapeDtypeStruct((slots, HD), jnp.int32),
    ]
    load_scratch = [
        pltpu.SMEM(lengths.shape, lengths.dtype),
        pltpu.SemaphoreType.DMA((2 + 2 * len(load_blocks(slots)),)),
    ]
    loaded = pl.pallas_call(
        prelude_stage,
        name="prelude_stage",
        out_shape=buffers,
        in_specs=[in_hbm] * 4,
        out_specs=[in_vmem] * 4,
        scratch_shapes=load_scratch,
        compiler_params=pltpu.CompilerParams(vmem_limit_bytes=8 * 2**20),
        cost_estimate=cost,
    )(*hbm)
    own, loaded = lax.optimization_barrier((own, loaded))
    if routed:
        early = [
            send(own, lambda i, core, step=step: (i ^ (step + core), 1 - core))
            for step in range(FOUR, loop_size, 2)
        ]
        early.append(send(own, first_route))
        final = send(own, second_route)
    else:
        early = [
            send(own, lambda i, core, step=step: ((i + step) % loop_size, core))
            for step in range(1, loop_size)
        ]
        final = early.pop()
    best, total, weighted, queries, *unused = pl.pallas_call(
        local_stage,
        name="local_stage",
        out_shape=[state] * 3 + buffers,
        in_specs=[in_hbm] * 4 + [in_vmem] * 4,
        out_specs=[in_vmem] * 7,
        scratch_shapes=load_scratch,
        input_output_aliases={4 + i: 3 + i for i in range(4)},
        compiler_params=pltpu.CompilerParams(vmem_limit_bytes=24 * 2**20),
        cost_estimate=cost,
    )(*hbm, *loaded)

    def add_shards(total, weighted, shards_now, by_swap):
        if not shards_now:
            return total, weighted
        return pl.pallas_call(
            functools.partial(add_stage, by_swap if routed else None),
            name="add_stage",
            out_shape=[state] * 2,
            in_specs=[in_vmem] * (4 + len(shards_now)),
            out_specs=[in_vmem] * 2,
            compiler_params=pltpu.CompilerParams(vmem_limit_bytes=24 * 2**20),
            cost_estimate=cost,
        )(queries, best, total, weighted, *shards_now)

    def swapped(shard):
        return send(shard, lambda i, core: (i, 1 - core))

    early, best = lax.optimization_barrier((early, best))
    early_swapped = [swapped(shard) for shard in early] if routed else []
    new_total, new_weighted = add_shards(total, weighted, early, False)
    final, new_total = lax.optimization_barrier((final, new_total))
    final_swapped = swapped(final) if routed else final
    new_total, new_weighted = add_shards(new_total, new_weighted, early_swapped, True)
    last_inputs = (queries, best, total, weighted, new_total, new_weighted)
    last_inputs += (*early[:-1], *early_swapped[:-1], *early[-1:], *early_swapped[-1:])
    last_inputs += (final, final_swapped)
    return pl.pallas_call(
        functools.partial(last_stage, routed),
        name="last_stage",
        out_shape=jax.ShapeDtypeStruct((slots, width), jnp.bfloat16),
        in_specs=[in_vmem] * len(last_inputs),
        out_specs=in_hbm,
        scratch_shapes=[
            pltpu.VMEM((slots, width), jnp.bfloat16),
            pltpu.SMEM((1,), jnp.int32),
            pltpu.SemaphoreType.DMA((len(row_blocks(slots, 80)),)),
        ],
        compiler_params=pltpu.CompilerParams(vmem_limit_bytes=32 * 2**20),
        cost_estimate=cost,
    )(*last_inputs)


def solution(mesh):
    placed = (
        P(("groups", "loop"), ("heads", "pair")),
        P(("groups", "loop"), "heads", None),
        P(("groups", "loop"), "heads", None),
        P("groups"),
    )
    return jax.shard_map(
        shards,
        mesh=mesh,
        in_specs=placed,
        out_specs=P(("groups", "loop"), ("heads", "pair")),
        check_vma=False,
    )
```

```python
import functools
import math

import jax
import jax.numpy as jnp
from jax import lax
from jax.experimental import pallas as pl
from jax.experimental.pallas import tpu as pltpu
from jax.sharding import PartitionSpec as P

HD = 128
AG_DEV = 2
MAXLEN = 320
BLK = 128
FOUR = 4

masked_score = -1e30
empty_best = 1e30
total_limit = 2.0**100
score_scale = math.log2(math.e) / math.sqrt(HD)


def scores_of(query_rows, key_rows):
    return (
        lax.dot_general(
            query_rows, key_rows, (((1,), (1,)), ((), ())), preferred_element_type=jnp.float32
        )
        * score_scale
    )


def with_ones(value_rows):
    return jnp.concatenate([value_rows, jnp.ones_like(value_rows)], axis=1)


def stacked(ref, rows, head_count):
    return jnp.concatenate([ref[rows, h * HD : (h + 1) * HD] for h in range(head_count)], axis=0)


def unstack(ref, rows, head_count, value):
    count = value.shape[0] // head_count
    for h in range(head_count):
        ref[rows, h * HD : (h + 1) * HD] = value[h * count : (h + 1) * count]


def widen(row_value, width):
    return jnp.concatenate([row_value] * (width // HD), axis=1)


def place():
    return lax.rem(lax.axis_index("loop"), FOUR), lax.axis_index("pair")


def load_blocks(count):
    return [pl.ds(first, BLK) for first in range(0, count, BLK)]


def load(
    lengths_hbm,
    query_hbm,
    suffix_hbm,
    own_hbm,
    query_ref,
    suffix_ref,
    own_ref,
    first_ref,
    lengths_ref,
    sems,
):
    pairs = [(lengths_hbm, lengths_ref), (own_hbm, own_ref)]
    for source, target in ((query_hbm, query_ref), (suffix_hbm, suffix_ref)):
        for rows in load_blocks(target.shape[0]):
            pairs.append((source.at[rows], target.at[rows]))
    copies = [
        pltpu.make_async_copy(source, target, sems.at[i])
        for i, (source, target) in enumerate(pairs)
    ]
    for copy in copies:
        copy.start()
    copies[0].wait()
    slots = query_ref.shape[0]
    position = lax.axis_index("loop")
    row_at = lax.broadcasted_iota(jnp.int32, first_ref.shape, 0)
    first = jnp.zeros_like(row_at)
    agent_end = 0
    for agent in range(AG_DEV):
        agent_end = agent_end + lengths_ref[position * AG_DEV + agent]
        first = jnp.where(row_at >= agent_end, agent_end if agent + 1 < AG_DEV else slots, first)
    first_ref[...] = first
    for copy in copies[1:]:
        copy.wait()


def prelude_stage(*refs):
    @pl.when(is_first_chip())
    def ahead():
        load(*refs)


def local_stage(*refs):
    sources, (best_ref, total_ref, sum_ref), loaded, scratch = (
        refs[:4],
        refs[8:11],
        refs[11:15],
        refs[15:],
    )
    query_ref, suffix_ref, own_ref, first_ref = loaded

    @pl.when(jnp.logical_not(is_first_chip()))
    def now():
        load(*sources, *loaded, *scratch)

    slots = query_ref.shape[0]
    heads = query_ref.shape[1] // HD
    own_keys = own_ref[:, :HD]
    own_values = with_ones(own_ref[:, HD:])
    window = BLK * ((MAXLEN + BLK - 2) // BLK) + BLK
    for block in range(slots // BLK):
        stop = (block + 1) * BLK
        start = max(0, stop - window)
        rows = slice(block * BLK, stop)
        row_at = block * BLK + lax.broadcasted_iota(jnp.int32, (BLK, stop - start), 0)
        key_at = start + lax.broadcasted_iota(jnp.int32, (BLK, stop - start), 1)
        first = first_ref[rows]
        allowed = (key_at <= row_at) & (key_at >= widen(first, stop - start))
        queries = stacked(query_ref, rows, heads)
        own_scores = scores_of(queries, own_keys)
        suffix_scores = jnp.where(
            jnp.concatenate([allowed] * heads, axis=0),
            scores_of(queries, suffix_ref[start:stop, :HD]),
            masked_score,
        )
        best = jnp.maximum(
            jnp.max(own_scores, axis=1, keepdims=True),
            jnp.max(suffix_scores, axis=1, keepdims=True),
        )
        own_weights = jnp.exp2(own_scores - best).astype(jnp.bfloat16)
        suffix_weights = jnp.exp2(suffix_scores - best).astype(jnp.bfloat16)
        result = jnp.dot(own_weights, own_values, preferred_element_type=jnp.float32)
        result = result + jnp.dot(
            suffix_weights,
            with_ones(suffix_ref[start:stop, HD:]),
            preferred_element_type=jnp.float32,
        )
        live = jnp.concatenate([first < slots] * heads, axis=0)
        unstack(best_ref, rows, heads, jnp.where(live, best, empty_best))
        unstack(sum_ref, rows, heads, jnp.where(live, result[:, :HD], 0.0))
        unstack(total_ref, rows, heads, jnp.where(live, result[:, HD:], 1.0))


def staged(blocks, start, finish):
    coming = start(blocks[0])
    for index, rows in enumerate(blocks):
        now = coming
        if index + 1 < len(blocks):
            coming = start(blocks[index + 1])
        finish(index, rows, now)


def row_blocks(count, largest):
    step = next(size for size in (largest, 128, 16, count) if count % size == 0)
    return [slice(first, first + step) for first in range(0, count, step)]


def is_first_chip():
    return lax.axis_index("groups") + lax.axis_index("loop") + lax.axis_index("heads") == 0


def penalty(is_there):
    return jnp.where(is_there, 0.0, empty_best)


def add_stage(by_swap, *refs):
    query_ref, best_ref, total_ref, sum_ref = refs[:4]
    shard_refs = refs[4:-2]
    total_out, sum_out = refs[-2:]
    heads = query_ref.shape[1] // HD
    shard = jnp.concatenate([ref[...] for ref in shard_refs], axis=0)
    key_rows, value_rows = shard[:, :HD], with_ones(shard[:, HD:])
    extra = None
    if by_swap is not None:
        position, core = place()
        extra = penalty((position == 0) | (core == int(by_swap)))

    def start(rows):
        return scores_of(stacked(query_ref, rows, heads), key_rows)

    def finish(index, rows, scores):
        best = stacked(best_ref, rows, heads)
        if extra is None:
            points = widen(best, scores.shape[1])
        else:
            held = shard_refs[-1].shape[0]
            points = [best] * ((scores.shape[1] - held) // HD) + [best + extra] * (held // HD)
            points = jnp.concatenate(points, axis=1)
        weights = jnp.exp2(scores - points).astype(jnp.bfloat16)
        result = jnp.dot(weights, value_rows, preferred_element_type=jnp.float32)
        unstack(total_out, rows, heads, stacked(total_ref, rows, heads) + result[:, HD:])
        unstack(sum_out, rows, heads, stacked(sum_ref, rows, heads) + result[:, :HD])

    staged(row_blocks(query_ref.shape[0], 80), start, finish)


def last_stage(routed, *refs):
    query_ref, best_ref, old_total_ref, old_sum_ref, total_ref, sum_ref = refs[:6]
    earlier_refs, refs = refs[6:-6], refs[-6:]
    direct_ref, swapped_ref, out_hbm, out_ref, trusted_ref, out_sems = refs
    heads = query_ref.shape[1] // HD
    blocks = row_blocks(query_ref.shape[0], 80)
    position, core = place()
    takes_both = (position != 0) & routed
    is_direct = core == 0

    def out_copy(index, rows):
        return pltpu.make_async_copy(out_ref.at[rows], out_hbm.at[rows], out_sems.at[index])

    def write(rows, total, weighted):
        inverse = pl.reciprocal(total, approx=True)
        inverse = inverse * (2.0 - total * inverse)
        unstack(out_ref, rows, heads, (weighted * inverse).astype(jnp.bfloat16))

    def process(shard):
        trusted = [jnp.full((8, HD), True)]
        key_rows, value_rows = shard[:, :HD], with_ones(shard[:, HD:])

        def start(rows):
            return scores_of(stacked(query_ref, rows, heads), key_rows)

        def finish(index, rows, scores):
            best = stacked(best_ref, rows, heads)
            weights = jnp.exp2(scores - widen(best, scores.shape[1])).astype(jnp.bfloat16)
            result = jnp.dot(weights, value_rows, preferred_element_type=jnp.float32)
            total = stacked(total_ref, rows, heads) + result[:, HD:]
            weighted = stacked(sum_ref, rows, heads) + result[:, :HD]
            good = (total < total_limit).reshape(total.shape[0] // 8, 8, HD)
            trusted[0] = trusted[0] & jnp.all(good, axis=0)
            write(rows, total, weighted)
            out_copy(index, rows).start()

        staged(blocks, start, finish)
        trusted_ref[0] = jnp.all(trusted[0]).astype(jnp.int32)
        for index, rows in enumerate(blocks):
            out_copy(index, rows).wait()

    @pl.when(jnp.logical_not(takes_both))
    def one_shard():
        process(jnp.where(is_direct, direct_ref[...], swapped_ref[...]))

    @pl.when(takes_both)
    def two_shards():
        process(jnp.concatenate([direct_ref[...], swapped_ref[...]], axis=0))

    @pl.when(trusted_ref[0] == 0)
    def exact_maximum():
        size = query_ref.shape[0] // len(blocks)
        counted = [(ref, 0.0) for ref in earlier_refs]
        if routed:
            counted[-2:] = [
                (ref, penalty((position == 0) | (core == by_swap)))
                for by_swap, ref in enumerate(earlier_refs[-2:])
            ]
        counted += [
            (direct_ref, penalty(takes_both | is_direct)),
            (swapped_ref, penalty(takes_both | jnp.logical_not(is_direct))),
        ]

        def visit(index, unused):
            rows = pl.ds(pl.multiple_of(index * size, size), size)
            queries = stacked(query_ref, rows, heads)
            best = stacked(best_ref, rows, heads)
            weighted = stacked(old_sum_ref, rows, heads)
            total = stacked(old_total_ref, rows, heads)
            for shard_ref, extra in counted:
                key_rows, value_rows = shard_ref[:, :HD], with_ones(shard_ref[:, HD:])
                scores = scores_of(queries, key_rows) - extra
                new_best = jnp.maximum(best, jnp.max(scores, axis=1, keepdims=True))
                factor = jnp.exp2(best - new_best)
                weights = jnp.exp2(scores - widen(new_best, scores.shape[1]))
                result = jnp.dot(
                    weights.astype(jnp.bfloat16), value_rows, preferred_element_type=jnp.float32
                )
                weighted = weighted * factor + result[:, :HD]
                total = total * factor + result[:, HD:]
                best = new_best
            write(rows, total, weighted)
            copy = out_copy(index, rows)
            copy.start()
            copy.wait()
            return unused

        lax.fori_loop(0, len(blocks), visit, 0)


def shards(queries, suffix_kv, prompt_kv, lengths):
    slots, width = queries.shape
    heads = width // HD
    loop_size = lax.axis_size("loop")
    own = prompt_kv[:, 0, :]
    suffix = suffix_kv[:, 0, :]
    shard_rows = own.shape[0]

    in_hbm = pl.BlockSpec(memory_space=pltpu.HBM)
    in_vmem = pl.BlockSpec(memory_space=pltpu.VMEM)
    state = jax.ShapeDtypeStruct((slots, width), jnp.float32)

    cost = pl.CostEstimate(flops=1, bytes_accessed=1, transcendentals=0)

    routed = loop_size >= FOUR and loop_size & (loop_size - 1) == 0

    def send(shard, route):
        hops = []
        for i in range(loop_size):
            for core in range(2):
                to, to_core = route(i, core)
                hops.append((2 * i + core, 2 * to + to_core))
        return lax.ppermute(shard, ("loop", "pair"), hops)

    def first_route(i, core):
        base = i - i % FOUR
        to, to_core = [((1, 0), (2, 0)), ((1, 1), (3, 0)), ((2, 1), (0, 0)), ((3, 1), (0, 1))][
            i % FOUR
        ][core]
        return base + to, to_core

    def second_route(i, core):
        base = i - i % FOUR
        to, to_core = [((0, 1), (3, 1)), ((0, 0), (2, 1)), ((3, 0), (1, 0)), ((2, 0), (1, 1))][
            i % FOUR
        ][core]
        return base + to, to_core

    hbm = [pltpu.with_memory_space_constraint(x, pltpu.HBM) for x in (lengths, queries, suffix, own)]
    buffers = [
        jax.ShapeDtypeStruct(queries.shape, queries.dtype),
        jax.ShapeDtypeStruct(suffix.shape, suffix.dtype),
        jax.ShapeDtypeStruct(own.shape, own.dtype),
        jax.ShapeDtypeStruct((slots, HD), jnp.int32),
    ]
    load_scratch = [
        pltpu.SMEM(lengths.shape, lengths.dtype),
        pltpu.SemaphoreType.DMA((2 + 2 * len(load_blocks(slots)),)),
    ]
    loaded = pl.pallas_call(
        prelude_stage,
        name="prelude_stage",
        out_shape=buffers,
        in_specs=[in_hbm] * 4,
        out_specs=[in_vmem] * 4,
        scratch_shapes=load_scratch,
        compiler_params=pltpu.CompilerParams(vmem_limit_bytes=8 * 2**20),
        cost_estimate=cost,
    )(*hbm)
    own, loaded = lax.optimization_barrier((own, loaded))
    if routed:
        early = [
            send(own, lambda i, core, step=step: (i ^ (step + core), 1 - core))
            for step in range(FOUR, loop_size, 2)
        ]
        early.append(send(own, first_route))
        final = send(own, second_route)
    else:
        early = [
            send(own, lambda i, core, step=step: ((i + step) % loop_size, core))
            for step in range(1, loop_size)
        ]
        final = early.pop()
    best, total, weighted, queries, *unused = pl.pallas_call(
        local_stage,
        name="local_stage",
        out_shape=[state] * 3 + buffers,
        in_specs=[in_hbm] * 4 + [in_vmem] * 4,
        out_specs=[in_vmem] * 7,
        scratch_shapes=load_scratch,
        input_output_aliases={4 + i: 3 + i for i in range(4)},
        compiler_params=pltpu.CompilerParams(vmem_limit_bytes=24 * 2**20),
        cost_estimate=cost,
    )(*hbm, *loaded)

    def add_shards(total, weighted, shards_now, by_swap):
        if not shards_now:
            return total, weighted
        return pl.pallas_call(
            functools.partial(add_stage, by_swap if routed else None),
            name="add_stage",
            out_shape=[state] * 2,
            in_specs=[in_vmem] * (4 + len(shards_now)),
            out_specs=[in_vmem] * 2,
            compiler_params=pltpu.CompilerParams(vmem_limit_bytes=24 * 2**20),
            cost_estimate=cost,
        )(queries, best, total, weighted, *shards_now)

    def swapped(shard):
        return send(shard, lambda i, core: (i, 1 - core))

    early, best = lax.optimization_barrier((early, best))
    early_swapped = [swapped(shard) for shard in early] if routed else []
    new_total, new_weighted = add_shards(total, weighted, early, False)
    final, new_total = lax.optimization_barrier((final, new_total))
    final_swapped = swapped(final) if routed else final
    new_total, new_weighted = add_shards(new_total, new_weighted, early_swapped, True)
    last_inputs = (queries, best, total, weighted, new_total, new_weighted)
    last_inputs += (*early[:-1], *early_swapped[:-1], *early[-1:], *early_swapped[-1:])
    last_inputs += (final, final_swapped)
    return pl.pallas_call(
        functools.partial(last_stage, routed),
        name="last_stage",
        out_shape=jax.ShapeDtypeStruct((slots, width), jnp.bfloat16),
        in_specs=[in_vmem] * len(last_inputs),
        out_specs=in_hbm,
        scratch_shapes=[
            pltpu.VMEM((slots, width), jnp.bfloat16),
            pltpu.SMEM((1,), jnp.int32),
            pltpu.SemaphoreType.DMA((len(row_blocks(slots, 80)),)),
        ],
        compiler_params=pltpu.CompilerParams(vmem_limit_bytes=32 * 2**20),
        cost_estimate=cost,
    )(*last_inputs)


def solution(mesh):
    placed = (
        P(("groups", "loop"), ("heads", "pair")),
        P(("groups", "loop"), "heads", None),
        P(("groups", "loop"), "heads", None),
        P("groups"),
    )
    return jax.shard_map(
        shards,
        mesh=mesh,
        in_specs=placed,
        out_specs=P(("groups", "loop"), ("heads", "pair")),
        check_vma=False,
    )
```

```python
import functools
import math

import jax
import jax.numpy as jnp
from jax import lax
from jax.experimental import pallas as pl
from jax.experimental.pallas import tpu as pltpu
from jax.sharding import PartitionSpec as P

HD = 128
AG_DEV = 2
MAXLEN = 320
BLK = 128
FOUR = 4

masked_score = -1e30
empty_best = 1e30
total_limit = 2.0**100
score_scale = math.log2(math.e) / math.sqrt(HD)


def scores_of(query_rows, key_rows):
    return (
        lax.dot_general(
            query_rows, key_rows, (((1,), (1,)), ((), ())), preferred_element_type=jnp.float32
        )
        * score_scale
    )


def with_ones(value_rows):
    return jnp.concatenate([value_rows, jnp.ones_like(value_rows)], axis=1)


def stacked(ref, rows, head_count):
    return jnp.concatenate([ref[rows, h * HD : (h + 1) * HD] for h in range(head_count)], axis=0)


def unstack(ref, rows, head_count, value):
    count = value.shape[0] // head_count
    for h in range(head_count):
        ref[rows, h * HD : (h + 1) * HD] = value[h * count : (h + 1) * count]


def widen(row_value, width):
    return jnp.concatenate([row_value] * (width // HD), axis=1)


def place():
    return lax.rem(lax.axis_index("loop"), FOUR), lax.axis_index("pair")


def load_blocks(count):
    return [pl.ds(first, BLK) for first in range(0, count, BLK)]


def load(
    lengths_hbm,
    query_hbm,
    suffix_hbm,
    own_hbm,
    query_ref,
    suffix_ref,
    own_ref,
    first_ref,
    lengths_ref,
    sems,
):
    pairs = [(lengths_hbm, lengths_ref), (own_hbm, own_ref)]
    for source, target in ((query_hbm, query_ref), (suffix_hbm, suffix_ref)):
        for rows in load_blocks(target.shape[0]):
            pairs.append((source.at[rows], target.at[rows]))
    copies = [
        pltpu.make_async_copy(source, target, sems.at[i])
        for i, (source, target) in enumerate(pairs)
    ]
    for i, copy in enumerate(copies):
        copy.start(priority=i % 2)
    copies[0].wait()
    slots = query_ref.shape[0]
    position = lax.axis_index("loop")
    row_at = lax.broadcasted_iota(jnp.int32, first_ref.shape, 0)
    first = jnp.zeros_like(row_at)
    agent_end = 0
    for agent in range(AG_DEV):
        agent_end = agent_end + lengths_ref[position * AG_DEV + agent]
        first = jnp.where(row_at >= agent_end, agent_end if agent + 1 < AG_DEV else slots, first)
    first_ref[...] = first
    for copy in copies[1:]:
        copy.wait()


def prelude_stage(*refs):
    @pl.when(is_first_chip())
    def ahead():
        load(*refs)


def local_stage(*refs):
    sources, (best_ref, total_ref, sum_ref), loaded, scratch = (
        refs[:4],
        refs[8:11],
        refs[11:15],
        refs[15:],
    )
    query_ref, suffix_ref, own_ref, first_ref = loaded

    @pl.when(jnp.logical_not(is_first_chip()))
    def now():
        load(*sources, *loaded, *scratch)

    slots = query_ref.shape[0]
    heads = query_ref.shape[1] // HD
    own_keys = own_ref[:, :HD]
    own_values = with_ones(own_ref[:, HD:])
    window = BLK * ((MAXLEN + BLK - 2) // BLK) + BLK
    for block in range(slots // BLK):
        stop = (block + 1) * BLK
        start = max(0, stop - window)
        rows = slice(block * BLK, stop)
        row_at = block * BLK + lax.broadcasted_iota(jnp.int32, (BLK, stop - start), 0)
        key_at = start + lax.broadcasted_iota(jnp.int32, (BLK, stop - start), 1)
        first = first_ref[rows]
        allowed = (key_at <= row_at) & (key_at >= widen(first, stop - start))
        queries = stacked(query_ref, rows, heads)
        own_scores = scores_of(queries, own_keys)
        suffix_scores = jnp.where(
            jnp.concatenate([allowed] * heads, axis=0),
            scores_of(queries, suffix_ref[start:stop, :HD]),
            masked_score,
        )
        best = jnp.maximum(
            jnp.max(own_scores, axis=1, keepdims=True),
            jnp.max(suffix_scores, axis=1, keepdims=True),
        )
        own_weights = jnp.exp2(own_scores - best).astype(jnp.bfloat16)
        suffix_weights = jnp.exp2(suffix_scores - best).astype(jnp.bfloat16)
        result = jnp.dot(own_weights, own_values, preferred_element_type=jnp.float32)
        result = result + jnp.dot(
            suffix_weights,
            with_ones(suffix_ref[start:stop, HD:]),
            preferred_element_type=jnp.float32,
        )
        live = jnp.concatenate([first < slots] * heads, axis=0)
        unstack(best_ref, rows, heads, jnp.where(live, best, empty_best))
        unstack(sum_ref, rows, heads, jnp.where(live, result[:, :HD], 0.0))
        unstack(total_ref, rows, heads, jnp.where(live, result[:, HD:], 1.0))


def staged(blocks, start, finish):
    coming = start(blocks[0])
    for index, rows in enumerate(blocks):
        now = coming
        if index + 1 < len(blocks):
            coming = start(blocks[index + 1])
        finish(index, rows, now)


def row_blocks(count, largest):
    step = next(size for size in (largest, 128, 16, count) if count % size == 0)
    return [slice(first, first + step) for first in range(0, count, step)]


def is_first_chip():
    return lax.axis_index("groups") + lax.axis_index("loop") + lax.axis_index("heads") == 0


def penalty(is_there):
    return jnp.where(is_there, 0.0, empty_best)


def add_stage(by_swap, *refs):
    query_ref, best_ref, total_ref, sum_ref = refs[:4]
    shard_refs = refs[4:-2]
    total_out, sum_out = refs[-2:]
    heads = query_ref.shape[1] // HD
    shard = jnp.concatenate([ref[...] for ref in shard_refs], axis=0)
    key_rows, value_rows = shard[:, :HD], with_ones(shard[:, HD:])
    extra = None
    if by_swap is not None:
        position, core = place()
        extra = penalty((position != 1) | (core == int(by_swap)))

    def start(rows):
        return scores_of(stacked(query_ref, rows, heads), key_rows)

    def finish(index, rows, scores):
        best = stacked(best_ref, rows, heads)
        if extra is None:
            points = widen(best, scores.shape[1])
        else:
            held = shard_refs[-1].shape[0]
            points = [best] * ((scores.shape[1] - held) // HD) + [best + extra] * (held // HD)
            points = jnp.concatenate(points, axis=1)
        weights = jnp.exp2(scores - points).astype(jnp.bfloat16)
        result = jnp.dot(weights, value_rows, preferred_element_type=jnp.float32)
        unstack(total_out, rows, heads, stacked(total_ref, rows, heads) + result[:, HD:])
        unstack(sum_out, rows, heads, stacked(sum_ref, rows, heads) + result[:, :HD])

    staged(row_blocks(query_ref.shape[0], 80), start, finish)


def last_stage(routed, *refs):
    query_ref, best_ref, old_total_ref, old_sum_ref, total_ref, sum_ref = refs[:6]
    earlier_refs, refs = refs[6:-6], refs[-6:]
    direct_ref, swapped_ref, out_hbm, out_ref, trusted_ref, out_sems = refs
    heads = query_ref.shape[1] // HD
    blocks = row_blocks(query_ref.shape[0], 80)
    position, core = place()
    takes_both = (position == 1) & routed
    is_direct = core == jnp.where(position == 0, 0, 1)

    def out_copy(index, rows):
        return pltpu.make_async_copy(out_ref.at[rows], out_hbm.at[rows], out_sems.at[index])

    def write(rows, total, weighted):
        inverse = pl.reciprocal(total, approx=True)
        inverse = inverse * (2.0 - total * inverse)
        unstack(out_ref, rows, heads, (weighted * inverse).astype(jnp.bfloat16))

    def process(shard):
        trusted = [jnp.full((8, HD), True)]
        key_rows, value_rows = shard[:, :HD], with_ones(shard[:, HD:])

        def start(rows):
            return scores_of(stacked(query_ref, rows, heads), key_rows)

        def finish(index, rows, scores):
            best = stacked(best_ref, rows, heads)
            weights = jnp.exp2(scores - widen(best, scores.shape[1])).astype(jnp.bfloat16)
            result = jnp.dot(weights, value_rows, preferred_element_type=jnp.float32)
            total = stacked(total_ref, rows, heads) + result[:, HD:]
            weighted = stacked(sum_ref, rows, heads) + result[:, :HD]
            good = (total < total_limit).reshape(total.shape[0] // 8, 8, HD)
            trusted[0] = trusted[0] & jnp.all(good, axis=0)
            write(rows, total, weighted)
            out_copy(index, rows).start(priority=index % 2)

        staged(blocks, start, finish)
        trusted_ref[0] = jnp.all(trusted[0]).astype(jnp.int32)
        for index, rows in enumerate(blocks):
            out_copy(index, rows).wait()

    @pl.when(jnp.logical_not(takes_both))
    def one_shard():
        process(jnp.where(is_direct, direct_ref[...], swapped_ref[...]))

    @pl.when(takes_both)
    def two_shards():
        process(jnp.concatenate([direct_ref[...], swapped_ref[...]], axis=0))

    @pl.when(trusted_ref[0] == 0)
    def exact_maximum():
        size = query_ref.shape[0] // len(blocks)
        counted = [(ref, 0.0) for ref in earlier_refs]
        if routed:
            counted[-2:] = [
                (ref, penalty((position != 1) | (core == by_swap)))
                for by_swap, ref in enumerate(earlier_refs[-2:])
            ]
        counted += [
            (direct_ref, penalty(takes_both | is_direct)),
            (swapped_ref, penalty(takes_both | jnp.logical_not(is_direct))),
        ]

        def visit(index, unused):
            rows = pl.ds(pl.multiple_of(index * size, size), size)
            queries = stacked(query_ref, rows, heads)
            best = stacked(best_ref, rows, heads)
            weighted = stacked(old_sum_ref, rows, heads)
            total = stacked(old_total_ref, rows, heads)
            for shard_ref, extra in counted:
                key_rows, value_rows = shard_ref[:, :HD], with_ones(shard_ref[:, HD:])
                scores = scores_of(queries, key_rows) - extra
                new_best = jnp.maximum(best, jnp.max(scores, axis=1, keepdims=True))
                factor = jnp.exp2(best - new_best)
                weights = jnp.exp2(scores - widen(new_best, scores.shape[1]))
                result = jnp.dot(
                    weights.astype(jnp.bfloat16), value_rows, preferred_element_type=jnp.float32
                )
                weighted = weighted * factor + result[:, :HD]
                total = total * factor + result[:, HD:]
                best = new_best
            write(rows, total, weighted)
            copy = out_copy(index, rows)
            copy.start()
            copy.wait()
            return unused

        lax.fori_loop(0, len(blocks), visit, 0)


def shards(queries, suffix_kv, prompt_kv, lengths):
    slots, width = queries.shape
    heads = width // HD
    loop_size = lax.axis_size("loop")
    own = prompt_kv[:, 0, :]
    suffix = suffix_kv[:, 0, :]
    shard_rows = own.shape[0]

    in_hbm = pl.BlockSpec(memory_space=pltpu.HBM)
    in_vmem = pl.BlockSpec(memory_space=pltpu.VMEM)
    state = jax.ShapeDtypeStruct((slots, width), jnp.float32)

    cost = pl.CostEstimate(flops=1, bytes_accessed=1, transcendentals=0)

    routed = loop_size >= FOUR and loop_size & (loop_size - 1) == 0

    def send(shard, route):
        hops = []
        for i in range(loop_size):
            for core in range(2):
                to, to_core = route(i, core)
                hops.append((2 * i + core, 2 * to + to_core))
        return lax.ppermute(shard, ("loop", "pair"), hops)

    def first_route(i, core):
        base = i - i % FOUR
        to, to_core = [((1, 0), (3, 1)), ((1, 1), (2, 0)), ((3, 0), (0, 0)), ((2, 1), (0, 1))][
            i % FOUR
        ][core]
        return base + to, to_core

    def second_route(i, core):
        base = i - i % FOUR
        to, to_core = [((0, 1), (2, 1)), ((0, 0), (3, 1)), ((3, 0), (1, 0)), ((2, 0), (1, 1))][
            i % FOUR
        ][core]
        return base + to, to_core

    hbm = [pltpu.with_memory_space_constraint(x, pltpu.HBM) for x in (lengths, queries, suffix, own)]
    buffers = [
        jax.ShapeDtypeStruct(queries.shape, queries.dtype),
        jax.ShapeDtypeStruct(suffix.shape, suffix.dtype),
        jax.ShapeDtypeStruct(own.shape, own.dtype),
        jax.ShapeDtypeStruct((slots, HD), jnp.int32),
    ]
    load_scratch = [
        pltpu.SMEM(lengths.shape, lengths.dtype),
        pltpu.SemaphoreType.DMA((2 + 2 * len(load_blocks(slots)),)),
    ]
    loaded = pl.pallas_call(
        prelude_stage,
        name="prelude_stage",
        out_shape=buffers,
        in_specs=[in_hbm] * 4,
        out_specs=[in_vmem] * 4,
        scratch_shapes=load_scratch,
        compiler_params=pltpu.CompilerParams(vmem_limit_bytes=8 * 2**20),
        cost_estimate=cost,
    )(*hbm)
    own, loaded = lax.optimization_barrier((own, loaded))
    if routed:
        early = [
            send(own, lambda i, core, step=step: (i ^ (step + core), 1 - core))
            for step in range(FOUR, loop_size, 2)
        ]
        early.append(send(own, first_route))
        final = send(own, second_route)
    else:
        early = [
            send(own, lambda i, core, step=step: ((i + step) % loop_size, core))
            for step in range(1, loop_size)
        ]
        final = early.pop()
    best, total, weighted, queries, *unused = pl.pallas_call(
        local_stage,
        name="local_stage",
        out_shape=[state] * 3 + buffers,
        in_specs=[in_hbm] * 4 + [in_vmem] * 4,
        out_specs=[in_vmem] * 7,
        scratch_shapes=load_scratch,
        input_output_aliases={4 + i: 3 + i for i in range(4)},
        compiler_params=pltpu.CompilerParams(vmem_limit_bytes=24 * 2**20),
        cost_estimate=cost,
    )(*hbm, *loaded)

    def add_shards(total, weighted, shards_now, by_swap):
        if not shards_now:
            return total, weighted
        return pl.pallas_call(
            functools.partial(add_stage, by_swap if routed else None),
            name="add_stage",
            out_shape=[state] * 2,
            in_specs=[in_vmem] * (4 + len(shards_now)),
            out_specs=[in_vmem] * 2,
            compiler_params=pltpu.CompilerParams(vmem_limit_bytes=24 * 2**20),
            cost_estimate=cost,
        )(queries, best, total, weighted, *shards_now)

    def swapped(shard):
        return send(shard, lambda i, core: (i, 1 - core))

    early, best = lax.optimization_barrier((early, best))
    early_swapped = [swapped(shard) for shard in early] if routed else []
    new_total, new_weighted = add_shards(total, weighted, early, False)
    final, new_total = lax.optimization_barrier((final, new_total))
    final_swapped = swapped(final) if routed else final
    new_total, new_weighted = add_shards(new_total, new_weighted, early_swapped, True)
    last_inputs = (queries, best, total, weighted, new_total, new_weighted)
    last_inputs += (*early[:-1], *early_swapped[:-1], *early[-1:], *early_swapped[-1:])
    last_inputs += (final, final_swapped)
    return pl.pallas_call(
        functools.partial(last_stage, routed),
        name="last_stage",
        out_shape=jax.ShapeDtypeStruct((slots, width), jnp.bfloat16),
        in_specs=[in_vmem] * len(last_inputs),
        out_specs=in_hbm,
        scratch_shapes=[
            pltpu.VMEM((slots, width), jnp.bfloat16),
            pltpu.SMEM((1,), jnp.int32),
            pltpu.SemaphoreType.DMA((len(row_blocks(slots, 80)),)),
        ],
        compiler_params=pltpu.CompilerParams(vmem_limit_bytes=32 * 2**20),
        cost_estimate=cost,
    )(*last_inputs)


def solution(mesh):
    placed = (
        P(("groups", "loop"), ("heads", "pair")),
        P(("groups", "loop"), "heads", None),
        P(("groups", "loop"), "heads", None),
        P("groups"),
    )
    return jax.shard_map(
        shards,
        mesh=mesh,
        in_specs=placed,
        out_specs=P(("groups", "loop"), ("heads", "pair")),
        check_vma=False,
    )
```
